32 devices in a mesh: seq: 1, ctx: 16 (over z, y, x), wsh: 2 (over core).
Axes of the slice: x: 2, y: 2, z: 4, core: 2. Of those that a mesh axis runs over, the one named last changes fastest.
Arguments:
- tokens: bfloat16 [4096, 1472], P(('seq', 'ctx', 'wsh')), may hold values from -6 to 6
- encoded: bfloat16 [2048, 1472], P(('seq', 'ctx', 'wsh')), may hold values from -6 to 6
- cotangent: bfloat16 [4096, 1472], P(('seq', 'ctx', 'wsh')), may hold values from -6 to 6
- assign: int32 [16], replicated, may hold values from 0 to 15, each once
- bucket_ids: int32 [4096], replicated, may hold values from 0 to 31, never falling along the last dimension, each value on 1 to 512 neighbouring positions
- gain_self: bfloat16 [1472], P('wsh'), may hold values from 0.5 to 1.5
- gain_cross: bfloat16 [1472], P('wsh'), may hold values from 0.5 to 1.5
- gain_ffn: bfloat16 [1472], P('wsh'), may hold values from 0.5 to 1.5
- query_weight: bfloat16 [1472, 384], P('wsh'), may hold values from -0.078125 to 0.078125
- key_weight: bfloat16 [1472, 384], P('wsh'), may hold values from -0.078125 to 0.078125
- value_weight: bfloat16 [1472, 384], P('wsh'), may hold values from -0.15625 to 0.15625
- out_weight: bfloat16 [384, 1472], P('wsh'), may hold values from -1.5 to 1.5
- cross_query: bfloat16 [1472, 384], P('wsh'), may hold values from -0.078125 to 0.078125
- cross_key: bfloat16 [1472, 384], P('wsh'), may hold values from -0.078125 to 0.078125
- cross_value: bfloat16 [1472, 384], P('wsh'), may hold values from -0.15625 to 0.15625
- cross_out: bfloat16 [384, 1472], P('wsh'), may hold values from -2 to 2
- gate_weight: bfloat16 [1472, 3584], P('wsh'), may hold values from -0.15625 to 0.15625
- up_weight: bfloat16 [1472, 3584], P('wsh'), may hold values from -0.15625 to 0.15625
- down_weight: bfloat16 [3584, 1472], P('wsh'), may hold values from -0.09375 to 0.09375
- bucket_table: bfloat16 [32, 6], replicated, may hold values from -4 to 4
Outputs:
- output: bfloat16 [4096, 1472], P(('seq', 'ctx', 'wsh'))
- tokens_grad: float32 [4096, 1472], P(('seq', 'ctx', 'wsh'))
- encoded_grad: float32 [2048, 1472], P(('seq', 'ctx', 'wsh'))
- gain_self_grad: float32 [1472], P('seq')
- gain_cross_grad: float32 [1472], P('seq')
- gain_ffn_grad: float32 [1472], P('seq')
- query_weight_grad: float32 [1472, 384], P('seq', ('ctx', 'wsh'))
- key_weight_grad: float32 [1472, 384], P('seq', ('ctx', 'wsh'))
- value_weight_grad: float32 [1472, 384], P('seq', ('ctx', 'wsh'))
- out_weight_grad: float32 [384, 1472], P(('seq', 'ctx', 'wsh'))
- cross_query_grad: float32 [1472, 384], P('seq', ('ctx', 'wsh'))
- cross_key_grad: float32 [1472, 384], P('seq', ('ctx', 'wsh'))
- cross_value_grad: float32 [1472, 384], P('seq', ('ctx', 'wsh'))
- cross_out_grad: float32 [384, 1472], P(('seq', 'ctx', 'wsh'))
- gate_weight_grad: float32 [1472, 3584], P('seq', ('ctx', 'wsh'))
- up_weight_grad: float32 [1472, 3584], P('seq', ('ctx', 'wsh'))
- down_weight_grad: float32 [3584, 1472], P(('seq', 'ctx', 'wsh'))
- bucket_table_grad: float32 [32, 6], P('seq')
The draws below stay inside these ranges and needn't reach their ends.
Inputs may be any that keep to these rules, and one draw needn't show every extreme that they name: `assign`: each early block 0 to 15 belongs to exactly one index of ctx, which also holds block 31 minus it. `bucket_ids`: starts at 0 and never falls as the distance grows; every bucket covers 1 to 512 consecutive distances, one exactly that many.
All inputs are finite; a program needn't handle non-finite values.
Results may differ from the reference program's by a relative error of at most 0.03.
The reference program's roundings to bfloat16 on the way count: a program that leaves them out, or rounds other values in their place, can miss the bound.
Values may be sent and summed in bfloat16 or wider, within the bound.
No kernel may reach another device: no remote copies, remote signals or barrier semaphores. Data moves between devices by JAX's collectives and lax.ppermute only.
A program may use at most 320 MiB of HBM per device.

```python
import math
import jax
import jax.numpy as jnp
import numpy as np
from jax import lax

D = 1472
HEADS = 6
DK = 64
FF = 3584
BUCKETS = 32
TOK_DEV = 128
ENC = 2048
INNER = 384
SEQ = 4096
BLOCK = 128
N_CTX = 16
N_WSH = 2


def block_scale(own_key, shape, pieces, low, top_value):
    def one(axis_at, blocks):
        heights = jax.random.uniform(jax.random.fold_in(jax.random.fold_in(own_key, 6), axis_at), (blocks,), jnp.float32, low / len(pieces), top_value / len(pieces))
        return jnp.repeat(jnp.exp(heights), shape[axis_at] // blocks).reshape((-1,) + (1,) * (len(shape) - axis_at - 1))

    factor_of = one(*pieces[0])
    for cut in pieces[1:]:
        factor_of = factor_of * one(*cut)
    return factor_of


def split_up(number_of, total, limit, skew):
    weights = [(1 << 20) // math.isqrt(rank ** skew) + 1 for rank in range(2, number_of + 1)]
    spare, counts = total - limit - (number_of - 1), [1] * (number_of - 1)
    while spare > 0:
        free = [i for i in range(number_of - 1) if counts[i] < limit]
        whole, left = sum([weights[i] for i in free]), spare
        for i in free:
            addition = min(limit - counts[i], max(1, left * weights[i] // whole), spare)
            counts[i] = counts[i] + addition
            spare = spare - addition
    return np.array([limit] + counts)


def ragged(stream_key, amount, total, bound, lean):
    if amount == 2:
        one = jax.random.randint(stream_key, (), max(1, total - bound), min(bound, total - 1) + 1)
        return jnp.stack([one, total - one])
    lengths = jnp.asarray(split_up(amount, total, bound, lean), jnp.int32)
    pairs = (amount - 1) // 2
    giver, receiver = lengths[1:1 + 2 * pairs:2], lengths[2:2 + 2 * pairs:2]
    margin = jnp.minimum(giver - 1, bound - receiver)
    passed = jax.random.randint(jax.random.fold_in(stream_key, 1), (pairs,), 0, 1 << 20) % (margin + 1)
    lengths = lengths.at[1:1 + 2 * pairs:2].set(giver - passed).at[2:2 + 2 * pairs:2].set(receiver + passed)
    return lengths[jax.random.permutation(jax.random.fold_in(stream_key, 2), amount)]


def noise(key, shape, deviation, limit, split=(), kind=jnp.bfloat16):
    values = deviation * jax.random.normal(key, shape, jnp.float32)
    if split:
        values = values * block_scale(key, shape, split, -0.22, 0.18)
    return jnp.clip(values, -limit, limit).astype(kind)


def setup_inputs(seed: int = 0, part: int = 0) -> dict:
    streams_of = jax.random.split(jax.random.key(seed), 21)
    part_keys = jax.random.split(jax.random.fold_in(streams_of[20], part), 21)
    tokens = noise(part_keys[0], (SEQ, D), 1.0, 6.0, ((0, 32),))
    encoded = noise(part_keys[1], (ENC, D), 1.0, 6.0, ((0, 32),))
    cotangent = noise(part_keys[2], (SEQ, D), 1.0, 6.0, ((0, 32),))
    assign = jax.random.permutation(streams_of[3], N_CTX).astype(jnp.int32)
    bucket_ids = jnp.searchsorted(jnp.cumsum(ragged(streams_of[4], BUCKETS, SEQ, SEQ // 8, 2)), jnp.arange(SEQ), side="right").astype(jnp.int32)
    gain_self = jnp.clip(1.0 + 0.1 * jax.random.normal(streams_of[5], (D,), jnp.float32), 0.5, 1.5).astype(jnp.bfloat16)
    gain_cross = jnp.clip(1.0 + 0.1 * jax.random.normal(streams_of[6], (D,), jnp.float32), 0.5, 1.5).astype(jnp.bfloat16)
    gain_ffn = jnp.clip(1.0 + 0.1 * jax.random.normal(streams_of[7], (D,), jnp.float32), 0.5, 1.5).astype(jnp.bfloat16)
    query_weight = noise(streams_of[8], (D, INNER), (4 * D) ** -0.5, 0.078125, ((0, 2),))
    key_weight = noise(streams_of[9], (D, INNER), (4 * D) ** -0.5, 0.078125, ((0, 2),))
    value_weight = noise(streams_of[10], (D, INNER), D ** -0.5, 0.15625, ((0, 2),))
    out_weight = noise(streams_of[11], (INNER, D), 16 ** -0.5, 1.5, ((0, 2),))
    cross_query = noise(streams_of[12], (D, INNER), (4 * D) ** -0.5, 0.078125, ((0, 2),))
    cross_key = noise(streams_of[13], (D, INNER), (4 * D) ** -0.5, 0.078125, ((0, 2),))
    cross_value = noise(streams_of[14], (D, INNER), D ** -0.5, 0.15625, ((0, 2),))
    cross_out = noise(streams_of[15], (INNER, D), 8 ** -0.5, 2.0, ((0, 2),))
    gate_weight = noise(streams_of[16], (D, FF), D ** -0.5, 0.15625, ((0, 2),))
    up_weight = noise(streams_of[17], (D, FF), D ** -0.5, 0.15625, ((0, 2),))
    down_weight = noise(streams_of[18], (FF, D), FF ** -0.5, 0.09375, ((0, 2),))
    bucket_table = noise(streams_of[19], (BUCKETS, HEADS), 1.0, 4.0)
    return {"tokens": tokens, "encoded": encoded, "cotangent": cotangent, "assign": assign, "bucket_ids": bucket_ids, "gain_self": gain_self, "gain_cross": gain_cross, "gain_ffn": gain_ffn, "query_weight": query_weight, "key_weight": key_weight, "value_weight": value_weight, "out_weight": out_weight, "cross_query": cross_query, "cross_key": cross_key, "cross_value": cross_value, "cross_out": cross_out, "gate_weight": gate_weight, "up_weight": up_weight, "down_weight": down_weight, "bucket_table": bucket_table}


@jax.custom_vjp
def low(v):
    return lax.optimization_barrier(v.astype(jnp.bfloat16)).astype(jnp.float32)

@jax.custom_vjp
def low_back(v):
    return v

def low_keep(v):
    return (low(v), None)

def low_pass(kept, grad):
    return (grad,)

def back_keep(v):
    return (v, None)

def back_low(kept, grad):
    return (low(grad),)
low.defvjp(low_keep, low_pass)
low_back.defvjp(back_keep, back_low)
EPS = 1e-06
NEG = -1e+30
HIGH = lax.Precision.HIGHEST

def product(first_op, second_op):
    return jnp.dot(first_op, second_op, precision=HIGH, preferred_element_type=jnp.float32)

def root_norm(inputs, gain_vec):
    return inputs * lax.rsqrt(lax.optimization_barrier(jnp.mean(inputs * inputs, axis=-1, keepdims=True)) + EPS) * gain_vec

def split_heads(matrix):
    return jnp.transpose(matrix.reshape(matrix.shape[0], HEADS, DK), (1, 0, 2))

def join_heads(tensor):
    return jnp.transpose(tensor, (1, 0, 2)).reshape(tensor.shape[1], HEADS * DK)

def device_positions(assign):
    half_rows = TOK_DEV // 2
    rows_all = jnp.arange(SEQ, dtype=jnp.int32)
    device = rows_all // TOK_DEV
    inside = rows_all % TOK_DEV
    ctx_lane = device // N_WSH
    wsh_lane = device % N_WSH
    early_block = jnp.take(assign, ctx_lane)
    block_all = jnp.where(inside >= half_rows, 2 * N_CTX - 1 - early_block, early_block)
    return (block_all * BLOCK + wsh_lane * half_rows + inside % half_rows).astype(jnp.int32)

def attend_self(queries, keys, values, table, bucket_ids):
    query_h = split_heads(queries)
    key_h = split_heads(keys)
    value_h = split_heads(values)
    row_span = min(256, SEQ)
    block_count = SEQ // row_span
    blocks = jnp.transpose(query_h.reshape(HEADS, block_count, row_span, DK), (1, 0, 2, 3))
    offsets = jnp.arange(block_count, dtype=jnp.int32) * row_span
    key_pos = jnp.arange(SEQ, dtype=jnp.int32)

    def one_block(inputs):
        query_block, offset = inputs
        distance = offset + jnp.arange(row_span, dtype=jnp.int32)[:, None] - key_pos[None, :]
        bucket = jnp.take(bucket_ids, jnp.maximum(distance, 0))
        rel_bias = jnp.transpose(jnp.take(table, bucket, axis=0), (2, 0, 1))
        scores = jnp.einsum('hqd,hkd->hqk', query_block, key_h, precision=HIGH) + rel_bias
        scores = jnp.where((distance >= 0)[None], low_back(scores), NEG)
        prob_tile = jax.nn.softmax(scores, axis=-1)
        return jnp.einsum('hqk,hkd->hqd', low(prob_tile), value_h, precision=HIGH)
    outputs = lax.map(jax.checkpoint(one_block), (blocks, offsets))
    return jnp.transpose(outputs, (1, 0, 2, 3)).reshape(HEADS, SEQ, DK)

def attend_cross(queries, keys, values):
    query_h = split_heads(queries)
    key_h = split_heads(keys)
    value_h = split_heads(values)
    row_span = min(256, SEQ)
    block_count = SEQ // row_span
    blocks = jnp.transpose(query_h.reshape(HEADS, block_count, row_span, DK), (1, 0, 2, 3))

    def one_block(query_block):
        scores = low_back(jnp.einsum('hqd,hkd->hqk', query_block, key_h, precision=HIGH))
        prob_tile = jax.nn.softmax(scores, axis=-1)
        return jnp.einsum('hqk,hkd->hqd', low(prob_tile), value_h, precision=HIGH)
    outputs = lax.map(jax.checkpoint(one_block), blocks)
    return jnp.transpose(outputs, (1, 0, 2, 3)).reshape(HEADS, SEQ, DK)

def forward(x_rows, enc_rows, gain_self, gain_cross, gain_ffn, query_weight, key_weight, value_weight, out_weight, cross_query, cross_key, cross_value, cross_out, gate_weight, up_weight, down_weight, bucket_table, bucket_ids):
    normed = low(root_norm(x_rows, gain_self))
    queries = low(low_back(product(normed, query_weight)))
    keys = low(low_back(product(normed, key_weight)))
    values = low(low_back(product(normed, value_weight)))
    attended = low(low_back(join_heads(attend_self(queries, keys, values, bucket_table, bucket_ids))))
    hidden_one = x_rows + low_back(product(attended, out_weight))
    normed = low(root_norm(hidden_one, gain_cross))
    cross_queries = low(low_back(product(normed, cross_query)))
    enc_keys = low(low_back(product(enc_rows, cross_key)))
    enc_values = low(low_back(product(enc_rows, cross_value)))
    attended = low(low_back(join_heads(attend_cross(cross_queries, enc_keys, enc_values))))
    hidden_two = hidden_one + low_back(product(attended, cross_out))
    normed = low(root_norm(hidden_two, gain_ffn))
    gate = low_back(product(normed, gate_weight))
    up_proj = low_back(product(normed, up_weight))
    activated = low(jax.nn.gelu(gate, approximate=True) * up_proj)
    return hidden_two + low_back(product(activated, down_weight))

def reference(tokens, encoded, cotangent, assign, bucket_ids, gain_self, gain_cross, gain_ffn, query_weight, key_weight, value_weight, out_weight, cross_query, cross_key, cross_value, cross_out, gate_weight, up_weight, down_weight, bucket_table):
    position = device_positions(assign)
    order = jnp.argsort(position).astype(jnp.int32)
    floats = (tokens.astype(jnp.float32)[order], encoded.astype(jnp.float32), gain_self.astype(jnp.float32), gain_cross.astype(jnp.float32), gain_ffn.astype(jnp.float32), query_weight.astype(jnp.float32), key_weight.astype(jnp.float32), value_weight.astype(jnp.float32), out_weight.astype(jnp.float32), cross_query.astype(jnp.float32), cross_key.astype(jnp.float32), cross_value.astype(jnp.float32), cross_out.astype(jnp.float32), gate_weight.astype(jnp.float32), up_weight.astype(jnp.float32), down_weight.astype(jnp.float32), bucket_table.astype(jnp.float32))

    def layer(*members):
        return forward(*members, bucket_ids)
    result, pullback = jax.vjp(layer, *floats)
    grads = pullback(cotangent.astype(jnp.float32)[order])
    return (result[position].astype(jnp.bfloat16), grads[0][position], grads[1], grads[2], grads[3], grads[4], grads[5], grads[6], grads[7], grads[8], grads[9], grads[10], grads[11], grads[12], grads[13], grads[14], grads[15], grads[16])
```

```python
import functools

import jax
import jax.numpy as jnp
from jax import lax
from jax.experimental import pallas as pl
from jax.experimental.pallas import tpu as pltpu
from jax.sharding import PartitionSpec as P

EPS = 1e-06
NEG = -1e30
F32 = jnp.float32
BF = jnp.bfloat16
BLK = 128
GRP = 4
CH = BLK * GRP
VLIM = 60 * 1024 * 1024


def dot(a, b):
    return lax.dot_general(a, b, (((1,), (0,)), ((), ())), preferred_element_type=F32)


def dot_nt(a, b):
    return lax.dot_general(a, b, (((1,), (1,)), ((), ())), preferred_element_type=F32)


def dot_tn(a, b):
    return lax.dot_general(a, b, (((0,), (0,)), ((), ())), preferred_element_type=F32)


def lane_of(shape):
    return lax.broadcasted_iota(jnp.int32, shape, 1)


def head_mask(value, head, hs):
    lane = lane_of(value.shape)
    keep = (lane >= head * hs) & (lane < (head + 1) * hs)
    return jnp.where(keep, value, jnp.zeros_like(value))


def lane_fold(value, op):
    out = value[:, :BLK]
    for i in range(1, value.shape[1] // BLK):
        out = op(out, value[:, i * BLK : (i + 1) * BLK])
    return out


def pieces_into(base, columns, first):
    lane = lane_of(base.shape)
    out = base
    for i, column in enumerate(columns):
        rest = column
        for j in range(3):
            part = rest.astype(BF).astype(F32)
            rest = rest - part
            out = jnp.where(lane == first + 3 * i + j, part, out)
    return out


def params(flops, nbytes, trans):
    return dict(
        compiler_params=pltpu.CompilerParams(vmem_limit_bytes=VLIM),
        cost_estimate=pl.CostEstimate(
            flops=int(flops), bytes_accessed=int(nbytes), transcendentals=int(trans)
        ),
    )


VM = pl.BlockSpec(memory_space=pltpu.VMEM)
SM = pl.BlockSpec(memory_space=pltpu.SMEM)


def bias_kernel(nb, nh, nat_ref, rev_ref, ts_ref, tt_ref):
    r = pl.program_id(0)
    row = lax.broadcasted_iota(jnp.int32, (BLK, BLK), 0)
    col = lax.broadcasted_iota(jnp.int32, (BLK, BLK), 1)

    def skew(first, second):
        line = jnp.concatenate([first, second], axis=1)
        spread = jnp.broadcast_to(line, (BLK, 2 * BLK))
        return pltpu.roll(spread, 0, 1, stride=1, stride_axis=0)[:, :BLK]

    d = nb - 1 - r
    dc = jnp.maximum(d, 0)
    a_all, b_all = rev_ref[nb - dc], rev_ref[nb - dc - 1]
    for h in range(nh):
        tile = skew(a_all[h : h + 1], b_all[h : h + 1])
        tile = jnp.where(d * BLK + row - col >= 0, tile, NEG)
        ts_ref[0, h] = tile.astype(BF)
    d = r - (GRP - 1)
    dc = jnp.maximum(d, 0)
    a_all, b_all = nat_ref[dc + 1], nat_ref[dc]
    for h in range(nh):
        tile = skew(a_all[h : h + 1], b_all[h : h + 1])
        tile = jnp.where(d * BLK + col - row >= 0, tile, NEG)
        tt_ref[0, h] = tile.astype(BF)


def bias_tiles(values):
    nh, length = values.shape
    nb = length // BLK
    zero = jnp.zeros((nh, 1), F32)
    nat = jnp.concatenate([jnp.zeros((nh, BLK), F32), values], axis=1)
    rev = jnp.concatenate([zero, jnp.flip(values, 1), jnp.zeros((nh, BLK - 1), F32)], axis=1)
    nat = jnp.transpose(nat.reshape(nh, nb + 1, BLK), (1, 0, 2))
    rev = jnp.transpose(rev.reshape(nh, nb + 1, BLK), (1, 0, 2))
    rows = nb + GRP - 1
    shape = jax.ShapeDtypeStruct((rows, nh, BLK, BLK), BF)
    spec = pl.BlockSpec((1, nh, BLK, BLK), lambda r: (r, 0, 0, 0))
    return pl.pallas_call(
        functools.partial(bias_kernel, nb, nh),
        grid=(rows,),
        in_specs=[VM, VM],
        out_specs=[spec, spec],
        out_shape=[shape, shape],
        **params(0, 4 * rows * nh * BLK * BLK, 0),
    )(nat, rev)


def gather_blocks(ref, meta_ref, nctx, first, lo, hi):
    parts = []
    for i in range(GRP):
        t = first + i
        early = t < nctx
        slot = meta_ref[jnp.where(early, t, 2 * nctx - 1 - t)]
        parts.append(ref[2 * slot + jnp.where(early, 0, 1), :, lo:hi])
    return jnp.concatenate(parts, axis=0)


def bias_of(ref, first, h):
    return jnp.concatenate([ref[first + i, h] for i in range(GRP)], axis=1).astype(F32)


def self_fwd_kernel(
    nctx, nh, hs, meta_ref, q_ref, kv_ref, ts_ref, o_ref, qe_ref, lse_ref, s_ref, acc_ref
):
    nb = 2 * nctx
    wide = nh * hs
    early = meta_ref[nctx]
    for half in range(2):
        blk = early if half == 0 else nb - 1 - early
        chunks = blk // GRP + 1
        q = q_ref[half * BLK : (half + 1) * BLK, :]
        qm = [head_mask(q, h, hs) for h in range(nh)]

        def score(ch, tops):
            keys = gather_blocks(kv_ref, meta_ref, nctx, ch * GRP, 0, 2 * BLK)
            out = []
            for h in range(nh):
                s = dot_nt(qm[h], keys) + bias_of(ts_ref, nb - 1 - blk + ch * GRP, h)
                s_ref[ch, h] = s
                out.append(jnp.maximum(tops[h], lane_fold(s, jnp.maximum)))
            return tuple(out)

        tops = lax.fori_loop(
            0, chunks, score, tuple(jnp.full((BLK, BLK), NEG, F32) for _ in range(nh))
        )
        tops = [jnp.max(t, axis=1, keepdims=True) for t in tops]
        acc_ref[...] = jnp.zeros_like(acc_ref)

        def weigh(ch, sums):
            vals = gather_blocks(kv_ref, meta_ref, nctx, ch * GRP, BLK, 3 * BLK)
            out = []
            for h in range(nh):
                p = jnp.exp(s_ref[ch, h] - tops[h])
                out.append(sums[h] + lane_fold(p, jnp.add))
                acc_ref[h] += dot(p.astype(BF), vals)
            return tuple(out)

        sums = lax.fori_loop(
            0, chunks, weigh, tuple(jnp.zeros((BLK, BLK), F32) for _ in range(nh))
        )
        sums = [jnp.sum(t, axis=1, keepdims=True) for t in sums]
        total = jnp.zeros((BLK, 2 * BLK), F32)
        for h in range(nh):
            total = total + head_mask(acc_ref[h] / sums[h], h + 1, hs)
        rows = slice(half * BLK, (half + 1) * BLK)
        o_ref[rows, :] = pltpu.roll(total, 2 * BLK - hs, 1)
        lse = [tops[h] + jnp.log(sums[h]) for h in range(nh)]
        lane = lane_of((BLK, BLK))
        cols = jnp.zeros((BLK, BLK), F32)
        for h in range(nh):
            cols = jnp.where(lane == h, lse[h], cols)
        lse_ref[rows, :] = cols
        qe_ref[rows, :] = pieces_into(q.astype(F32), [-t for t in lse], wide).astype(BF)


def self_fwd(meta, q, kv, ts, nh, hs):
    nb = kv.shape[0]
    nctx = nb // 2
    pairs = (nb + 1) * BLK * BLK * nh
    return pl.pallas_call(
        functools.partial(self_fwd_kernel, nctx, nh, hs),
        in_specs=[SM, VM, VM, VM],
        out_specs=[VM, VM, VM],
        out_shape=[
            jax.ShapeDtypeStruct((2 * BLK, 2 * BLK), F32),
            jax.ShapeDtypeStruct((2 * BLK, 2 * BLK), BF),
            jax.ShapeDtypeStruct((2 * BLK, BLK), F32),
        ],
        scratch_shapes=[
            pltpu.VMEM((nb // GRP, nh, BLK, CH), F32),
            pltpu.VMEM((nh, BLK, 2 * BLK), F32),
        ],
        **params(pairs * 2 * 512, 10e6, pairs),
    )(meta, q, kv, ts)


def self_dq_kernel(
    nctx, nh, hs, meta_ref, q_ref, da_ref, lse_ref, del_ref, kv_ref, ts_ref, dq_ref, rev_ref, acc_ref
):
    nb = 2 * nctx
    early = meta_ref[nctx]
    rev_ref[...] = jnp.zeros_like(rev_ref)
    row = lax.broadcasted_iota(jnp.int32, (BLK, BLK), 0)
    col = lax.broadcasted_iota(jnp.int32, (BLK, BLK), 1)
    flip = (row + col == BLK - 1).astype(BF)
    for half in range(2):
        blk = early if half == 0 else nb - 1 - early
        chunks = blk // GRP + 1
        rows = slice(half * BLK, (half + 1) * BLK)
        q = q_ref[rows, :]
        da = da_ref[rows, :]
        qm = [head_mask(q, h, hs) for h in range(nh)]
        dm = [head_mask(da, h + 1, hs) for h in range(nh)]
        lse = [lse_ref[rows, h : h + 1] for h in range(nh)]
        delta = [del_ref[rows, h : h + 1] for h in range(nh)]
        acc_ref[...] = jnp.zeros_like(acc_ref)

        def step(ch, carry):
            both = gather_blocks(kv_ref, meta_ref, nctx, ch * GRP, 0, 3 * BLK)
            keys, vals = both[:, : 2 * BLK], both[:, BLK:]
            off = pl.multiple_of((ch * GRP - blk + nb - 1) * BLK, BLK)
            for h in range(nh):
                s = dot_nt(qm[h], keys) + bias_of(ts_ref, nb - 1 - blk + ch * GRP, h)
                p = jnp.exp(s - lse[h])
                ds = (p * (dot_nt(dm[h], vals) - delta[h])).astype(BF)
                acc_ref[h] += dot(ds, keys)
                flat = jnp.concatenate([dot(flip, ds), jnp.zeros((BLK, BLK), F32)], axis=1)
                flat = pltpu.roll(flat, 0, 1, stride=1, stride_axis=0)
                line = jnp.sum(flat.reshape(BLK // 8, 8, CH + BLK), axis=0)
                rev_ref[h * 8 : (h + 1) * 8, pl.ds(off, CH + BLK)] += line
            return carry

        lax.fori_loop(0, chunks, step, 0)
        total = jnp.zeros((BLK, 2 * BLK), F32)
        for h in range(nh):
            total = total + head_mask(acc_ref[h], h, hs)
        dq_ref[rows, :] = total.astype(BF)


def self_dq(meta, q, da, lse, delta, kv, ts, nh, hs):
    nb = kv.shape[0]
    pairs = (nb + 1) * BLK * BLK * nh
    return pl.pallas_call(
        functools.partial(self_dq_kernel, nb // 2, nh, hs),
        in_specs=[SM] + [VM] * 6,
        out_specs=[VM, VM],
        out_shape=[
            jax.ShapeDtypeStruct((2 * BLK, 2 * BLK), BF),
            jax.ShapeDtypeStruct((8 * nh, nb * BLK + CH), F32),
        ],
        scratch_shapes=[pltpu.VMEM((nh, BLK, 2 * BLK), F32)],
        **params(pairs * 2 * 896, 10e6, pairs),
    )(meta, q, da, lse, delta, kv, ts)


def self_dkv_kernel(
    nctx, nh, hs, meta_ref, k_ref, v_ref, qg_ref, dg_ref, tt_ref, dk_ref, dv_ref, ka_ref, va_ref
):
    nb = 2 * nctx
    wide = nh * hs
    early = meta_ref[nctx]

    def extended(value, h):
        lane = lane_of(value.shape)
        first = wide + 3 * h
        ones = (lane >= first) & (lane < first + 3)
        return jnp.where(ones, jnp.ones_like(value), head_mask(value, h, hs))

    for half in range(2):
        blk = early if half == 0 else nb - 1 - early
        rows = slice(half * BLK, (half + 1) * BLK)
        km = [extended(k_ref[rows, :], h) for h in range(nh)]
        vm = [extended(v_ref[rows, :], h) for h in range(nh)]
        ka_ref[...] = jnp.zeros_like(ka_ref)
        va_ref[...] = jnp.zeros_like(va_ref)

        def step(ch, carry):
            qc = gather_blocks(qg_ref, meta_ref, nctx, ch * GRP, 0, 2 * BLK)
            dc = gather_blocks(dg_ref, meta_ref, nctx, ch * GRP, 0, 2 * BLK)
            for h in range(nh):
                s = dot_nt(km[h], qc) + bias_of(tt_ref, ch * GRP - blk + GRP - 1, h)
                p = jnp.exp(s)
                ds = (p * dot_nt(vm[h], dc)).astype(BF)
                ka_ref[h] += dot(ds, qc)
                va_ref[h] += dot(p.astype(BF), dc)
            return carry

        lax.fori_loop(blk // GRP, nb // GRP, step, 0)
        dk = jnp.zeros((BLK, 2 * BLK), F32)
        dv = jnp.zeros((BLK, 2 * BLK), F32)
        for h in range(nh):
            dk = dk + head_mask(ka_ref[h], h, hs)
            dv = dv + head_mask(va_ref[h], h, hs)
        dk_ref[rows, :] = dk.astype(BF)
        dv_ref[rows, :] = dv.astype(BF)


def self_dkv(meta, k, v, qg, dg, tt, nh, hs):
    nb = qg.shape[0]
    pairs = (nb + 1) * BLK * BLK * nh
    shape = jax.ShapeDtypeStruct((2 * BLK, 2 * BLK), BF)
    return pl.pallas_call(
        functools.partial(self_dkv_kernel, nb // 2, nh, hs),
        in_specs=[SM] + [VM] * 5,
        out_specs=[VM, VM],
        out_shape=[shape, shape],
        scratch_shapes=[pltpu.VMEM((nh, BLK, 2 * BLK), F32)] * 2,
        **params(pairs * 2 * 1024, 10e6, pairs),
    )(meta, k, v, qg, dg, tt)


def cross_fwd_kernel(nh, hs, q_ref, e_ref, o_ref, qe_ref, s_ref):
    wide = nh * hs
    chunks = e_ref.shape[0] // CH
    for half in range(2):
        rows = slice(half * BLK, (half + 1) * BLK)
        q = q_ref[rows, :]
        total = jnp.zeros((BLK, 2 * BLK), F32)
        lse = []
        for h in range(nh):
            qm = head_mask(q, h, hs)
            top = jnp.full((BLK, BLK), NEG, F32)
            for ch in range(chunks):
                s = dot_nt(qm, e_ref[ch * CH : (ch + 1) * CH, : 2 * BLK])
                s_ref[ch] = s
                top = jnp.maximum(top, lane_fold(s, jnp.maximum))
            top = jnp.max(top, axis=1, keepdims=True)
            summed = jnp.zeros((BLK, BLK), F32)
            acc = jnp.zeros((BLK, 2 * BLK), F32)
            for ch in range(chunks):
                p = jnp.exp(s_ref[ch] - top)
                summed = summed + lane_fold(p, jnp.add)
                acc = acc + dot(p.astype(BF), e_ref[ch * CH : (ch + 1) * CH, 2 * BLK :])
            summed = jnp.sum(summed, axis=1, keepdims=True)
            total = total + head_mask(acc / summed, h, hs)
            lse.append(top + jnp.log(summed))
        o_ref[rows, :] = total
        qe_ref[rows, :] = pieces_into(q.astype(F32), [-t for t in lse], wide).astype(BF)


def cross_fwd(q, e, nh, hs):
    pairs = 2 * BLK * e.shape[0] * nh
    return pl.pallas_call(
        functools.partial(cross_fwd_kernel, nh, hs),
        in_specs=[VM, VM],
        out_specs=[VM, VM],
        out_shape=[
            jax.ShapeDtypeStruct((2 * BLK, 2 * BLK), F32),
            jax.ShapeDtypeStruct((2 * BLK, 2 * BLK), BF),
        ],
        scratch_shapes=[pltpu.VMEM((e.shape[0] // CH, BLK, CH), F32)],
        **params(pairs * 2 * 512, 4e6, pairs),
    )(q, e)


def cross_bwd_kernel(nh, hs, qe_ref, de_ref, e_ref, dq_ref, dke_ref, dve_ref, acc_ref):
    wide = nh * hs
    ch = pl.program_id(0)

    @pl.when(ch == 0)
    def _():
        acc_ref[...] = jnp.zeros_like(acc_ref)

    ek = e_ref[:, : 2 * BLK]
    ev = e_ref[:, 2 * BLK :]
    ek_t = jnp.transpose(ek.astype(F32)).astype(BF)

    def kept(value, h):
        lane = lane_of(value.shape)
        first = wide + 3 * h
        keep = ((lane >= h * hs) & (lane < (h + 1) * hs)) | ((lane >= first) & (lane < first + 3))
        return jnp.where(keep, value, jnp.zeros_like(value))

    dk = jnp.zeros((e_ref.shape[0], 2 * BLK), F32)
    dv = jnp.zeros((e_ref.shape[0], 2 * BLK), F32)
    for h in range(nh):
        qm = kept(qe_ref[...], h)
        dm = kept(de_ref[...], h)
        p = jnp.exp(dot_nt(ek, qm))
        ds = (p * dot_nt(ev, dm)).astype(BF)
        dk = dk + dot(ds, qm)
        dv = dv + dot(p.astype(BF), dm)
        acc_ref[h * hs : (h + 1) * hs, :] += dot(ek_t[h * hs : (h + 1) * hs, :], ds)
    dke_ref[...] = dk.astype(BF)
    dve_ref[...] = dv.astype(BF)

    @pl.when(ch == pl.num_programs(0) - 1)
    def _():
        dq_ref[...] = acc_ref[...].astype(BF)


def cross_bwd(qe, de, e, nh, hs):
    rows = e.shape[0]
    pairs = 2 * BLK * rows * nh
    const = pl.BlockSpec((2 * BLK, 2 * BLK), lambda i: (0, 0))
    part = pl.BlockSpec((CH, 2 * BLK), lambda i: (i, 0))
    shape = jax.ShapeDtypeStruct((rows, 2 * BLK), BF)
    return pl.pallas_call(
        functools.partial(cross_bwd_kernel, nh, hs),
        grid=(rows // CH,),
        in_specs=[const, const, pl.BlockSpec((CH, 4 * BLK), lambda i: (i, 0))],
        out_specs=[pl.BlockSpec((nh * hs, 2 * BLK), lambda i: (0, 0)), part, part],
        out_shape=[jax.ShapeDtypeStruct((nh * hs, 2 * BLK), BF), shape, shape],
        scratch_shapes=[pltpu.VMEM((nh * hs, 2 * BLK), F32)],
        **params(pairs * 2 * 1024, 4e6, pairs),
    )(qe, de, e)


def grad_prep_kernel(nh, hs, dy_ref, w_ref, o_ref, de_ref, dh_ref, del_ref):
    wide = nh * hs
    da = dot_nt(dy_ref[...], w_ref[...]).astype(BF)
    terms = da.astype(F32) * o_ref[...]
    delta = [jnp.sum(head_mask(terms, h, hs), axis=1, keepdims=True) for h in range(nh)]
    dh_ref[...] = pltpu.roll(da.astype(F32), hs, 1).astype(BF)
    lane = lane_of(del_ref.shape)
    cols = jnp.zeros(del_ref.shape, F32)
    for h in range(nh):
        cols = jnp.where(lane == h, delta[h], cols)
    del_ref[...] = cols
    de_ref[...] = pieces_into(da.astype(F32), [-t for t in delta], wide).astype(BF)


def grad_prep(dy, weight, o, nh, hs):
    rows = dy.shape[0]
    padded = jnp.pad(weight, ((0, 2 * BLK - weight.shape[0]), (0, 0)))
    shape = jax.ShapeDtypeStruct((rows, 2 * BLK), BF)
    return pl.pallas_call(
        functools.partial(grad_prep_kernel, nh, hs),
        in_specs=[VM] * 3,
        out_specs=[VM] * 3,
        out_shape=[shape, shape, jax.ShapeDtypeStruct((rows, BLK), F32)],
        **params(2 * rows * 2 * BLK * dy.shape[1], 2e6, 0),
    )(dy, padded, o)


def scale_of(rows):
    return lax.rsqrt(jnp.mean(rows * rows, axis=-1, keepdims=True) + EPS)


def norm_back(rows, gain, grad):
    rr = scale_of(rows)
    scaled = gain * grad
    shared = jnp.mean(rows * scaled, axis=-1, keepdims=True)
    dv = rr * scaled - rows * (rr * rr * rr) * shared
    return dv, jnp.sum(rows * rr * grad, axis=0)


def local(
    tokens,
    encoded,
    cotangent,
    assign,
    bucket_ids,
    gain_self,
    gain_cross,
    gain_ffn,
    query_weight,
    key_weight,
    value_weight,
    out_weight,
    cross_query,
    cross_key,
    cross_value,
    cross_out,
    gate_weight,
    up_weight,
    down_weight,
    bucket_table,
):
    nctx = lax.axis_size("ctx")
    nw = lax.axis_size("wsh")
    c = lax.axis_index("ctx")
    w = lax.axis_index("wsh")
    both = ("ctx", "wsh")
    rows, width = tokens.shape
    half = rows // 2
    length = rows * nw * nctx
    buckets, heads = bucket_table.shape
    inner = query_weight.shape[1]
    hs = inner // heads
    nh = heads // nw
    wide = nh * hs
    plane = 4
    nz = nctx // plane
    spot = (c % plane) * nw + w
    zed = c // plane
    hidden = gate_weight.shape[1]
    share = hidden // (nctx * nw)

    def pair(x, axis=0, tiled=True):
        return lax.all_gather(x, "wsh", axis=axis, tiled=tiled)

    def own_heads(x, axis):
        return lax.dynamic_slice_in_dim(x, w * wide, wide, axis)

    def chip_order(x):
        x = x.reshape((nw, 2, half) + x.shape[1:])
        return jnp.swapaxes(x, 0, 1).reshape((2 * nw * half,) + x.shape[3:])

    def own_rows(x):
        x = x.reshape((2, nw, half) + x.shape[1:])
        x = lax.dynamic_index_in_dim(x, w, 1, keepdims=False)
        return x.reshape((2 * half,) + x.shape[2:])

    def near(x, k):
        return lax.ppermute(x, "ctx", [(i, i ^ k) for i in range(nctx)])

    def plane_gather(x):
        parts = jnp.stack([x] + [near(x, k) for k in range(1, plane)])
        return pair(parts, tiled=False).reshape((nw * plane * x.shape[0],) + x.shape[1:])

    def plane_scatter(partial):
        parts = partial.reshape(nw, plane, rows, width)
        mine = lax.dynamic_index_in_dim(parts, w, 0, keepdims=False)
        other = lax.dynamic_index_in_dim(parts, 1 - w, 0, keepdims=False).astype(BF)
        swap = [(i, (i + 1) % nw) for i in range(nw)]
        mine = mine + lax.ppermute(other, "wsh", swap).astype(F32)
        total = mine[0]
        for k in range(1, plane):
            total = total + near(mine[k].astype(BF), k).astype(F32)
        return total

    def zed_scatter(parts):
        total = lax.dynamic_index_in_dim(parts, zed, 0, keepdims=False)
        for k in range(1, nz):
            piece = lax.dynamic_index_in_dim(parts, (zed + k) % nz, 0, keepdims=False)
            perm = [(i, ((i // plane + k) % nz) * plane + i % plane) for i in range(nctx)]
            total = total + lax.ppermute(piece.astype(BF), "ctx", perm).astype(F32)
        return total

    lanes = jnp.arange(nctx, dtype=jnp.int32)
    owner = jnp.sum(jnp.where(assign[None, :] == lanes[:, None], lanes[None, :], 0), axis=1)
    meta = jnp.concatenate([owner, jnp.take(assign, c)[None]]).astype(jnp.int32)

    gains = pair(jnp.stack([gain_self, gain_cross, gain_ffn]), axis=1).astype(F32)
    tok = chip_order(pair(tokens)).astype(F32)
    qkv_full = pair(jnp.concatenate([query_weight, key_weight, value_weight], axis=1))
    qkv_heads = jnp.concatenate(
        [own_heads(qkv_full[:, i * inner : (i + 1) * inner], 1) for i in range(3)], axis=1
    )
    n1 = (tok * scale_of(tok) * gains[0]).astype(BF)
    qkv = dot(n1, qkv_heads).astype(BF)
    lane_pad = ((0, 0), (0, 2 * BLK - wide))
    q = jnp.pad(qkv[:, :wide], lane_pad)
    k_own = jnp.pad(qkv[:, wide : 2 * wide], lane_pad)
    v_own = jnp.pad(qkv[:, 2 * wide :], lane_pad)
    kv = lax.all_gather(qkv[:, wide:], "ctx", axis=0, tiled=True)
    kv = kv.reshape(2 * nctx, BLK, 2 * wide)

    enc_pair = pair(encoded)
    ck_full, cv_full, cq_full = pair(cross_key), pair(cross_value), pair(cross_query)
    ekv_heads = jnp.concatenate([own_heads(ck_full, 1), own_heads(cv_full, 1)], axis=1)
    ekv = dot(enc_pair, ekv_heads).astype(BF)
    ones = jnp.ones((ekv.shape[0], 2 * BLK - wide), BF)
    ekv = jnp.concatenate([ekv[:, :wide], ones, ekv[:, wide:], ones], axis=1)
    ekv = lax.all_gather(ekv, "ctx", axis=0, tiled=True)

    hot = (bucket_ids[None, :] == jnp.arange(buckets, dtype=jnp.int32)[:, None]).astype(BF)
    values = dot_tn(lax.dynamic_slice_in_dim(bucket_table, w * nh, nh, 1), hot)
    ts, tt = bias_tiles(values)

    def units(matrix, index):
        parts = [
            lax.dynamic_slice_in_dim(matrix, (z * plane * nw + index) * share, share, 1)
            for z in range(nz)
        ]
        return jnp.concatenate(parts, axis=1)

    mates = [(c % plane) * nw + i for i in range(nw)]
    up_gate = jnp.stack(
        [jnp.concatenate([units(gate_weight, m), units(up_weight, m)], axis=1) for m in mates]
    )
    up_gate = lax.all_to_all(up_gate, "wsh", 0, 0, tiled=True)
    up_gate = up_gate.reshape(width, 2 * nz * share)
    wg, wu = up_gate[:, : nz * share], up_gate[:, nz * share :]
    down_parts = down_weight.reshape(nz // nw, plane * nw, share, width)
    wd = jnp.stack([lax.dynamic_index_in_dim(down_parts, m, 1, keepdims=False) for m in mates])
    wd = lax.all_to_all(wd, "wsh", 0, 0, tiled=True).reshape(nz * share, width)

    out_full, cross_out_full = pair(out_weight), pair(cross_out)
    g_plane = plane_gather(cotangent)

    o1, qe1, lse1 = self_fwd(meta, q, kv, ts, nh, hs)
    a1_heads = o1[:, :wide].astype(BF)
    a1 = jnp.swapaxes(pair(a1_heads, tiled=False), 0, 1).reshape(nw * rows, inner)
    h1 = tok + dot(a1, out_full)
    n2 = (h1 * scale_of(h1) * gains[1]).astype(BF)
    cq = jnp.pad(dot(n2, own_heads(cq_full, 1)).astype(BF), lane_pad)
    qg = lax.all_gather(qe1, "ctx", axis=0, tiled=True).reshape(2 * nctx, BLK, 2 * BLK)

    o2, qe2 = cross_fwd(cq, ekv, nh, hs)
    a2 = pair(o2[:, :wide].astype(BF), tiled=False)
    a2 = own_rows(jnp.swapaxes(a2, 0, 1).reshape(nw * rows, inner))
    h1_own = own_rows(h1)
    h2 = h1_own + dot(a2, cross_out_full)
    n3 = (h2 * scale_of(h2) * gains[2]).astype(BF)

    n3_plane = plane_gather(n3)
    gate = dot(n3_plane, wg)
    up = dot(n3_plane, wu)
    act = (jax.nn.gelu(gate, approximate=True) * up).astype(BF)
    dact = dot_nt(g_plane, wd)
    _, pull = jax.vjp(lambda a, b: jax.nn.gelu(a, approximate=True) * b, gate, up)
    dgate, dup = pull(dact)
    dgate, dup = dgate.astype(BF), dup.astype(BF)
    dn3 = plane_scatter(dot_nt(dgate, wg) + dot_nt(dup, wu))
    output = (h2 + plane_scatter(dot(act, wd))).astype(BF)
    ffn = jnp.concatenate(
        [
            dot_tn(m, v).astype(BF).reshape(nz, share, width)
            for m, v in ((dgate, n3_plane), (dup, n3_plane), (act, g_plane))
        ],
        axis=1,
    )
    ffn = zed_scatter(ffn)
    dh2_part, gain3 = norm_back(h2, gains[2], dn3)
    dh2 = cotangent.astype(F32) + dh2_part

    dy2 = dh2.astype(BF)
    de2, _, _ = grad_prep(chip_order(pair(dy2)), cross_out, o2, nh, hs)
    dcq_t, dek, dev = cross_bwd(qe2, de2, ekv, nh, hs)
    dcq = jnp.swapaxes(pair(dcq_t, tiled=True), 0, 1)
    dcq_own = own_rows(dcq)
    dn2 = dot_nt(dcq_own, cq_full)
    dh1_part, gain2 = norm_back(h1_own, gains[1], dn2)
    dh1 = dh2 + dh1_part
    dekv = jnp.concatenate([dek[:, :wide], dev[:, :wide]], axis=1)
    dekv = lax.psum_scatter(dekv, "ctx", scatter_dimension=0, tiled=True)
    dekv = pair(dekv, tiled=False)
    dekv = lax.dynamic_slice_in_dim(dekv, w * encoded.shape[0], encoded.shape[0], 1)
    dek_own = jnp.swapaxes(dekv[:, :, :wide], 0, 1).reshape(encoded.shape[0], inner)
    dev_own = jnp.swapaxes(dekv[:, :, wide:], 0, 1).reshape(encoded.shape[0], inner)
    encoded_grad = dot_nt(dek_own, ck_full) + dot_nt(dev_own, cv_full)

    dy1 = dh1.astype(BF)
    de1, dhi1, delta1 = grad_prep(chip_order(pair(dy1)), out_weight, o1, nh, hs)
    dg = lax.all_gather(de1, "ctx", axis=0, tiled=True).reshape(2 * nctx, BLK, 2 * BLK)
    dq, rev = self_dq(meta, q, dhi1, lse1, delta1, kv, ts, nh, hs)
    dk, dv = self_dkv(meta, k_own, v_own, qg, dg, tt, nh, hs)
    dqkv = jnp.concatenate([dq[:, :wide], dk[:, :wide], dv[:, :wide]], axis=1)
    dqkv = jnp.swapaxes(pair(dqkv, tiled=False), 0, 1)
    dqkv = own_rows(dqkv).reshape(rows, nw, 3, wide)
    dqkv = jnp.swapaxes(dqkv, 1, 2).reshape(rows, 3 * inner)
    dn1 = dot_nt(dqkv, qkv_full)
    tok_part, gain1 = norm_back(tokens.astype(F32), gains[0], dn1)
    tokens_grad = dh1 + tok_part

    by_distance = jnp.sum(rev.reshape(nh, 8, -1), axis=1)[:, :length]
    hot_rev = (
        jnp.flip(bucket_ids)[None, :] == jnp.arange(buckets, dtype=jnp.int32)[:, None]
    ).astype(F32)
    table_own = lax.dot_general(
        hot_rev, by_distance, (((1,), (1,)), ((), ())), precision=lax.Precision.HIGHEST
    )
    table = lax.dynamic_update_slice_in_dim(
        jnp.zeros((buckets, heads), F32), table_own, w * nh, 1
    )

    def to_owners(grads):
        each = [g.astype(BF).reshape(nctx * nw, inner // (nctx * nw), width) for g in grads]
        joined = jnp.concatenate(each, axis=1)
        extra = -joined.shape[1] % 16
        joined = jnp.pad(joined, ((0, 0), (0, extra), (0, 0)))
        got = lax.psum_scatter(joined, both, scatter_dimension=0, tiled=True)[0].astype(F32)
        each = inner // (nctx * nw)
        return [got[i * each : (i + 1) * each] for i in range(len(grads))]

    n1_own, n2_own, a1_own = own_rows(n1), own_rows(n2), own_rows(a1)
    out_share, cross_out_share, cq_t, ck_t, cv_t = to_owners(
        [
            dot_tn(a1_own, dy1),
            dot_tn(a2, dy2),
            dot_tn(dcq_own, n2_own),
            dot_tn(dek_own, encoded),
            dot_tn(dev_own, encoded),
        ]
    )
    q_t, k_t, v_t = to_owners(
        [dot_tn(dqkv[:, i * inner : (i + 1) * inner], n1_own) for i in range(3)]
    )
    gain1, gain2, gain3, table = lax.psum((gain1, gain2, gain3, table), both)
    return (
        output,
        tokens_grad,
        encoded_grad,
        gain1,
        gain2,
        gain3,
        q_t.T,
        k_t.T,
        v_t.T,
        out_share,
        cq_t.T,
        ck_t.T,
        cv_t.T,
        cross_out_share,
        ffn[:share].T,
        ffn[share : 2 * share].T,
        ffn[2 * share :],
        table,
    )


def solution(mesh):
    rows = P(("seq", "ctx", "wsh"), None)
    cols = P("seq", ("ctx", "wsh"))
    split = P("wsh", None)
    return jax.shard_map(
        local,
        mesh=mesh,
        in_specs=(rows, rows, rows, P(), P(), P("wsh"), P("wsh"), P("wsh"))
        + (split,) * 11
        + (P(),),
        out_specs=(
            rows,
            rows,
            rows,
            P("seq"),
            P("seq"),
            P("seq"),
            cols,
            cols,
            cols,
            rows,
            cols,
            cols,
            cols,
            rows,
            cols,
            cols,
            rows,
            P("seq", None),
        ),
        check_vma=False,
    )
```

```python
import functools

import jax
import jax.numpy as jnp
from jax import lax
from jax.experimental import pallas as pl
from jax.experimental.pallas import tpu as pltpu
from jax.sharding import PartitionSpec as P

EPS = 1e-06
NEG = -1e30
F32 = jnp.float32
BF = jnp.bfloat16
BLK = 128
GRP = 4
CH = BLK * GRP
VLIM = 60 * 1024 * 1024
SLOW = 64


def dot(a, b):
    return lax.dot_general(a, b, (((1,), (0,)), ((), ())), preferred_element_type=F32)


def dot_nt(a, b):
    return lax.dot_general(a, b, (((1,), (1,)), ((), ())), preferred_element_type=F32)


def dot_tn(a, b):
    return lax.dot_general(a, b, (((0,), (0,)), ((), ())), preferred_element_type=F32)


def lane_of(shape):
    return lax.broadcasted_iota(jnp.int32, shape, 1)


def head_mask(value, head, hs):
    lane = lane_of(value.shape)
    keep = (lane >= head * hs) & (lane < (head + 1) * hs)
    return jnp.where(keep, value, jnp.zeros_like(value))


def lane_fold(value, op):
    out = value[:, :BLK]
    for i in range(1, value.shape[1] // BLK):
        out = op(out, value[:, i * BLK : (i + 1) * BLK])
    return out


def pieces_into(base, columns, first):
    lane = lane_of(base.shape)
    out = base
    for i, column in enumerate(columns):
        rest = column
        for j in range(3):
            part = rest.astype(BF).astype(F32)
            rest = rest - part
            out = jnp.where(lane == first + 3 * i + j, part, out)
    return out


def params(flops, nbytes, trans):
    return dict(
        compiler_params=pltpu.CompilerParams(vmem_limit_bytes=VLIM),
        cost_estimate=pl.CostEstimate(
            flops=int(flops) // SLOW,
            bytes_accessed=int(nbytes) // SLOW,
            transcendentals=int(trans) // SLOW,
        ),
    )


def after(value, *deps):
    return lax.optimization_barrier((value,) + deps)[0]


def f32_shape(*dims):
    return jax.ShapeDtypeStruct(dims, F32)


def bf_shape(*dims):
    return jax.ShapeDtypeStruct(dims, BF)


def plain(kernel, scalars, inputs, outputs, cost=(1e9, 4e6, 0), deps=()):
    count, late = len(scalars) + len(inputs), len(deps)

    def body(*refs):
        kernel(*refs[:count], *refs[count + late :])

    return pl.pallas_call(
        body,
        in_specs=[SM] * len(scalars) + [VM] * len(inputs) + [ANY] * late,
        out_specs=[VM] * len(outputs),
        out_shape=list(outputs),
        **params(*cost),
    )(*scalars, *inputs, *deps)


VM = pl.BlockSpec(memory_space=pltpu.VMEM)
ANY = pl.BlockSpec(memory_space=pl.ANY)
SM = pl.BlockSpec(memory_space=pltpu.SMEM)


def bias_kernel(nb, nh, nat_ref, rev_ref, ts_ref, tt_ref, old_rev_ref, old_nat_ref):
    r = pl.program_id(0)
    row = lax.broadcasted_iota(jnp.int32, (BLK, BLK), 0)
    col = lax.broadcasted_iota(jnp.int32, (BLK, BLK), 1)

    def skew(line):
        eight = pltpu.roll(jnp.broadcast_to(line, (8, BLK)), 0, 1, stride=1, stride_axis=0)
        return jnp.concatenate(
            [eight] + [pltpu.roll(eight, 8 * i, 1) for i in range(1, BLK // 8)], axis=0
        )

    d = nb - 1 - r
    lines = rev_ref[nb - jnp.maximum(d, 0)]

    @pl.when(r == 0)
    def _():
        for h in range(nh):
            old_rev_ref[h] = skew(rev_ref[0][h : h + 1])

    for h in range(nh):
        now = skew(lines[h : h + 1])
        tile = jnp.where(col >= row, now, old_rev_ref[h])
        old_rev_ref[h] = now
        ts_ref[0, h] = jnp.where(d * BLK + row - col >= 0, tile, NEG).astype(BF)
    d = r - (GRP - 1)
    lines = nat_ref[jnp.maximum(d, 0) + 1]
    for h in range(nh):
        now = skew(lines[h : h + 1])
        tile = jnp.where(col >= row, now, old_nat_ref[h])
        old_nat_ref[h] = now
        tt_ref[0, h] = jnp.where(d * BLK + col - row >= 0, tile, NEG).astype(BF)


def bias_tiles(values):
    nh, length = values.shape
    nb = length // BLK
    zero = jnp.zeros((nh, 1), F32)
    nat = jnp.concatenate([jnp.zeros((nh, BLK), F32), values], axis=1)
    rev = jnp.concatenate([zero, jnp.flip(values, 1), jnp.zeros((nh, BLK - 1), F32)], axis=1)
    nat = jnp.transpose(nat.reshape(nh, nb + 1, BLK), (1, 0, 2))
    rev = jnp.transpose(rev.reshape(nh, nb + 1, BLK), (1, 0, 2))
    rows = nb + GRP - 1
    shape = jax.ShapeDtypeStruct((rows, nh, BLK, BLK), BF)
    spec = pl.BlockSpec((1, nh, BLK, BLK), lambda r: (r, 0, 0, 0))
    return pl.pallas_call(
        functools.partial(bias_kernel, nb, nh),
        grid=(rows,),
        in_specs=[VM, VM],
        out_specs=[spec, spec],
        out_shape=[shape, shape],
        scratch_shapes=[pltpu.VMEM((nh, BLK, BLK), F32)] * 2,
        **params(0, 4 * rows * nh * BLK * BLK, 0),
    )(nat, rev)


def gather_blocks(ref, meta_ref, nctx, first, lo, hi, base=0):
    parts = []
    for i in range(GRP):
        t = first + i
        early = t < nctx
        slot = meta_ref[base + jnp.where(early, t, 2 * nctx - 1 - t)]
        at = pl.multiple_of(jnp.where(early, 0, BLK), BLK)
        parts.append(ref[slot, pl.ds(at, BLK), lo:hi])
    return jnp.concatenate(parts, axis=0)


def bias_of(ref, first, h):
    return jnp.concatenate([ref[first + i, h] for i in range(GRP)], axis=1).astype(F32)


def self_fwd_kernel(nctx, nh, hs, meta_ref, q_ref, ts_ref, kv_ref, *rest):
    o_ref, qe_ref, lse_ref, s_ref, acc_ref = rest[-5:]
    nb = 2 * nctx
    wide = nh * hs
    early = meta_ref[nctx]
    for half in range(2):
        blk = early if half == 0 else nb - 1 - early
        chunks = blk // GRP + 1
        q = q_ref[half * BLK : (half + 1) * BLK, :]
        qm = [head_mask(q, h, hs) for h in range(nh)]

        def score(ch, tops):
            keys = gather_blocks(kv_ref, meta_ref, nctx, ch * GRP, 0, 2 * BLK)
            out = []
            for h in range(nh):
                s = dot_nt(qm[h], keys) + bias_of(ts_ref, nb - 1 - blk + ch * GRP, h)
                s_ref[ch, h] = s
                out.append(jnp.maximum(tops[h], lane_fold(s, jnp.maximum)))
            return tuple(out)

        tops = lax.fori_loop(
            0, chunks, score, tuple(jnp.full((BLK, BLK), NEG, F32) for _ in range(nh))
        )
        tops = [jnp.max(t, axis=1, keepdims=True) for t in tops]
        acc_ref[...] = jnp.zeros_like(acc_ref)

        def weigh(ch, sums):
            vals = gather_blocks(kv_ref, meta_ref, nctx, ch * GRP, BLK, 3 * BLK)
            out = []
            for h in range(nh):
                p = jnp.exp(s_ref[ch, h] - tops[h])
                out.append(sums[h] + lane_fold(p, jnp.add))
                acc_ref[h] += dot(p.astype(BF), vals)
            return tuple(out)

        sums = lax.fori_loop(
            0, chunks, weigh, tuple(jnp.zeros((BLK, BLK), F32) for _ in range(nh))
        )
        sums = [jnp.sum(t, axis=1, keepdims=True) for t in sums]
        total = jnp.zeros((BLK, 2 * BLK), F32)
        for h in range(nh):
            total = total + head_mask(acc_ref[h] / sums[h], h + 1, hs)
        rows = slice(half * BLK, (half + 1) * BLK)
        o_ref[rows, :] = pltpu.roll(total, 2 * BLK - hs, 1)
        lse = [tops[h] + jnp.log(sums[h]) for h in range(nh)]
        lane = lane_of((BLK, BLK))
        cols = jnp.zeros((BLK, BLK), F32)
        for h in range(nh):
            cols = jnp.where(lane == h, lse[h], cols)
        lse_ref[rows, :] = cols
        qe_ref[rows, :] = pieces_into(q.astype(F32), [-t for t in lse], wide).astype(BF)


def self_fwd(meta, q, kv, ts, nh, hs, deps=()):
    nctx = kv.shape[0]
    nb = 2 * nctx
    pairs = (nb + 1) * BLK * BLK * nh
    return pl.pallas_call(
        functools.partial(self_fwd_kernel, nctx, nh, hs),
        in_specs=[SM, VM, VM, VM] + [ANY] * len(deps),
        out_specs=[VM, VM, VM],
        out_shape=[
            jax.ShapeDtypeStruct((2 * BLK, 2 * BLK), F32),
            jax.ShapeDtypeStruct((2 * BLK, 2 * BLK), BF),
            jax.ShapeDtypeStruct((2 * BLK, BLK), F32),
        ],
        scratch_shapes=[
            pltpu.VMEM((nb // GRP, nh, BLK, CH), F32),
            pltpu.VMEM((nh, BLK, 2 * BLK), F32),
        ],
        **params(pairs * 2 * 512, 10e6, pairs),
    )(meta, q, ts, kv, *deps)


def self_dq_kernel(nctx, nh, hs, meta_ref, q_ref, da_ref, lse_ref, del_ref, ts_ref, kv_ref, *rest):
    dq_ref, rev_ref, acc_ref = rest[-3:]
    nb = 2 * nctx
    early = meta_ref[nctx]
    rev_ref[...] = jnp.zeros_like(rev_ref)
    row = lax.broadcasted_iota(jnp.int32, (BLK, BLK), 0)
    col = lax.broadcasted_iota(jnp.int32, (BLK, BLK), 1)
    flip = (row + col == BLK - 1).astype(BF)
    for half in range(2):
        blk = early if half == 0 else nb - 1 - early
        chunks = blk // GRP + 1
        rows = slice(half * BLK, (half + 1) * BLK)
        q = q_ref[rows, :]
        da = da_ref[rows, :]
        qm = [head_mask(q, h, hs) for h in range(nh)]
        dm = [head_mask(da, h + 1, hs) for h in range(nh)]
        lse = [lse_ref[rows, h : h + 1] for h in range(nh)]
        delta = [del_ref[rows, h : h + 1] for h in range(nh)]
        acc_ref[...] = jnp.zeros_like(acc_ref)

        def step(ch, carry):
            both = gather_blocks(kv_ref, meta_ref, nctx, ch * GRP, 0, 3 * BLK)
            keys, vals = both[:, : 2 * BLK], both[:, BLK:]
            off = pl.multiple_of((ch * GRP - blk + nb - 1) * BLK, BLK)
            for h in range(nh):
                s = dot_nt(qm[h], keys) + bias_of(ts_ref, nb - 1 - blk + ch * GRP, h)
                p = jnp.exp(s - lse[h])
                ds = (p * (dot_nt(dm[h], vals) - delta[h])).astype(BF)
                acc_ref[h] += dot(ds, keys)
                flat = jnp.concatenate([dot(flip, ds), jnp.zeros((BLK, BLK), F32)], axis=1)
                line = flat[:8]
                for i in range(1, BLK // 8):
                    line = line + pltpu.roll(flat[8 * i : 8 * i + 8], 8 * i, 1)
                rev_ref[h * 8 : (h + 1) * 8, pl.ds(off, CH + BLK)] += line
            return carry

        lax.fori_loop(0, chunks, step, 0)
        total = jnp.zeros((BLK, 2 * BLK), F32)
        for h in range(nh):
            total = total + head_mask(acc_ref[h], h, hs)
        dq_ref[rows, :] = total.astype(BF)
    for h in range(nh):
        rows = slice(8 * h, 8 * h + 8)
        rev_ref[rows, :] = pltpu.roll(rev_ref[rows, :], 0, 1, stride=1, stride_axis=0)


def self_dq(meta, q, da, lse, delta, kv, ts, nh, hs, deps=()):
    nctx = kv.shape[0]
    nb = 2 * nctx
    pairs = (nb + 1) * BLK * BLK * nh
    return pl.pallas_call(
        functools.partial(self_dq_kernel, nctx, nh, hs),
        in_specs=[SM] + [VM] * 6 + [ANY] * len(deps),
        out_specs=[VM, VM],
        out_shape=[
            jax.ShapeDtypeStruct((2 * BLK, 2 * BLK), BF),
            jax.ShapeDtypeStruct((8 * nh, nb * BLK + CH), F32),
        ],
        scratch_shapes=[pltpu.VMEM((nh, BLK, 2 * BLK), F32)],
        **params(pairs * 2 * 896, 10e6, pairs),
    )(meta, q, da, lse, delta, ts, kv, *deps)


def self_dkv_kernel(nctx, nh, hs, meta_ref, k_ref, v_ref, qg_ref, dg_ref, tt_ref, *rest):
    dk_ref, dv_ref, ka_ref, va_ref = rest[-4:]
    nb = 2 * nctx
    wide = nh * hs
    early = meta_ref[nctx]

    def extended(value, h):
        lane = lane_of(value.shape)
        first = wide + 3 * h
        ones = (lane >= first) & (lane < first + 3)
        return jnp.where(ones, jnp.ones_like(value), head_mask(value, h, hs))

    for half in range(2):
        blk = early if half == 0 else nb - 1 - early
        rows = slice(half * BLK, (half + 1) * BLK)
        km = [extended(k_ref[rows, :], h) for h in range(nh)]
        vm = [extended(v_ref[rows, :], h) for h in range(nh)]
        ka_ref[...] = jnp.zeros_like(ka_ref)
        va_ref[...] = jnp.zeros_like(va_ref)

        def step(ch, carry):
            qc = gather_blocks(qg_ref, meta_ref, nctx, ch * GRP, 0, 2 * BLK)
            dc = gather_blocks(dg_ref, meta_ref, nctx, ch * GRP, 0, 2 * BLK, nctx + 1)
            for h in range(nh):
                s = dot_nt(km[h], qc) + bias_of(tt_ref, ch * GRP - blk + GRP - 1, h)
                p = jnp.exp(s)
                ds = (p * dot_nt(vm[h], dc)).astype(BF)
                ka_ref[h] += dot(ds, qc)
                va_ref[h] += dot(p.astype(BF), dc)
            return carry

        lax.fori_loop(blk // GRP, nb // GRP, step, 0)
        dk = jnp.zeros((BLK, 2 * BLK), F32)
        dv = jnp.zeros((BLK, 2 * BLK), F32)
        for h in range(nh):
            dk = dk + head_mask(ka_ref[h], h, hs)
            dv = dv + head_mask(va_ref[h], h, hs)
        dk_ref[rows, :] = dk.astype(BF)
        dv_ref[rows, :] = dv.astype(BF)


def self_dkv(meta, k, v, qg, dg, tt, nh, hs, deps=()):
    nctx = qg.shape[0]
    nb = 2 * nctx
    pairs = (nb + 1) * BLK * BLK * nh
    shape = jax.ShapeDtypeStruct((2 * BLK, 2 * BLK), BF)
    return pl.pallas_call(
        functools.partial(self_dkv_kernel, nctx, nh, hs),
        in_specs=[SM] + [VM] * 5 + [ANY] * len(deps),
        out_specs=[VM, VM],
        out_shape=[shape, shape],
        scratch_shapes=[
            pltpu.VMEM((nh, BLK, 2 * BLK), F32),
            pltpu.VMEM((nh, BLK, 2 * BLK), F32),
        ],
        **params(pairs * 2 * 1024, 10e6, pairs),
    )(meta, k, v, qg, dg, tt, *deps)


def fetch(place_ref, parts, held_ref, sem):
    plane, nz = len(parts), sem.shape[1]
    rows = parts[0].shape[0] // nz
    copies = []
    for k, part in enumerate(parts):
        for z in range(nz):
            at = ((place_ref[0] ^ k) * nz + (place_ref[1] ^ z)) * rows
            copies.append(
                pltpu.make_async_copy(
                    part.at[pl.ds(z * rows, rows)],
                    held_ref.at[pl.ds(pl.multiple_of(at, rows), rows)],
                    sem.at[k, z],
                )
            )
    for copy in copies:
        copy.start()
    for copy in copies:
        copy.wait()


def cross_fwd_kernel(count, nh, hs, place_ref, q_ref, *rest):
    o_ref, qe_ref, e_ref, s_ref, sem = rest[count:]
    fetch(place_ref, rest[:count], e_ref, sem)
    wide = nh * hs
    chunks = e_ref.shape[0] // CH
    for half in range(2):
        rows = slice(half * BLK, (half + 1) * BLK)
        q = q_ref[rows, :]
        total = jnp.zeros((BLK, 2 * BLK), F32)
        lse = []
        for h in range(nh):
            qm = head_mask(q, h, hs)
            top = jnp.full((BLK, BLK), NEG, F32)
            for ch in range(chunks):
                s = dot_nt(qm, e_ref[ch * CH : (ch + 1) * CH, : 2 * BLK])
                s_ref[ch] = s
                top = jnp.maximum(top, lane_fold(s, jnp.maximum))
            top = jnp.max(top, axis=1, keepdims=True)
            summed = jnp.zeros((BLK, BLK), F32)
            acc = jnp.zeros((BLK, 2 * BLK), F32)
            for ch in range(chunks):
                p = jnp.exp(s_ref[ch] - top)
                summed = summed + lane_fold(p, jnp.add)
                acc = acc + dot(p.astype(BF), e_ref[ch * CH : (ch + 1) * CH, 2 * BLK :])
            summed = jnp.sum(summed, axis=1, keepdims=True)
            total = total + head_mask(acc / summed, h, hs)
            lse.append(top + jnp.log(summed))
        o_ref[rows, :] = total
        qe_ref[rows, :] = pieces_into(q.astype(F32), [-t for t in lse], wide).astype(BF)


def cross_fwd(place, q, e, nz, nh, hs):
    enc = len(e) * e[0].shape[0]
    pairs = 2 * BLK * enc * nh
    return pl.pallas_call(
        functools.partial(cross_fwd_kernel, len(e), nh, hs),
        in_specs=[SM, VM] + [ANY] * len(e),
        out_specs=[VM, VM],
        out_shape=[f32_shape(2 * BLK, 2 * BLK), bf_shape(2 * BLK, 2 * BLK)],
        scratch_shapes=[
            pltpu.VMEM((enc, 4 * BLK), BF),
            pltpu.VMEM((enc // CH, BLK, CH), F32),
            pltpu.SemaphoreType.DMA((len(e), nz)),
        ],
        **params(pairs * 2 * 512, 4e6, pairs),
    )(place, q, *e)


def cross_bwd_kernel(count, nh, hs, place_ref, qe_ref, de_ref, *rest):
    dq_ref, dkv_ref, e_ref, acc_ref, sem = rest[count:]
    fetch(place_ref, rest[:count], e_ref, sem)
    wide = nh * hs
    acc_ref[...] = jnp.zeros_like(acc_ref)

    def kept(value, h):
        lane = lane_of(value.shape)
        first = wide + 3 * h
        keep = ((lane >= h * hs) & (lane < (h + 1) * hs)) | ((lane >= first) & (lane < first + 3))
        return jnp.where(keep, value, jnp.zeros_like(value))

    qm = [kept(qe_ref[...], h) for h in range(nh)]
    dm = [kept(de_ref[...], h) for h in range(nh)]

    def step(ch, carry):
        rows = pl.ds(pl.multiple_of(ch * CH, CH), CH)
        ek = e_ref[rows, : 2 * BLK]
        ev = e_ref[rows, 2 * BLK :]
        ek_t = jnp.transpose(ek.astype(F32)).astype(BF)
        dk = jnp.zeros((CH, 2 * BLK), F32)
        dv = jnp.zeros((CH, 2 * BLK), F32)
        for h in range(nh):
            p = jnp.exp(dot_nt(ek, qm[h]))
            ds = (p * dot_nt(ev, dm[h])).astype(BF)
            dk = dk + dot(ds, qm[h])
            dv = dv + dot(p.astype(BF), dm[h])
            acc_ref[h * hs : (h + 1) * hs, :] += dot(ek_t[h * hs : (h + 1) * hs, :], ds)
        dkv_ref[rows, :] = jnp.concatenate([dk[:, :wide], dv[:, :wide]], axis=1).astype(BF)
        return carry

    lax.fori_loop(0, e_ref.shape[0] // CH, step, 0)
    dq_ref[...] = jnp.transpose(acc_ref[...]).astype(BF)


def cross_bwd(place, qe, de, e, nz, nh, hs):
    enc = len(e) * e[0].shape[0]
    pairs = 2 * BLK * enc * nh
    return pl.pallas_call(
        functools.partial(cross_bwd_kernel, len(e), nh, hs),
        in_specs=[SM, VM, VM] + [ANY] * len(e),
        out_specs=[VM, VM],
        out_shape=[bf_shape(2 * BLK, 2 * BLK), bf_shape(enc, 2 * nh * hs)],
        scratch_shapes=[
            pltpu.VMEM((enc, 4 * BLK), BF),
            pltpu.VMEM((2 * BLK, 2 * BLK), F32),
            pltpu.SemaphoreType.DMA((len(e), nz)),
        ],
        **params(pairs * 2 * 1024, 4e6, pairs),
    )(place, qe, de, *e)


def scale_of(rows):
    return lax.rsqrt(jnp.mean(rows * rows, axis=-1, keepdims=True) + EPS)


def norm_back(rows, gain, grad):
    rr = scale_of(rows)
    scaled = gain * grad
    shared = jnp.mean(rows * scaled, axis=-1, keepdims=True)
    dv = rr * scaled - rows * (rr * rr * rr) * shared
    return dv, jnp.sum(rows * rr * grad, axis=0, keepdims=True)


def in_blocks(pair_ref):
    half = pair_ref.shape[1] // 2
    return jnp.concatenate(
        [pair_ref[m, i * half : (i + 1) * half] for i in range(2) for m in range(2)], axis=0
    )


def put(ref, value):
    cols = value.shape[1]
    ref[:, :cols] = value
    if ref.shape[1] > cols:
        ref[:, cols:] = jnp.zeros((ref.shape[0], ref.shape[1] - cols), ref.dtype)


def own_of(ref, w, half):
    return jnp.concatenate(
        [ref[pl.ds(pl.multiple_of(i * BLK + w * half, half), half), :] for i in range(2)], axis=0
    )


def project_kernel(wide, tok_ref, w_ref, gain_ref, n1_ref, q_ref, k_ref, v_ref, kv_ref):
    x = in_blocks(tok_ref).astype(F32)
    n1 = (x * scale_of(x) * gain_ref[...]).astype(BF)
    n1_ref[...] = n1
    cut = w_ref.shape[1]
    made = (dot(n1[:, :cut], w_ref[0]) + dot(n1[:, cut:], w_ref[1])).astype(BF)
    zero = jnp.zeros((x.shape[0], 2 * BLK), BF)
    for ref, first in ((k_ref, 0), (v_ref, wide), (q_ref, 2 * wide)):
        ref[...] = zero
        ref[:, :wide] = made[:, first : first + wide]
    kv_ref[...] = made[:, : 2 * wide]


def encode_kernel(wide, enc_ref, w_ref, out_ref):
    x = enc_ref[...]
    cut = w_ref.shape[1]
    made = dot(x[:, :cut], w_ref[0, :, : 2 * wide]) + dot(x[:, cut:], w_ref[1, :, : 2 * wide])
    made = made.astype(BF)
    out_ref[...] = jnp.ones(out_ref.shape, BF)
    out_ref[:, :wide] = made[:, :wide]
    out_ref[:, 2 * BLK : 2 * BLK + wide] = made[:, wide:]


def middle_kernel(wide, tok_ref, a_ref, out_ref, gain_ref, w_ref, h_ref, n_ref, cq_ref):
    h = in_blocks(tok_ref).astype(F32)
    h = h + dot(a_ref[0], out_ref[:wide]) + dot(a_ref[1], out_ref[wide:])
    h_ref[...] = h
    n = (h * scale_of(h) * gain_ref[...]).astype(BF)
    n_ref[...] = n
    cut = w_ref.shape[1]
    cols = slice(2 * wide, 3 * wide)
    made = dot(n[:, :cut], w_ref[0, :, cols]) + dot(n[:, cut:], w_ref[1, :, cols])
    cq_ref[...] = jnp.zeros(cq_ref.shape, BF)
    cq_ref[:, :wide] = made.astype(BF)


def third_kernel(wide, half, w_ref, h1_ref, a_ref, out_ref, gain_ref, h_ref, n_ref):
    w = w_ref[0]
    h = own_of(h1_ref, w, half)
    for m in range(2):
        h = h + dot(own_of(a_ref.at[m], w, half), out_ref[m * wide : (m + 1) * wide])
    h_ref[...] = h
    put(n_ref, (h * scale_of(h) * gain_ref[...]).astype(BF))


def heads_kernel(wide, *refs):
    *weights, out_ref = refs
    last = out_ref.shape[2] - len(weights) * wide
    for m in range(out_ref.shape[0]):
        out_ref[m, :, len(weights) * wide :] = jnp.zeros((out_ref.shape[1], last), BF)
    for i, ref in enumerate(weights):
        for m in range(out_ref.shape[0]):
            out_ref[m, :, i * wide : (i + 1) * wide] = ref[:, m * wide : (m + 1) * wide]


def units_kernel(nz, step, share, slot, spot_ref, gate_ref, up_ref, down_ref, ug_ref, wd_ref):
    def move(ref, out, first, at):
        base = pl.multiple_of(jnp.minimum(first // BLK * BLK, ref.shape[1] - 2 * BLK), BLK)
        window = ref[:, pl.ds(base, 2 * BLK)].astype(F32)
        window = pltpu.roll(window, 2 * BLK - (first - base), 1)[:, :BLK]
        window = jnp.where(lane_of(window.shape) < share, window, 0.0)
        out[:, at : at + slot] = window.astype(BF)[:, :slot]

    for m in range(ug_ref.shape[0]):
        for z in range(nz):
            first = (z * step + spot_ref[m]) * share
            move(gate_ref, ug_ref.at[m], first, z * slot)
            move(up_ref, ug_ref.at[m], first, (nz + z) * slot)
        for z in range(wd_ref.shape[2] // slot):
            move(down_ref, wd_ref.at[m], (z * step + spot_ref[m]) * share, z * slot)


def ffn_early_kernel(g0_ref, g1_ref, wd_ref, out_ref):
    width = wd_ref.shape[1]
    rows, cut = g0_ref.shape[0], wd_ref.shape[2]
    for m in range(wd_ref.shape[0]):
        for i, ref in enumerate((g0_ref, g1_ref)):
            made = dot(ref[:, :width], wd_ref[m])
            out_ref[i * rows : (i + 1) * rows, m * cut : (m + 1) * cut] = made


def ffn_kernel(n0_ref, n1_ref, da_ref, ug_ref, act_ref, dgu_ref, d0_ref, d1_ref):
    own = pl.program_id(0) < pl.num_programs(0) // 2
    units = act_ref.shape[1]
    width = ug_ref.shape[0]
    n = jnp.where(own, n0_ref[:, :width], n1_ref[:, :width])
    gate = dot(n, ug_ref[:, :units])
    up = dot(n, ug_ref[:, units:])
    da = da_ref[...]
    scale = 0.7978845608028654
    inner = jnp.tanh(scale * (gate + 0.044715 * gate * gate * gate))
    gelu = 0.5 * gate * (1.0 + inner)
    slope = 0.5 * (1.0 + inner) + 0.5 * gate * (1.0 - inner * inner) * scale * (
        1.0 + 3.0 * 0.044715 * gate * gate
    )
    act_ref[...] = (gelu * up).astype(BF)
    dg = (da * up * slope).astype(BF)
    du = (da * gelu).astype(BF)
    dgu_ref[:, :units] = dg
    dgu_ref[:, units:] = du
    dn = (dot_nt(dg, ug_ref[:, :units]) + dot_nt(du, ug_ref[:, units:])).astype(BF)

    @pl.when(own)
    def _():
        put(d0_ref, dn)

    @pl.when(jnp.logical_not(own))
    def _():
        put(d1_ref, dn)


def half_specs(tiles, cols):
    tile = 4 * BLK
    return [
        pl.BlockSpec((tile, cols), lambda i: (jnp.minimum(i, tiles // 2 - 1), 0)),
        pl.BlockSpec((tile, cols), lambda i: (jnp.maximum(i - tiles // 2, 0), 0)),
    ]


def ffn_both(n, da, ug):
    rows, padded = 2 * n[0].shape[0], n[0].shape[1]
    width, units = ug.shape[0], ug.shape[1] // 2
    tiles = rows // (4 * BLK)

    def row(cols):
        return pl.BlockSpec((4 * BLK, cols), lambda i: (i, 0))

    halved = half_specs(tiles, padded)
    return pl.pallas_call(
        ffn_kernel,
        grid=(tiles,),
        in_specs=halved + [row(units), pl.BlockSpec(ug.shape, lambda i: (0, 0))],
        out_specs=[row(units), row(2 * units)] + halved,
        out_shape=[bf_shape(rows, units), bf_shape(rows, 2 * units)]
        + [bf_shape(rows // 2, padded)] * 2,
        **params(10 * rows * width * units, 12e6, rows * units),
    )(*n, da, ug)


def ffn_late_kernel(nz, share, late, n0_ref, n1_ref, g0_ref, g1_ref, act_ref, dgu_ref, wd_ref, *rest):
    w_ref, o0_ref, o1_ref, acc_ref = rest[late:]
    i = pl.program_id(0)
    own = i < pl.num_programs(0) // 2
    units = act_ref.shape[1]
    width = wd_ref.shape[1]

    @pl.when(i == 0)
    def _():
        acc_ref[...] = jnp.zeros_like(acc_ref)

    n = jnp.where(own, n0_ref[...], n1_ref[...])
    g = jnp.where(own, g0_ref[...], g1_ref[...])
    acc_ref[: 2 * units, :] += dot_tn(dgu_ref[...], n)
    acc_ref[2 * units :, :] += dot_tn(act_ref[...], g)
    cut = wd_ref.shape[2]
    made = jnp.zeros((act_ref.shape[0], width), F32)
    for m in range(wd_ref.shape[0]):
        made = made + dot_nt(act_ref[:, m * cut : (m + 1) * cut], wd_ref[m])
    made = made.astype(BF)

    @pl.when(own)
    def _():
        put(o0_ref, made)

    @pl.when(jnp.logical_not(own))
    def _():
        put(o1_ref, made)

    @pl.when(i == pl.num_programs(0) - 1)
    def _():
        for z in range(nz):
            for j in range(3):
                first = j * units + z * (units // nz)
                w_ref[z, j] = acc_ref[first : first + share, :].astype(BF)


def ffn_late(n, g, act, dgu, wd, nz, share, deps):
    rows, padded = act.shape[0], n[0].shape[1]
    width, units = wd.shape[1], act.shape[1]
    tiles = rows // (4 * BLK)

    def row(cols):
        return pl.BlockSpec((4 * BLK, cols), lambda i: (i, 0))

    halved = half_specs(tiles, padded)
    return pl.pallas_call(
        functools.partial(ffn_late_kernel, nz, share, len(deps)),
        grid=(tiles,),
        in_specs=halved
        + halved
        + [row(units), row(2 * units), pl.BlockSpec(wd.shape, lambda i: (0, 0, 0))]
        + [ANY] * len(deps),
        out_specs=[pl.BlockSpec((nz, 3, share, padded), lambda i: (0, 0, 0, 0))] + halved,
        out_shape=[bf_shape(nz, 3, share, padded)] + [bf_shape(rows // 2, padded)] * 2,
        scratch_shapes=[pltpu.VMEM((3 * units, padded), F32)],
        **params(8 * rows * width * units, 20e6, 0),
    )(*n, *g, act, dgu, wd, *deps)


def add_kernel(a_ref, b_ref, *outs):
    rows = outs[0].shape[0]
    for k, out in enumerate(outs):
        at = slice(k * rows, (k + 1) * rows)
        out[...] = (a_ref[at].astype(F32) + b_ref[at].astype(F32)).astype(BF)


def output_kernel(*refs):
    *parts, out_ref = refs
    width = out_ref.shape[1]
    total = parts[0][:, :width].astype(F32)
    for part in parts[1:]:
        total = total + part[:, :width].astype(F32)
    out_ref[...] = total.astype(BF)


def join_kernel(*refs):
    *parts, out_ref = refs
    rows = parts[0].shape[0]
    for i, part in enumerate(parts):
        out_ref[i * rows : (i + 1) * rows, :] = part[...]


def spread_kernel(x_ref, out_ref):
    for i in range(out_ref.shape[0]):
        out_ref[i] = x_ref[...]


def owners_kernel(wide, plan, target_ref, *refs):
    sets = 1 + max(s for group in plan for s, _ in group)
    xs, ys, out_ref = refs[:sets], refs[sets : sets + len(plan)], refs[sets + len(plan)]
    rows = out_ref.shape[1]
    for k in range(out_ref.shape[0]):
        target = target_ref[k * rows : (k + 1) * rows, :]
        total = jnp.zeros((rows, ys[0].shape[1]), F32)
        column = 0
        for group, y in zip(plan, ys):
            picked = jnp.zeros((rows, y.shape[0]), F32)
            for which, first in group:
                x = xs[which]
                lane = lane_of((rows, x.shape[2]))
                inside = (lane >= first) & (lane < first + wide)
                for m in range(2):
                    hit = inside & (lane - first + m * wide == target[:, column : column + 1])
                    picked = picked + dot_nt(hit.astype(BF), x[m])
                column += 1
            total = total + dot(picked.astype(BF), y[...])
        put(out_ref.at[k], total.astype(BF))


def deal_kernel(*refs):
    *parts, out_ref = refs
    at = 0
    for part in parts:
        total = jnp.sum(part[...].astype(F32), axis=0)
        rows = total.shape[0] // out_ref.shape[0]
        for i in range(out_ref.shape[0]):
            out_ref[i, at : at + rows, :] = total[i * rows : (i + 1) * rows].astype(BF)
        at += rows


def dh2_kernel(*refs):
    *parts, h_ref, cot_ref, gain_ref, dh_ref, dy_ref, gain_out = refs
    width = h_ref.shape[1]
    grad = parts[0][:, :width].astype(F32)
    for part in parts[1:]:
        grad = grad + part[:, :width].astype(F32)
    dv, gain_out[...] = norm_back(h_ref[...], gain_ref[...], grad)
    dh = cot_ref[:, :width].astype(F32) + dv
    dh_ref[...] = dh
    put(dy_ref, dh.astype(BF))


def dh1_kernel(wide, half, w_ref, dq_ref, cq_ref, h1_ref, dh2_ref, gain_ref, dh_ref, dy_ref, gain_out):
    w = w_ref[0]
    dq = jnp.concatenate([own_of(dq_ref.at[m], w, half)[:, :wide] for m in range(2)], axis=1)
    grad = dot_nt(dq, cq_ref[...])
    dv, gain_out[...] = norm_back(own_of(h1_ref, w, half), gain_ref[...], grad)
    dh = dh2_ref[...] + dv
    dh_ref[...] = dh
    put(dy_ref, dh.astype(BF))


def last_kernel(wide, half, w_ref, d_ref, weight_ref, tok_ref, dh1_ref, gain_ref, out_ref, gain_out):
    w = w_ref[0]
    d = jnp.concatenate(
        [own_of(d_ref.at[m, i], w, half)[:, :wide] for i in range(3) for m in range(2)], axis=1
    )
    grad = dot_nt(d, weight_ref[...])
    dv, gain_out[...] = norm_back(tok_ref[w].astype(F32), gain_ref[...], grad)
    out_ref[...] = dh1_ref[...] + dv


def grad_prep_kernel(nh, hs, dy_ref, w_ref, o_ref, out_ref, de_ref, dh_ref, del_ref):
    wide = nh * hs
    dy = in_blocks(dy_ref)[:, : w_ref.shape[1]]
    out_ref[...] = dy
    da = dot_nt(dy, w_ref[...]).astype(BF)
    terms = da.astype(F32) * o_ref[...]
    delta = [jnp.sum(head_mask(terms, h, hs), axis=1, keepdims=True) for h in range(nh)]
    dh_ref[...] = pltpu.roll(da.astype(F32), hs, 1).astype(BF)
    lane = lane_of(del_ref.shape)
    cols = jnp.zeros(del_ref.shape, F32)
    for h in range(nh):
        cols = jnp.where(lane == h, delta[h], cols)
    del_ref[...] = cols
    de = pieces_into(da.astype(F32), [-t for t in delta], wide).astype(BF)
    for i in range(de_ref.shape[0]):
        de_ref[i] = de


def grad_prep(dy, padded, o, nh, hs, copies=1, deps=()):
    rows, width = o.shape[0], padded.shape[1]
    return plain(
        functools.partial(grad_prep_kernel, nh, hs),
        [],
        [dy, padded, o],
        [
            bf_shape(rows, width),
            bf_shape(copies, rows, 2 * BLK),
            bf_shape(rows, 2 * BLK),
            f32_shape(rows, BLK),
        ],
        deps=deps,
    )


def local(
    tokens,
    encoded,
    cotangent,
    assign,
    bucket_ids,
    gain_self,
    gain_cross,
    gain_ffn,
    query_weight,
    key_weight,
    value_weight,
    out_weight,
    cross_query,
    cross_key,
    cross_value,
    cross_out,
    gate_weight,
    up_weight,
    down_weight,
    bucket_table,
):
    nctx = lax.axis_size("ctx")
    nw = lax.axis_size("wsh")
    c = lax.axis_index("ctx")
    w = lax.axis_index("wsh")
    both = ("ctx", "wsh")
    rows, width = tokens.shape
    half = rows // 2
    length = rows * nw * nctx
    buckets, heads = bucket_table.shape
    inner = query_weight.shape[1]
    hs = inner // heads
    nh = heads // nw
    wide = nh * hs
    plane = 4
    nz = nctx // plane
    spot = (c % plane) * nw + w
    zed = c // plane
    hidden = gate_weight.shape[1]
    share = hidden // (nctx * nw)
    slot = -(-share // 32) * 32

    def pair(x, axis=0, tiled=True):
        return lax.all_gather(x, "wsh", axis=axis, tiled=tiled)

    def halves(parts):
        return lax.all_to_all(parts, "wsh", 0, 0, tiled=True)

    def mate(x):
        return lax.ppermute(x, "wsh", [(i, (i + 1) % nw) for i in range(nw)])

    planes = [[z * plane + i for i in range(plane)] for z in range(nz)]
    columns = [[z * plane + i for z in range(nz)] for i in range(plane)]

    def in_plane(x):
        return lax.all_to_all(x, "ctx", 0, 0, tiled=True, axis_index_groups=planes)

    def in_column(x):
        return lax.all_to_all(x, "ctx", 0, 0, tiled=True, axis_index_groups=columns)

    padded = -(-width // BLK) * BLK

    def spread(x, count, deps=()):
        x = x.reshape(-1, x.shape[-1])
        return plain(spread_kernel, [], [x], [bf_shape(count, *x.shape)], (0, 1e6, 0), deps)[0]

    def add(a, b, deps=()):
        return plain(add_kernel, [], [a, b], [bf_shape(rows, padded)] * plane, (0, 1e6, 0), deps)

    def deal(parts, count, deps=()):
        shape = bf_shape(count, sum(x.shape[1] for x in parts) // count, parts[0].shape[2])
        return plain(deal_kernel, [], parts, [shape], (0, 1e6, 0), deps)[0]

    def tree(parts):
        while len(parts) > 1:
            parts = [parts[i] + parts[i + 1] for i in range(0, len(parts), 2)]
        return parts[0]

    def near(x, k):
        return lax.ppermute(x, "ctx", [(i, i ^ k) for i in range(nctx)])

    def stacked(parts, deps=()):
        shape = bf_shape(len(parts) * parts[0].shape[0], parts[0].shape[1])
        return plain(join_kernel, [], parts, [shape], (0, 1e6, 0), deps)[0]

    cut = inner // (nctx * nw)

    def targets(count):
        index = jnp.arange(plane * nz * count * cut, dtype=jnp.int32)
        to_k, to_z = index // (nz * count * cut), index // (count * cut) % nz
        to_i, to_t = index // cut % count, index % cut
        column = ((to_z * plane + to_k) * nw + w) * cut + to_t
        which = jnp.arange(count, dtype=jnp.int32)
        return jnp.where(to_i[:, None] == which[None, :], column[:, None], -1).astype(jnp.int32)

    def owner_parts(plan, xs, ys, deps=()):
        count = sum(len(group) for group in plan)
        return plain(
            functools.partial(owners_kernel, wide, plan),
            [],
            [targets(count)] + xs + ys,
            [bf_shape(plane, nz * count * cut, padded)],
            (3e9, 6e6, 0),
            deps,
        )[0]

    def owner_sums(parts, count):
        total = jnp.sum(parts.astype(F32), axis=0)
        return [total[i * cut : (i + 1) * cut, :width] for i in range(count)]

    lanes = jnp.arange(nctx, dtype=jnp.int32)
    owner = jnp.sum(jnp.where(assign[None, :] == lanes[:, None], lanes[None, :], 0), axis=1)
    chip_slot = owner % plane * nz + owner // plane
    meta = jnp.concatenate([owner, jnp.take(assign, c)[None], chip_slot]).astype(jnp.int32)
    core = w.astype(jnp.int32)[None]
    place = jnp.stack([c % plane, zed]).astype(jnp.int32)
    chip = nw * rows

    gains = pair(jnp.stack([gain_self, gain_cross, gain_ffn]), axis=1).astype(F32)
    gains = [gains[i : i + 1] for i in range(3)]
    tok = pair(tokens, tiled=False)

    def head_parts(weights, deps=()):
        shape = bf_shape(nw, weights[0].shape[0], -(-3 * wide // BLK) * BLK)
        return plain(functools.partial(heads_kernel, wide), [], weights, [shape], deps=deps)[0]

    g_own = jnp.pad(cotangent, ((0, 0), (0, padded - width)))
    g_parts = [g_own] + [near(g_own, k) for k in range(1, plane)]
    out_full, cross_out_full = pair(out_weight), pair(cross_out)
    qkv_heads = halves(head_parts([key_weight, value_weight, query_weight]))
    n1, q, k_own, v_own, kv_own = plain(
        functools.partial(project_kernel, wide),
        [],
        [tok, qkv_heads, gains[0]],
        [bf_shape(chip, width)] + [bf_shape(chip, 2 * BLK)] * 3 + [bf_shape(chip, 2 * wide)],
        deps=(out_full, cross_out_full),
    )
    kv = lax.all_gather(kv_own, "ctx", axis=0, tiled=True).reshape(nctx, chip, 2 * wide)

    cross_heads = halves(head_parts([cross_key, cross_value, cross_query], deps=(kv_own,)))
    enc_pair = pair(after(encoded, kv_own))
    (ekv_own,) = plain(
        functools.partial(encode_kernel, wide),
        [],
        [enc_pair, cross_heads],
        [bf_shape(enc_pair.shape[0], 4 * BLK)],
    )
    ekv = [ekv_own] + [near(ekv_own, plane * k) for k in range(1, nz)]

    hot = (bucket_ids[None, :] == jnp.arange(buckets, dtype=jnp.int32)[:, None]).astype(BF)
    values = dot_tn(lax.dynamic_slice_in_dim(bucket_table, w * nh, nh, 1), hot)
    ts, tt = bias_tiles(after(values, kv_own))

    spots = jnp.stack([(c % plane) * nw + i for i in range(nw)]).astype(jnp.int32)
    ug, wd = plain(
        functools.partial(units_kernel, nz, plane * nw, share, slot),
        [spots],
        [gate_weight, up_weight, down_weight.T],
        [
            bf_shape(nw, gate_weight.shape[0], 2 * nz * slot),
            bf_shape(nw, width, nz // nw * slot),
        ],
        deps=(kv_own,),
    )
    ug_parts, wd_parts = ug, wd

    ekv = stacked(ekv, deps=(ug_parts,))
    ug = halves(ug_parts).reshape(width, -1)
    wd = halves(wd_parts)
    ekv = [ekv] + [near(ekv, k) for k in range(1, plane)]
    g_plane = stacked(g_parts, deps=(ts,))
    g_plane = g_plane, mate(g_plane)
    row_pad = ((0, 2 * BLK - wide), (0, 0))
    out_padded, cross_out_padded = jnp.pad(out_weight, row_pad), jnp.pad(cross_out, row_pad)
    o1, qe1, lse1 = self_fwd(
        meta, q, kv, ts, nh, hs, deps=(ug, wd, *ekv, *g_plane, out_padded, cross_out_padded)
    )
    a1_pair = pair(o1[:, :wide].astype(BF), tiled=False)
    h1, n2, cq = plain(
        functools.partial(middle_kernel, wide),
        [],
        [tok, a1_pair, out_full, gains[1], cross_heads],
        [f32_shape(chip, width), bf_shape(chip, width), bf_shape(chip, 2 * BLK)],
    )
    qg = lax.all_gather(qe1, "ctx", axis=0, tiled=True).reshape(nctx, chip, 2 * BLK)
    cq_full, ck_full, cv_full = pair(cross_query), pair(cross_key), pair(cross_value)
    qkv_full = pair(jnp.concatenate([query_weight, key_weight, value_weight], axis=1))

    o2, qe2 = cross_fwd(place, cq, ekv, nz, nh, hs)
    a2_pair = pair(o2[:, :wide].astype(BF), tiled=False)
    h2, n3 = plain(
        functools.partial(third_kernel, wide, half),
        [core],
        [h1, a2_pair, cross_out_full, gains[2]],
        [f32_shape(rows, width), bf_shape(rows, padded)],
    )

    (dact,) = plain(
        ffn_early_kernel, [], [*g_plane, wd], [f32_shape(nw * plane * rows, nz * slot)], deps=(n3,)
    )
    n3_plane = stacked([n3] + [near(n3, k) for k in range(1, plane)], deps=(dact,))
    n3_plane = n3_plane, mate(n3_plane)
    act, dgu, dn0, dn1 = ffn_both(n3_plane, dact, ug)
    sent = add(dn0, mate(dn1), deps=(qg,))
    got = [near(sent[k], k) for k in range(1, plane)]
    ffn, out0, out1 = ffn_late(n3_plane, g_plane, act, dgu, wd, nz, share, (sent[0],))
    dh2, dy2, gain3 = plain(
        dh2_kernel,
        [],
        [sent[0]] + got + [h2, g_own, gains[2]],
        [f32_shape(rows, width), bf_shape(rows, padded), f32_shape(1, width)],
        deps=(out0,),
    )
    ffn, out0, out1, _ = lax.optimization_barrier((ffn, out0, out1, gain3))

    dy2, de2, _, _ = grad_prep(pair(dy2, tiled=False), cross_out_padded, o2, nh, hs)
    dcq, dekv = cross_bwd(place, qe2, de2[0], ekv, nz, nh, hs)
    dekv = in_plane(dekv.reshape(plane, -1, 2 * wide))
    dcq_pair = pair(dcq, tiled=False)
    dh1, dy1, gain2 = plain(
        functools.partial(dh1_kernel, wide, half),
        [core],
        [dcq_pair, cq_full, h1, dh2, gains[1]],
        [f32_shape(rows, width), bf_shape(rows, padded), f32_shape(1, width)],
    )

    dy1, de1, dhi1, delta1 = grad_prep(
        pair(dy1, tiled=False), out_padded, o1, nh, hs, copies=nz
    )
    dg = in_column(de1)
    dekv = deal([dekv], nz, deps=(de1,))
    dq, rev = self_dq(meta, q, dhi1, lse1, delta1, kv, ts, nh, hs, deps=(dekv,))
    dg = spread(dg, plane, deps=(dq, qg, ck_full, cv_full, qkv_full))
    dq, rev, ffn, dekv, out0, out1, _ = lax.optimization_barrier(
        (dq, rev, ffn, dekv, out0, out1, dg[0, 0])
    )
    dekv = in_column(dekv)
    dg = in_plane(dg).reshape(nctx, chip, 2 * BLK)

    dekv_pair = pair(deal([dekv], 1)[0], tiled=False)
    made = owner_parts(
        (((0, 0),), ((1, 0),), ((2, 0),), ((3, 0), (3, wide))),
        [a1_pair, a2_pair, dcq_pair, dekv_pair],
        [dy1, dy2, n2, enc_pair],
    )
    ffn = lax.psum_scatter(
        ffn.reshape(nz, 3 * share, padded),
        "ctx",
        scatter_dimension=0,
        axis_index_groups=columns,
        tiled=True,
    )
    dk, dv = self_dkv(meta, k_own, v_own, qg, dg, tt, nh, hs, deps=(made,))
    made = in_plane(after(made, dg))

    dqkv_pair = pair(jnp.stack([dq, dk, dv]), tiled=False).reshape(nw, 3, chip, 2 * BLK)
    dqkv = [dqkv_pair[:, i] for i in range(3)]
    second = in_plane(owner_parts((((0, 0), (1, 0), (2, 0)),), dqkv, [n1], deps=(made,)))
    tokens_grad, gain1 = plain(
        functools.partial(last_kernel, wide, half),
        [core],
        [dqkv_pair, qkv_full, tok, dh1, gains[0]],
        [f32_shape(rows, width), f32_shape(1, width)],
    )
    out_sent = add(out0, mate(after(out1, dk)), deps=(tokens_grad,))
    both_sums = deal([made, second], nz, deps=(out_sent[0],))
    gain1, rev, dekv_pair, _ = lax.optimization_barrier(
        (gain1, rev, dekv_pair, both_sums[0, 0])
    )
    out_sent = lax.optimization_barrier((out_sent, both_sums))[0]
    out_got = [near(out_sent[k], k) for k in range(1, plane)]
    (output,) = plain(output_kernel, [], [h2, out_sent[0]] + out_got, [bf_shape(rows, width)])
    out_share, cross_out_share, cq_t, ck_t, cv_t, q_t, k_t, v_t = owner_sums(
        in_column(both_sums), 8
    )
    ffn = ffn[0, :, :width].astype(F32).reshape(3, share, width)

    def joined(x):
        return jnp.swapaxes(x[:, :, :wide], 0, 1).reshape(-1, inner)

    def own_encoder(x):
        return lax.dynamic_slice_in_dim(x, w * encoded.shape[0], encoded.shape[0], 0)

    dek, dev = joined(dekv_pair), joined(dekv_pair[:, :, wide:])
    encoded_grad = dot_nt(own_encoder(dek), ck_full) + dot_nt(own_encoder(dev), cv_full)

    by_distance = jnp.sum(rev.reshape(nh, 8, -1), axis=1)[:, :length]
    hot_rev = (
        jnp.flip(bucket_ids)[None, :] == jnp.arange(buckets, dtype=jnp.int32)[:, None]
    ).astype(F32)
    table_own = lax.dot_general(
        hot_rev, by_distance, (((1,), (1,)), ((), ())), precision=lax.Precision.HIGHEST
    )
    table = lax.dynamic_update_slice_in_dim(
        jnp.zeros((buckets, heads), F32), table_own, w * nh, 1
    )

    small = jnp.concatenate([gain1[0], gain2[0], gain3[0], table.reshape(-1)])
    small = jnp.pad(small, (0, -small.shape[0] % BLK)).reshape(-1, BLK)
    small = small + mate(small)
    small = tree([small] + [near(small, k) for k in range(1, plane)])
    small = tree([small] + [near(small, plane * k) for k in range(1, nz)])
    small = small.reshape(-1)
    table = small[3 * width : 3 * width + buckets * heads].reshape(buckets, heads)
    return (
        output,
        tokens_grad,
        encoded_grad,
        small[:width],
        small[width : 2 * width],
        small[2 * width : 3 * width],
        q_t.T,
        k_t.T,
        v_t.T,
        out_share,
        cq_t.T,
        ck_t.T,
        cv_t.T,
        cross_out_share,
        ffn[0].T,
        ffn[1].T,
        ffn[2],
        table,
    )


def solution(mesh):
    rows = P(("seq", "ctx", "wsh"), None)
    cols = P("seq", ("ctx", "wsh"))
    split = P("wsh", None)
    return jax.shard_map(
        local,
        mesh=mesh,
        in_specs=(rows, rows, rows, P(), P(), P("wsh"), P("wsh"), P("wsh"))
        + (split,) * 11
        + (P(),),
        out_specs=(
            rows,
            rows,
            rows,
            P("seq"),
            P("seq"),
            P("seq"),
            cols,
            cols,
            cols,
            rows,
            cols,
            cols,
            cols,
            rows,
            cols,
            cols,
            rows,
            P("seq", None),
        ),
        check_vma=False,
    )
```

```python
import functools

import jax
import jax.numpy as jnp
from jax import lax
from jax.experimental import pallas as pl
from jax.experimental.pallas import tpu as pltpu
from jax.sharding import PartitionSpec as P

EPS = 1e-06
NEG = -1e30
F32 = jnp.float32
BF = jnp.bfloat16
BLK = 128
GRP = 4
CH = BLK * GRP
VLIM = 60 * 1024 * 1024
SLOW = 64


def dot(a, b):
    return lax.dot_general(a, b, (((1,), (0,)), ((), ())), preferred_element_type=F32)


def dot_nt(a, b):
    return lax.dot_general(a, b, (((1,), (1,)), ((), ())), preferred_element_type=F32)


def dot_tn(a, b):
    return lax.dot_general(a, b, (((0,), (0,)), ((), ())), preferred_element_type=F32)


def lane_of(shape):
    return lax.broadcasted_iota(jnp.int32, shape, 1)


def head_mask(value, head, hs):
    lane = lane_of(value.shape)
    keep = (lane >= head * hs) & (lane < (head + 1) * hs)
    return jnp.where(keep, value, jnp.zeros_like(value))


def lane_fold(value, op):
    out = value[:, :BLK]
    for i in range(1, value.shape[1] // BLK):
        out = op(out, value[:, i * BLK : (i + 1) * BLK])
    return out


def pieces_into(base, columns, first):
    lane = lane_of(base.shape)
    out = base
    for i, column in enumerate(columns):
        rest = column
        for j in range(3):
            part = rest.astype(BF).astype(F32)
            rest = rest - part
            out = jnp.where(lane == first + 3 * i + j, part, out)
    return out


def params(flops, nbytes, trans):
    return dict(
        compiler_params=pltpu.CompilerParams(vmem_limit_bytes=VLIM),
        cost_estimate=pl.CostEstimate(
            flops=int(flops) // SLOW,
            bytes_accessed=int(nbytes) // SLOW,
            transcendentals=int(trans) // SLOW,
        ),
    )


def after(value, *deps):
    return lax.optimization_barrier((value,) + deps)[0]


def f32_shape(*dims):
    return jax.ShapeDtypeStruct(dims, F32)


def bf_shape(*dims):
    return jax.ShapeDtypeStruct(dims, BF)


def plain(kernel, scalars, inputs, outputs, cost=(1e9, 4e6, 0), deps=()):
    count, late = len(scalars) + len(inputs), len(deps)

    def body(*refs):
        kernel(*refs[:count], *refs[count + late :])

    return pl.pallas_call(
        body,
        in_specs=[SM] * len(scalars) + [VM] * len(inputs) + [ANY] * late,
        out_specs=[VM] * len(outputs),
        out_shape=list(outputs),
        **params(*cost),
    )(*scalars, *inputs, *deps)


VM = pl.BlockSpec(memory_space=pltpu.VMEM)
ANY = pl.BlockSpec(memory_space=pl.ANY)
SM = pl.BlockSpec(memory_space=pltpu.SMEM)


def tie(x, *deps):
    return pl.pallas_call(
        lambda *refs: None,
        in_specs=[ANY] * (1 + len(deps)),
        out_specs=ANY,
        out_shape=jax.ShapeDtypeStruct(x.shape, x.dtype),
        input_output_aliases={0: 0},
        **params(0, 0, 0),
    )(x, *deps)


def bias_kernel(nb, nh, nat_ref, rev_ref, ts_ref, tt_ref):
    row = lax.broadcasted_iota(jnp.int32, (BLK, BLK), 0)
    col = lax.broadcasted_iota(jnp.int32, (BLK, BLK), 1)
    upper = col >= row

    def skew(line):
        eight = pltpu.roll(jnp.broadcast_to(line, (8, BLK)), 0, 1, stride=1, stride_axis=0)
        return jnp.concatenate(
            [eight] + [pltpu.roll(eight, 8 * i, 1) for i in range(1, BLK // 8)], axis=0
        )

    def step(r, carry):
        d = nb - 1 - r
        first, second = rev_ref[nb - jnp.maximum(d, 0)], rev_ref[nb - 1 - jnp.maximum(d, 0)]
        for h in range(nh):
            tile = jnp.where(upper, skew(first[h : h + 1]), skew(second[h : h + 1]))
            ts_ref[r, h] = jnp.where(d * BLK + row - col >= 0, tile, NEG).astype(BF)
        d = r - (GRP - 1)
        first, second = nat_ref[jnp.maximum(d, 0) + 1], nat_ref[jnp.maximum(d, 0)]
        for h in range(nh):
            tile = jnp.where(upper, skew(first[h : h + 1]), skew(second[h : h + 1]))
            tt_ref[r, h] = jnp.where(d * BLK + col - row >= 0, tile, NEG).astype(BF)
        return carry

    lax.fori_loop(0, nb + GRP - 1, step, 0)


def bias_tiles(values, deps=()):
    nh, length = values.shape
    nb = length // BLK
    zero = jnp.zeros((nh, 1), F32)
    nat = jnp.concatenate([jnp.zeros((nh, BLK), F32), values], axis=1)
    rev = jnp.concatenate([zero, jnp.flip(values, 1), jnp.zeros((nh, BLK - 1), F32)], axis=1)
    nat = jnp.transpose(nat.reshape(nh, nb + 1, BLK), (1, 0, 2))
    rev = jnp.transpose(rev.reshape(nh, nb + 1, BLK), (1, 0, 2))
    shape = bf_shape(nb + GRP - 1, nh, BLK, BLK)
    return plain(
        functools.partial(bias_kernel, nb, nh), [], [nat, rev], [shape, shape], deps=deps
    )


def gather_blocks(ref, meta_ref, nctx, first, lo, hi, base=0):
    parts = []
    for i in range(GRP):
        t = first + i
        early = t < nctx
        slot = meta_ref[base + jnp.where(early, t, 2 * nctx - 1 - t)]
        at = pl.multiple_of(jnp.where(early, 0, BLK), BLK)
        parts.append(ref[slot, pl.ds(at, BLK), lo:hi])
    return jnp.concatenate(parts, axis=0)


def fetch(parts, held_ref, sem):
    rows = parts[0].shape[0]
    copies = [
        pltpu.make_async_copy(part, held_ref.at[pl.ds(k * rows, rows)], sem.at[k])
        for k, part in enumerate(parts)
    ]
    for copy in copies:
        copy.start()
    for copy in copies:
        copy.wait()


def bias_of(ref, first):
    rows = ref.shape[1] * BLK
    return jnp.concatenate(
        [ref[first + i].reshape(rows, BLK) for i in range(GRP)], axis=1
    ).astype(F32)


def stack_heads(value, hs, nh, shift=0):
    return jnp.concatenate([head_mask(value, h + shift, hs) for h in range(nh)], axis=0)


def merge_heads(stacked, hs, nh, shift=0):
    rows = stacked.shape[0] // nh
    total = jnp.zeros((rows, stacked.shape[1]), F32)
    for h in range(nh):
        total = total + head_mask(stacked[h * rows : (h + 1) * rows], h + shift, hs)
    return total


def pick_columns(columns, nh, rows):
    out = jnp.zeros((rows, BLK), F32)
    lane = lane_of(out.shape)
    for h in range(nh):
        out = jnp.where(lane == h, columns[h * rows : (h + 1) * rows], out)
    return out


def stack_columns(ref, rows, nh):
    return jnp.concatenate([ref[rows, h : h + 1] for h in range(nh)], axis=0)


def self_fwd_kernel(count, nctx, nh, hs, meta_ref, q_ref, ts_ref, *rest):
    o_ref, a_ref, qe_ref, lse_ref, s_ref, acc_ref, flat_ref, sem = rest[-8:]
    fetch(rest[:count], flat_ref, sem)
    kv_ref = flat_ref.reshape(nctx, 2 * BLK, flat_ref.shape[1])
    nb = 2 * nctx
    wide = nh * hs
    early = meta_ref[nctx]
    for half in range(2):
        blk = early if half == 0 else nb - 1 - early
        chunks = blk // GRP + 1
        rows = slice(half * BLK, (half + 1) * BLK)
        q = q_ref[rows, :]
        qm = stack_heads(q, hs, nh)

        def score(ch, top):
            keys = gather_blocks(kv_ref, meta_ref, nctx, ch * GRP, 0, 2 * BLK, 2 * nctx + 1)
            s = dot_nt(qm, keys) + bias_of(ts_ref, nb - 1 - blk + ch * GRP)
            s_ref[ch] = s
            return jnp.maximum(top, lane_fold(s, jnp.maximum))

        top = lax.fori_loop(0, chunks, score, jnp.full((nh * BLK, BLK), NEG, F32))
        top = jnp.max(top, axis=1, keepdims=True)
        acc_ref[...] = jnp.zeros_like(acc_ref)

        def weigh(ch, total):
            vals = gather_blocks(kv_ref, meta_ref, nctx, ch * GRP, BLK, 3 * BLK, 2 * nctx + 1)
            p = jnp.exp(s_ref[ch] - top)
            acc_ref[...] += dot(p.astype(BF), vals)
            return total + lane_fold(p, jnp.add)

        total = lax.fori_loop(0, chunks, weigh, jnp.zeros((nh * BLK, BLK), F32))
        total = jnp.sum(total, axis=1, keepdims=True)
        o = pltpu.roll(merge_heads(acc_ref[...] / total, hs, nh, 1), 2 * BLK - hs, 1)
        o_ref[rows, :] = o
        a_ref[rows, :] = o[:, :wide].astype(BF)
        lse = pick_columns(top + jnp.log(total), nh, BLK)
        lse_ref[rows, :] = lse
        minus = [-lse[:, h : h + 1] for h in range(nh)]
        qe_ref[rows, :] = pieces_into(q.astype(F32), minus, wide).astype(BF)


def self_fwd(meta, q, kv, ts, nh, hs, deps=()):
    nctx = len(kv) * kv[0].shape[0] // (2 * BLK)
    nb = 2 * nctx
    rows = 2 * BLK
    pairs = (nb + 1) * BLK * BLK * nh
    return pl.pallas_call(
        functools.partial(self_fwd_kernel, len(kv), nctx, nh, hs),
        in_specs=[SM, VM, VM] + [ANY] * (len(kv) + len(deps)),
        out_specs=[VM] * 4,
        out_shape=[
            f32_shape(rows, rows),
            bf_shape(rows, nh * hs),
            bf_shape(rows, rows),
            f32_shape(rows, BLK),
        ],
        scratch_shapes=[
            pltpu.VMEM((nb // GRP, nh * BLK, CH), F32),
            pltpu.VMEM((nh * BLK, 2 * BLK), F32),
            pltpu.VMEM((nb * BLK, kv[0].shape[1]), BF),
            pltpu.SemaphoreType.DMA((len(kv),)),
        ],
        **params(pairs * 2 * 512, 10e6, pairs),
    )(meta, q, ts, *kv, *deps)


def self_dq_kernel(count, nctx, nh, hs, meta_ref, q_ref, da_ref, lse_ref, del_ref, ts_ref, *rest):
    dq_ref, rev_ref, acc_ref, flat_ref, sem = rest[-5:]
    fetch(rest[:count], flat_ref, sem)
    kv_ref = flat_ref.reshape(nctx, 2 * BLK, flat_ref.shape[1])
    nb = 2 * nctx
    early = meta_ref[nctx]
    span = CH + BLK
    rev_ref[...] = jnp.zeros_like(rev_ref)
    for half in range(2):
        blk = early if half == 0 else nb - 1 - early
        chunks = blk // GRP + 1
        rows = slice(half * BLK, (half + 1) * BLK)
        qm = stack_heads(q_ref[rows, :], hs, nh)
        dm = stack_heads(da_ref[rows, :], hs, nh, 1)
        lse = stack_columns(lse_ref, rows, nh)
        delta = stack_columns(del_ref, rows, nh)
        acc_ref[...] = jnp.zeros_like(acc_ref)

        def step(ch, carry):
            held = gather_blocks(kv_ref, meta_ref, nctx, ch * GRP, 0, 3 * BLK, 2 * nctx + 1)
            keys, vals = held[:, : 2 * BLK], held[:, BLK:]
            off = pl.multiple_of((ch * GRP - blk + nb - 1) * BLK, BLK)
            s = dot_nt(qm, keys) + bias_of(ts_ref, nb - 1 - blk + ch * GRP)
            p = jnp.exp(s - lse)
            ds = (p * (dot_nt(dm, vals) - delta)).astype(BF)
            acc_ref[...] += dot(ds, keys)
            flat = jnp.concatenate([jnp.zeros((nh * BLK, BLK), F32), ds.astype(F32)], axis=1)
            for h in range(nh):
                line = flat[h * BLK : h * BLK + 8]
                for i in range(1, BLK // 8):
                    at = h * BLK + 8 * i
                    line = line + pltpu.roll(flat[at : at + 8], span - 8 * i, 1)
                rev_ref[h * 8 : (h + 1) * 8, pl.ds(off, span)] += line
            return carry

        lax.fori_loop(0, chunks, step, 0)
        dq_ref[rows, :] = merge_heads(acc_ref[...], hs, nh).astype(BF)


def self_dq(meta, q, da, lse, delta, kv, ts, nh, hs, deps=()):
    nctx = len(kv) * kv[0].shape[0] // (2 * BLK)
    nb = 2 * nctx
    pairs = (nb + 1) * BLK * BLK * nh
    return pl.pallas_call(
        functools.partial(self_dq_kernel, len(kv), nctx, nh, hs),
        in_specs=[SM] + [VM] * 5 + [ANY] * (len(kv) + len(deps)),
        out_specs=[VM, VM],
        out_shape=[
            jax.ShapeDtypeStruct((2 * BLK, 2 * BLK), BF),
            jax.ShapeDtypeStruct((8 * nh, nb * BLK + CH), F32),
        ],
        scratch_shapes=[
            pltpu.VMEM((nh * BLK, 2 * BLK), F32),
            pltpu.VMEM((nb * BLK, kv[0].shape[1]), BF),
            pltpu.SemaphoreType.DMA((len(kv),)),
        ],
        **params(pairs * 2 * 896, 10e6, pairs),
    )(meta, q, da, lse, delta, ts, *kv, *deps)


def self_dkv_kernel(nctx, nh, hs, meta_ref, k_ref, v_ref, qg_ref, dg_ref, tt_ref, *rest):
    dk_ref, dv_ref, ka_ref, va_ref = rest[-4:]
    nb = 2 * nctx
    wide = nh * hs
    early = meta_ref[nctx]

    def extended(value):
        lane = lane_of(value.shape)
        parts = []
        for h in range(nh):
            first = wide + 3 * h
            ones = (lane >= first) & (lane < first + 3)
            parts.append(jnp.where(ones, jnp.ones_like(value), head_mask(value, h, hs)))
        return jnp.concatenate(parts, axis=0)

    for half in range(2):
        blk = early if half == 0 else nb - 1 - early
        rows = slice(half * BLK, (half + 1) * BLK)
        km = extended(k_ref[rows, :])
        vm = extended(v_ref[rows, :])
        ka_ref[...] = jnp.zeros_like(ka_ref)
        va_ref[...] = jnp.zeros_like(va_ref)

        def step(ch, carry):
            qc = gather_blocks(qg_ref, meta_ref, nctx, ch * GRP, 0, 2 * BLK)
            dc = gather_blocks(dg_ref, meta_ref, nctx, ch * GRP, 0, 2 * BLK, nctx + 1)
            p = jnp.exp(dot_nt(km, qc) + bias_of(tt_ref, ch * GRP - blk + GRP - 1))
            ds = (p * dot_nt(vm, dc)).astype(BF)
            ka_ref[...] += dot(ds, qc)
            va_ref[...] += dot(p.astype(BF), dc)
            return carry

        lax.fori_loop(blk // GRP, nb // GRP, step, 0)
        dk_ref[rows, :] = merge_heads(ka_ref[...], hs, nh).astype(BF)
        dv_ref[rows, :] = merge_heads(va_ref[...], hs, nh).astype(BF)


def self_dkv(meta, k, v, qg, dg, tt, nh, hs, deps=()):
    nctx = qg.shape[0]
    nb = 2 * nctx
    pairs = (nb + 1) * BLK * BLK * nh
    shape = jax.ShapeDtypeStruct((2 * BLK, 2 * BLK), BF)
    return pl.pallas_call(
        functools.partial(self_dkv_kernel, nctx, nh, hs),
        in_specs=[SM] + [VM] * 5 + [ANY] * len(deps),
        out_specs=[VM, VM],
        out_shape=[shape, shape],
        scratch_shapes=[
            pltpu.VMEM((nh * BLK, 2 * BLK), F32),
            pltpu.VMEM((nh * BLK, 2 * BLK), F32),
        ],
        **params(pairs * 2 * 1024, 10e6, pairs),
    )(meta, k, v, qg, dg, tt, *deps)


def cross_fwd_kernel(nh, hs, q_ref, e_ref, o_ref, a_ref, qe_ref, s_ref):
    wide = nh * hs
    chunks = e_ref.shape[0] // CH
    rows = q_ref.shape[0]
    q = q_ref[...]
    qm = stack_heads(q, hs, nh)
    top = jnp.full((nh * rows, BLK), NEG, F32)
    for ch in range(chunks):
        s = dot_nt(qm, e_ref[ch * CH : (ch + 1) * CH, : 2 * BLK])
        s_ref[ch] = s
        top = jnp.maximum(top, lane_fold(s, jnp.maximum))
    top = jnp.max(top, axis=1, keepdims=True)
    total = jnp.zeros((nh * rows, BLK), F32)
    acc = jnp.zeros((nh * rows, 2 * BLK), F32)
    for ch in range(chunks):
        p = jnp.exp(s_ref[ch] - top)
        total = total + lane_fold(p, jnp.add)
        acc = acc + dot(p.astype(BF), e_ref[ch * CH : (ch + 1) * CH, 2 * BLK :])
    total = jnp.sum(total, axis=1, keepdims=True)
    o = merge_heads(acc / total, hs, nh)
    o_ref[...] = o
    a_ref[...] = o[:, :wide].astype(BF)
    lse = pick_columns(top + jnp.log(total), nh, rows)
    minus = [-lse[:, h : h + 1] for h in range(nh)]
    qe_ref[...] = pieces_into(q.astype(F32), minus, wide).astype(BF)


def cross_fwd(q, e, nh, hs):
    enc = e.shape[0]
    rows = 2 * BLK
    pairs = rows * enc * nh
    return pl.pallas_call(
        functools.partial(cross_fwd_kernel, nh, hs),
        in_specs=[VM, VM],
        out_specs=[VM] * 3,
        out_shape=[f32_shape(rows, rows), bf_shape(rows, nh * hs), bf_shape(rows, rows)],
        scratch_shapes=[pltpu.VMEM((enc // CH, nh * rows, CH), F32)],
        **params(pairs * 2 * 512, 4e6, pairs),
    )(q, e)


def cross_bwd_kernel(plane, nz, nh, hs, qe_ref, de_ref, all_ref, dq_ref, dkv_ref, e_ref, acc_ref, sem):
    size = all_ref.shape[0] // (plane * nz)
    copies = []
    for k in range(plane):
        for z in range(nz):
            source = all_ref.at[pl.ds((z * plane + k) * size, size)]
            target = e_ref.at[pl.ds((k * nz + z) * size, size)]
            copies.append(pltpu.make_async_copy(source, target, sem.at[k, z]))
    for copy in copies:
        copy.start()
    for copy in copies:
        copy.wait()
    wide = nh * hs
    acc_ref[...] = jnp.zeros_like(acc_ref)

    def kept(value, h):
        lane = lane_of(value.shape)
        first = wide + 3 * h
        keep = ((lane >= h * hs) & (lane < (h + 1) * hs)) | ((lane >= first) & (lane < first + 3))
        return jnp.where(keep, value, jnp.zeros_like(value))

    qm = [kept(qe_ref[...], h) for h in range(nh)]
    dm = [kept(de_ref[...], h) for h in range(nh)]

    for ch in range(e_ref.shape[0] // CH):
        rows = slice(ch * CH, (ch + 1) * CH)
        ek = e_ref[rows, : 2 * BLK]
        ev = e_ref[rows, 2 * BLK :]
        ek_t = jnp.transpose(ek.astype(F32)).astype(BF)
        dk = jnp.zeros((CH, 2 * BLK), F32)
        dv = jnp.zeros((CH, 2 * BLK), F32)
        for h in range(nh):
            p = jnp.exp(dot_nt(ek, qm[h]))
            ds = (p * dot_nt(ev, dm[h])).astype(BF)
            dk = dk + dot(ds, qm[h])
            dv = dv + dot(p.astype(BF), dm[h])
            acc_ref[h * hs : (h + 1) * hs, :] += dot(ek_t[h * hs : (h + 1) * hs, :], ds)
        dkv_ref[rows, :] = jnp.concatenate([dk[:, :wide], dv[:, :wide]], axis=1).astype(BF)
    dq_ref[...] = jnp.transpose(acc_ref[...]).astype(BF)


def cross_bwd(qe, de, e, plane, nz, nh, hs):
    enc = e.shape[0]
    pairs = 2 * BLK * enc * nh
    return pl.pallas_call(
        functools.partial(cross_bwd_kernel, plane, nz, nh, hs),
        in_specs=[VM, VM, ANY],
        out_specs=[VM, VM],
        out_shape=[bf_shape(2 * BLK, 2 * BLK), bf_shape(enc, 2 * nh * hs)],
        scratch_shapes=[
            pltpu.VMEM((enc, 4 * BLK), BF),
            pltpu.VMEM((2 * BLK, 2 * BLK), F32),
            pltpu.SemaphoreType.DMA((plane, nz)),
        ],
        **params(pairs * 2 * 1024, 4e6, pairs),
    )(qe, de, e)


def scale_of(rows):
    return lax.rsqrt(jnp.mean(rows * rows, axis=-1, keepdims=True) + EPS)


def norm_back(rows, gain, grad):
    rr = scale_of(rows)
    scaled = gain * grad
    shared = jnp.mean(rows * scaled, axis=-1, keepdims=True)
    dv = rr * scaled - rows * (rr * rr * rr) * shared
    return dv, jnp.sum(rows * rr * grad, axis=0, keepdims=True)


def in_blocks(pair_ref):
    half = pair_ref.shape[1] // 2
    return jnp.concatenate(
        [pair_ref[m, i * half : (i + 1) * half] for i in range(2) for m in range(2)], axis=0
    )


def put(ref, value):
    cols = value.shape[1]
    ref[:, :cols] = value
    if ref.shape[1] > cols:
        ref[:, cols:] = jnp.zeros((ref.shape[0], ref.shape[1] - cols), ref.dtype)


def own_of(ref, w, half):
    return jnp.concatenate(
        [ref[pl.ds(pl.multiple_of(i * BLK + w * half, half), half), :] for i in range(2)], axis=0
    )


def project_kernel(wide, tok_ref, w_ref, gain_ref, n1_ref, q_ref, k_ref, v_ref, kv_ref):
    x = in_blocks(tok_ref).astype(F32)
    n1 = (x * scale_of(x) * gain_ref[...]).astype(BF)
    n1_ref[...] = n1
    cut = w_ref.shape[1]

    def product(first, count):
        cols = slice(first * wide, (first + count) * wide)
        return (dot(n1[:, :cut], w_ref[0, :, cols]) + dot(n1[:, cut:], w_ref[1, :, cols])).astype(BF)

    kv = product(0, 2)
    kv_ref[...] = kv
    zero = jnp.zeros((x.shape[0], 2 * BLK), BF)
    for ref, value in ((k_ref, kv[:, :wide]), (v_ref, kv[:, wide:]), (q_ref, product(4, 1))):
        ref[...] = zero
        ref[:, :wide] = value


def encode_kernel(wide, enc_ref, w_ref, out_ref):
    x = enc_ref[...]
    cut = w_ref.shape[1]
    cols = slice(2 * wide, 4 * wide)
    made = dot(x[:, :cut], w_ref[0, :, cols]) + dot(x[:, cut:], w_ref[1, :, cols])
    made = made.astype(BF)
    out_ref[...] = jnp.ones(out_ref.shape, BF)
    out_ref[:, :wide] = made[:, :wide]
    out_ref[:, 2 * BLK : 2 * BLK + wide] = made[:, wide:]


def middle_kernel(
    wide, core_ref, tok_ref, a_ref, own_ref, mate_ref, gain_ref, w_ref, h_ref, n_ref, cq_ref
):
    w = core_ref[0]
    h = in_blocks(tok_ref).astype(F32)
    h = h + (dot(a_ref[w], own_ref[...]) + dot(a_ref[1 - w], mate_ref[...]))
    h_ref[...] = h
    n = (h * scale_of(h) * gain_ref[...]).astype(BF)
    n_ref[...] = n
    cut = w_ref.shape[1]
    cols = slice(5 * wide, 6 * wide)
    made = dot(n[:, :cut], w_ref[0, :, cols]) + dot(n[:, cut:], w_ref[1, :, cols])
    cq_ref[...] = jnp.zeros(cq_ref.shape, BF)
    cq_ref[:, :wide] = made.astype(BF)


def third_kernel(half, w_ref, h1_ref, a_ref, own_ref, mate_ref, gain_ref, h_ref, n_ref):
    w = w_ref[0]
    h = own_of(h1_ref, w, half)
    for m, ref in ((w, own_ref), (1 - w, mate_ref)):
        h = h + dot(own_of(a_ref.at[m], w, half), ref[...])
    h_ref[...] = h
    put(n_ref, (h * scale_of(h) * gain_ref[...]).astype(BF))


def heads_kernel(wide, *refs):
    *weights, out_ref = refs
    last = out_ref.shape[2] - len(weights) * wide
    for m in range(out_ref.shape[0] if last else 0):
        out_ref[m, :, len(weights) * wide :] = jnp.zeros((out_ref.shape[1], last), BF)
    for i, ref in enumerate(weights):
        for m in range(out_ref.shape[0]):
            out_ref[m, :, i * wide : (i + 1) * wide] = ref[:, m * wide : (m + 1) * wide]


def units_kernel(nz, step, share, slot, spot_ref, gate_ref, up_ref, down_ref, *outs):
    def move(ref, out, first, at):
        base = pl.multiple_of(jnp.minimum(first // BLK * BLK, ref.shape[1] - 2 * BLK), BLK)
        window = ref[:, pl.ds(base, 2 * BLK)].astype(F32)
        window = pltpu.roll(window, 2 * BLK - (first - base), 1)[:, :BLK]
        window = jnp.where(lane_of(window.shape) < share, window, 0.0)
        out[:, at : at + slot] = window.astype(BF)[:, :slot]

    for m in range(2):
        ug_ref, wd_ref = outs[m], outs[2 + m]
        for z in range(nz):
            first = (z * step + spot_ref[m]) * share
            move(gate_ref, ug_ref, first, z * slot)
            move(up_ref, ug_ref, first, (nz + z) * slot)
        for z in range(wd_ref.shape[1] // slot):
            move(down_ref, wd_ref, (z * step + spot_ref[m]) * share, z * slot)


def in_order(w, own_ref, mate_ref, axis):
    own, other = own_ref[...], mate_ref[...]
    return jnp.concatenate(
        [jnp.where(w == 0, own, other), jnp.where(w == 0, other, own)], axis=axis
    )


def order_kernel(core_ref, own_ref, mate_ref, down_ref, down_mate_ref, ug_ref, wd_ref):
    ug_ref[...] = in_order(core_ref[0], own_ref, mate_ref, 0)
    wd_ref[...] = in_order(core_ref[0], down_ref, down_mate_ref, 1)


def ffn_early_kernel(g0_ref, g1_ref, wd_ref, out_ref):
    width = wd_ref.shape[0]
    rows = g0_ref.shape[0]
    for i, ref in enumerate((g0_ref, g1_ref)):
        out_ref[i * rows : (i + 1) * rows, :] = dot(ref[:, :width], wd_ref[...])


def ffn_kernel(n0_ref, n1_ref, da_ref, ug_ref, act_ref, dgu_ref, d0_ref, d1_ref):
    own = pl.program_id(0) < pl.num_programs(0) // 2
    units = act_ref.shape[1]
    width = ug_ref.shape[0]
    n = jnp.where(own, n0_ref[:, :width], n1_ref[:, :width])
    gate = dot(n, ug_ref[:, :units])
    up = dot(n, ug_ref[:, units:])
    da = da_ref[...]
    scale = 0.7978845608028654
    inner = jnp.tanh(scale * (gate + 0.044715 * gate * gate * gate))
    gelu = 0.5 * gate * (1.0 + inner)
    slope = 0.5 * (1.0 + inner) + 0.5 * gate * (1.0 - inner * inner) * scale * (
        1.0 + 3.0 * 0.044715 * gate * gate
    )
    act_ref[...] = (gelu * up).astype(BF)
    dg = (da * up * slope).astype(BF)
    du = (da * gelu).astype(BF)
    dgu_ref[:, :units] = dg
    dgu_ref[:, units:] = du
    dn = (dot_nt(dg, ug_ref[:, :units]) + dot_nt(du, ug_ref[:, units:])).astype(BF)

    @pl.when(own)
    def _():
        put(d0_ref, dn)

    @pl.when(jnp.logical_not(own))
    def _():
        put(d1_ref, dn)


def half_specs(tiles, cols):
    tile = 4 * BLK
    return [
        pl.BlockSpec((tile, cols), lambda i: (jnp.minimum(i, tiles // 2 - 1), 0)),
        pl.BlockSpec((tile, cols), lambda i: (jnp.maximum(i - tiles // 2, 0), 0)),
    ]


def ffn_both(n, da, ug):
    rows, padded = 2 * n[0].shape[0], n[0].shape[1]
    width, units = ug.shape[0], ug.shape[1] // 2
    tiles = rows // (4 * BLK)

    def row(cols):
        return pl.BlockSpec((4 * BLK, cols), lambda i: (i, 0))

    halved = half_specs(tiles, padded)
    return pl.pallas_call(
        ffn_kernel,
        grid=(tiles,),
        in_specs=halved + [row(units), pl.BlockSpec(ug.shape, lambda i: (0, 0))],
        out_specs=[row(units), row(2 * units)] + halved,
        out_shape=[bf_shape(rows, units), bf_shape(rows, 2 * units)]
        + [bf_shape(rows // 2, padded)] * 2,
        **params(10 * rows * width * units, 12e6, rows * units),
    )(*n, da, ug)


def ffn_late_kernel(nz, share, late, n0_ref, n1_ref, g0_ref, g1_ref, act_ref, dgu_ref, wd_ref, *rest):
    w_ref, o0_ref, o1_ref, acc_ref = rest[late:]
    i = pl.program_id(0)
    own = i < pl.num_programs(0) // 2
    units = act_ref.shape[1]
    @pl.when(i == 0)
    def _():
        acc_ref[...] = jnp.zeros_like(acc_ref)

    n = jnp.where(own, n0_ref[...], n1_ref[...])
    g = jnp.where(own, g0_ref[...], g1_ref[...])
    acc_ref[: 2 * units, :] += dot_tn(dgu_ref[...], n)
    acc_ref[2 * units :, :] += dot_tn(act_ref[...], g)
    made = dot_nt(act_ref[...], wd_ref[...]).astype(BF)

    @pl.when(own)
    def _():
        put(o0_ref, made)

    @pl.when(jnp.logical_not(own))
    def _():
        put(o1_ref, made)

    @pl.when(i == pl.num_programs(0) - 1)
    def _():
        for z in range(nz):
            for j in range(3):
                first = j * units + z * (units // nz)
                w_ref[z, j] = acc_ref[first : first + share, :].astype(BF)


def ffn_late(n, g, act, dgu, wd, nz, share, deps):
    rows, padded = act.shape[0], n[0].shape[1]
    width, units = wd.shape
    tiles = rows // (4 * BLK)

    def row(cols):
        return pl.BlockSpec((4 * BLK, cols), lambda i: (i, 0))

    halved = half_specs(tiles, padded)
    return pl.pallas_call(
        functools.partial(ffn_late_kernel, nz, share, len(deps)),
        grid=(tiles,),
        in_specs=halved
        + halved
        + [row(units), row(2 * units), pl.BlockSpec(wd.shape, lambda i: (0, 0))]
        + [ANY] * len(deps),
        out_specs=[pl.BlockSpec((nz, 3, share, padded), lambda i: (0, 0, 0, 0))] + halved,
        out_shape=[bf_shape(nz, 3, share, padded)] + [bf_shape(rows // 2, padded)] * 2,
        scratch_shapes=[pltpu.VMEM((3 * units, padded), F32)],
        **params(8 * rows * width * units, 20e6, 0),
    )(*n, *g, act, dgu, wd, *deps)


def add_kernel(a_ref, b_ref, *outs):
    rows = outs[0].shape[0]
    for k, out in enumerate(outs):
        at = slice(k * rows, (k + 1) * rows)
        out[...] = (a_ref[at].astype(F32) + b_ref[at].astype(F32)).astype(BF)


def output_kernel(*refs):
    *parts, out_ref = refs
    width = out_ref.shape[1]
    total = parts[0][:, :width].astype(F32)
    for part in parts[1:]:
        total = total + part[:, :width].astype(F32)
    out_ref[...] = total.astype(BF)


def join_kernel(*refs):
    *parts, out_ref = refs
    rows = parts[0].shape[0]
    for i, part in enumerate(parts):
        out_ref[i * rows : (i + 1) * rows, :] = part[...]


def spread_kernel(*refs):
    *parts, out_ref = refs
    rows = parts[0].shape[0]
    for i in range(out_ref.shape[0]):
        for j, part in enumerate(parts):
            out_ref[i, j * rows : (j + 1) * rows, :] = part[...]


def split_rows(value):
    parts = []
    for _ in range(3):
        part = value.astype(BF).astype(F32)
        value = value - part
        parts.append(part)
    return jnp.concatenate(parts, axis=0)


def owners_kernel(wide, plan, target_ref, *refs):
    sets = 1 + max(s for group in plan for s, _ in group)
    xs, ys, out_ref = refs[:sets], refs[sets : sets + len(plan)], refs[-1]
    rows = target_ref.shape[0] // out_ref.shape[0]
    extra = refs[-2] if len(refs) > sets + len(plan) + 1 else None
    for k in range(out_ref.shape[0]):
        target = target_ref[k * rows : (k + 1) * rows, :]
        total = jnp.zeros((rows, ys[0].shape[1]), F32)
        column = 0
        for group, y in zip(plan, ys):
            picked = jnp.zeros((rows, y.shape[0]), F32)
            for which, first in group:
                x = xs[which]
                lane = lane_of((rows, x.shape[2]))
                inside = (lane >= first) & (lane < first + wide)
                for m in range(2):
                    hit = inside & (lane - first + m * wide == target[:, column : column + 1])
                    picked = picked + dot_nt(hit.astype(BF), x[m])
                column += 1
            total = total + dot(picked.astype(BF), y[...])
        total = total.astype(BF)
        if extra is None:
            put(out_ref.at[k], total)
        else:
            out_ref[k] = jnp.zeros(out_ref.shape[1:], BF)
            out_ref[k, :rows, : total.shape[1]] = total
            out_ref[k, rows : rows + 3 * extra.shape[0], :] = split_rows(extra[...]).astype(BF)


def layers_kernel(nz, zed_ref, x_ref, *outs):
    total = jnp.sum(x_ref[...].astype(F32), axis=0)
    rows = total.shape[0] // nz
    for k, out in enumerate(outs):
        want = zed_ref[0] ^ k
        value = total[:rows]
        for z in range(1, nz):
            value = jnp.where(want == z, total[z * rows : (z + 1) * rows], value)
        out[...] = value.astype(BF)


def deal_last_kernel(rows, extra, x_ref, out_ref):
    total = jnp.sum(x_ref[...].astype(F32), axis=0)
    each = rows // out_ref.shape[0]
    small = total[rows : rows + extra]
    for i in range(1, 3):
        small = small + total[rows + i * extra : rows + (i + 1) * extra]
    small = split_rows(small).astype(BF)
    for i in range(out_ref.shape[0]):
        out_ref[i] = jnp.zeros(out_ref.shape[1:], BF)
        out_ref[i, :each, :] = total[i * each : (i + 1) * each].astype(BF)
        out_ref[i, each : each + 3 * extra, :] = small


def deal_kernel(*refs):
    *parts, out_ref = refs
    at = 0
    for part in parts:
        total = jnp.sum(part[...].astype(F32), axis=0)
        rows = total.shape[0] // out_ref.shape[0]
        for i in range(out_ref.shape[0]):
            out_ref[i, at : at + rows, :] = total[i * rows : (i + 1) * rows].astype(BF)
        at += rows


def dh2_kernel(*refs):
    *parts, h_ref, cot_ref, gain_ref, dh_ref, dy_ref, gain_out = refs
    width = h_ref.shape[1]
    grad = parts[0][:, :width].astype(F32)
    for part in parts[1:]:
        grad = grad + part[:, :width].astype(F32)
    dv, gain_out[...] = norm_back(h_ref[...], gain_ref[...], grad)
    dh = cot_ref[:, :width].astype(F32) + dv
    dh_ref[...] = dh
    put(dy_ref, dh.astype(BF))


def dh1_kernel(wide, half, w_ref, dq_ref, cq_ref, h1_ref, dh2_ref, gain_ref, dh_ref, dy_ref, gain_out):
    w = w_ref[0]
    dq = jnp.concatenate([own_of(dq_ref.at[m], w, half)[:, :wide] for m in range(2)], axis=1)
    grad = dot_nt(dq, cq_ref[...])
    dv, gain_out[...] = norm_back(own_of(h1_ref, w, half), gain_ref[...], grad)
    dh = dh2_ref[...] + dv
    dh_ref[...] = dh
    put(dy_ref, dh.astype(BF))


def last_kernel(wide, half, w_ref, d_ref, weight_ref, tok_ref, dh1_ref, gain_ref, out_ref, gain_out):
    w = w_ref[0]
    d = jnp.concatenate(
        [own_of(d_ref.at[m, i], w, half)[:, :wide] for i in range(3) for m in range(2)], axis=1
    )
    grad = dot_nt(d, weight_ref[...])
    dv, gain_out[...] = norm_back(tok_ref[w].astype(F32), gain_ref[...], grad)
    out_ref[...] = dh1_ref[...] + dv


def grad_prep_kernel(nh, hs, dy_ref, w_ref, o_ref, out_ref, de_ref, dh_ref, del_ref):
    wide = nh * hs
    dy = in_blocks(dy_ref)[:, : w_ref.shape[1]]
    out_ref[...] = dy
    da = dot_nt(dy, w_ref[...]).astype(BF)
    da = jnp.concatenate([da, jnp.zeros((da.shape[0], 2 * BLK - wide), BF)], axis=1)
    terms = da.astype(F32) * o_ref[...]
    delta = [jnp.sum(head_mask(terms, h, hs), axis=1, keepdims=True) for h in range(nh)]
    dh_ref[...] = pltpu.roll(da.astype(F32), hs, 1).astype(BF)
    lane = lane_of(del_ref.shape)
    cols = jnp.zeros(del_ref.shape, F32)
    for h in range(nh):
        cols = jnp.where(lane == h, delta[h], cols)
    del_ref[...] = cols
    de = pieces_into(da.astype(F32), [-t for t in delta], wide).astype(BF)
    for i in range(de_ref.shape[0]):
        de_ref[i] = de


def grad_prep(dy, weight, o, nh, hs, copies=1, deps=()):
    rows, width = o.shape[0], weight.shape[1]
    return plain(
        functools.partial(grad_prep_kernel, nh, hs),
        [],
        [dy, weight, o],
        [
            bf_shape(rows, width),
            bf_shape(copies, rows, 2 * BLK),
            bf_shape(rows, 2 * BLK),
            f32_shape(rows, BLK),
        ],
        deps=deps,
    )


def local(
    tokens,
    encoded,
    cotangent,
    assign,
    bucket_ids,
    gain_self,
    gain_cross,
    gain_ffn,
    query_weight,
    key_weight,
    value_weight,
    out_weight,
    cross_query,
    cross_key,
    cross_value,
    cross_out,
    gate_weight,
    up_weight,
    down_weight,
    bucket_table,
):
    nctx = lax.axis_size("ctx")
    nw = lax.axis_size("wsh")
    c = lax.axis_index("ctx")
    w = lax.axis_index("wsh")
    both = ("ctx", "wsh")
    rows, width = tokens.shape
    half = rows // 2
    length = rows * nw * nctx
    buckets, heads = bucket_table.shape
    inner = query_weight.shape[1]
    hs = inner // heads
    nh = heads // nw
    wide = nh * hs
    plane = 4
    nz = nctx // plane
    spot = (c % plane) * nw + w
    zed = c // plane
    hidden = gate_weight.shape[1]
    share = hidden // (nctx * nw)
    slot = -(-share // 32) * 32

    def pair(x, axis=0, tiled=True):
        return lax.all_gather(x, "wsh", axis=axis, tiled=tiled)

    def halves(parts):
        return lax.all_to_all(parts, "wsh", 0, 0, tiled=True)

    def mate(x):
        return lax.ppermute(x, "wsh", [(i, (i + 1) % nw) for i in range(nw)])

    planes = [[z * plane + i for i in range(plane)] for z in range(nz)]
    columns = [[z * plane + i for z in range(nz)] for i in range(plane)]

    def in_plane(x):
        return lax.all_to_all(x, "ctx", 0, 0, tiled=True, axis_index_groups=planes)

    def in_column(x):
        return lax.all_to_all(x, "ctx", 0, 0, tiled=True, axis_index_groups=columns)

    padded = -(-width // BLK) * BLK

    def spread(parts, count, deps=()):
        shape = bf_shape(count, len(parts) * parts[0].shape[0], parts[0].shape[1])
        return plain(spread_kernel, [], parts, [shape], (0, 1e6, 0), deps)[0]

    def add(a, b, deps=()):
        return plain(add_kernel, [], [a, b], [bf_shape(rows, padded)] * plane, (0, 1e6, 0), deps)

    def deal(parts, count, deps=()):
        shape = bf_shape(count, sum(x.shape[1] for x in parts) // count, parts[0].shape[2])
        return plain(deal_kernel, [], parts, [shape], (0, 1e6, 0), deps)[0]

    def tree(parts):
        while len(parts) > 1:
            parts = [parts[i] + parts[i + 1] for i in range(0, len(parts), 2)]
        return parts[0]

    def near(x, k):
        return lax.ppermute(x, "ctx", [(i, i ^ k) for i in range(nctx)])

    def stacked(parts, deps=()):
        shape = bf_shape(len(parts) * parts[0].shape[0], parts[0].shape[1])
        return plain(join_kernel, [], parts, [shape], (0, 1e6, 0), deps)[0]

    cut = inner // (nctx * nw)

    def targets(count):
        index = jnp.arange(plane * nz * count * cut, dtype=jnp.int32)
        to_k, to_z = index // (nz * count * cut), index // (count * cut) % nz
        to_i, to_t = index // cut % count, index % cut
        column = ((to_z * plane + to_k) * nw + w) * cut + to_t
        which = jnp.arange(count, dtype=jnp.int32)
        return jnp.where(to_i[:, None] == which[None, :], column[:, None], -1).astype(jnp.int32)

    def owner_parts(plan, xs, ys, small=None, deps=()):
        count = sum(len(group) for group in plan)
        total = nz * count * cut
        if small is not None:
            total = -(-(total + 3 * small.shape[0]) // 16) * 16
            ys = ys + [small]
        return plain(
            functools.partial(owners_kernel, wide, plan),
            [],
            [targets(count)] + xs + ys,
            [bf_shape(plane, total, padded)],
            (3e9, 6e6, 0),
            deps,
        )[0]

    def layers(x, deps=()):
        return plain(
            functools.partial(layers_kernel, nz),
            [zed.astype(jnp.int32)[None]],
            [x],
            [bf_shape(x.shape[1] // nz, x.shape[2])] * nz,
            (0, 1e6, 0),
            deps,
        )

    def owner_sums(total, count):
        return [total[i * cut : (i + 1) * cut, :width] for i in range(count)]

    lanes = jnp.arange(nctx, dtype=jnp.int32)
    owner = jnp.sum(jnp.where(assign[None, :] == lanes[:, None], lanes[None, :], 0), axis=1)
    chip_slot = owner % plane * nz + (owner // plane ^ zed)
    near_slot = (owner ^ c) % plane * nz + (owner ^ c) // plane
    meta = jnp.concatenate([owner, jnp.take(assign, c)[None], chip_slot, near_slot])
    meta = meta.astype(jnp.int32)
    core = w.astype(jnp.int32)[None]
    chip = nw * rows

    gains = pair(jnp.stack([gain_self, gain_cross, gain_ffn]), axis=1).astype(F32)
    gains = [gains[i : i + 1] for i in range(3)]
    tok = pair(tokens, tiled=False)

    def head_parts(weights, deps=()):
        count = len(weights) * wide
        shape = bf_shape(nw, weights[0].shape[0], -(-count // BLK) * BLK)
        return plain(functools.partial(heads_kernel, wide), [], weights, [shape], deps=deps)[0]

    g_own = jnp.pad(cotangent, ((0, 0), (0, padded - width)))
    g_parts = [g_own] + [near(g_own, k) for k in range(1, plane)]
    all_heads = halves(
        head_parts(
            [key_weight, value_weight, cross_key, cross_value, query_weight, cross_query]
        )
    )
    n1, q, k_own, v_own, kv_own = plain(
        functools.partial(project_kernel, wide),
        [],
        [tok, all_heads, gains[0]],
        [bf_shape(chip, width)] + [bf_shape(chip, 2 * BLK)] * 3 + [bf_shape(chip, 2 * wide)],
    )

    enc_pair = pair(encoded)
    (ekv_own,) = plain(
        functools.partial(encode_kernel, wide),
        [],
        [enc_pair, all_heads],
        [bf_shape(enc_pair.shape[0], 4 * BLK)],
        deps=(kv_own,),
    )

    hot = (bucket_ids[None, :] == jnp.arange(buckets, dtype=jnp.int32)[:, None]).astype(BF)
    values = dot_tn(lax.dynamic_slice_in_dim(bucket_table, w * nh, nh, 1), hot)
    ts, tt = bias_tiles(values, deps=(ekv_own,))

    kv = [kv_own] + [near(kv_own, plane * k) for k in range(1, nz)]
    kv = stacked(kv, deps=(ts, *g_parts[1:]))
    kv = [kv] + [near(kv, k) for k in range(1, plane)]

    ekv = lax.all_gather(ekv_own, "ctx", axis=0, tiled=True)
    spots = jnp.stack([(c % plane) * nw + i for i in (w, 1 - w)]).astype(jnp.int32)
    ug_own, ug_sent, wd_own, wd_sent = plain(
        functools.partial(units_kernel, nz, plane * nw, share, slot),
        [spots],
        [gate_weight, up_weight, down_weight.T],
        [bf_shape(gate_weight.shape[0], 2 * nz * slot)] * 2
        + [bf_shape(width, nz // nw * slot)] * 2,
        deps=(kv[0],),
    )
    g_plane = stacked(g_parts, deps=(ug_own,))
    out_mate, cross_out_mate = mate(out_weight), mate(cross_out)
    o1, a1, qe1, lse1 = self_fwd(
        meta, q, kv, ts, nh, hs, deps=(g_plane, out_mate, cross_out_mate)
    )
    a1_pair = pair(a1, tiled=False)
    h1, n2, cq = plain(
        functools.partial(middle_kernel, wide),
        [core],
        [tok, a1_pair, out_weight, out_mate, gains[1], all_heads],
        [f32_shape(chip, width), bf_shape(chip, width), bf_shape(chip, 2 * BLK)],
    )
    qg = lax.all_gather(qe1, "ctx", axis=0, tiled=True).reshape(nctx, chip, 2 * BLK)
    cq_full, ck_full, cv_full = pair(cross_query), pair(cross_key), pair(cross_value)
    qkv_full = pair(jnp.concatenate([query_weight, key_weight, value_weight], axis=1))

    o2, a2, qe2 = cross_fwd(cq, ekv, nh, hs)
    a2_pair = pair(a2, tiled=False)
    h2, n3 = plain(
        functools.partial(third_kernel, half),
        [core],
        [h1, a2_pair, cross_out, cross_out_mate, gains[2]],
        [f32_shape(rows, width), bf_shape(rows, padded)],
    )

    ug_sent, wd_sent, g_plane, _ = lax.optimization_barrier((ug_sent, wd_sent, g_plane, a2_pair))
    g_plane = g_plane, mate(g_plane)
    ug, wd = plain(
        order_kernel,
        [core],
        [ug_own, mate(ug_sent), wd_own, mate(wd_sent)],
        [bf_shape(width, 2 * nz * slot), bf_shape(width, nz * slot)],
        deps=(n3,),
    )
    (dact,) = plain(
        ffn_early_kernel, [], [*g_plane, wd], [f32_shape(nw * plane * rows, nz * slot)], deps=(n3,)
    )
    n3_plane = stacked([n3] + [near(n3, k) for k in range(1, plane)], deps=(dact,))
    n3_plane = n3_plane, mate(n3_plane)
    act, dgu, dn0, dn1 = ffn_both(n3_plane, dact, ug)
    sent = add(dn0, mate(dn1), deps=(qg,))
    got = [near(sent[k], k) for k in range(1, plane)]
    ffn, out0, out1 = ffn_late(n3_plane, g_plane, act, dgu, wd, nz, share, (sent[0],))
    dh2, dy2, gain3 = plain(
        dh2_kernel,
        [],
        [sent[0]] + got + [h2, g_own, gains[2]],
        [f32_shape(rows, width), bf_shape(rows, padded), f32_shape(1, width)],
        deps=(out0,),
    )

    dy2, de2, _, _ = grad_prep(pair(dy2, tiled=False), cross_out, o2, nh, hs)
    dcq, dekv = cross_bwd(qe2, de2[0], ekv, plane, nz, nh, hs)
    dekv = in_plane(dekv.reshape(plane, -1, 2 * wide))
    dcq_pair = pair(dcq, tiled=False)
    dh1, dy1, gain2 = plain(
        functools.partial(dh1_kernel, wide, half),
        [core],
        [dcq_pair, cq_full, h1, dh2, gains[1]],
        [f32_shape(rows, width), bf_shape(rows, padded), f32_shape(1, width)],
    )

    dy1, de1, dhi1, delta1 = grad_prep(pair(dy1, tiled=False), out_weight, o1, nh, hs)
    dg = [de1[0]] + [near(de1[0], plane * k) for k in range(1, nz)]
    dekv = layers(dekv, deps=(de1,))
    dg = spread(dg, plane, deps=(dekv[0], qg, ck_full, cv_full, qkv_full))
    spread_out = dg
    dekv = [dekv[0]] + [near(dekv[k], plane * k) for k in range(1, nz)]

    dq, rev = self_dq(meta, q, dhi1, lse1, delta1, kv, ts, nh, hs, deps=(dg,))
    dg = in_plane(dg).reshape(nctx, chip, 2 * BLK)
    (dekv,) = plain(output_kernel, [], dekv, [bf_shape(*dekv[0].shape)], deps=(dq,))
    dekv_pair = pair(dekv, tiled=False)
    made = owner_parts(
        (((0, 0),), ((1, 0),), ((2, 0),), ((3, 0), (3, wide))),
        [a1_pair, a2_pair, dcq_pair, dekv_pair],
        [dy1, dy2, n2, enc_pair],
        deps=(dq,),
    )
    ffn = lax.psum_scatter(
        tie(ffn, spread_out).reshape(nz, 3 * share, padded),
        "ctx",
        scatter_dimension=0,
        axis_index_groups=columns,
        tiled=True,
    )
    dk, dv = self_dkv(meta, k_own, v_own, qg, dg, tt, nh, hs, deps=(made, dq))
    made = in_plane(made)
    rev = tie(rev, dk)

    dqkv_pair = pair(jnp.stack([dq, dk, dv]), tiled=False).reshape(nw, 3, chip, 2 * BLK)
    dqkv = [dqkv_pair[:, i] for i in range(3)]
    tokens_grad, gain1 = plain(
        functools.partial(last_kernel, wide, half),
        [core],
        [dqkv_pair, qkv_full, tok, dh1, gains[0]],
        [f32_shape(rows, width), f32_shape(1, width)],
    )

    rev = rev.reshape(nh, 8, -1)
    by_distance = sum(rev[:, i, 1 + i : 1 + i + length] for i in range(8))
    hot_rev = (
        jnp.flip(bucket_ids)[None, :] == jnp.arange(buckets, dtype=jnp.int32)[:, None]
    ).astype(F32)
    table_own = lax.dot_general(
        hot_rev, by_distance, (((1,), (1,)), ((), ())), precision=lax.Precision.HIGHEST
    )
    table = lax.dynamic_update_slice_in_dim(
        jnp.zeros((buckets, heads), F32), table_own, w * nh, 1
    )

    small = jnp.concatenate([gain1[0], gain2[0], gain3[0], table.reshape(-1)])
    small = jnp.pad(small, (0, -small.shape[0] % padded)).reshape(-1, padded)
    extra = small.shape[0]
    second = owner_parts((((0, 0), (1, 0), (2, 0)),), dqkv, [n1], small)
    second = in_plane(tie(second, made))
    first = layers(made)
    out_sent = add(out0, mate(tie(out1, gain1)), deps=(made,))
    first = [first[0]] + [near(first[k], plane * k) for k in range(1, nz)]
    (second,) = plain(
        functools.partial(deal_last_kernel, 3 * nz * cut, extra),
        [],
        [second],
        [bf_shape(nz, -(-(3 * cut + 3 * extra) // 16) * 16, padded)],
        deps=(*first, out_sent[0]),
    )
    out_sent = [tie(m, second) for m in out_sent[1:]], out_sent[0]
    out_got = [near(m, k + 1) for k, m in enumerate(out_sent[0])]
    (output,) = plain(output_kernel, [], [h2, out_sent[1]] + out_got, [bf_shape(rows, width)])
    dekv_pair = tie(dekv_pair, second)
    second = jnp.sum(in_column(second).astype(F32), axis=0)
    small = [second[3 * cut + i * extra : 3 * cut + (i + 1) * extra] for i in range(3)]
    small = (small[0] + small[1]) + small[2]
    small = small + mate(small)
    q_t, k_t, v_t = owner_sums(second, 3)
    first = tree([m.astype(F32) for m in first])
    out_share, cross_out_share, cq_t, ck_t, cv_t = owner_sums(first, 5)
    ffn = ffn[0, :, :width].astype(F32).reshape(3, share, width)

    def joined(x):
        return jnp.swapaxes(x[:, :, :wide], 0, 1).reshape(-1, inner)

    def own_encoder(x):
        return lax.dynamic_slice_in_dim(x, w * encoded.shape[0], encoded.shape[0], 0)

    dek, dev = joined(dekv_pair), joined(dekv_pair[:, :, wide:])
    encoded_grad = dot_nt(own_encoder(dek), ck_full) + dot_nt(own_encoder(dev), cv_full)

    small = small.reshape(-1)
    table = small[3 * width : 3 * width + buckets * heads].reshape(buckets, heads)
    return (
        output,
        tokens_grad,
        encoded_grad,
        small[:width],
        small[width : 2 * width],
        small[2 * width : 3 * width],
        q_t.T,
        k_t.T,
        v_t.T,
        out_share,
        cq_t.T,
        ck_t.T,
        cv_t.T,
        cross_out_share,
        ffn[0].T,
        ffn[1].T,
        ffn[2],
        table,
    )


def solution(mesh):
    rows = P(("seq", "ctx", "wsh"), None)
    cols = P("seq", ("ctx", "wsh"))
    split = P("wsh", None)
    return jax.shard_map(
        local,
        mesh=mesh,
        in_specs=(rows, rows, rows, P(), P(), P("wsh"), P("wsh"), P("wsh"))
        + (split,) * 11
        + (P(),),
        out_specs=(
            rows,
            rows,
            rows,
            P("seq"),
            P("seq"),
            P("seq"),
            cols,
            cols,
            cols,
            rows,
            cols,
            cols,
            cols,
            rows,
            cols,
            cols,
            rows,
            P("seq", None),
        ),
        check_vma=False,
    )
```

```python
import functools

import jax
import jax.numpy as jnp
from jax import lax
from jax.experimental import pallas as pl
from jax.experimental.pallas import tpu as pltpu
from jax.sharding import PartitionSpec as P

EPS = 1e-06
NEG = -1e30
F32 = jnp.float32
BF = jnp.bfloat16
BLK = 128
GRP = 4
CH = BLK * GRP
VLIM = 60 * 1024 * 1024
SLOW = 64


def dot(a, b):
    return lax.dot_general(a, b, (((1,), (0,)), ((), ())), preferred_element_type=F32)


def dot_nt(a, b):
    return lax.dot_general(a, b, (((1,), (1,)), ((), ())), preferred_element_type=F32)


def dot_tn(a, b):
    return lax.dot_general(a, b, (((0,), (0,)), ((), ())), preferred_element_type=F32)


def lane_of(shape):
    return lax.broadcasted_iota(jnp.int32, shape, 1)


def head_mask(value, head, hs):
    lane = lane_of(value.shape)
    keep = (lane >= head * hs) & (lane < (head + 1) * hs)
    return jnp.where(keep, value, jnp.zeros_like(value))


def lane_fold(value, op):
    out = value[:, :BLK]
    for i in range(1, value.shape[1] // BLK):
        out = op(out, value[:, i * BLK : (i + 1) * BLK])
    return out


def pieces_into(base, columns, first):
    lane = lane_of(base.shape)
    out = base
    for i, column in enumerate(columns):
        rest = column
        for j in range(3):
            part = rest.astype(BF).astype(F32)
            rest = rest - part
            out = jnp.where(lane == first + 3 * i + j, part, out)
    return out


def params(flops, nbytes, trans):
    return dict(
        compiler_params=pltpu.CompilerParams(vmem_limit_bytes=VLIM),
        cost_estimate=pl.CostEstimate(
            flops=int(flops) // SLOW,
            bytes_accessed=int(nbytes) // SLOW,
            transcendentals=int(trans) // SLOW,
        ),
    )


def after(value, *deps):
    return lax.optimization_barrier((value,) + deps)[0]


def f32_shape(*dims):
    return jax.ShapeDtypeStruct(dims, F32)


def bf_shape(*dims):
    return jax.ShapeDtypeStruct(dims, BF)


def plain(kernel, scalars, inputs, outputs, cost=(1e9, 4e6, 0), deps=()):
    count, late = len(scalars) + len(inputs), len(deps)

    def body(*refs):
        kernel(*refs[:count], *refs[count + late :])

    return pl.pallas_call(
        body,
        in_specs=[SM] * len(scalars) + [VM] * len(inputs) + [ANY] * late,
        out_specs=[VM] * len(outputs),
        out_shape=list(outputs),
        **params(*cost),
    )(*scalars, *inputs, *deps)


VM = pl.BlockSpec(memory_space=pltpu.VMEM)
ANY = pl.BlockSpec(memory_space=pl.ANY)
SM = pl.BlockSpec(memory_space=pltpu.SMEM)


def tie(x, *deps):
    return pl.pallas_call(
        lambda *refs: None,
        in_specs=[ANY] * (1 + len(deps)),
        out_specs=ANY,
        out_shape=jax.ShapeDtypeStruct(x.shape, x.dtype),
        input_output_aliases={0: 0},
        **params(0, 0, 0),
    )(x, *deps)


def bias_kernel(nb, nh, nat_ref, rev_ref, ts_ref, tt_ref):
    row = lax.broadcasted_iota(jnp.int32, (BLK, BLK), 0)
    col = lax.broadcasted_iota(jnp.int32, (BLK, BLK), 1)
    upper = col >= row

    def skew(line):
        eight = pltpu.roll(jnp.broadcast_to(line, (8, BLK)), 0, 1, stride=1, stride_axis=0)
        return jnp.concatenate(
            [eight] + [pltpu.roll(eight, 8 * i, 1) for i in range(1, BLK // 8)], axis=0
        )

    def step(r, carry):
        d = nb - 1 - r
        first, second = rev_ref[nb - jnp.maximum(d, 0)], rev_ref[nb - 1 - jnp.maximum(d, 0)]
        for h in range(nh):
            tile = jnp.where(upper, skew(first[h : h + 1]), skew(second[h : h + 1]))
            ts_ref[r, h] = jnp.where(d * BLK + row - col >= 0, tile, NEG).astype(BF)
        d = r - (GRP - 1)
        first, second = nat_ref[jnp.maximum(d, 0) + 1], nat_ref[jnp.maximum(d, 0)]
        for h in range(nh):
            tile = jnp.where(upper, skew(first[h : h + 1]), skew(second[h : h + 1]))
            tt_ref[r, h] = jnp.where(d * BLK + col - row >= 0, tile, NEG).astype(BF)
        return carry

    lax.fori_loop(0, nb + GRP - 1, step, 0)


def bias_tiles(values, deps=()):
    nh, length = values.shape
    nb = length // BLK
    zero = jnp.zeros((nh, 1), F32)
    nat = jnp.concatenate([jnp.zeros((nh, BLK), F32), values], axis=1)
    rev = jnp.concatenate([zero, jnp.flip(values, 1), jnp.zeros((nh, BLK - 1), F32)], axis=1)
    nat = jnp.transpose(nat.reshape(nh, nb + 1, BLK), (1, 0, 2))
    rev = jnp.transpose(rev.reshape(nh, nb + 1, BLK), (1, 0, 2))
    shape = bf_shape(nb + GRP - 1, nh, BLK, BLK)
    return plain(
        functools.partial(bias_kernel, nb, nh), [], [nat, rev], [shape, shape], deps=deps
    )


def gather_blocks(ref, meta_ref, nctx, first, lo, hi, base=0):
    parts = []
    for i in range(GRP):
        t = first + i
        early = t < nctx
        slot = meta_ref[base + jnp.where(early, t, 2 * nctx - 1 - t)]
        at = pl.multiple_of(jnp.where(early, 0, BLK), BLK)
        parts.append(ref[slot, pl.ds(at, BLK), lo:hi])
    return jnp.concatenate(parts, axis=0)


def fetch(parts, held_ref, sem):
    rows = parts[0].shape[0]
    copies = [
        pltpu.make_async_copy(part, held_ref.at[pl.ds(k * rows, rows)], sem.at[k])
        for k, part in enumerate(parts)
    ]
    for copy in copies:
        copy.start()
    for copy in copies:
        copy.wait()


def bias_of(ref, first):
    rows = ref.shape[1] * BLK
    return jnp.concatenate(
        [ref[first + i].reshape(rows, BLK) for i in range(GRP)], axis=1
    ).astype(F32)


def stack_heads(value, hs, nh, shift=0):
    return jnp.concatenate([head_mask(value, h + shift, hs) for h in range(nh)], axis=0)


def merge_heads(stacked, hs, nh, shift=0):
    rows = stacked.shape[0] // nh
    total = jnp.zeros((rows, stacked.shape[1]), F32)
    for h in range(nh):
        total = total + head_mask(stacked[h * rows : (h + 1) * rows], h + shift, hs)
    return total


def pick_columns(columns, nh, rows):
    out = jnp.zeros((rows, BLK), F32)
    lane = lane_of(out.shape)
    for h in range(nh):
        out = jnp.where(lane == h, columns[h * rows : (h + 1) * rows], out)
    return out


def stack_columns(ref, rows, nh):
    return jnp.concatenate([ref[rows, h : h + 1] for h in range(nh)], axis=0)


def self_fwd_kernel(count, nctx, nh, hs, meta_ref, q_ref, ts_ref, *rest):
    o_ref, a_ref, qe_ref, lse_ref, s_ref, acc_ref, flat_ref, sem = rest[-8:]
    fetch(rest[:count], flat_ref, sem)
    kv_ref = flat_ref.reshape(nctx, 2 * BLK, flat_ref.shape[1])
    nb = 2 * nctx
    wide = nh * hs
    early = meta_ref[nctx]
    for half in range(2):
        blk = early if half == 0 else nb - 1 - early
        chunks = blk // GRP + 1
        rows = slice(half * BLK, (half + 1) * BLK)
        q = q_ref[rows, :]
        qm = stack_heads(q, hs, nh)

        def score(ch, top):
            keys = gather_blocks(kv_ref, meta_ref, nctx, ch * GRP, 0, 2 * BLK, 2 * nctx + 1)
            s = dot_nt(qm, keys) + bias_of(ts_ref, nb - 1 - blk + ch * GRP)
            s_ref[ch] = s
            return jnp.maximum(top, lane_fold(s, jnp.maximum))

        top = lax.fori_loop(0, chunks, score, jnp.full((nh * BLK, BLK), NEG, F32))
        top = jnp.max(top, axis=1, keepdims=True)
        acc_ref[...] = jnp.zeros_like(acc_ref)

        def weigh(ch, total):
            vals = gather_blocks(kv_ref, meta_ref, nctx, ch * GRP, BLK, 3 * BLK, 2 * nctx + 1)
            p = jnp.exp(s_ref[ch] - top)
            acc_ref[...] += dot(p.astype(BF), vals)
            return total + lane_fold(p, jnp.add)

        total = lax.fori_loop(0, chunks, weigh, jnp.zeros((nh * BLK, BLK), F32))
        total = jnp.sum(total, axis=1, keepdims=True)
        o = pltpu.roll(merge_heads(acc_ref[...] / total, hs, nh, 1), 2 * BLK - hs, 1)
        o_ref[rows, :] = o
        a_ref[rows, :] = o[:, :wide].astype(BF)
        lse = pick_columns(top + jnp.log(total), nh, BLK)
        lse_ref[rows, :] = lse
        minus = [-lse[:, h : h + 1] for h in range(nh)]
        qe_ref[rows, :] = pieces_into(q.astype(F32), minus, wide).astype(BF)


def self_fwd(meta, q, kv, ts, nh, hs, deps=()):
    nctx = len(kv) * kv[0].shape[0] // (2 * BLK)
    nb = 2 * nctx
    rows = 2 * BLK
    pairs = (nb + 1) * BLK * BLK * nh
    return pl.pallas_call(
        functools.partial(self_fwd_kernel, len(kv), nctx, nh, hs),
        in_specs=[SM, VM, VM] + [ANY] * (len(kv) + len(deps)),
        out_specs=[VM] * 4,
        out_shape=[
            f32_shape(rows, rows),
            bf_shape(rows, nh * hs),
            bf_shape(rows, rows),
            f32_shape(rows, BLK),
        ],
        scratch_shapes=[
            pltpu.VMEM((nb // GRP, nh * BLK, CH), F32),
            pltpu.VMEM((nh * BLK, 2 * BLK), F32),
            pltpu.VMEM((nb * BLK, kv[0].shape[1]), BF),
            pltpu.SemaphoreType.DMA((len(kv),)),
        ],
        **params(pairs * 2 * 512, 10e6, pairs),
    )(meta, q, ts, *kv, *deps)


def self_dq_kernel(count, nctx, nh, hs, meta_ref, q_ref, da_ref, lse_ref, del_ref, ts_ref, *rest):
    dq_ref, rev_ref, acc_ref, flat_ref, sem = rest[-5:]
    fetch(rest[:count], flat_ref, sem)
    kv_ref = flat_ref.reshape(nctx, 2 * BLK, flat_ref.shape[1])
    nb = 2 * nctx
    early = meta_ref[nctx]
    span = CH + BLK
    rev_ref[...] = jnp.zeros_like(rev_ref)
    for half in range(2):
        blk = early if half == 0 else nb - 1 - early
        chunks = blk // GRP + 1
        rows = slice(half * BLK, (half + 1) * BLK)
        qm = stack_heads(q_ref[rows, :], hs, nh)
        dm = stack_heads(da_ref[rows, :], hs, nh, 1)
        lse = stack_columns(lse_ref, rows, nh)
        delta = stack_columns(del_ref, rows, nh)
        acc_ref[...] = jnp.zeros_like(acc_ref)

        def step(ch, carry):
            held = gather_blocks(kv_ref, meta_ref, nctx, ch * GRP, 0, 3 * BLK, 2 * nctx + 1)
            keys, vals = held[:, : 2 * BLK], held[:, BLK:]
            off = pl.multiple_of((ch * GRP - blk + nb - 1) * BLK, BLK)
            s = dot_nt(qm, keys) + bias_of(ts_ref, nb - 1 - blk + ch * GRP)
            p = jnp.exp(s - lse)
            ds = (p * (dot_nt(dm, vals) - delta)).astype(BF)
            acc_ref[...] += dot(ds, keys)
            flat = jnp.concatenate([jnp.zeros((nh * BLK, BLK), F32), ds.astype(F32)], axis=1)
            for h in range(nh):
                line = flat[h * BLK : h * BLK + 8]
                for i in range(1, BLK // 8):
                    at = h * BLK + 8 * i
                    line = line + pltpu.roll(flat[at : at + 8], span - 8 * i, 1)
                rev_ref[h * 8 : (h + 1) * 8, pl.ds(off, span)] += line
            return carry

        lax.fori_loop(0, chunks, step, 0)
        dq_ref[rows, :] = merge_heads(acc_ref[...], hs, nh).astype(BF)


def self_dq(meta, q, da, lse, delta, kv, ts, nh, hs, deps=()):
    nctx = len(kv) * kv[0].shape[0] // (2 * BLK)
    nb = 2 * nctx
    pairs = (nb + 1) * BLK * BLK * nh
    return pl.pallas_call(
        functools.partial(self_dq_kernel, len(kv), nctx, nh, hs),
        in_specs=[SM] + [VM] * 5 + [ANY] * (len(kv) + len(deps)),
        out_specs=[VM, VM],
        out_shape=[
            jax.ShapeDtypeStruct((2 * BLK, 2 * BLK), BF),
            jax.ShapeDtypeStruct((8 * nh, nb * BLK + CH), F32),
        ],
        scratch_shapes=[
            pltpu.VMEM((nh * BLK, 2 * BLK), F32),
            pltpu.VMEM((nb * BLK, kv[0].shape[1]), BF),
            pltpu.SemaphoreType.DMA((len(kv),)),
        ],
        **params(pairs * 2 * 896, 10e6, pairs),
    )(meta, q, da, lse, delta, ts, *kv, *deps)


def self_dkv_kernel(nctx, nh, hs, meta_ref, k_ref, v_ref, qg_ref, dg_ref, tt_ref, *rest):
    dk_ref, dv_ref, ka_ref, va_ref = rest[-4:]
    nb = 2 * nctx
    wide = nh * hs
    early = meta_ref[nctx]

    def extended(value):
        lane = lane_of(value.shape)
        parts = []
        for h in range(nh):
            first = wide + 3 * h
            ones = (lane >= first) & (lane < first + 3)
            parts.append(jnp.where(ones, jnp.ones_like(value), head_mask(value, h, hs)))
        return jnp.concatenate(parts, axis=0)

    for half in range(2):
        blk = early if half == 0 else nb - 1 - early
        rows = slice(half * BLK, (half + 1) * BLK)
        km = extended(k_ref[rows, :])
        vm = extended(v_ref[rows, :])
        ka_ref[...] = jnp.zeros_like(ka_ref)
        va_ref[...] = jnp.zeros_like(va_ref)

        def step(ch, carry):
            qc = gather_blocks(qg_ref, meta_ref, nctx, ch * GRP, 0, 2 * BLK)
            dc = gather_blocks(dg_ref, meta_ref, nctx, ch * GRP, 0, 2 * BLK, nctx + 1)
            p = jnp.exp(dot_nt(km, qc) + bias_of(tt_ref, ch * GRP - blk + GRP - 1))
            ds = (p * dot_nt(vm, dc)).astype(BF)
            ka_ref[...] += dot(ds, qc)
            va_ref[...] += dot(p.astype(BF), dc)
            return carry

        lax.fori_loop(blk // GRP, nb // GRP, step, 0)
        dk_ref[rows, :] = merge_heads(ka_ref[...], hs, nh).astype(BF)
        dv_ref[rows, :] = merge_heads(va_ref[...], hs, nh).astype(BF)


def self_dkv(meta, k, v, qg, dg, tt, nh, hs, deps=()):
    nctx = qg.shape[0]
    nb = 2 * nctx
    pairs = (nb + 1) * BLK * BLK * nh
    shape = jax.ShapeDtypeStruct((2 * BLK, 2 * BLK), BF)
    return pl.pallas_call(
        functools.partial(self_dkv_kernel, nctx, nh, hs),
        in_specs=[SM] + [VM] * 5 + [ANY] * len(deps),
        out_specs=[VM, VM],
        out_shape=[shape, shape],
        scratch_shapes=[
            pltpu.VMEM((nh * BLK, 2 * BLK), F32),
            pltpu.VMEM((nh * BLK, 2 * BLK), F32),
        ],
        **params(pairs * 2 * 1024, 10e6, pairs),
    )(meta, k, v, qg, dg, tt, *deps)


def cross_fwd_kernel(nh, hs, q_ref, e_ref, o_ref, a_ref, qe_ref, s_ref):
    wide = nh * hs
    chunks = e_ref.shape[0] // CH
    rows = q_ref.shape[0]
    q = q_ref[...]
    qm = stack_heads(q, hs, nh)
    top = jnp.full((nh * rows, BLK), NEG, F32)
    for ch in range(chunks):
        s = dot_nt(qm, e_ref[ch * CH : (ch + 1) * CH, : 2 * BLK])
        s_ref[ch] = s
        top = jnp.maximum(top, lane_fold(s, jnp.maximum))
    top = jnp.max(top, axis=1, keepdims=True)
    total = jnp.zeros((nh * rows, BLK), F32)
    acc = jnp.zeros((nh * rows, 2 * BLK), F32)
    for ch in range(chunks):
        p = jnp.exp(s_ref[ch] - top)
        total = total + lane_fold(p, jnp.add)
        acc = acc + dot(p.astype(BF), e_ref[ch * CH : (ch + 1) * CH, 2 * BLK :])
    total = jnp.sum(total, axis=1, keepdims=True)
    o = merge_heads(acc / total, hs, nh)
    o_ref[...] = o
    a_ref[...] = o[:, :wide].astype(BF)
    lse = pick_columns(top + jnp.log(total), nh, rows)
    minus = [-lse[:, h : h + 1] for h in range(nh)]
    qe_ref[...] = pieces_into(q.astype(F32), minus, wide).astype(BF)


def cross_fwd(q, e, nh, hs):
    enc = e.shape[0]
    rows = 2 * BLK
    pairs = rows * enc * nh
    return pl.pallas_call(
        functools.partial(cross_fwd_kernel, nh, hs),
        in_specs=[VM, VM],
        out_specs=[VM] * 3,
        out_shape=[f32_shape(rows, rows), bf_shape(rows, nh * hs), bf_shape(rows, rows)],
        scratch_shapes=[pltpu.VMEM((enc // CH, nh * rows, CH), F32)],
        **params(pairs * 2 * 512, 4e6, pairs),
    )(q, e)


def cross_bwd_kernel(plane, nz, nh, hs, qe_ref, de_ref, all_ref, dq_ref, dkv_ref, e_ref, acc_ref, sem):
    size = all_ref.shape[0] // (plane * nz)
    copies = []
    for k in range(plane):
        for z in range(nz):
            source = all_ref.at[pl.ds((z * plane + k) * size, size)]
            target = e_ref.at[pl.ds((k * nz + z) * size, size)]
            copies.append(pltpu.make_async_copy(source, target, sem.at[k, z]))
    for copy in copies:
        copy.start()
    for copy in copies:
        copy.wait()
    wide = nh * hs
    acc_ref[...] = jnp.zeros_like(acc_ref)

    def kept(value, h):
        lane = lane_of(value.shape)
        first = wide + 3 * h
        keep = ((lane >= h * hs) & (lane < (h + 1) * hs)) | ((lane >= first) & (lane < first + 3))
        return jnp.where(keep, value, jnp.zeros_like(value))

    qm = [kept(qe_ref[...], h) for h in range(nh)]
    dm = [kept(de_ref[...], h) for h in range(nh)]

    for ch in range(e_ref.shape[0] // CH):
        rows = slice(ch * CH, (ch + 1) * CH)
        ek = e_ref[rows, : 2 * BLK]
        ev = e_ref[rows, 2 * BLK :]
        ek_t = jnp.transpose(ek.astype(F32)).astype(BF)
        dk = jnp.zeros((CH, 2 * BLK), F32)
        dv = jnp.zeros((CH, 2 * BLK), F32)
        for h in range(nh):
            p = jnp.exp(dot_nt(ek, qm[h]))
            ds = (p * dot_nt(ev, dm[h])).astype(BF)
            dk = dk + dot(ds, qm[h])
            dv = dv + dot(p.astype(BF), dm[h])
            acc_ref[h * hs : (h + 1) * hs, :] += dot(ek_t[h * hs : (h + 1) * hs, :], ds)
        dkv_ref[rows, :] = jnp.concatenate([dk[:, :wide], dv[:, :wide]], axis=1).astype(BF)
    dq_ref[...] = jnp.transpose(acc_ref[...]).astype(BF)


def cross_bwd(qe, de, e, plane, nz, nh, hs):
    enc = e.shape[0]
    pairs = 2 * BLK * enc * nh
    return pl.pallas_call(
        functools.partial(cross_bwd_kernel, plane, nz, nh, hs),
        in_specs=[VM, VM, ANY],
        out_specs=[VM, VM],
        out_shape=[bf_shape(2 * BLK, 2 * BLK), bf_shape(enc, 2 * nh * hs)],
        scratch_shapes=[
            pltpu.VMEM((enc, 4 * BLK), BF),
            pltpu.VMEM((2 * BLK, 2 * BLK), F32),
            pltpu.SemaphoreType.DMA((plane, nz)),
        ],
        **params(pairs * 2 * 1024, 4e6, pairs),
    )(qe, de, e)


def scale_of(rows):
    return lax.rsqrt(jnp.mean(rows * rows, axis=-1, keepdims=True) + EPS)


def norm_back(rows, gain, grad):
    rr = scale_of(rows)
    scaled = gain * grad
    shared = jnp.mean(rows * scaled, axis=-1, keepdims=True)
    dv = rr * scaled - rows * (rr * rr * rr) * shared
    return dv, jnp.sum(rows * rr * grad, axis=0, keepdims=True)


def in_blocks(pair_ref):
    half = pair_ref.shape[1] // 2
    return jnp.concatenate(
        [pair_ref[m, i * half : (i + 1) * half] for i in range(2) for m in range(2)], axis=0
    )


def put(ref, value):
    cols = value.shape[1]
    ref[:, :cols] = value
    if ref.shape[1] > cols:
        ref[:, cols:] = jnp.zeros((ref.shape[0], ref.shape[1] - cols), ref.dtype)


def own_of(ref, w, half):
    return jnp.concatenate(
        [ref[pl.ds(pl.multiple_of(i * BLK + w * half, half), half), :] for i in range(2)], axis=0
    )


def project_kernel(wide, tok_ref, w_ref, gain_ref, n1_ref, q_ref, k_ref, v_ref, kv_ref):
    x = in_blocks(tok_ref).astype(F32)
    n1 = (x * scale_of(x) * gain_ref[...]).astype(BF)
    n1_ref[...] = n1
    cut = w_ref.shape[1]

    def product(first, count):
        cols = slice(first * wide, (first + count) * wide)
        return (dot(n1[:, :cut], w_ref[0, :, cols]) + dot(n1[:, cut:], w_ref[1, :, cols])).astype(BF)

    kv = product(0, 2)
    for i in range(kv_ref.shape[0]):
        kv_ref[i] = kv
    zero = jnp.zeros((x.shape[0], 2 * BLK), BF)
    for ref, value in ((k_ref, kv[:, :wide]), (v_ref, kv[:, wide:]), (q_ref, product(4, 1))):
        ref[...] = zero
        ref[:, :wide] = value


def encode_kernel(wide, enc_ref, w_ref, out_ref):
    x = enc_ref[...]
    cut = w_ref.shape[1]
    cols = slice(2 * wide, 4 * wide)
    made = dot(x[:, :cut], w_ref[0, :, cols]) + dot(x[:, cut:], w_ref[1, :, cols])
    made = made.astype(BF)
    out_ref[...] = jnp.ones(out_ref.shape, BF)
    out_ref[:, :wide] = made[:, :wide]
    out_ref[:, 2 * BLK : 2 * BLK + wide] = made[:, wide:]


def middle_kernel(
    wide, core_ref, tok_ref, a_ref, own_ref, mate_ref, gain_ref, w_ref, h_ref, n_ref, cq_ref
):
    w = core_ref[0]
    h = in_blocks(tok_ref).astype(F32)
    h = h + (dot(a_ref[w], own_ref[...]) + dot(a_ref[1 - w], mate_ref[...]))
    h_ref[...] = h
    n = (h * scale_of(h) * gain_ref[...]).astype(BF)
    n_ref[...] = n
    cut = w_ref.shape[1]
    cols = slice(5 * wide, 6 * wide)
    made = dot(n[:, :cut], w_ref[0, :, cols]) + dot(n[:, cut:], w_ref[1, :, cols])
    cq_ref[...] = jnp.zeros(cq_ref.shape, BF)
    cq_ref[:, :wide] = made.astype(BF)


def third_kernel(half, w_ref, h1_ref, a_ref, own_ref, mate_ref, gain_ref, h_ref, n_ref):
    w = w_ref[0]
    h = own_of(h1_ref, w, half)
    for m, ref in ((w, own_ref), (1 - w, mate_ref)):
        h = h + dot(own_of(a_ref.at[m], w, half), ref[...])
    h_ref[...] = h
    put(n_ref, (h * scale_of(h) * gain_ref[...]).astype(BF))


def heads_kernel(wide, *refs):
    *weights, out_ref = refs
    last = out_ref.shape[2] - len(weights) * wide
    for m in range(out_ref.shape[0] if last else 0):
        out_ref[m, :, len(weights) * wide :] = jnp.zeros((out_ref.shape[1], last), BF)
    for i, ref in enumerate(weights):
        for m in range(out_ref.shape[0]):
            out_ref[m, :, i * wide : (i + 1) * wide] = ref[:, m * wide : (m + 1) * wide]


def units_kernel(nz, step, share, slot, spot_ref, gate_ref, up_ref, down_ref, *outs):
    def move(ref, out, first, at):
        base = pl.multiple_of(jnp.minimum(first // BLK * BLK, ref.shape[1] - 2 * BLK), BLK)
        window = ref[:, pl.ds(base, 2 * BLK)].astype(F32)
        window = pltpu.roll(window, 2 * BLK - (first - base), 1)[:, :BLK]
        window = jnp.where(lane_of(window.shape) < share, window, 0.0)
        out[:, at : at + slot] = window.astype(BF)[:, :slot]

    for m in range(2):
        ug_ref, wd_ref = outs[m], outs[2 + m]
        for z in range(nz):
            first = (z * step + spot_ref[m]) * share
            move(gate_ref, ug_ref, first, z * slot)
            move(up_ref, ug_ref, first, (nz + z) * slot)
        for z in range(wd_ref.shape[1] // slot):
            move(down_ref, wd_ref, (z * step + spot_ref[m]) * share, z * slot)


def in_order(w, own_ref, mate_ref, axis):
    own, other = own_ref[...], mate_ref[...]
    return jnp.concatenate(
        [jnp.where(w == 0, own, other), jnp.where(w == 0, other, own)], axis=axis
    )


def order_kernel(core_ref, own_ref, mate_ref, down_ref, down_mate_ref, ug_ref, wd_ref):
    ug_ref[...] = in_order(core_ref[0], own_ref, mate_ref, 0)
    wd_ref[...] = in_order(core_ref[0], down_ref, down_mate_ref, 1)


def ffn_early_kernel(g0_ref, g1_ref, wd_ref, out_ref):
    width = wd_ref.shape[0]
    rows = g0_ref.shape[0]
    for i, ref in enumerate((g0_ref, g1_ref)):
        out_ref[i * rows : (i + 1) * rows, :] = dot(ref[:, :width], wd_ref[...])


def ffn_kernel(n0_ref, n1_ref, da_ref, ug_ref, act_ref, dgu_ref, d0_ref, d1_ref):
    own = pl.program_id(0) < pl.num_programs(0) // 2
    units = act_ref.shape[1]
    width = ug_ref.shape[0]
    n = jnp.where(own, n0_ref[:, :width], n1_ref[:, :width])
    gate = dot(n, ug_ref[:, :units])
    up = dot(n, ug_ref[:, units:])
    da = da_ref[...]
    scale = 0.7978845608028654
    inner = jnp.tanh(scale * (gate + 0.044715 * gate * gate * gate))
    gelu = 0.5 * gate * (1.0 + inner)
    slope = 0.5 * (1.0 + inner) + 0.5 * gate * (1.0 - inner * inner) * scale * (
        1.0 + 3.0 * 0.044715 * gate * gate
    )
    act_ref[...] = (gelu * up).astype(BF)
    dg = (da * up * slope).astype(BF)
    du = (da * gelu).astype(BF)
    dgu_ref[:, :units] = dg
    dgu_ref[:, units:] = du
    dn = (dot_nt(dg, ug_ref[:, :units]) + dot_nt(du, ug_ref[:, units:])).astype(BF)

    @pl.when(own)
    def _():
        put(d0_ref, dn)

    @pl.when(jnp.logical_not(own))
    def _():
        put(d1_ref, dn)


def half_specs(tiles, cols):
    tile = 4 * BLK
    return [
        pl.BlockSpec((tile, cols), lambda i: (jnp.minimum(i, tiles // 2 - 1), 0)),
        pl.BlockSpec((tile, cols), lambda i: (jnp.maximum(i - tiles // 2, 0), 0)),
    ]


def ffn_both(n, da, ug):
    rows, padded = 2 * n[0].shape[0], n[0].shape[1]
    width, units = ug.shape[0], ug.shape[1] // 2
    tiles = rows // (4 * BLK)

    def row(cols):
        return pl.BlockSpec((4 * BLK, cols), lambda i: (i, 0))

    halved = half_specs(tiles, padded)
    return pl.pallas_call(
        ffn_kernel,
        grid=(tiles,),
        in_specs=halved + [row(units), pl.BlockSpec(ug.shape, lambda i: (0, 0))],
        out_specs=[row(units), row(2 * units)] + halved,
        out_shape=[bf_shape(rows, units), bf_shape(rows, 2 * units)]
        + [bf_shape(rows // 2, padded)] * 2,
        **params(10 * rows * width * units, 12e6, rows * units),
    )(*n, da, ug)


def ffn_late_kernel(nz, share, late, n0_ref, n1_ref, g0_ref, g1_ref, act_ref, dgu_ref, wd_ref, *rest):
    w_ref, o0_ref, o1_ref, acc_ref = rest[late:]
    i = pl.program_id(0)
    own = i < pl.num_programs(0) // 2
    units = act_ref.shape[1]
    @pl.when(i == 0)
    def _():
        acc_ref[...] = jnp.zeros_like(acc_ref)

    n = jnp.where(own, n0_ref[...], n1_ref[...])
    g = jnp.where(own, g0_ref[...], g1_ref[...])
    acc_ref[: 2 * units, :] += dot_tn(dgu_ref[...], n)
    acc_ref[2 * units :, :] += dot_tn(act_ref[...], g)
    made = dot_nt(act_ref[...], wd_ref[...]).astype(BF)

    @pl.when(own)
    def _():
        put(o0_ref, made)

    @pl.when(jnp.logical_not(own))
    def _():
        put(o1_ref, made)

    @pl.when(i == pl.num_programs(0) - 1)
    def _():
        for z in range(nz):
            for j in range(3):
                first = j * units + z * (units // nz)
                w_ref[z, j] = acc_ref[first : first + share, :].astype(BF)


def ffn_late(n, g, act, dgu, wd, nz, share, deps):
    rows, padded = act.shape[0], n[0].shape[1]
    width, units = wd.shape
    tiles = rows // (4 * BLK)

    def row(cols):
        return pl.BlockSpec((4 * BLK, cols), lambda i: (i, 0))

    halved = half_specs(tiles, padded)
    return pl.pallas_call(
        functools.partial(ffn_late_kernel, nz, share, len(deps)),
        grid=(tiles,),
        in_specs=halved
        + halved
        + [row(units), row(2 * units), pl.BlockSpec(wd.shape, lambda i: (0, 0))]
        + [ANY] * len(deps),
        out_specs=[pl.BlockSpec((nz, 3, share, padded), lambda i: (0, 0, 0, 0))] + halved,
        out_shape=[bf_shape(nz, 3, share, padded)] + [bf_shape(rows // 2, padded)] * 2,
        scratch_shapes=[pltpu.VMEM((3 * units, padded), F32)],
        **params(8 * rows * width * units, 20e6, 0),
    )(*n, *g, act, dgu, wd, *deps)


def add_kernel(a_ref, b_ref, *outs):
    rows = outs[0].shape[0]
    for k, out in enumerate(outs):
        at = slice(k * rows, (k + 1) * rows)
        out[...] = (a_ref[at].astype(F32) + b_ref[at].astype(F32)).astype(BF)


def output_kernel(*refs):
    *parts, out_ref = refs
    width = out_ref.shape[1]
    total = parts[0][:, :width].astype(F32)
    for part in parts[1:]:
        total = total + part[:, :width].astype(F32)
    out_ref[...] = total.astype(BF)


def join_kernel(*refs):
    *parts, out_ref = refs
    rows = parts[0].shape[0]
    for i, part in enumerate(parts):
        out_ref[i * rows : (i + 1) * rows, :] = part[...]


def spread_kernel(*refs):
    *parts, out_ref = refs
    rows = parts[0].shape[0]
    for i in range(out_ref.shape[0]):
        for j, part in enumerate(parts):
            out_ref[i, j * rows : (j + 1) * rows, :] = part[...]


def split_rows(value):
    parts = []
    for _ in range(3):
        part = value.astype(BF).astype(F32)
        value = value - part
        parts.append(part)
    return jnp.concatenate(parts, axis=0)


def owners_kernel(wide, plan, target_ref, *refs):
    sets = 1 + max(s for group in plan for s, _ in group)
    xs, ys, out_ref = refs[:sets], refs[sets : sets + len(plan)], refs[-1]
    rows = target_ref.shape[0] // out_ref.shape[0]
    extra = refs[-2] if len(refs) > sets + len(plan) + 1 else None
    count = target_ref.shape[0]
    total = jnp.zeros((count, ys[0].shape[1]), F32)
    column = 0
    for group, y in zip(plan, ys):
        picked = jnp.zeros((count, y.shape[0]), F32)
        for which, first in group:
            x = xs[which]
            lane = lane_of((count, x.shape[2]))
            inside = (lane >= first) & (lane < first + wide)
            for m in range(2):
                hit = inside & (lane - first + m * wide == target_ref[:, column : column + 1])
                picked = picked + dot_nt(hit.astype(BF), x[m])
            column += 1
        total = total + dot(picked.astype(BF), y[...])
    for k in range(out_ref.shape[0]):
        part = total[k * rows : (k + 1) * rows].astype(BF)
        if extra is None:
            put(out_ref.at[k], part)
        else:
            out_ref[k] = jnp.zeros(out_ref.shape[1:], BF)
            out_ref[k, :rows, : part.shape[1]] = part
            out_ref[k, rows : rows + 3 * extra.shape[0], :] = split_rows(extra[...]).astype(BF)


def layers_kernel(nz, zed_ref, x_ref, *outs):
    total = jnp.sum(x_ref[...].astype(F32), axis=0)
    rows = total.shape[0] // nz
    for k, out in enumerate(outs):
        want = zed_ref[0] ^ k
        value = total[:rows]
        for z in range(1, nz):
            value = jnp.where(want == z, total[z * rows : (z + 1) * rows], value)
        out[...] = value.astype(BF)


def deal_last_kernel(rows, extra, x_ref, out_ref):
    total = jnp.sum(x_ref[...].astype(F32), axis=0)
    each = rows // out_ref.shape[0]
    small = total[rows : rows + extra]
    for i in range(1, 3):
        small = small + total[rows + i * extra : rows + (i + 1) * extra]
    small = split_rows(small).astype(BF)
    for i in range(out_ref.shape[0]):
        out_ref[i] = jnp.zeros(out_ref.shape[1:], BF)
        out_ref[i, :each, :] = total[i * each : (i + 1) * each].astype(BF)
        out_ref[i, each : each + 3 * extra, :] = small


def deal_kernel(*refs):
    *parts, out_ref = refs
    at = 0
    for part in parts:
        total = jnp.sum(part[...].astype(F32), axis=0)
        rows = total.shape[0] // out_ref.shape[0]
        for i in range(out_ref.shape[0]):
            out_ref[i, at : at + rows, :] = total[i * rows : (i + 1) * rows].astype(BF)
        at += rows


def dh2_kernel(*refs):
    *parts, h_ref, cot_ref, gain_ref, dh_ref, dy_ref, gain_out = refs
    width = h_ref.shape[1]
    grad = parts[0][:, :width].astype(F32)
    for part in parts[1:]:
        grad = grad + part[:, :width].astype(F32)
    dv, gain_out[...] = norm_back(h_ref[...], gain_ref[...], grad)
    dh = cot_ref[:, :width].astype(F32) + dv
    dh_ref[...] = dh
    put(dy_ref, dh.astype(BF))


def dh1_kernel(wide, half, w_ref, dq_ref, cq_ref, h1_ref, dh2_ref, gain_ref, dh_ref, dy_ref, gain_out):
    w = w_ref[0]
    dq = jnp.concatenate([own_of(dq_ref.at[m], w, half)[:, :wide] for m in range(2)], axis=1)
    grad = dot_nt(dq, cq_ref[...])
    dv, gain_out[...] = norm_back(own_of(h1_ref, w, half), gain_ref[...], grad)
    dh = dh2_ref[...] + dv
    dh_ref[...] = dh
    put(dy_ref, dh.astype(BF))


def last_kernel(wide, half, w_ref, d_ref, weight_ref, tok_ref, dh1_ref, gain_ref, out_ref, gain_out):
    w = w_ref[0]
    d = jnp.concatenate(
        [own_of(d_ref.at[m, i], w, half)[:, :wide] for i in range(3) for m in range(2)], axis=1
    )
    grad = dot_nt(d, weight_ref[...])
    dv, gain_out[...] = norm_back(tok_ref[w].astype(F32), gain_ref[...], grad)
    out_ref[...] = dh1_ref[...] + dv


def grad_prep_kernel(nh, hs, dy_ref, w_ref, o_ref, out_ref, de_ref, dh_ref, del_ref):
    wide = nh * hs
    dy = in_blocks(dy_ref)[:, : w_ref.shape[1]]
    out_ref[...] = dy
    da = dot_nt(dy, w_ref[...]).astype(BF)
    da = jnp.concatenate([da, jnp.zeros((da.shape[0], 2 * BLK - wide), BF)], axis=1)
    terms = da.astype(F32) * o_ref[...]
    delta = [jnp.sum(head_mask(terms, h, hs), axis=1, keepdims=True) for h in range(nh)]
    dh_ref[...] = pltpu.roll(da.astype(F32), hs, 1).astype(BF)
    lane = lane_of(del_ref.shape)
    cols = jnp.zeros(del_ref.shape, F32)
    for h in range(nh):
        cols = jnp.where(lane == h, delta[h], cols)
    del_ref[...] = cols
    de = pieces_into(da.astype(F32), [-t for t in delta], wide).astype(BF)
    for i in range(de_ref.shape[0]):
        de_ref[i] = de


def grad_prep(dy, weight, o, nh, hs, copies=1, deps=()):
    rows, width = o.shape[0], weight.shape[1]
    return plain(
        functools.partial(grad_prep_kernel, nh, hs),
        [],
        [dy, weight, o],
        [
            bf_shape(rows, width),
            bf_shape(copies, rows, 2 * BLK),
            bf_shape(rows, 2 * BLK),
            f32_shape(rows, BLK),
        ],
        deps=deps,
    )


def local(
    tokens,
    encoded,
    cotangent,
    assign,
    bucket_ids,
    gain_self,
    gain_cross,
    gain_ffn,
    query_weight,
    key_weight,
    value_weight,
    out_weight,
    cross_query,
    cross_key,
    cross_value,
    cross_out,
    gate_weight,
    up_weight,
    down_weight,
    bucket_table,
):
    nctx = lax.axis_size("ctx")
    nw = lax.axis_size("wsh")
    c = lax.axis_index("ctx")
    w = lax.axis_index("wsh")
    both = ("ctx", "wsh")
    rows, width = tokens.shape
    half = rows // 2
    length = rows * nw * nctx
    buckets, heads = bucket_table.shape
    inner = query_weight.shape[1]
    hs = inner // heads
    nh = heads // nw
    wide = nh * hs
    plane = 4
    nz = nctx // plane
    spot = (c % plane) * nw + w
    zed = c // plane
    hidden = gate_weight.shape[1]
    share = hidden // (nctx * nw)
    slot = -(-share // 32) * 32

    def pair(x, axis=0, tiled=True):
        return lax.all_gather(x, "wsh", axis=axis, tiled=tiled)

    def halves(parts):
        return lax.all_to_all(parts, "wsh", 0, 0, tiled=True)

    def mate(x):
        return lax.ppermute(x, "wsh", [(i, (i + 1) % nw) for i in range(nw)])

    planes = [[z * plane + i for i in range(plane)] for z in range(nz)]
    columns = [[z * plane + i for z in range(nz)] for i in range(plane)]

    def in_plane(x):
        return lax.all_to_all(x, "ctx", 0, 0, tiled=True, axis_index_groups=planes)

    def in_column(x):
        return lax.all_to_all(x, "ctx", 0, 0, tiled=True, axis_index_groups=columns)

    padded = -(-width // BLK) * BLK

    def spread(parts, count, deps=()):
        shape = bf_shape(count, len(parts) * parts[0].shape[0], parts[0].shape[1])
        return plain(spread_kernel, [], parts, [shape], (0, 1e6, 0), deps)[0]

    def add(a, b, deps=()):
        return plain(add_kernel, [], [a, b], [bf_shape(rows, padded)] * plane, (0, 1e6, 0), deps)

    def deal(parts, count, deps=()):
        shape = bf_shape(count, sum(x.shape[1] for x in parts) // count, parts[0].shape[2])
        return plain(deal_kernel, [], parts, [shape], (0, 1e6, 0), deps)[0]

    def tree(parts):
        while len(parts) > 1:
            parts = [parts[i] + parts[i + 1] for i in range(0, len(parts), 2)]
        return parts[0]

    def near(x, k):
        return lax.ppermute(x, "ctx", [(i, i ^ k) for i in range(nctx)])

    def stacked(parts, deps=()):
        shape = bf_shape(len(parts) * parts[0].shape[0], parts[0].shape[1])
        return plain(join_kernel, [], parts, [shape], (0, 1e6, 0), deps)[0]

    cut = inner // (nctx * nw)

    def targets(count):
        index = jnp.arange(plane * nz * count * cut, dtype=jnp.int32)
        to_k, to_z = index // (nz * count * cut), index // (count * cut) % nz
        to_i, to_t = index // cut % count, index % cut
        column = ((to_z * plane + to_k) * nw + w) * cut + to_t
        which = jnp.arange(count, dtype=jnp.int32)
        return jnp.where(to_i[:, None] == which[None, :], column[:, None], -1).astype(jnp.int32)

    def owner_parts(plan, xs, ys, small=None, deps=()):
        count = sum(len(group) for group in plan)
        total = nz * count * cut
        if small is not None:
            total = -(-(total + 3 * small.shape[0]) // 16) * 16
            ys = ys + [small]
        return plain(
            functools.partial(owners_kernel, wide, plan),
            [],
            [targets(count)] + xs + ys,
            [bf_shape(plane, total, padded)],
            (3e9, 6e6, 0),
            deps,
        )[0]

    def layers(x, deps=()):
        return plain(
            functools.partial(layers_kernel, nz),
            [zed.astype(jnp.int32)[None]],
            [x],
            [bf_shape(x.shape[1] // nz, x.shape[2])] * nz,
            (0, 1e6, 0),
            deps,
        )

    def owner_sums(total, count):
        return [total[i * cut : (i + 1) * cut, :width] for i in range(count)]

    lanes = jnp.arange(nctx, dtype=jnp.int32)
    owner = jnp.sum(jnp.where(assign[None, :] == lanes[:, None], lanes[None, :], 0), axis=1)
    chip_slot = owner % plane * nz + (owner // plane ^ zed)
    near_slot = (owner ^ c) % plane * nz + owner // plane
    meta = jnp.concatenate([owner, jnp.take(assign, c)[None], chip_slot, near_slot])
    meta = meta.astype(jnp.int32)
    core = w.astype(jnp.int32)[None]
    chip = nw * rows

    gains = pair(jnp.stack([gain_self, gain_cross, gain_ffn]), axis=1).astype(F32)
    gains = [gains[i : i + 1] for i in range(3)]
    tok = pair(tokens, tiled=False)

    def head_parts(weights, deps=()):
        count = len(weights) * wide
        shape = bf_shape(nw, weights[0].shape[0], -(-count // BLK) * BLK)
        return plain(functools.partial(heads_kernel, wide), [], weights, [shape], deps=deps)[0]

    g_own = jnp.pad(cotangent, ((0, 0), (0, padded - width)))
    g_parts = [g_own] + [near(g_own, k) for k in range(1, plane)]
    all_heads = halves(
        head_parts(
            [key_weight, value_weight, cross_key, cross_value, query_weight, cross_query]
        )
    )
    n1, q, k_own, v_own, kv_own = plain(
        functools.partial(project_kernel, wide),
        [],
        [tok, all_heads, gains[0]],
        [bf_shape(chip, width)] + [bf_shape(chip, 2 * BLK)] * 3 + [bf_shape(nz, chip, 2 * wide)],
    )

    enc_pair = pair(encoded)
    (ekv_own,) = plain(
        functools.partial(encode_kernel, wide),
        [],
        [enc_pair, all_heads],
        [bf_shape(enc_pair.shape[0], 4 * BLK)],
        deps=(kv_own,),
    )

    kv = in_column(kv_own).reshape(-1, 2 * wide)
    kv = [kv] + [near(kv, k) for k in range(1, plane)]

    hot = (bucket_ids[None, :] == jnp.arange(buckets, dtype=jnp.int32)[:, None]).astype(BF)
    values = dot_tn(lax.dynamic_slice_in_dim(bucket_table, w * nh, nh, 1), hot)
    ts, tt = bias_tiles(values, deps=(kv[0], ekv_own, *g_parts[1:]))

    ekv = lax.all_gather(ekv_own, "ctx", axis=0, tiled=True)
    spots = jnp.stack([(c % plane) * nw + i for i in (w, 1 - w)]).astype(jnp.int32)
    ug_own, ug_sent, wd_own, wd_sent = plain(
        functools.partial(units_kernel, nz, plane * nw, share, slot),
        [spots],
        [gate_weight, up_weight, down_weight.T],
        [bf_shape(gate_weight.shape[0], 2 * nz * slot)] * 2
        + [bf_shape(width, nz // nw * slot)] * 2,
        deps=(ts,),
    )
    g_plane = stacked(g_parts, deps=(ug_own,))
    out_mate, cross_out_mate = mate(out_weight), mate(cross_out)
    o1, a1, qe1, lse1 = self_fwd(
        meta, q, kv, ts, nh, hs, deps=(g_plane, out_mate, cross_out_mate)
    )
    a1_pair = pair(a1, tiled=False)
    h1, n2, cq = plain(
        functools.partial(middle_kernel, wide),
        [core],
        [tok, a1_pair, out_weight, out_mate, gains[1], all_heads],
        [f32_shape(chip, width), bf_shape(chip, width), bf_shape(chip, 2 * BLK)],
    )
    qg = lax.all_gather(qe1, "ctx", axis=0, tiled=True).reshape(nctx, chip, 2 * BLK)
    cq_full, ck_full, cv_full = pair(cross_query), pair(cross_key), pair(cross_value)
    qkv_full = pair(jnp.concatenate([query_weight, key_weight, value_weight], axis=1))

    o2, a2, qe2 = cross_fwd(cq, ekv, nh, hs)
    a2_pair = pair(a2, tiled=False)
    h2, n3 = plain(
        functools.partial(third_kernel, half),
        [core],
        [h1, a2_pair, cross_out, cross_out_mate, gains[2]],
        [f32_shape(rows, width), bf_shape(rows, padded)],
    )

    ug_sent, wd_sent, g_plane, _ = lax.optimization_barrier((ug_sent, wd_sent, g_plane, a2_pair))
    g_plane = g_plane, mate(g_plane)
    ug, wd = plain(
        order_kernel,
        [core],
        [ug_own, mate(ug_sent), wd_own, mate(wd_sent)],
        [bf_shape(width, 2 * nz * slot), bf_shape(width, nz * slot)],
        deps=(n3,),
    )
    (dact,) = plain(
        ffn_early_kernel, [], [*g_plane, wd], [f32_shape(nw * plane * rows, nz * slot)], deps=(n3,)
    )
    n3_plane = stacked([n3] + [near(n3, k) for k in range(1, plane)], deps=(dact,))
    n3_plane = n3_plane, mate(n3_plane)
    act, dgu, dn0, dn1 = ffn_both(n3_plane, dact, ug)
    sent = add(dn0, mate(dn1), deps=(qg,))
    got = [near(sent[k], k) for k in range(1, plane)]
    ffn, out0, out1 = ffn_late(n3_plane, g_plane, act, dgu, wd, nz, share, (sent[0],))
    dh2, dy2, gain3 = plain(
        dh2_kernel,
        [],
        [sent[0]] + got + [h2, g_own, gains[2]],
        [f32_shape(rows, width), bf_shape(rows, padded), f32_shape(1, width)],
        deps=(out0,),
    )

    dy2, de2, _, _ = grad_prep(pair(dy2, tiled=False), cross_out, o2, nh, hs)
    dcq, dekv = cross_bwd(qe2, de2[0], ekv, plane, nz, nh, hs)
    dekv = in_plane(dekv.reshape(plane, -1, 2 * wide))
    dcq_pair = pair(dcq, tiled=False)
    dh1, dy1, gain2 = plain(
        functools.partial(dh1_kernel, wide, half),
        [core],
        [dcq_pair, cq_full, h1, dh2, gains[1]],
        [f32_shape(rows, width), bf_shape(rows, padded), f32_shape(1, width)],
    )

    dy1, de1, dhi1, delta1 = grad_prep(pair(dy1, tiled=False), out_weight, o1, nh, hs)
    dg = [de1[0]] + [near(de1[0], plane * k) for k in range(1, nz)]
    dekv = layers(dekv, deps=(de1,))
    dg = spread(dg, plane, deps=(dekv[0], qg, ck_full, cv_full, qkv_full))
    spread_out = dg
    dekv = [dekv[0]] + [near(dekv[k], plane * k) for k in range(1, nz)]

    dq, rev = self_dq(meta, q, dhi1, lse1, delta1, kv, ts, nh, hs, deps=(dg,))
    dg = in_plane(dg).reshape(nctx, chip, 2 * BLK)
    (dekv,) = plain(output_kernel, [], dekv, [bf_shape(*dekv[0].shape)], deps=(dq,))
    dekv_pair = pair(dekv, tiled=False)
    made = owner_parts(
        (((0, 0),), ((1, 0),), ((2, 0),), ((3, 0), (3, wide))),
        [a1_pair, a2_pair, dcq_pair, dekv_pair],
        [dy1, dy2, n2, enc_pair],
        deps=(dq,),
    )
    ffn = lax.psum_scatter(
        tie(ffn, spread_out).reshape(nz, 3 * share, padded),
        "ctx",
        scatter_dimension=0,
        axis_index_groups=columns,
        tiled=True,
    )
    dk, dv = self_dkv(meta, k_own, v_own, qg, dg, tt, nh, hs, deps=(made, dq))
    made = in_plane(made)
    rev = tie(rev, dk)

    dqkv_pair = pair(jnp.stack([dq, dk, dv]), tiled=False).reshape(nw, 3, chip, 2 * BLK)
    dqkv = [dqkv_pair[:, i] for i in range(3)]
    tokens_grad, gain1 = plain(
        functools.partial(last_kernel, wide, half),
        [core],
        [dqkv_pair, qkv_full, tok, dh1, gains[0]],
        [f32_shape(rows, width), f32_shape(1, width)],
    )

    rev = rev.reshape(nh, 8, -1)
    by_distance = sum(rev[:, i, 1 + i : 1 + i + length] for i in range(8))
    hot_rev = (
        jnp.flip(bucket_ids)[None, :] == jnp.arange(buckets, dtype=jnp.int32)[:, None]
    ).astype(F32)
    table_own = lax.dot_general(
        hot_rev, by_distance, (((1,), (1,)), ((), ())), precision=lax.Precision.HIGHEST
    )
    table = lax.dynamic_update_slice_in_dim(
        jnp.zeros((buckets, heads), F32), table_own, w * nh, 1
    )

    small = jnp.concatenate([gain1[0], gain2[0], gain3[0], table.reshape(-1)])
    small = jnp.pad(small, (0, -small.shape[0] % padded)).reshape(-1, padded)
    extra = small.shape[0]
    second = owner_parts((((0, 0), (1, 0), (2, 0)),), dqkv, [n1], small)
    second = in_plane(tie(second, made))
    first = layers(made)
    out_sent = add(out0, mate(tie(out1, gain1)), deps=(made,))
    first = [first[0]] + [near(first[k], plane * k) for k in range(1, nz)]
    (second,) = plain(
        functools.partial(deal_last_kernel, 3 * nz * cut, extra),
        [],
        [second],
        [bf_shape(nz, -(-(3 * cut + 3 * extra) // 16) * 16, padded)],
        deps=(*first, out_sent[0]),
    )
    out_sent = [tie(m, second) for m in out_sent[1:]], out_sent[0]
    out_got = [near(m, k + 1) for k, m in enumerate(out_sent[0])]
    (output,) = plain(output_kernel, [], [h2, out_sent[1]] + out_got, [bf_shape(rows, width)])
    dekv_pair = tie(dekv_pair, second)
    second = jnp.sum(in_column(second).astype(F32), axis=0)
    small = [second[3 * cut + i * extra : 3 * cut + (i + 1) * extra] for i in range(3)]
    small = (small[0] + small[1]) + small[2]
    small = small + mate(small)
    q_t, k_t, v_t = owner_sums(second, 3)
    first = tree([m.astype(F32) for m in first])
    out_share, cross_out_share, cq_t, ck_t, cv_t = owner_sums(first, 5)
    ffn = ffn[0, :, :width].astype(F32).reshape(3, share, width)

    def joined(x):
        return jnp.swapaxes(x[:, :, :wide], 0, 1).reshape(-1, inner)

    def own_encoder(x):
        return lax.dynamic_slice_in_dim(x, w * encoded.shape[0], encoded.shape[0], 0)

    dek, dev = joined(dekv_pair), joined(dekv_pair[:, :, wide:])
    encoded_grad = dot_nt(own_encoder(dek), ck_full) + dot_nt(own_encoder(dev), cv_full)

    small = small.reshape(-1)
    table = small[3 * width : 3 * width + buckets * heads].reshape(buckets, heads)
    return (
        output,
        tokens_grad,
        encoded_grad,
        small[:width],
        small[width : 2 * width],
        small[2 * width : 3 * width],
        q_t.T,
        k_t.T,
        v_t.T,
        out_share,
        cq_t.T,
        ck_t.T,
        cv_t.T,
        cross_out_share,
        ffn[0].T,
        ffn[1].T,
        ffn[2],
        table,
    )


def solution(mesh):
    rows = P(("seq", "ctx", "wsh"), None)
    cols = P("seq", ("ctx", "wsh"))
    split = P("wsh", None)
    return jax.shard_map(
        local,
        mesh=mesh,
        in_specs=(rows, rows, rows, P(), P(), P("wsh"), P("wsh"), P("wsh"))
        + (split,) * 11
        + (P(),),
        out_specs=(
            rows,
            rows,
            rows,
            P("seq"),
            P("seq"),
            P("seq"),
            cols,
            cols,
            cols,
            rows,
            cols,
            cols,
            cols,
            rows,
            cols,
            cols,
            rows,
            P("seq", None),
        ),
        check_vma=False,
    )
```

```python
import functools

import jax
import jax.numpy as jnp
from jax import lax
from jax.experimental import pallas as pl
from jax.experimental.pallas import tpu as pltpu
from jax.sharding import PartitionSpec as P

EPS = 1e-06
NEG = -1e30
F32 = jnp.float32
BF = jnp.bfloat16
BLK = 128
GRP = 4
CH = BLK * GRP
VLIM = 60 * 1024 * 1024
SLOW = 64


def dot(a, b):
    return lax.dot_general(a, b, (((1,), (0,)), ((), ())), preferred_element_type=F32)


def dot_nt(a, b):
    return lax.dot_general(a, b, (((1,), (1,)), ((), ())), preferred_element_type=F32)


def dot_tn(a, b):
    return lax.dot_general(a, b, (((0,), (0,)), ((), ())), preferred_element_type=F32)


def lane_of(shape):
    return lax.broadcasted_iota(jnp.int32, shape, 1)


def head_mask(value, head, hs):
    lane = lane_of(value.shape)
    keep = (lane >= head * hs) & (lane < (head + 1) * hs)
    return jnp.where(keep, value, jnp.zeros_like(value))


def lane_fold(value, op):
    out = value[:, :BLK]
    for i in range(1, value.shape[1] // BLK):
        out = op(out, value[:, i * BLK : (i + 1) * BLK])
    return out


def pieces_into(base, columns, first):
    lane = lane_of(base.shape)
    out = base
    for i, column in enumerate(columns):
        rest = column
        for j in range(3):
            part = rest.astype(BF).astype(F32)
            rest = rest - part
            out = jnp.where(lane == first + 3 * i + j, part, out)
    return out


def params(flops, nbytes, trans):
    return dict(
        compiler_params=pltpu.CompilerParams(vmem_limit_bytes=VLIM),
        cost_estimate=pl.CostEstimate(
            flops=int(flops) // SLOW,
            bytes_accessed=int(nbytes) // SLOW,
            transcendentals=int(trans) // SLOW,
        ),
    )


def after(value, *deps):
    return lax.optimization_barrier((value,) + deps)[0]


def f32_shape(*dims):
    return jax.ShapeDtypeStruct(dims, F32)


def bf_shape(*dims):
    return jax.ShapeDtypeStruct(dims, BF)


def plain(kernel, scalars, inputs, outputs, cost=(1e9, 4e6, 0), deps=()):
    count, late = len(scalars) + len(inputs), len(deps)

    def body(*refs):
        kernel(*refs[:count], *refs[count + late :])

    return pl.pallas_call(
        body,
        in_specs=[SM] * len(scalars) + [VM] * len(inputs) + [ANY] * late,
        out_specs=[VM] * len(outputs),
        out_shape=list(outputs),
        **params(*cost),
    )(*scalars, *inputs, *deps)


VM = pl.BlockSpec(memory_space=pltpu.VMEM)
ANY = pl.BlockSpec(memory_space=pl.ANY)
SM = pl.BlockSpec(memory_space=pltpu.SMEM)


def tie(x, *deps):
    return pl.pallas_call(
        lambda *refs: None,
        in_specs=[ANY] * (1 + len(deps)),
        out_specs=ANY,
        out_shape=jax.ShapeDtypeStruct(x.shape, x.dtype),
        input_output_aliases={0: 0},
        **params(0, 0, 0),
    )(x, *deps)


def bias_kernel(nb, nh, nat_ref, rev_ref, ts_ref, tt_ref):
    row = lax.broadcasted_iota(jnp.int32, (BLK, BLK), 0)
    col = lax.broadcasted_iota(jnp.int32, (BLK, BLK), 1)
    upper = col >= row

    def skew(line):
        eight = pltpu.roll(jnp.broadcast_to(line, (8, BLK)), 0, 1, stride=1, stride_axis=0)
        return jnp.concatenate(
            [eight] + [pltpu.roll(eight, 8 * i, 1) for i in range(1, BLK // 8)], axis=0
        )

    def step(r, carry):
        d = nb - 1 - r
        first, second = rev_ref[nb - jnp.maximum(d, 0)], rev_ref[nb - 1 - jnp.maximum(d, 0)]
        for h in range(nh):
            tile = jnp.where(upper, skew(first[h : h + 1]), skew(second[h : h + 1]))
            ts_ref[r, h] = jnp.where(d * BLK + row - col >= 0, tile, NEG).astype(BF)
        d = r - (GRP - 1)
        first, second = nat_ref[jnp.maximum(d, 0) + 1], nat_ref[jnp.maximum(d, 0)]
        for h in range(nh):
            tile = jnp.where(upper, skew(first[h : h + 1]), skew(second[h : h + 1]))
            tt_ref[r, h] = jnp.where(d * BLK + col - row >= 0, tile, NEG).astype(BF)
        return carry

    lax.fori_loop(0, nb + GRP - 1, step, 0)


def bias_rows(values):
    nh, length = values.shape
    nb = length // BLK
    zero = jnp.zeros((nh, 1), F32)
    nat = jnp.concatenate([jnp.zeros((nh, BLK), F32), values], axis=1)
    rev = jnp.concatenate([zero, jnp.flip(values, 1), jnp.zeros((nh, BLK - 1), F32)], axis=1)
    nat = jnp.transpose(nat.reshape(nh, nb + 1, BLK), (1, 0, 2))
    rev = jnp.transpose(rev.reshape(nh, nb + 1, BLK), (1, 0, 2))
    return nat, rev


def bias_tiles(nat, rev, deps=()):
    nb, nh = nat.shape[0] - 1, nat.shape[1]
    shape = bf_shape(nb + GRP - 1, nh, BLK, BLK)
    return plain(
        functools.partial(bias_kernel, nb, nh), [], [nat, rev], [shape, shape], deps=deps
    )


def gather_blocks(ref, meta_ref, nctx, first, lo, hi, base=0):
    parts = []
    for i in range(GRP):
        t = first + i
        early = t < nctx
        slot = meta_ref[base + jnp.where(early, t, 2 * nctx - 1 - t)]
        at = pl.multiple_of(jnp.where(early, 0, BLK), BLK)
        parts.append(ref[slot, pl.ds(at, BLK), lo:hi])
    return jnp.concatenate(parts, axis=0)


def fetch(parts, held_ref, sem):
    rows = parts[0].shape[0]
    copies = [
        pltpu.make_async_copy(part, held_ref.at[pl.ds(k * rows, rows)], sem.at[k])
        for k, part in enumerate(parts)
    ]
    for copy in copies:
        copy.start()
    for copy in copies:
        copy.wait()


def bias_of(ref, first):
    rows = ref.shape[1] * BLK
    return jnp.concatenate(
        [ref[first + i].reshape(rows, BLK) for i in range(GRP)], axis=1
    ).astype(F32)


def stack_heads(value, hs, nh, shift=0):
    return jnp.concatenate([head_mask(value, h + shift, hs) for h in range(nh)], axis=0)


def merge_heads(stacked, hs, nh, shift=0):
    rows = stacked.shape[0] // nh
    total = jnp.zeros((rows, stacked.shape[1]), F32)
    for h in range(nh):
        total = total + head_mask(stacked[h * rows : (h + 1) * rows], h + shift, hs)
    return total


def pick_columns(columns, nh, rows):
    out = jnp.zeros((rows, BLK), F32)
    lane = lane_of(out.shape)
    for h in range(nh):
        out = jnp.where(lane == h, columns[h * rows : (h + 1) * rows], out)
    return out


def stack_columns(ref, rows, nh):
    return jnp.concatenate([ref[rows, h : h + 1] for h in range(nh)], axis=0)


def self_fwd_kernel(count, nctx, nh, hs, meta_ref, q_ref, ts_ref, *rest):
    o_ref, a_ref, qe_ref, lse_ref, s_ref, acc_ref, flat_ref, sem = rest[-8:]
    fetch(rest[:count], flat_ref, sem)
    kv_ref = flat_ref.reshape(nctx, 2 * BLK, flat_ref.shape[1])
    nb = 2 * nctx
    wide = nh * hs
    early = meta_ref[nctx]
    for half in range(2):
        blk = early if half == 0 else nb - 1 - early
        chunks = blk // GRP + 1
        rows = slice(half * BLK, (half + 1) * BLK)
        q = q_ref[rows, :]
        qm = stack_heads(q, hs, nh)

        def score(ch, top):
            keys = gather_blocks(kv_ref, meta_ref, nctx, ch * GRP, 0, 2 * BLK, 2 * nctx + 1)
            s = dot_nt(qm, keys) + bias_of(ts_ref, nb - 1 - blk + ch * GRP)
            s_ref[ch] = s
            return jnp.maximum(top, lane_fold(s, jnp.maximum))

        top = lax.fori_loop(0, chunks, score, jnp.full((nh * BLK, BLK), NEG, F32))
        top = jnp.max(top, axis=1, keepdims=True)
        acc_ref[...] = jnp.zeros_like(acc_ref)

        def weigh(ch, total):
            vals = gather_blocks(kv_ref, meta_ref, nctx, ch * GRP, BLK, 3 * BLK, 2 * nctx + 1)
            p = jnp.exp(s_ref[ch] - top)
            acc_ref[...] += dot(p.astype(BF), vals)
            return total + lane_fold(p, jnp.add)

        total = lax.fori_loop(0, chunks, weigh, jnp.zeros((nh * BLK, BLK), F32))
        total = jnp.sum(total, axis=1, keepdims=True)
        o = pltpu.roll(merge_heads(acc_ref[...] / total, hs, nh, 1), 2 * BLK - hs, 1)
        o_ref[rows, :] = o
        a_ref[rows, :] = o[:, :wide].astype(BF)
        lse = pick_columns(top + jnp.log(total), nh, BLK)
        lse_ref[rows, :] = lse
        minus = [-lse[:, h : h + 1] for h in range(nh)]
        qe_ref[rows, :] = pieces_into(q.astype(F32), minus, wide).astype(BF)


def self_fwd(meta, q, kv, ts, nh, hs, deps=()):
    nctx = len(kv) * kv[0].shape[0] // (2 * BLK)
    nb = 2 * nctx
    rows = 2 * BLK
    pairs = (nb + 1) * BLK * BLK * nh
    return pl.pallas_call(
        functools.partial(self_fwd_kernel, len(kv), nctx, nh, hs),
        in_specs=[SM, VM, VM] + [ANY] * (len(kv) + len(deps)),
        out_specs=[VM] * 4,
        out_shape=[
            f32_shape(rows, rows),
            bf_shape(rows, nh * hs),
            bf_shape(rows, rows),
            f32_shape(rows, BLK),
        ],
        scratch_shapes=[
            pltpu.VMEM((nb // GRP, nh * BLK, CH), F32),
            pltpu.VMEM((nh * BLK, 2 * BLK), F32),
            pltpu.VMEM((nb * BLK, kv[0].shape[1]), BF),
            pltpu.SemaphoreType.DMA((len(kv),)),
        ],
        **params(pairs * 2 * 512, 10e6, pairs),
    )(meta, q, ts, *kv, *deps)


def self_dq_kernel(count, nctx, nh, hs, meta_ref, q_ref, da_ref, lse_ref, del_ref, ts_ref, *rest):
    dq_ref, rev_ref, acc_ref, flat_ref, sem = rest[-5:]
    fetch(rest[:count], flat_ref, sem)
    kv_ref = flat_ref.reshape(nctx, 2 * BLK, flat_ref.shape[1])
    nb = 2 * nctx
    early = meta_ref[nctx]
    span = CH + BLK
    rev_ref[...] = jnp.zeros_like(rev_ref)
    for half in range(2):
        blk = early if half == 0 else nb - 1 - early
        chunks = blk // GRP + 1
        rows = slice(half * BLK, (half + 1) * BLK)
        qm = stack_heads(q_ref[rows, :], hs, nh)
        dm = stack_heads(da_ref[rows, :], hs, nh, 1)
        lse = stack_columns(lse_ref, rows, nh)
        delta = stack_columns(del_ref, rows, nh)
        acc_ref[...] = jnp.zeros_like(acc_ref)

        def step(ch, carry):
            held = gather_blocks(kv_ref, meta_ref, nctx, ch * GRP, 0, 3 * BLK, 2 * nctx + 1)
            keys, vals = held[:, : 2 * BLK], held[:, BLK:]
            off = pl.multiple_of((ch * GRP - blk + nb - 1) * BLK, BLK)
            s = dot_nt(qm, keys) + bias_of(ts_ref, nb - 1 - blk + ch * GRP)
            p = jnp.exp(s - lse)
            ds = (p * (dot_nt(dm, vals) - delta)).astype(BF)
            acc_ref[...] += dot(ds, keys)
            flat = jnp.concatenate([jnp.zeros((nh * BLK, BLK), F32), ds.astype(F32)], axis=1)
            for h in range(nh):
                line = flat[h * BLK : h * BLK + 8]
                for i in range(1, BLK // 8):
                    at = h * BLK + 8 * i
                    line = line + pltpu.roll(flat[at : at + 8], span - 8 * i, 1)
                rev_ref[h * 8 : (h + 1) * 8, pl.ds(off, span)] += line
            return carry

        lax.fori_loop(0, chunks, step, 0)
        dq_ref[rows, :] = merge_heads(acc_ref[...], hs, nh).astype(BF)


def self_dq(meta, q, da, lse, delta, kv, ts, nh, hs, deps=()):
    nctx = len(kv) * kv[0].shape[0] // (2 * BLK)
    nb = 2 * nctx
    pairs = (nb + 1) * BLK * BLK * nh
    return pl.pallas_call(
        functools.partial(self_dq_kernel, len(kv), nctx, nh, hs),
        in_specs=[SM] + [VM] * 5 + [ANY] * (len(kv) + len(deps)),
        out_specs=[VM, VM],
        out_shape=[
            jax.ShapeDtypeStruct((2 * BLK, 2 * BLK), BF),
            jax.ShapeDtypeStruct((8 * nh, nb * BLK + CH), F32),
        ],
        scratch_shapes=[
            pltpu.VMEM((nh * BLK, 2 * BLK), F32),
            pltpu.VMEM((nb * BLK, kv[0].shape[1]), BF),
            pltpu.SemaphoreType.DMA((len(kv),)),
        ],
        **params(pairs * 2 * 896, 10e6, pairs),
    )(meta, q, da, lse, delta, ts, *kv, *deps)


def self_dkv_kernel(nctx, nh, hs, meta_ref, k_ref, v_ref, qg_ref, dg_ref, tt_ref, *rest):
    dk_ref, dv_ref, ka_ref, va_ref = rest[-4:]
    nb = 2 * nctx
    wide = nh * hs
    early = meta_ref[nctx]

    def extended(value):
        lane = lane_of(value.shape)
        parts = []
        for h in range(nh):
            first = wide + 3 * h
            ones = (lane >= first) & (lane < first + 3)
            parts.append(jnp.where(ones, jnp.ones_like(value), head_mask(value, h, hs)))
        return jnp.concatenate(parts, axis=0)

    for half in range(2):
        blk = early if half == 0 else nb - 1 - early
        rows = slice(half * BLK, (half + 1) * BLK)
        km = extended(k_ref[rows, :])
        vm = extended(v_ref[rows, :])
        ka_ref[...] = jnp.zeros_like(ka_ref)
        va_ref[...] = jnp.zeros_like(va_ref)

        def step(ch, carry):
            qc = gather_blocks(qg_ref, meta_ref, nctx, ch * GRP, 0, 2 * BLK)
            dc = gather_blocks(dg_ref, meta_ref, nctx, ch * GRP, 0, 2 * BLK, nctx + 1)
            p = jnp.exp(dot_nt(km, qc) + bias_of(tt_ref, ch * GRP - blk + GRP - 1))
            ds = (p * dot_nt(vm, dc)).astype(BF)
            ka_ref[...] += dot(ds, qc)
            va_ref[...] += dot(p.astype(BF), dc)
            return carry

        lax.fori_loop(blk // GRP, nb // GRP, step, 0)
        dk_ref[rows, :] = merge_heads(ka_ref[...], hs, nh).astype(BF)
        dv_ref[rows, :] = merge_heads(va_ref[...], hs, nh).astype(BF)


def self_dkv(meta, k, v, qg, dg, tt, nh, hs, deps=()):
    nctx = qg.shape[0]
    nb = 2 * nctx
    pairs = (nb + 1) * BLK * BLK * nh
    shape = jax.ShapeDtypeStruct((2 * BLK, 2 * BLK), BF)
    return pl.pallas_call(
        functools.partial(self_dkv_kernel, nctx, nh, hs),
        in_specs=[SM] + [VM] * 5 + [ANY] * len(deps),
        out_specs=[VM, VM],
        out_shape=[shape, shape],
        scratch_shapes=[
            pltpu.VMEM((nh * BLK, 2 * BLK), F32),
            pltpu.VMEM((nh * BLK, 2 * BLK), F32),
        ],
        **params(pairs * 2 * 1024, 10e6, pairs),
    )(meta, k, v, qg, dg, tt, *deps)


def cross_fwd_kernel(nh, hs, q_ref, e_ref, o_ref, a_ref, qe_ref, s_ref):
    wide = nh * hs
    chunks = e_ref.shape[0] // CH
    rows = q_ref.shape[0]
    q = q_ref[...]
    qm = stack_heads(q, hs, nh)
    top = jnp.full((nh * rows, BLK), NEG, F32)
    for ch in range(chunks):
        s = dot_nt(qm, e_ref[ch * CH : (ch + 1) * CH, : 2 * BLK])
        s_ref[ch] = s
        top = jnp.maximum(top, lane_fold(s, jnp.maximum))
    top = jnp.max(top, axis=1, keepdims=True)
    total = jnp.zeros((nh * rows, BLK), F32)
    acc = jnp.zeros((nh * rows, 2 * BLK), F32)
    for ch in range(chunks):
        p = jnp.exp(s_ref[ch] - top)
        total = total + lane_fold(p, jnp.add)
        acc = acc + dot(p.astype(BF), e_ref[ch * CH : (ch + 1) * CH, 2 * BLK :])
    total = jnp.sum(total, axis=1, keepdims=True)
    o = merge_heads(acc / total, hs, nh)
    o_ref[...] = o
    a_ref[...] = o[:, :wide].astype(BF)
    lse = pick_columns(top + jnp.log(total), nh, rows)
    minus = [-lse[:, h : h + 1] for h in range(nh)]
    qe_ref[...] = pieces_into(q.astype(F32), minus, wide).astype(BF)


def cross_fwd(q, e, nh, hs):
    enc = e.shape[0]
    rows = 2 * BLK
    pairs = rows * enc * nh
    return pl.pallas_call(
        functools.partial(cross_fwd_kernel, nh, hs),
        in_specs=[VM, VM],
        out_specs=[VM] * 3,
        out_shape=[f32_shape(rows, rows), bf_shape(rows, nh * hs), bf_shape(rows, rows)],
        scratch_shapes=[pltpu.VMEM((enc // CH, nh * rows, CH), F32)],
        **params(pairs * 2 * 512, 4e6, pairs),
    )(q, e)


def cross_bwd_kernel(plane, nz, nh, hs, qe_ref, de_ref, all_ref, dq_ref, dkv_ref, e_ref, acc_ref, sem):
    size = all_ref.shape[0] // (plane * nz)
    copies = []
    for k in range(plane):
        for z in range(nz):
            source = all_ref.at[pl.ds((z * plane + k) * size, size)]
            target = e_ref.at[pl.ds((k * nz + z) * size, size)]
            copies.append(pltpu.make_async_copy(source, target, sem.at[k, z]))
    for copy in copies:
        copy.start()
    for copy in copies:
        copy.wait()
    wide = nh * hs
    acc_ref[...] = jnp.zeros_like(acc_ref)

    def kept(value, h):
        lane = lane_of(value.shape)
        first = wide + 3 * h
        keep = ((lane >= h * hs) & (lane < (h + 1) * hs)) | ((lane >= first) & (lane < first + 3))
        return jnp.where(keep, value, jnp.zeros_like(value))

    qm = [kept(qe_ref[...], h) for h in range(nh)]
    dm = [kept(de_ref[...], h) for h in range(nh)]

    for ch in range(e_ref.shape[0] // CH):
        rows = slice(ch * CH, (ch + 1) * CH)
        ek = e_ref[rows, : 2 * BLK]
        ev = e_ref[rows, 2 * BLK :]
        ek_t = jnp.transpose(ek.astype(F32)).astype(BF)
        dk = jnp.zeros((CH, 2 * BLK), F32)
        dv = jnp.zeros((CH, 2 * BLK), F32)
        for h in range(nh):
            p = jnp.exp(dot_nt(ek, qm[h]))
            ds = (p * dot_nt(ev, dm[h])).astype(BF)
            dk = dk + dot(ds, qm[h])
            dv = dv + dot(p.astype(BF), dm[h])
            acc_ref[h * hs : (h + 1) * hs, :] += dot(ek_t[h * hs : (h + 1) * hs, :], ds)
        dkv_ref[rows, :] = jnp.concatenate([dk[:, :wide], dv[:, :wide]], axis=1).astype(BF)
    dq_ref[...] = jnp.transpose(acc_ref[...]).astype(BF)


def cross_bwd(qe, de, e, plane, nz, nh, hs):
    enc = e.shape[0]
    pairs = 2 * BLK * enc * nh
    return pl.pallas_call(
        functools.partial(cross_bwd_kernel, plane, nz, nh, hs),
        in_specs=[VM, VM, ANY],
        out_specs=[VM, VM],
        out_shape=[bf_shape(2 * BLK, 2 * BLK), bf_shape(enc, 2 * nh * hs)],
        scratch_shapes=[
            pltpu.VMEM((enc, 4 * BLK), BF),
            pltpu.VMEM((2 * BLK, 2 * BLK), F32),
            pltpu.SemaphoreType.DMA((plane, nz)),
        ],
        **params(pairs * 2 * 1024, 4e6, pairs),
    )(qe, de, e)


def scale_of(rows):
    return lax.rsqrt(jnp.mean(rows * rows, axis=-1, keepdims=True) + EPS)


def norm_back(rows, gain, grad):
    rr = scale_of(rows)
    scaled = gain * grad
    shared = jnp.mean(rows * scaled, axis=-1, keepdims=True)
    dv = rr * scaled - rows * (rr * rr * rr) * shared
    return dv, jnp.sum(rows * rr * grad, axis=0, keepdims=True)


def in_blocks(pair_ref):
    half = pair_ref.shape[1] // 2
    return jnp.concatenate(
        [pair_ref[m, i * half : (i + 1) * half] for i in range(2) for m in range(2)], axis=0
    )


def put(ref, value):
    cols = value.shape[1]
    ref[:, :cols] = value
    if ref.shape[1] > cols:
        ref[:, cols:] = jnp.zeros((ref.shape[0], ref.shape[1] - cols), ref.dtype)


def own_of(ref, w, half):
    return jnp.concatenate(
        [ref[pl.ds(pl.multiple_of(i * BLK + w * half, half), half), :] for i in range(2)], axis=0
    )


def project_kernel(wide, tok_ref, w_ref, gain_ref, n1_ref, q_ref, k_ref, v_ref, kv_ref):
    x = in_blocks(tok_ref).astype(F32)
    n1 = (x * scale_of(x) * gain_ref[...]).astype(BF)
    n1_ref[...] = n1
    cut = w_ref.shape[1]

    def product(first, count):
        cols = slice(first * wide, (first + count) * wide)
        return (dot(n1[:, :cut], w_ref[0, :, cols]) + dot(n1[:, cut:], w_ref[1, :, cols])).astype(BF)

    kv = product(0, 2)
    for i in range(kv_ref.shape[0]):
        kv_ref[i] = kv
    zero = jnp.zeros((x.shape[0], 2 * BLK), BF)
    for ref, value in ((k_ref, kv[:, :wide]), (v_ref, kv[:, wide:]), (q_ref, product(4, 1))):
        ref[...] = zero
        ref[:, :wide] = value


def encode_kernel(wide, enc_ref, w_ref, out_ref):
    x = enc_ref[...]
    cut = w_ref.shape[1]
    cols = slice(2 * wide, 4 * wide)
    made = dot(x[:, :cut], w_ref[0, :, cols]) + dot(x[:, cut:], w_ref[1, :, cols])
    made = made.astype(BF)
    out_ref[...] = jnp.ones(out_ref.shape, BF)
    out_ref[:, :wide] = made[:, :wide]
    out_ref[:, 2 * BLK : 2 * BLK + wide] = made[:, wide:]


def middle_kernel(
    wide, core_ref, tok_ref, a_ref, own_ref, mate_ref, gain_ref, w_ref, h_ref, n_ref, cq_ref
):
    w = core_ref[0]
    h = in_blocks(tok_ref).astype(F32)
    h = h + (dot(a_ref[w], own_ref[...]) + dot(a_ref[1 - w], mate_ref[...]))
    h_ref[...] = h
    n = (h * scale_of(h) * gain_ref[...]).astype(BF)
    n_ref[...] = n
    cut = w_ref.shape[1]
    cols = slice(5 * wide, 6 * wide)
    made = dot(n[:, :cut], w_ref[0, :, cols]) + dot(n[:, cut:], w_ref[1, :, cols])
    cq_ref[...] = jnp.zeros(cq_ref.shape, BF)
    cq_ref[:, :wide] = made.astype(BF)


def third_kernel(half, w_ref, h1_ref, a_ref, own_ref, mate_ref, gain_ref, h_ref, n_ref):
    w = w_ref[0]
    h = own_of(h1_ref, w, half)
    for m, ref in ((w, own_ref), (1 - w, mate_ref)):
        h = h + dot(own_of(a_ref.at[m], w, half), ref[...])
    h_ref[...] = h
    put(n_ref, (h * scale_of(h) * gain_ref[...]).astype(BF))


def heads_kernel(wide, *refs):
    *weights, out_ref = refs
    last = out_ref.shape[2] - len(weights) * wide
    for m in range(out_ref.shape[0] if last else 0):
        out_ref[m, :, len(weights) * wide :] = jnp.zeros((out_ref.shape[1], last), BF)
    for i, ref in enumerate(weights):
        for m in range(out_ref.shape[0]):
            out_ref[m, :, i * wide : (i + 1) * wide] = ref[:, m * wide : (m + 1) * wide]


def units_kernel(nz, step, share, slot, spot_ref, gate_ref, up_ref, down_ref, *outs):
    def move(ref, out, first, at):
        base = pl.multiple_of(jnp.minimum(first // BLK * BLK, ref.shape[1] - 2 * BLK), BLK)
        window = ref[:, pl.ds(base, 2 * BLK)].astype(F32)
        window = pltpu.roll(window, 2 * BLK - (first - base), 1)[:, :BLK]
        window = jnp.where(lane_of(window.shape) < share, window, 0.0)
        out[:, at : at + slot] = window.astype(BF)[:, :slot]

    for m in range(2):
        ug_ref, wd_ref = outs[m], outs[2 + m]
        for z in range(nz):
            first = (z * step + spot_ref[m]) * share
            move(gate_ref, ug_ref, first, z * slot)
            move(up_ref, ug_ref, first, (nz + z) * slot)
        for z in range(wd_ref.shape[1] // slot):
            move(down_ref, wd_ref, (z * step + spot_ref[m]) * share, z * slot)


def in_order(w, own_ref, mate_ref, axis):
    own, other = own_ref[...], mate_ref[...]
    return jnp.concatenate(
        [jnp.where(w == 0, own, other), jnp.where(w == 0, other, own)], axis=axis
    )


def order_kernel(core_ref, own_ref, mate_ref, down_ref, down_mate_ref, ug_ref, wd_ref):
    ug_ref[...] = in_order(core_ref[0], own_ref, mate_ref, 0)
    wd_ref[...] = in_order(core_ref[0], down_ref, down_mate_ref, 1)


def ffn_early_kernel(g0_ref, g1_ref, wd_ref, out_ref):
    width = wd_ref.shape[0]
    rows = g0_ref.shape[0]
    for i, ref in enumerate((g0_ref, g1_ref)):
        out_ref[i * rows : (i + 1) * rows, :] = dot(ref[:, :width], wd_ref[...])


def ffn_kernel(n0_ref, n1_ref, da_ref, ug_ref, act_ref, dgu_ref, d0_ref, d1_ref):
    own = pl.program_id(0) < pl.num_programs(0) // 2
    units = act_ref.shape[1]
    width = ug_ref.shape[0]
    n = jnp.where(own, n0_ref[:, :width], n1_ref[:, :width])
    gate = dot(n, ug_ref[:, :units])
    up = dot(n, ug_ref[:, units:])
    da = da_ref[...]
    scale = 0.7978845608028654
    inner = jnp.tanh(scale * (gate + 0.044715 * gate * gate * gate))
    gelu = 0.5 * gate * (1.0 + inner)
    slope = 0.5 * (1.0 + inner) + 0.5 * gate * (1.0 - inner * inner) * scale * (
        1.0 + 3.0 * 0.044715 * gate * gate
    )
    act_ref[...] = (gelu * up).astype(BF)
    dg = (da * up * slope).astype(BF)
    du = (da * gelu).astype(BF)
    dgu_ref[:, :units] = dg
    dgu_ref[:, units:] = du
    dn = (dot_nt(dg, ug_ref[:, :units]) + dot_nt(du, ug_ref[:, units:])).astype(BF)

    @pl.when(own)
    def _():
        put(d0_ref, dn)

    @pl.when(jnp.logical_not(own))
    def _():
        put(d1_ref, dn)


def half_specs(tiles, cols):
    tile = 4 * BLK
    return [
        pl.BlockSpec((tile, cols), lambda i: (jnp.minimum(i, tiles // 2 - 1), 0)),
        pl.BlockSpec((tile, cols), lambda i: (jnp.maximum(i - tiles // 2, 0), 0)),
    ]


def ffn_both(n, da, ug):
    rows, padded = 2 * n[0].shape[0], n[0].shape[1]
    width, units = ug.shape[0], ug.shape[1] // 2
    tiles = rows // (4 * BLK)

    def row(cols):
        return pl.BlockSpec((4 * BLK, cols), lambda i: (i, 0))

    halved = half_specs(tiles, padded)
    return pl.pallas_call(
        ffn_kernel,
        grid=(tiles,),
        in_specs=halved + [row(units), pl.BlockSpec(ug.shape, lambda i: (0, 0))],
        out_specs=[row(units), row(2 * units)] + halved,
        out_shape=[bf_shape(rows, units), bf_shape(rows, 2 * units)]
        + [bf_shape(rows // 2, padded)] * 2,
        **params(10 * rows * width * units, 12e6, rows * units),
    )(*n, da, ug)


def ffn_late_kernel(nz, share, late, n0_ref, n1_ref, g0_ref, g1_ref, act_ref, dgu_ref, wd_ref, *rest):
    w_ref, o0_ref, o1_ref, acc_ref = rest[late:]
    i = pl.program_id(0)
    own = i < pl.num_programs(0) // 2
    units = act_ref.shape[1]
    @pl.when(i == 0)
    def _():
        acc_ref[...] = jnp.zeros_like(acc_ref)

    n = jnp.where(own, n0_ref[...], n1_ref[...])
    g = jnp.where(own, g0_ref[...], g1_ref[...])
    acc_ref[: 2 * units, :] += dot_tn(dgu_ref[...], n)
    acc_ref[2 * units :, :] += dot_tn(act_ref[...], g)
    made = dot_nt(act_ref[...], wd_ref[...]).astype(BF)

    @pl.when(own)
    def _():
        put(o0_ref, made)

    @pl.when(jnp.logical_not(own))
    def _():
        put(o1_ref, made)

    @pl.when(i == pl.num_programs(0) - 1)
    def _():
        for z in range(nz):
            for j in range(3):
                first = j * units + z * (units // nz)
                w_ref[z, j] = acc_ref[first : first + share, :].astype(BF)


def ffn_late(n, g, act, dgu, wd, nz, share, deps):
    rows, padded = act.shape[0], n[0].shape[1]
    width, units = wd.shape
    tiles = rows // (4 * BLK)

    def row(cols):
        return pl.BlockSpec((4 * BLK, cols), lambda i: (i, 0))

    halved = half_specs(tiles, padded)
    return pl.pallas_call(
        functools.partial(ffn_late_kernel, nz, share, len(deps)),
        grid=(tiles,),
        in_specs=halved
        + halved
        + [row(units), row(2 * units), pl.BlockSpec(wd.shape, lambda i: (0, 0))]
        + [ANY] * len(deps),
        out_specs=[pl.BlockSpec((nz, 3, share, padded), lambda i: (0, 0, 0, 0))] + halved,
        out_shape=[bf_shape(nz, 3, share, padded)] + [bf_shape(rows // 2, padded)] * 2,
        scratch_shapes=[pltpu.VMEM((3 * units, padded), F32)],
        **params(8 * rows * width * units, 20e6, 0),
    )(*n, *g, act, dgu, wd, *deps)


def add_kernel(a_ref, b_ref, *outs):
    rows = outs[0].shape[0]
    for k, out in enumerate(outs):
        at = slice(k * rows, (k + 1) * rows)
        out[...] = (a_ref[at].astype(F32) + b_ref[at].astype(F32)).astype(BF)


def output_kernel(*refs):
    *parts, out_ref = refs
    width = out_ref.shape[1]
    total = parts[0][:, :width].astype(F32)
    for part in parts[1:]:
        total = total + part[:, :width].astype(F32)
    out_ref[...] = total.astype(out_ref.dtype)


def join_kernel(*refs):
    *parts, out_ref = refs
    rows = parts[0].shape[0]
    for i, part in enumerate(parts):
        out_ref[i * rows : (i + 1) * rows, :] = part[...]


def spread_kernel(*refs):
    *parts, out_ref = refs
    rows = parts[0].shape[0]
    for i in range(out_ref.shape[0]):
        for j, part in enumerate(parts):
            out_ref[i, j * rows : (j + 1) * rows, :] = part[...]


def split_rows(value):
    parts = []
    for _ in range(3):
        part = value.astype(BF).astype(F32)
        value = value - part
        parts.append(part)
    return jnp.concatenate(parts, axis=0)


def owners_kernel(wide, plan, target_ref, *refs):
    sets = 1 + max(s for group in plan for s, _ in group)
    xs, ys, out_ref = refs[:sets], refs[sets : sets + len(plan)], refs[-1]
    rows = target_ref.shape[0] // out_ref.shape[0]
    extra = refs[-2] if len(refs) > sets + len(plan) + 1 else None
    count = target_ref.shape[0]
    total = jnp.zeros((count, ys[0].shape[1]), F32)
    column = 0
    for group, y in zip(plan, ys):
        picked = jnp.zeros((count, y.shape[0]), F32)
        for which, first in group:
            x = xs[which]
            lane = lane_of((count, x.shape[2]))
            inside = (lane >= first) & (lane < first + wide)
            for m in range(2):
                hit = inside & (lane - first + m * wide == target_ref[:, column : column + 1])
                picked = picked + dot_nt(hit.astype(BF), x[m])
            column += 1
        total = total + dot(picked.astype(BF), y[...])
    for k in range(out_ref.shape[0]):
        part = total[k * rows : (k + 1) * rows].astype(BF)
        if extra is None:
            put(out_ref.at[k], part)
        else:
            out_ref[k] = jnp.zeros(out_ref.shape[1:], BF)
            out_ref[k, :rows, : part.shape[1]] = part
            out_ref[k, rows : rows + 3 * extra.shape[0], :] = split_rows(extra[...]).astype(BF)


def layers_kernel(nz, zed_ref, x_ref, *outs):
    total = jnp.sum(x_ref[...].astype(F32), axis=0)
    rows = total.shape[0] // nz
    for k, out in enumerate(outs):
        want = zed_ref[0] ^ k
        value = total[:rows]
        for z in range(1, nz):
            value = jnp.where(want == z, total[z * rows : (z + 1) * rows], value)
        out[...] = value.astype(BF)


def deal_last_kernel(rows, extra, x_ref, out_ref):
    total = jnp.sum(x_ref[...].astype(F32), axis=0)
    each = rows // out_ref.shape[0]
    small = total[rows : rows + extra]
    for i in range(1, 3):
        small = small + total[rows + i * extra : rows + (i + 1) * extra]
    small = split_rows(small).astype(BF)
    for i in range(out_ref.shape[0]):
        out_ref[i] = jnp.zeros(out_ref.shape[1:], BF)
        out_ref[i, :each, :] = total[i * each : (i + 1) * each].astype(BF)
        out_ref[i, each : each + 3 * extra, :] = small


def deal_kernel(*refs):
    *parts, out_ref = refs
    at = 0
    for part in parts:
        total = jnp.sum(part[...].astype(F32), axis=0)
        rows = total.shape[0] // out_ref.shape[0]
        for i in range(out_ref.shape[0]):
            out_ref[i, at : at + rows, :] = total[i * rows : (i + 1) * rows].astype(BF)
        at += rows


def dh2_kernel(*refs):
    *parts, h_ref, cot_ref, gain_ref, dh_ref, dy_ref, gain_out = refs
    width = h_ref.shape[1]
    grad = parts[0][:, :width].astype(F32)
    for part in parts[1:]:
        grad = grad + part[:, :width].astype(F32)
    dv, gain_out[...] = norm_back(h_ref[...], gain_ref[...], grad)
    dh = cot_ref[:, :width].astype(F32) + dv
    dh_ref[...] = dh
    put(dy_ref, dh.astype(BF))


def dh1_kernel(wide, half, w_ref, dq_ref, cq_ref, h1_ref, dh2_ref, gain_ref, dh_ref, dy_ref, gain_out):
    w = w_ref[0]
    dq = jnp.concatenate([own_of(dq_ref.at[m], w, half)[:, :wide] for m in range(2)], axis=1)
    grad = dot_nt(dq, cq_ref[...])
    dv, gain_out[...] = norm_back(own_of(h1_ref, w, half), gain_ref[...], grad)
    dh = dh2_ref[...] + dv
    dh_ref[...] = dh
    put(dy_ref, dh.astype(BF))


def last_kernel(wide, half, w_ref, d_ref, weight_ref, tok_ref, dh1_ref, gain_ref, out_ref, gain_out):
    w = w_ref[0]
    d = jnp.concatenate(
        [own_of(d_ref.at[m, i], w, half)[:, :wide] for i in range(3) for m in range(2)], axis=1
    )
    grad = dot_nt(d, weight_ref[...])
    dv, gain_out[...] = norm_back(tok_ref[w].astype(F32), gain_ref[...], grad)
    out_ref[...] = dh1_ref[...] + dv


def grad_prep_kernel(nh, hs, dy_ref, w_ref, o_ref, out_ref, de_ref, dh_ref, del_ref):
    wide = nh * hs
    dy = in_blocks(dy_ref)[:, : w_ref.shape[1]]
    out_ref[...] = dy
    da = dot_nt(dy, w_ref[...]).astype(BF)
    da = jnp.concatenate([da, jnp.zeros((da.shape[0], 2 * BLK - wide), BF)], axis=1)
    terms = da.astype(F32) * o_ref[...]
    delta = [jnp.sum(head_mask(terms, h, hs), axis=1, keepdims=True) for h in range(nh)]
    dh_ref[...] = pltpu.roll(da.astype(F32), hs, 1).astype(BF)
    lane = lane_of(del_ref.shape)
    cols = jnp.zeros(del_ref.shape, F32)
    for h in range(nh):
        cols = jnp.where(lane == h, delta[h], cols)
    del_ref[...] = cols
    de = pieces_into(da.astype(F32), [-t for t in delta], wide).astype(BF)
    for i in range(de_ref.shape[0]):
        de_ref[i] = de


def grad_prep(dy, weight, o, nh, hs, copies=1, deps=()):
    rows, width = o.shape[0], weight.shape[1]
    return plain(
        functools.partial(grad_prep_kernel, nh, hs),
        [],
        [dy, weight, o],
        [
            bf_shape(rows, width),
            bf_shape(copies, rows, 2 * BLK),
            bf_shape(rows, 2 * BLK),
            f32_shape(rows, BLK),
        ],
        deps=deps,
    )


def local(
    tokens,
    encoded,
    cotangent,
    assign,
    bucket_ids,
    gain_self,
    gain_cross,
    gain_ffn,
    query_weight,
    key_weight,
    value_weight,
    out_weight,
    cross_query,
    cross_key,
    cross_value,
    cross_out,
    gate_weight,
    up_weight,
    down_weight,
    bucket_table,
):
    nctx = lax.axis_size("ctx")
    nw = lax.axis_size("wsh")
    c = lax.axis_index("ctx")
    w = lax.axis_index("wsh")
    both = ("ctx", "wsh")
    rows, width = tokens.shape
    half = rows // 2
    length = rows * nw * nctx
    buckets, heads = bucket_table.shape
    inner = query_weight.shape[1]
    hs = inner // heads
    nh = heads // nw
    wide = nh * hs
    plane = 4
    nz = nctx // plane
    spot = (c % plane) * nw + w
    zed = c // plane
    hidden = gate_weight.shape[1]
    share = hidden // (nctx * nw)
    slot = -(-share // 32) * 32

    def pair(x, axis=0, tiled=True):
        return lax.all_gather(x, "wsh", axis=axis, tiled=tiled)

    def halves(parts):
        return lax.all_to_all(parts, "wsh", 0, 0, tiled=True)

    def mate(x):
        return lax.ppermute(x, "wsh", [(i, (i + 1) % nw) for i in range(nw)])

    planes = [[z * plane + i for i in range(plane)] for z in range(nz)]
    columns = [[z * plane + i for z in range(nz)] for i in range(plane)]

    def in_plane(x):
        return lax.all_to_all(x, "ctx", 0, 0, tiled=True, axis_index_groups=planes)

    def in_column(x):
        return lax.all_to_all(x, "ctx", 0, 0, tiled=True, axis_index_groups=columns)

    padded = -(-width // BLK) * BLK

    def spread(parts, count, deps=()):
        shape = bf_shape(count, len(parts) * parts[0].shape[0], parts[0].shape[1])
        return plain(spread_kernel, [], parts, [shape], (0, 1e6, 0), deps)[0]

    def add(a, b, deps=()):
        return plain(add_kernel, [], [a, b], [bf_shape(rows, padded)] * plane, (0, 1e6, 0), deps)

    def deal(parts, count, deps=()):
        shape = bf_shape(count, sum(x.shape[1] for x in parts) // count, parts[0].shape[2])
        return plain(deal_kernel, [], parts, [shape], (0, 1e6, 0), deps)[0]

    def tree(parts):
        while len(parts) > 1:
            parts = [parts[i] + parts[i + 1] for i in range(0, len(parts), 2)]
        return parts[0]

    def near(x, k):
        return lax.ppermute(x, "ctx", [(i, i ^ k) for i in range(nctx)])

    def stacked(parts, deps=()):
        shape = bf_shape(len(parts) * parts[0].shape[0], parts[0].shape[1])
        return plain(join_kernel, [], parts, [shape], (0, 1e6, 0), deps)[0]

    cut = inner // (nctx * nw)

    def targets(count):
        index = jnp.arange(plane * nz * count * cut, dtype=jnp.int32)
        to_k, to_z = index // (nz * count * cut), index // (count * cut) % nz
        to_i, to_t = index // cut % count, index % cut
        column = ((to_z * plane + to_k) * nw + w) * cut + to_t
        which = jnp.arange(count, dtype=jnp.int32)
        return jnp.where(to_i[:, None] == which[None, :], column[:, None], -1).astype(jnp.int32)

    def owner_parts(plan, xs, ys, small=None, deps=()):
        count = sum(len(group) for group in plan)
        total = nz * count * cut
        if small is not None:
            total = -(-(total + 3 * small.shape[0]) // 16) * 16
            ys = ys + [small]
        return plain(
            functools.partial(owners_kernel, wide, plan),
            [],
            [targets(count)] + xs + ys,
            [bf_shape(plane, total, padded)],
            (3e9, 6e6, 0),
            deps,
        )[0]

    def layers(x, deps=()):
        return plain(
            functools.partial(layers_kernel, nz),
            [zed.astype(jnp.int32)[None]],
            [x],
            [bf_shape(x.shape[1] // nz, x.shape[2])] * nz,
            (0, 1e6, 0),
            deps,
        )

    def owner_sums(total, count):
        return [total[i * cut : (i + 1) * cut, :width] for i in range(count)]

    lanes = jnp.arange(nctx, dtype=jnp.int32)
    owner = jnp.sum(jnp.where(assign[None, :] == lanes[:, None], lanes[None, :], 0), axis=1)
    chip_slot = owner % plane * nz + (owner // plane ^ zed)
    near_slot = (owner ^ c) % plane * nz + owner // plane
    meta = jnp.concatenate([owner, jnp.take(assign, c)[None], chip_slot, near_slot])
    meta = meta.astype(jnp.int32)
    core = w.astype(jnp.int32)[None]
    chip = nw * rows

    gains = pair(jnp.stack([gain_self, gain_cross, gain_ffn]), axis=1).astype(F32)
    gains = [gains[i : i + 1] for i in range(3)]
    tok = pair(tokens, tiled=False)

    def head_parts(weights, deps=()):
        count = len(weights) * wide
        shape = bf_shape(nw, weights[0].shape[0], -(-count // BLK) * BLK)
        return plain(functools.partial(heads_kernel, wide), [], weights, [shape], deps=deps)[0]

    g_own = jnp.pad(cotangent, ((0, 0), (0, padded - width)))
    g_parts = [g_own] + [near(g_own, k) for k in range(1, plane)]
    all_heads = halves(
        head_parts(
            [key_weight, value_weight, cross_key, cross_value, query_weight, cross_query]
        )
    )
    n1, q, k_own, v_own, kv_own = plain(
        functools.partial(project_kernel, wide),
        [],
        [tok, all_heads, gains[0]],
        [bf_shape(chip, width)] + [bf_shape(chip, 2 * BLK)] * 3 + [bf_shape(nz, chip, 2 * wide)],
    )

    kv = in_column(kv_own).reshape(-1, 2 * wide)

    hot = (bucket_ids[None, :] == jnp.arange(buckets, dtype=jnp.int32)[:, None]).astype(BF)
    values = dot_tn(lax.dynamic_slice_in_dim(bucket_table, w * nh, nh, 1), hot)
    lines = bias_rows(values)

    enc_pair = pair(encoded)
    (ekv_own,) = plain(
        functools.partial(encode_kernel, wide),
        [],
        [enc_pair, all_heads],
        [bf_shape(enc_pair.shape[0], 4 * BLK)],
        deps=(kv, *g_parts[1:], *lines),
    )

    kv = [kv] + [near(kv, k) for k in range(1, plane)]

    ts, tt = bias_tiles(*lines, deps=(kv[0], ekv_own))

    ekv = lax.all_gather(ekv_own, "ctx", axis=0, tiled=True)
    spots = jnp.stack([(c % plane) * nw + i for i in (w, 1 - w)]).astype(jnp.int32)
    ug_own, ug_sent, wd_own, wd_sent = plain(
        functools.partial(units_kernel, nz, plane * nw, share, slot),
        [spots],
        [gate_weight, up_weight, down_weight.T],
        [bf_shape(gate_weight.shape[0], 2 * nz * slot)] * 2
        + [bf_shape(width, nz // nw * slot)] * 2,
        deps=(ts,),
    )
    g_plane = stacked(g_parts, deps=(ug_own,))
    out_mate, cross_out_mate = mate(out_weight), mate(cross_out)
    o1, a1, qe1, lse1 = self_fwd(
        meta, q, kv, ts, nh, hs, deps=(g_plane, out_mate, cross_out_mate)
    )
    a1_pair = pair(a1, tiled=False)
    h1, n2, cq = plain(
        functools.partial(middle_kernel, wide),
        [core],
        [tok, a1_pair, out_weight, out_mate, gains[1], all_heads],
        [f32_shape(chip, width), bf_shape(chip, width), bf_shape(chip, 2 * BLK)],
    )
    qg = lax.all_gather(qe1, "ctx", axis=0, tiled=True).reshape(nctx, chip, 2 * BLK)
    cq_full, ck_full, cv_full = pair(cross_query), pair(cross_key), pair(cross_value)
    qkv_full = pair(jnp.concatenate([query_weight, key_weight, value_weight], axis=1))

    o2, a2, qe2 = cross_fwd(cq, ekv, nh, hs)
    a2_pair = pair(a2, tiled=False)
    h2, n3 = plain(
        functools.partial(third_kernel, half),
        [core],
        [h1, a2_pair, cross_out, cross_out_mate, gains[2]],
        [f32_shape(rows, width), bf_shape(rows, padded)],
    )

    ug_sent, wd_sent, g_plane, _ = lax.optimization_barrier((ug_sent, wd_sent, g_plane, a2_pair))
    g_plane = g_plane, mate(g_plane)
    ug, wd = plain(
        order_kernel,
        [core],
        [ug_own, mate(ug_sent), wd_own, mate(wd_sent)],
        [bf_shape(width, 2 * nz * slot), bf_shape(width, nz * slot)],
        deps=(n3,),
    )
    (dact,) = plain(
        ffn_early_kernel, [], [*g_plane, wd], [f32_shape(nw * plane * rows, nz * slot)], deps=(n3,)
    )
    n3_plane = stacked([n3] + [near(n3, k) for k in range(1, plane)], deps=(dact,))
    n3_plane = n3_plane, mate(n3_plane)
    act, dgu, dn0, dn1 = ffn_both(n3_plane, dact, ug)
    sent = add(dn0, mate(dn1), deps=(qg,))
    got = [near(sent[k], k) for k in range(1, plane)]
    ffn, out0, out1 = ffn_late(n3_plane, g_plane, act, dgu, wd, nz, share, (sent[0],))
    dh2, dy2, gain3 = plain(
        dh2_kernel,
        [],
        [sent[0]] + got + [h2, g_own, gains[2]],
        [f32_shape(rows, width), bf_shape(rows, padded), f32_shape(1, width)],
        deps=(out0,),
    )

    dy2, de2, _, _ = grad_prep(pair(dy2, tiled=False), cross_out, o2, nh, hs)
    dcq, dekv = cross_bwd(qe2, de2[0], ekv, plane, nz, nh, hs)
    dekv = in_plane(dekv.reshape(plane, -1, 2 * wide))
    dcq_pair = pair(dcq, tiled=False)
    dh1, dy1, gain2 = plain(
        functools.partial(dh1_kernel, wide, half),
        [core],
        [dcq_pair, cq_full, h1, dh2, gains[1]],
        [f32_shape(rows, width), bf_shape(rows, padded), f32_shape(1, width)],
    )

    dy1, de1, dhi1, delta1 = grad_prep(pair(dy1, tiled=False), out_weight, o1, nh, hs)
    dg = [de1[0]] + [near(de1[0], plane * k) for k in range(1, nz)]
    dekv = layers(dekv, deps=(de1,))
    dg = spread(dg, plane, deps=(dekv[0], qg, ck_full, cv_full, qkv_full))
    spread_out = dg
    dekv = [dekv[0]] + [near(dekv[k], plane * k) for k in range(1, nz)]

    dq, rev = self_dq(meta, q, dhi1, lse1, delta1, kv, ts, nh, hs, deps=(dg,))
    dg = in_plane(dg).reshape(nctx, chip, 2 * BLK)
    (dekv,) = plain(output_kernel, [], dekv, [bf_shape(*dekv[0].shape)], deps=(dq,))
    dekv_pair = pair(dekv, tiled=False)
    made = owner_parts(
        (((0, 0),), ((1, 0),), ((2, 0),), ((3, 0), (3, wide))),
        [a1_pair, a2_pair, dcq_pair, dekv_pair],
        [dy1, dy2, n2, enc_pair],
        deps=(dq,),
    )
    ffn = lax.psum_scatter(
        tie(ffn, spread_out).reshape(nz, 3 * share, padded),
        "ctx",
        scatter_dimension=0,
        axis_index_groups=columns,
        tiled=True,
    )
    dk, dv = self_dkv(meta, k_own, v_own, qg, dg, tt, nh, hs, deps=(made, dq))
    made = in_plane(made)
    rev = tie(rev, dk)

    dqkv_pair = pair(jnp.stack([dq, dk, dv]), tiled=False).reshape(nw, 3, chip, 2 * BLK)
    dqkv = [dqkv_pair[:, i] for i in range(3)]
    tokens_grad, gain1 = plain(
        functools.partial(last_kernel, wide, half),
        [core],
        [dqkv_pair, qkv_full, tok, dh1, gains[0]],
        [f32_shape(rows, width), f32_shape(1, width)],
    )

    rev = rev.reshape(nh, 8, -1)
    by_distance = sum(rev[:, i, 1 + i : 1 + i + length] for i in range(8))
    hot_rev = (
        jnp.flip(bucket_ids)[None, :] == jnp.arange(buckets, dtype=jnp.int32)[:, None]
    ).astype(F32)
    table_own = lax.dot_general(
        hot_rev, by_distance, (((1,), (1,)), ((), ())), precision=lax.Precision.HIGHEST
    )
    table = lax.dynamic_update_slice_in_dim(
        jnp.zeros((buckets, heads), F32), table_own, w * nh, 1
    )

    small = jnp.concatenate([gain1[0], gain2[0], gain3[0], table.reshape(-1)])
    small = jnp.pad(small, (0, -small.shape[0] % padded)).reshape(-1, padded)
    extra = small.shape[0]
    second = owner_parts((((0, 0), (1, 0), (2, 0)),), dqkv, [n1], small)
    second = in_plane(tie(second, made))
    first = layers(made)
    out_sent = add(out0, mate(tie(out1, gain1)), deps=(made,))
    first = [first[0]] + [near(first[k], plane * k) for k in range(1, nz)]
    (second,) = plain(
        functools.partial(deal_last_kernel, 3 * nz * cut, extra),
        [],
        [second],
        [bf_shape(nz, -(-(3 * cut + 3 * extra) // 16) * 16, padded)],
        deps=(first[0], out_sent[0]),
    )
    dealt = second
    out_sent = [tie(m, second) for m in out_sent[1:]], out_sent[0]
    out_got = [near(m, k + 1) for k, m in enumerate(out_sent[0])]
    (output,) = plain(output_kernel, [], [h2, out_sent[1]] + out_got, [bf_shape(rows, width)])
    dekv_pair = tie(dekv_pair, second)
    second = jnp.sum(in_column(second).astype(F32), axis=0)
    small = [second[3 * cut + i * extra : 3 * cut + (i + 1) * extra] for i in range(3)]
    small = (small[0] + small[1]) + small[2]
    small = small + mate(small)
    q_t, k_t, v_t = owner_sums(second, 3)
    (first,) = plain(output_kernel, [], first, [f32_shape(5 * cut, padded)], deps=(dealt,))
    out_share, cross_out_share, cq_t, ck_t, cv_t = owner_sums(first, 5)
    ffn = ffn[0, :, :width].astype(F32).reshape(3, share, width)

    def joined(x):
        return jnp.swapaxes(x[:, :, :wide], 0, 1).reshape(-1, inner)

    def own_encoder(x):
        return lax.dynamic_slice_in_dim(x, w * encoded.shape[0], encoded.shape[0], 0)

    dek, dev = joined(dekv_pair), joined(dekv_pair[:, :, wide:])
    encoded_grad = dot_nt(own_encoder(dek), ck_full) + dot_nt(own_encoder(dev), cv_full)

    small = small.reshape(-1)
    table = small[3 * width : 3 * width + buckets * heads].reshape(buckets, heads)
    return (
        output,
        tokens_grad,
        encoded_grad,
        small[:width],
        small[width : 2 * width],
        small[2 * width : 3 * width],
        q_t.T,
        k_t.T,
        v_t.T,
        out_share,
        cq_t.T,
        ck_t.T,
        cv_t.T,
        cross_out_share,
        ffn[0].T,
        ffn[1].T,
        ffn[2],
        table,
    )


def solution(mesh):
    rows = P(("seq", "ctx", "wsh"), None)
    cols = P("seq", ("ctx", "wsh"))
    split = P("wsh", None)
    return jax.shard_map(
        local,
        mesh=mesh,
        in_specs=(rows, rows, rows, P(), P(), P("wsh"), P("wsh"), P("wsh"))
        + (split,) * 11
        + (P(),),
        out_specs=(
            rows,
            rows,
            rows,
            P("seq"),
            P("seq"),
            P("seq"),
            cols,
            cols,
            cols,
            rows,
            cols,
            cols,
            cols,
            rows,
            cols,
            cols,
            rows,
            P("seq", None),
        ),
        check_vma=False,
    )
```

```python
import functools

import jax
import jax.numpy as jnp
from jax import lax
from jax.experimental import pallas as pl
from jax.experimental.pallas import tpu as pltpu
from jax.sharding import PartitionSpec as P

EPS = 1e-06
NEG = -1e30
F32 = jnp.float32
BF = jnp.bfloat16
BLK = 128
GRP = 4
UNROLL = 3
CH = BLK * GRP
VLIM = 60 * 1024 * 1024
SLOW = 64


def dot(a, b):
    return lax.dot_general(a, b, (((1,), (0,)), ((), ())), preferred_element_type=F32)


def dot_nt(a, b):
    return lax.dot_general(a, b, (((1,), (1,)), ((), ())), preferred_element_type=F32)


def dot_tn(a, b):
    return lax.dot_general(a, b, (((0,), (0,)), ((), ())), preferred_element_type=F32)


def lane_of(shape):
    return lax.broadcasted_iota(jnp.int32, shape, 1)


def head_mask(value, head, hs):
    lane = lane_of(value.shape)
    keep = (lane >= head * hs) & (lane < (head + 1) * hs)
    return jnp.where(keep, value, jnp.zeros_like(value))


def lane_fold(value, op):
    out = value[:, :BLK]
    for i in range(1, value.shape[1] // BLK):
        out = op(out, value[:, i * BLK : (i + 1) * BLK])
    return out


def pieces_into(base, columns, first):
    lane = lane_of(base.shape)
    out = base
    for i, column in enumerate(columns):
        rest = column
        for j in range(3):
            part = rest.astype(BF).astype(F32)
            rest = rest - part
            out = jnp.where(lane == first + 3 * i + j, part, out)
    return out


def params(flops, nbytes, trans):
    return dict(
        compiler_params=pltpu.CompilerParams(vmem_limit_bytes=VLIM),
        cost_estimate=pl.CostEstimate(
            flops=int(flops) // SLOW,
            bytes_accessed=int(nbytes) // SLOW,
            transcendentals=int(trans) // SLOW,
        ),
    )


def after(value, *deps):
    return lax.optimization_barrier((value,) + deps)[0]


def f32_shape(*dims):
    return jax.ShapeDtypeStruct(dims, F32)


def bf_shape(*dims):
    return jax.ShapeDtypeStruct(dims, BF)


def plain(kernel, scalars, inputs, outputs, cost=(1e9, 4e6, 0), deps=()):
    count, late = len(scalars) + len(inputs), len(deps)

    def body(*refs):
        kernel(*refs[:count], *refs[count + late :])

    return pl.pallas_call(
        body,
        in_specs=[SM] * len(scalars) + [VM] * len(inputs) + [ANY] * late,
        out_specs=[VM] * len(outputs),
        out_shape=list(outputs),
        **params(*cost),
    )(*scalars, *inputs, *deps)


VM = pl.BlockSpec(memory_space=pltpu.VMEM)
ANY = pl.BlockSpec(memory_space=pl.ANY)
SM = pl.BlockSpec(memory_space=pltpu.SMEM)


def tie(x, *deps):
    return pl.pallas_call(
        lambda *refs: None,
        in_specs=[ANY] * (1 + len(deps)),
        out_specs=ANY,
        out_shape=jax.ShapeDtypeStruct(x.shape, x.dtype),
        input_output_aliases={0: 0},
        **params(0, 0, 0),
    )(x, *deps)


def bias_kernel(nb, nh, nat_ref, rev_ref, ts_ref, tt_ref):
    row = lax.broadcasted_iota(jnp.int32, (BLK, BLK), 0)
    col = lax.broadcasted_iota(jnp.int32, (BLK, BLK), 1)
    upper = col >= row

    def skew(line):
        eight = pltpu.roll(jnp.broadcast_to(line, (8, BLK)), 0, 1, stride=1, stride_axis=0)
        return jnp.concatenate(
            [eight] + [pltpu.roll(eight, 8 * i, 1) for i in range(1, BLK // 8)], axis=0
        )

    def step(r, carry):
        d = nb - 1 - r
        first, second = rev_ref[nb - jnp.maximum(d, 0)], rev_ref[nb - 1 - jnp.maximum(d, 0)]
        for h in range(nh):
            tile = jnp.where(upper, skew(first[h : h + 1]), skew(second[h : h + 1]))
            ts_ref[r, h] = jnp.where(d * BLK + row - col >= 0, tile, NEG).astype(BF)
        d = r - (GRP - 1)
        first, second = nat_ref[jnp.maximum(d, 0) + 1], nat_ref[jnp.maximum(d, 0)]
        for h in range(nh):
            tile = jnp.where(upper, skew(first[h : h + 1]), skew(second[h : h + 1]))
            tt_ref[r, h] = jnp.where(d * BLK + col - row >= 0, tile, NEG).astype(BF)
        return carry

    lax.fori_loop(0, nb + GRP - 1, step, 0)


def bias_rows(values):
    nh, length = values.shape
    nb = length // BLK
    zero = jnp.zeros((nh, 1), F32)
    nat = jnp.concatenate([jnp.zeros((nh, BLK), F32), values], axis=1)
    rev = jnp.concatenate([zero, jnp.flip(values, 1), jnp.zeros((nh, BLK - 1), F32)], axis=1)
    nat = jnp.transpose(nat.reshape(nh, nb + 1, BLK), (1, 0, 2))
    rev = jnp.transpose(rev.reshape(nh, nb + 1, BLK), (1, 0, 2))
    return nat, rev


def bias_tiles(nat, rev, deps=()):
    nb, nh = nat.shape[0] - 1, nat.shape[1]
    shape = bf_shape(nb + GRP - 1, nh, BLK, BLK)
    return plain(
        functools.partial(bias_kernel, nb, nh), [], [nat, rev], [shape, shape], deps=deps
    )


def gather_blocks(ref, meta_ref, nctx, first, lo, hi, base=0):
    parts = []
    for i in range(GRP):
        t = first + i
        early = t < nctx
        slot = meta_ref[base + jnp.where(early, t, 2 * nctx - 1 - t)]
        at = pl.multiple_of(jnp.where(early, 0, BLK), BLK)
        parts.append(ref[slot, pl.ds(at, BLK), lo:hi])
    return jnp.concatenate(parts, axis=0)


def fetch(parts, held_ref, sem):
    rows = parts[0].shape[0]
    copies = [
        pltpu.make_async_copy(part, held_ref.at[pl.ds(k * rows, rows)], sem.at[k])
        for k, part in enumerate(parts)
    ]
    for copy in copies:
        copy.start()
    for copy in copies:
        copy.wait()


def bias_of(ref, first):
    rows = ref.shape[1] * BLK
    return jnp.concatenate(
        [ref[first + i].reshape(rows, BLK) for i in range(GRP)], axis=1
    ).astype(F32)


def stack_heads(value, hs, nh, shift=0):
    return jnp.concatenate([head_mask(value, h + shift, hs) for h in range(nh)], axis=0)


def merge_heads(stacked, hs, nh, shift=0):
    rows = stacked.shape[0] // nh
    total = jnp.zeros((rows, stacked.shape[1]), F32)
    for h in range(nh):
        total = total + head_mask(stacked[h * rows : (h + 1) * rows], h + shift, hs)
    return total


def pick_columns(columns, nh, rows):
    out = jnp.zeros((rows, BLK), F32)
    lane = lane_of(out.shape)
    for h in range(nh):
        out = jnp.where(lane == h, columns[h * rows : (h + 1) * rows], out)
    return out


def stack_columns(ref, rows, nh):
    return jnp.concatenate([ref[rows, h : h + 1] for h in range(nh)], axis=0)


def self_fwd_kernel(count, nctx, nh, hs, meta_ref, q_ref, ts_ref, *rest):
    o_ref, a_ref, qe_ref, lse_ref, qm_ref, s_ref, acc_ref, top_ref, sum_ref, flat_ref, sem = rest[-11:]
    fetch(rest[:count], flat_ref, sem)
    kv_ref = flat_ref.reshape(nctx, 2 * BLK, flat_ref.shape[1])
    nb = 2 * nctx
    wide = nh * hs
    early = meta_ref[nctx]
    split = early // GRP + 1
    base = 2 * nctx + 1
    for half in range(2):
        qm_ref[half] = stack_heads(q_ref[half * BLK : (half + 1) * BLK, :], hs, nh)
    top_ref[...] = jnp.full(top_ref.shape, NEG, F32)
    sum_ref[...] = jnp.zeros_like(sum_ref)
    acc_ref[...] = jnp.zeros_like(acc_ref)

    def place(step):
        half = (step >= split).astype(jnp.int32)
        return half, step - half * split

    def score(step, carry):
        half, ch = place(step)
        blk = jnp.where(half == 0, early, nb - 1 - early)
        keys = gather_blocks(kv_ref, meta_ref, nctx, ch * GRP, 0, 2 * BLK, base)
        s = dot_nt(qm_ref[half], keys) + bias_of(ts_ref, nb - 1 - blk + ch * GRP)
        s_ref[step] = s
        top_ref[half] = jnp.maximum(top_ref[half], lane_fold(s, jnp.maximum))
        return carry

    steps = nb // GRP + 1
    lax.fori_loop(0, steps, score, 0, unroll=UNROLL)
    for half in range(2):
        top = jnp.max(top_ref[half], axis=1, keepdims=True)
        top_ref[half] = jnp.broadcast_to(top, top_ref.shape[1:])

    def weigh(step, carry):
        half, ch = place(step)
        vals = gather_blocks(kv_ref, meta_ref, nctx, ch * GRP, BLK, 3 * BLK, base)
        top = top_ref[half]
        p = jnp.exp(s_ref[step] - jnp.concatenate([top] * GRP, axis=1))
        acc_ref[half] += dot(p.astype(BF), vals)
        sum_ref[half] += lane_fold(p, jnp.add)
        return carry

    lax.fori_loop(0, steps, weigh, 0, unroll=UNROLL)
    for half in range(2):
        rows = slice(half * BLK, (half + 1) * BLK)
        total = jnp.sum(sum_ref[half], axis=1, keepdims=True)
        o = pltpu.roll(merge_heads(acc_ref[half] / total, hs, nh, 1), 2 * BLK - hs, 1)
        o_ref[rows, :] = o
        a_ref[rows, :] = o[:, :wide].astype(BF)
        lse = pick_columns(top_ref[half][:, :1] + jnp.log(total), nh, BLK)
        lse_ref[rows, :] = lse
        minus = [-lse[:, h : h + 1] for h in range(nh)]
        qe_ref[rows, :] = pieces_into(q_ref[rows, :].astype(F32), minus, wide).astype(BF)


def self_fwd(meta, q, kv, ts, nh, hs, deps=()):
    nctx = len(kv) * kv[0].shape[0] // (2 * BLK)
    nb = 2 * nctx
    rows = 2 * BLK
    pairs = (nb + 1) * BLK * BLK * nh
    return pl.pallas_call(
        functools.partial(self_fwd_kernel, len(kv), nctx, nh, hs),
        in_specs=[SM, VM, VM] + [ANY] * (len(kv) + len(deps)),
        out_specs=[VM] * 4,
        out_shape=[
            f32_shape(rows, rows),
            bf_shape(rows, nh * hs),
            bf_shape(rows, rows),
            f32_shape(rows, BLK),
        ],
        scratch_shapes=[
            pltpu.VMEM((2, nh * BLK, 2 * BLK), BF),
            pltpu.VMEM((nb // GRP + 1, nh * BLK, CH), F32),
            pltpu.VMEM((2, nh * BLK, 2 * BLK), F32),
            pltpu.VMEM((2, nh * BLK, BLK), F32),
            pltpu.VMEM((2, nh * BLK, BLK), F32),
            pltpu.VMEM((nb * BLK, kv[0].shape[1]), BF),
            pltpu.SemaphoreType.DMA((len(kv),)),
        ],
        **params(pairs * 2 * 512, 10e6, pairs),
    )(meta, q, ts, *kv, *deps)


def self_dq_kernel(count, nctx, nh, hs, meta_ref, q_ref, da_ref, lse_ref, del_ref, ts_ref, *rest):
    dq_ref, rev_ref, qm_ref, dm_ref, col_ref, acc_ref, flat_ref, sem = rest[-8:]
    fetch(rest[:count], flat_ref, sem)
    kv_ref = flat_ref.reshape(nctx, 2 * BLK, flat_ref.shape[1])
    nb = 2 * nctx
    early = meta_ref[nctx]
    split = early // GRP + 1
    span = CH + BLK
    rev_ref[...] = jnp.zeros_like(rev_ref)
    acc_ref[...] = jnp.zeros_like(acc_ref)
    for half in range(2):
        rows = slice(half * BLK, (half + 1) * BLK)
        qm_ref[half] = stack_heads(q_ref[rows, :], hs, nh)
        dm_ref[half] = stack_heads(da_ref[rows, :], hs, nh, 1)
        for i, ref in enumerate((lse_ref, del_ref)):
            col_ref[half, i] = jnp.broadcast_to(stack_columns(ref, rows, nh), col_ref.shape[2:])

    def step(at, carry):
        half = (at >= split).astype(jnp.int32)
        ch = at - half * split
        blk = jnp.where(half == 0, early, nb - 1 - early)
        held = gather_blocks(kv_ref, meta_ref, nctx, ch * GRP, 0, 3 * BLK, 2 * nctx + 1)
        keys, vals = held[:, : 2 * BLK], held[:, BLK:]
        off = pl.multiple_of((ch * GRP - blk + nb - 1) * BLK, BLK)
        s = dot_nt(qm_ref[half], keys) + bias_of(ts_ref, nb - 1 - blk + ch * GRP)
        p = jnp.exp(s - jnp.concatenate([col_ref[half, 0]] * GRP, axis=1))
        delta = jnp.concatenate([col_ref[half, 1]] * GRP, axis=1)
        ds = (p * (dot_nt(dm_ref[half], vals) - delta)).astype(BF)
        acc_ref[half] += dot(ds, keys)
        flat = jnp.concatenate([jnp.zeros((nh * BLK, BLK), F32), ds.astype(F32)], axis=1)
        for h in range(nh):
            line = flat[h * BLK : h * BLK + 8]
            for i in range(1, BLK // 8):
                first = h * BLK + 8 * i
                line = line + pltpu.roll(flat[first : first + 8], span - 8 * i, 1)
            rev_ref[h * 8 : (h + 1) * 8, pl.ds(off, span)] += line
        return carry

    lax.fori_loop(0, nb // GRP + 1, step, 0, unroll=UNROLL)
    for half in range(2):
        dq_ref[half * BLK : (half + 1) * BLK, :] = merge_heads(acc_ref[half], hs, nh).astype(BF)


def self_dq(meta, q, da, lse, delta, kv, ts, nh, hs, deps=()):
    nctx = len(kv) * kv[0].shape[0] // (2 * BLK)
    nb = 2 * nctx
    pairs = (nb + 1) * BLK * BLK * nh
    return pl.pallas_call(
        functools.partial(self_dq_kernel, len(kv), nctx, nh, hs),
        in_specs=[SM] + [VM] * 5 + [ANY] * (len(kv) + len(deps)),
        out_specs=[VM, VM],
        out_shape=[
            jax.ShapeDtypeStruct((2 * BLK, 2 * BLK), BF),
            jax.ShapeDtypeStruct((8 * nh, nb * BLK + CH), F32),
        ],
        scratch_shapes=[
            pltpu.VMEM((2, nh * BLK, 2 * BLK), BF),
            pltpu.VMEM((2, nh * BLK, 2 * BLK), BF),
            pltpu.VMEM((2, 2, nh * BLK, BLK), F32),
            pltpu.VMEM((2, nh * BLK, 2 * BLK), F32),
            pltpu.VMEM((nb * BLK, kv[0].shape[1]), BF),
            pltpu.SemaphoreType.DMA((len(kv),)),
        ],
        **params(pairs * 2 * 896, 10e6, pairs),
    )(meta, q, da, lse, delta, ts, *kv, *deps)


def self_dkv_kernel(
    nctx, nh, hs, meta_ref, k_ref, v_ref, qg_ref, dg_ref, tt_ref, dq_ref, *rest
):
    out_ref, km_ref, vm_ref, ka_ref, va_ref = rest[-5:]
    nb = 2 * nctx
    wide = nh * hs
    early = meta_ref[nctx]
    late = nb - 1 - early
    split = nb // GRP - early // GRP

    def extended(value):
        lane = lane_of(value.shape)
        parts = []
        for h in range(nh):
            first = wide + 3 * h
            ones = (lane >= first) & (lane < first + 3)
            parts.append(jnp.where(ones, jnp.ones_like(value), head_mask(value, h, hs)))
        return jnp.concatenate(parts, axis=0)

    out_ref[0] = dq_ref[...]
    ka_ref[...] = jnp.zeros_like(ka_ref)
    va_ref[...] = jnp.zeros_like(va_ref)
    for half in range(2):
        rows = slice(half * BLK, (half + 1) * BLK)
        km_ref[half] = extended(k_ref[rows, :])
        vm_ref[half] = extended(v_ref[rows, :])

    def step(at, carry):
        half = (at >= split).astype(jnp.int32)
        blk = jnp.where(half == 0, early, late)
        ch = at - half * split + blk // GRP
        qc = gather_blocks(qg_ref, meta_ref, nctx, ch * GRP, 0, 2 * BLK)
        dc = gather_blocks(dg_ref, meta_ref, nctx, ch * GRP, 0, 2 * BLK, nctx + 1)
        p = jnp.exp(dot_nt(km_ref[half], qc) + bias_of(tt_ref, ch * GRP - blk + GRP - 1))
        ds = (p * dot_nt(vm_ref[half], dc)).astype(BF)
        ka_ref[half] += dot(ds, qc)
        va_ref[half] += dot(p.astype(BF), dc)
        return carry

    lax.fori_loop(0, nb // GRP + 1, step, 0, unroll=UNROLL)
    for half in range(2):
        rows = slice(half * BLK, (half + 1) * BLK)
        out_ref[1, rows, :] = merge_heads(ka_ref[half], hs, nh).astype(BF)
        out_ref[2, rows, :] = merge_heads(va_ref[half], hs, nh).astype(BF)


def self_dkv(meta, k, v, qg, dg, tt, dq, nh, hs, deps=()):
    nctx = qg.shape[0]
    nb = 2 * nctx
    pairs = (nb + 1) * BLK * BLK * nh
    return pl.pallas_call(
        functools.partial(self_dkv_kernel, nctx, nh, hs),
        in_specs=[SM] + [VM] * 6 + [ANY] * len(deps),
        out_specs=VM,
        out_shape=bf_shape(3, 2 * BLK, 2 * BLK),
        scratch_shapes=[
            pltpu.VMEM((2, nh * BLK, 2 * BLK), BF),
            pltpu.VMEM((2, nh * BLK, 2 * BLK), BF),
            pltpu.VMEM((2, nh * BLK, 2 * BLK), F32),
            pltpu.VMEM((2, nh * BLK, 2 * BLK), F32),
        ],
        **params(pairs * 2 * 1024, 10e6, pairs),
    )(meta, k, v, qg, dg, tt, dq, *deps)


def cross_fwd_kernel(nh, hs, q_ref, e_ref, o_ref, a_ref, qe_ref, s_ref):
    wide = nh * hs
    chunks = e_ref.shape[0] // CH
    rows = q_ref.shape[0]
    q = q_ref[...]
    qm = stack_heads(q, hs, nh)
    top = jnp.full((nh * rows, BLK), NEG, F32)
    for ch in range(chunks):
        s = dot_nt(qm, e_ref[ch * CH : (ch + 1) * CH, : 2 * BLK])
        s_ref[ch] = s
        top = jnp.maximum(top, lane_fold(s, jnp.maximum))
    top = jnp.max(top, axis=1, keepdims=True)
    total = jnp.zeros((nh * rows, BLK), F32)
    acc = jnp.zeros((nh * rows, 2 * BLK), F32)
    for ch in range(chunks):
        p = jnp.exp(s_ref[ch] - top)
        total = total + lane_fold(p, jnp.add)
        acc = acc + dot(p.astype(BF), e_ref[ch * CH : (ch + 1) * CH, 2 * BLK :])
    total = jnp.sum(total, axis=1, keepdims=True)
    o = merge_heads(acc / total, hs, nh)
    o_ref[...] = o
    a_ref[...] = o[:, :wide].astype(BF)
    lse = pick_columns(top + jnp.log(total), nh, rows)
    minus = [-lse[:, h : h + 1] for h in range(nh)]
    qe_ref[...] = pieces_into(q.astype(F32), minus, wide).astype(BF)


def cross_fwd(q, e, nh, hs):
    enc = e.shape[0]
    rows = 2 * BLK
    pairs = rows * enc * nh
    return pl.pallas_call(
        functools.partial(cross_fwd_kernel, nh, hs),
        in_specs=[VM, VM],
        out_specs=[VM] * 3,
        out_shape=[f32_shape(rows, rows), bf_shape(rows, nh * hs), bf_shape(rows, rows)],
        scratch_shapes=[pltpu.VMEM((enc // CH, nh * rows, CH), F32)],
        **params(pairs * 2 * 512, 4e6, pairs),
    )(q, e)


def cross_bwd_kernel(plane, nz, nh, hs, qe_ref, de_ref, all_ref, dq_ref, dkv_ref, e_ref, acc_ref, sem):
    size = all_ref.shape[0] // (plane * nz)
    copies = []
    for k in range(plane):
        for z in range(nz):
            source = all_ref.at[pl.ds((z * plane + k) * size, size)]
            target = e_ref.at[pl.ds((k * nz + z) * size, size)]
            copies.append(pltpu.make_async_copy(source, target, sem.at[k, z]))
    for copy in copies:
        copy.start()
    for copy in copies:
        copy.wait()
    wide = nh * hs
    acc_ref[...] = jnp.zeros_like(acc_ref)

    def kept(value, h):
        lane = lane_of(value.shape)
        first = wide + 3 * h
        keep = ((lane >= h * hs) & (lane < (h + 1) * hs)) | ((lane >= first) & (lane < first + 3))
        return jnp.where(keep, value, jnp.zeros_like(value))

    qm = [kept(qe_ref[...], h) for h in range(nh)]
    dm = [kept(de_ref[...], h) for h in range(nh)]

    for ch in range(e_ref.shape[0] // CH):
        rows = slice(ch * CH, (ch + 1) * CH)
        ek = e_ref[rows, : 2 * BLK]
        ev = e_ref[rows, 2 * BLK :]
        ek_t = jnp.transpose(ek.astype(F32)).astype(BF)
        dk = jnp.zeros((CH, 2 * BLK), F32)
        dv = jnp.zeros((CH, 2 * BLK), F32)
        for h in range(nh):
            p = jnp.exp(dot_nt(ek, qm[h]))
            ds = (p * dot_nt(ev, dm[h])).astype(BF)
            dk = dk + dot(ds, qm[h])
            dv = dv + dot(p.astype(BF), dm[h])
            acc_ref[h * hs : (h + 1) * hs, :] += dot(ek_t[h * hs : (h + 1) * hs, :], ds)
        dkv_ref[rows, :] = jnp.concatenate([dk[:, :wide], dv[:, :wide]], axis=1).astype(BF)
    dq_ref[...] = jnp.transpose(acc_ref[...]).astype(BF)


def cross_bwd(qe, de, e, plane, nz, nh, hs):
    enc = e.shape[0]
    pairs = 2 * BLK * enc * nh
    return pl.pallas_call(
        functools.partial(cross_bwd_kernel, plane, nz, nh, hs),
        in_specs=[VM, VM, ANY],
        out_specs=[VM, VM],
        out_shape=[bf_shape(2 * BLK, 2 * BLK), bf_shape(enc, 2 * nh * hs)],
        scratch_shapes=[
            pltpu.VMEM((enc, 4 * BLK), BF),
            pltpu.VMEM((2 * BLK, 2 * BLK), F32),
            pltpu.SemaphoreType.DMA((plane, nz)),
        ],
        **params(pairs * 2 * 1024, 4e6, pairs),
    )(qe, de, e)


def scale_of(rows):
    return lax.rsqrt(jnp.mean(rows * rows, axis=-1, keepdims=True) + EPS)


def norm_back(rows, gain, grad):
    rr = scale_of(rows)
    scaled = gain * grad
    shared = jnp.mean(rows * scaled, axis=-1, keepdims=True)
    dv = rr * scaled - rows * (rr * rr * rr) * shared
    return dv, jnp.sum(rows * rr * grad, axis=0, keepdims=True)


def in_blocks(pair_ref):
    half = pair_ref.shape[1] // 2
    return jnp.concatenate(
        [pair_ref[m, i * half : (i + 1) * half] for i in range(2) for m in range(2)], axis=0
    )


def put(ref, value):
    cols = value.shape[1]
    ref[:, :cols] = value
    if ref.shape[1] > cols:
        ref[:, cols:] = jnp.zeros((ref.shape[0], ref.shape[1] - cols), ref.dtype)


def own_of(ref, w, half):
    return jnp.concatenate(
        [ref[pl.ds(pl.multiple_of(i * BLK + w * half, half), half), :] for i in range(2)], axis=0
    )


def project_kernel(wide, tok_ref, w_ref, gain_ref, n1_ref, q_ref, k_ref, v_ref, kv_ref):
    x = in_blocks(tok_ref).astype(F32)
    n1 = (x * scale_of(x) * gain_ref[...]).astype(BF)
    n1_ref[...] = n1
    cut = w_ref.shape[1]

    def product(first, count):
        cols = slice(first * wide, (first + count) * wide)
        return (dot(n1[:, :cut], w_ref[0, :, cols]) + dot(n1[:, cut:], w_ref[1, :, cols])).astype(BF)

    kv = product(0, 2)
    for i in range(kv_ref.shape[0]):
        kv_ref[i] = kv
    zero = jnp.zeros((x.shape[0], 2 * BLK), BF)
    for ref, value in ((k_ref, kv[:, :wide]), (v_ref, kv[:, wide:]), (q_ref, product(4, 1))):
        ref[...] = zero
        ref[:, :wide] = value


def encode_kernel(wide, enc_ref, w_ref, out_ref):
    x = enc_ref[...]
    cut = w_ref.shape[1]
    cols = slice(2 * wide, 4 * wide)
    made = dot(x[:, :cut], w_ref[0, :, cols]) + dot(x[:, cut:], w_ref[1, :, cols])
    made = made.astype(BF)
    out_ref[...] = jnp.ones(out_ref.shape, BF)
    out_ref[:, :wide] = made[:, :wide]
    out_ref[:, 2 * BLK : 2 * BLK + wide] = made[:, wide:]


def middle_kernel(
    wide, core_ref, tok_ref, a_ref, own_ref, mate_ref, gain_ref, w_ref, h_ref, n_ref, cq_ref
):
    w = core_ref[0]
    h = in_blocks(tok_ref).astype(F32)
    h = h + (dot(a_ref[w], own_ref[...]) + dot(a_ref[1 - w], mate_ref[...]))
    h_ref[...] = h
    n = (h * scale_of(h) * gain_ref[...]).astype(BF)
    n_ref[...] = n
    cut = w_ref.shape[1]
    cols = slice(5 * wide, 6 * wide)
    made = dot(n[:, :cut], w_ref[0, :, cols]) + dot(n[:, cut:], w_ref[1, :, cols])
    cq_ref[...] = jnp.zeros(cq_ref.shape, BF)
    cq_ref[:, :wide] = made.astype(BF)


def third_kernel(half, w_ref, h1_ref, a_ref, own_ref, mate_ref, gain_ref, h_ref, n_ref):
    w = w_ref[0]
    h = own_of(h1_ref, w, half)
    for m, ref in ((w, own_ref), (1 - w, mate_ref)):
        h = h + dot(own_of(a_ref.at[m], w, half), ref[...])
    h_ref[...] = h
    put(n_ref, (h * scale_of(h) * gain_ref[...]).astype(BF))


def heads_kernel(wide, *refs):
    *weights, out_ref = refs
    last = out_ref.shape[2] - len(weights) * wide
    for m in range(out_ref.shape[0] if last else 0):
        out_ref[m, :, len(weights) * wide :] = jnp.zeros((out_ref.shape[1], last), BF)
    for i, ref in enumerate(weights):
        for m in range(out_ref.shape[0]):
            out_ref[m, :, i * wide : (i + 1) * wide] = ref[:, m * wide : (m + 1) * wide]


def units_kernel(nz, step, share, slot, spot_ref, gate_ref, up_ref, down_ref, *outs):
    def move(ref, out, first, at):
        base = pl.multiple_of(jnp.minimum(first // BLK * BLK, ref.shape[1] - 2 * BLK), BLK)
        window = ref[:, pl.ds(base, 2 * BLK)].astype(F32)
        window = pltpu.roll(window, 2 * BLK - (first - base), 1)[:, :BLK]
        window = jnp.where(lane_of(window.shape) < share, window, 0.0)
        out[:, at : at + slot] = window.astype(BF)[:, :slot]

    for m in range(2):
        ug_ref, wd_ref = outs[m], outs[2 + m]
        for z in range(nz):
            first = (z * step + spot_ref[m]) * share
            move(gate_ref, ug_ref, first, z * slot)
            move(up_ref, ug_ref, first, (nz + z) * slot)
        for z in range(wd_ref.shape[1] // slot):
            move(down_ref, wd_ref, (z * step + spot_ref[m]) * share, z * slot)


def in_order(w, own_ref, mate_ref, axis):
    own, other = own_ref[...], mate_ref[...]
    return jnp.concatenate(
        [jnp.where(w == 0, own, other), jnp.where(w == 0, other, own)], axis=axis
    )


def order_kernel(core_ref, own_ref, mate_ref, down_ref, down_mate_ref, ug_ref, wd_ref):
    ug_ref[...] = in_order(core_ref[0], own_ref, mate_ref, 0)
    wd_ref[...] = in_order(core_ref[0], down_ref, down_mate_ref, 1)


def ffn_early_kernel(g0_ref, g1_ref, wd_ref, out_ref):
    width = wd_ref.shape[0]
    rows = g0_ref.shape[0]
    for i, ref in enumerate((g0_ref, g1_ref)):
        out_ref[i * rows : (i + 1) * rows, :] = dot(ref[:, :width], wd_ref[...])


def ffn_kernel(n0_ref, n1_ref, da_ref, ug_ref, act_ref, dgu_ref, d0_ref, d1_ref):
    own = pl.program_id(0) < pl.num_programs(0) // 2
    units = act_ref.shape[1]
    width = ug_ref.shape[0]
    n = jnp.where(own, n0_ref[:, :width], n1_ref[:, :width])
    gate = dot(n, ug_ref[:, :units])
    up = dot(n, ug_ref[:, units:])
    da = da_ref[...]
    scale = 0.7978845608028654
    inner = jnp.tanh(scale * (gate + 0.044715 * gate * gate * gate))
    gelu = 0.5 * gate * (1.0 + inner)
    slope = 0.5 * (1.0 + inner) + 0.5 * gate * (1.0 - inner * inner) * scale * (
        1.0 + 3.0 * 0.044715 * gate * gate
    )
    act_ref[...] = (gelu * up).astype(BF)
    dg = (da * up * slope).astype(BF)
    du = (da * gelu).astype(BF)
    dgu_ref[:, :units] = dg
    dgu_ref[:, units:] = du
    dn = (dot_nt(dg, ug_ref[:, :units]) + dot_nt(du, ug_ref[:, units:])).astype(BF)

    @pl.when(own)
    def _():
        put(d0_ref, dn)

    @pl.when(jnp.logical_not(own))
    def _():
        put(d1_ref, dn)


def half_specs(tiles, cols):
    tile = 4 * BLK
    return [
        pl.BlockSpec((tile, cols), lambda i: (jnp.minimum(i, tiles // 2 - 1), 0)),
        pl.BlockSpec((tile, cols), lambda i: (jnp.maximum(i - tiles // 2, 0), 0)),
    ]


def ffn_both(n, da, ug):
    rows, padded = 2 * n[0].shape[0], n[0].shape[1]
    width, units = ug.shape[0], ug.shape[1] // 2
    tiles = rows // (4 * BLK)

    def row(cols):
        return pl.BlockSpec((4 * BLK, cols), lambda i: (i, 0))

    halved = half_specs(tiles, padded)
    return pl.pallas_call(
        ffn_kernel,
        grid=(tiles,),
        in_specs=halved + [row(units), pl.BlockSpec(ug.shape, lambda i: (0, 0))],
        out_specs=[row(units), row(2 * units)] + halved,
        out_shape=[bf_shape(rows, units), bf_shape(rows, 2 * units)]
        + [bf_shape(rows // 2, padded)] * 2,
        **params(10 * rows * width * units, 12e6, rows * units),
    )(*n, da, ug)


def ffn_late_kernel(nz, share, late, n0_ref, n1_ref, g0_ref, g1_ref, act_ref, dgu_ref, wd_ref, *rest):
    w_ref, o0_ref, o1_ref, acc_ref = rest[late:]
    i = pl.program_id(0)
    own = i < pl.num_programs(0) // 2
    units = act_ref.shape[1]
    @pl.when(i == 0)
    def _():
        acc_ref[...] = jnp.zeros_like(acc_ref)

    n = jnp.where(own, n0_ref[...], n1_ref[...])
    g = jnp.where(own, g0_ref[...], g1_ref[...])
    acc_ref[: 2 * units, :] += dot_tn(dgu_ref[...], n)
    acc_ref[2 * units :, :] += dot_tn(act_ref[...], g)
    made = dot_nt(act_ref[...], wd_ref[...]).astype(BF)

    @pl.when(own)
    def _():
        put(o0_ref, made)

    @pl.when(jnp.logical_not(own))
    def _():
        put(o1_ref, made)

    @pl.when(i == pl.num_programs(0) - 1)
    def _():
        for z in range(nz):
            for j in range(3):
                first = j * units + z * (units // nz)
                w_ref[z, j] = acc_ref[first : first + share, :].astype(BF)


def ffn_late(n, g, act, dgu, wd, nz, share, deps):
    rows, padded = act.shape[0], n[0].shape[1]
    width, units = wd.shape
    tiles = rows // (4 * BLK)

    def row(cols):
        return pl.BlockSpec((4 * BLK, cols), lambda i: (i, 0))

    halved = half_specs(tiles, padded)
    return pl.pallas_call(
        functools.partial(ffn_late_kernel, nz, share, len(deps)),
        grid=(tiles,),
        in_specs=halved
        + halved
        + [row(units), row(2 * units), pl.BlockSpec(wd.shape, lambda i: (0, 0))]
        + [ANY] * len(deps),
        out_specs=[pl.BlockSpec((nz, 3, share, padded), lambda i: (0, 0, 0, 0))] + halved,
        out_shape=[bf_shape(nz, 3, share, padded)] + [bf_shape(rows // 2, padded)] * 2,
        scratch_shapes=[pltpu.VMEM((3 * units, padded), F32)],
        **params(8 * rows * width * units, 20e6, 0),
    )(*n, *g, act, dgu, wd, *deps)


def add_kernel(a_ref, b_ref, *outs):
    rows = outs[0].shape[0]
    for k, out in enumerate(outs):
        at = slice(k * rows, (k + 1) * rows)
        out[...] = (a_ref[at].astype(F32) + b_ref[at].astype(F32)).astype(BF)


def output_kernel(*refs):
    *parts, out_ref = refs
    width = out_ref.shape[1]
    total = parts[0][:, :width].astype(F32)
    for part in parts[1:]:
        total = total + part[:, :width].astype(F32)
    out_ref[...] = total.astype(out_ref.dtype)


def join_kernel(*refs):
    *parts, out_ref = refs
    rows = parts[0].shape[0]
    for i, part in enumerate(parts):
        out_ref[i * rows : (i + 1) * rows, :] = part[...]


def spread_kernel(*refs):
    *parts, out_ref = refs
    rows = parts[0].shape[0]
    for i in range(out_ref.shape[0]):
        for j, part in enumerate(parts):
            out_ref[i, j * rows : (j + 1) * rows, :] = part[...]


def split_rows(value):
    parts = []
    for _ in range(3):
        part = value.astype(BF).astype(F32)
        value = value - part
        parts.append(part)
    return jnp.concatenate(parts, axis=0)


def owners_kernel(wide, plan, target_ref, *refs):
    sets = 1 + max(s for group in plan for s, _ in group)
    xs, ys, out_ref = refs[:sets], refs[sets : sets + len(plan)], refs[-1]
    rows = target_ref.shape[0] // out_ref.shape[0]
    extra = refs[-2] if len(refs) > sets + len(plan) + 1 else None
    count = target_ref.shape[0]
    total = jnp.zeros((count, ys[0].shape[1]), F32)
    column = 0
    for group, y in zip(plan, ys):
        picked = jnp.zeros((count, y.shape[0]), F32)
        for which, first in group:
            x = xs[which]
            lane = lane_of((count, x.shape[2]))
            inside = (lane >= first) & (lane < first + wide)
            for m in range(2):
                hit = inside & (lane - first + m * wide == target_ref[:, column : column + 1])
                picked = picked + dot_nt(hit.astype(BF), x[m])
            column += 1
        total = total + dot(picked.astype(BF), y[...])
    for k in range(out_ref.shape[0]):
        part = total[k * rows : (k + 1) * rows].astype(BF)
        if extra is None:
            put(out_ref.at[k], part)
        else:
            out_ref[k] = jnp.zeros(out_ref.shape[1:], BF)
            out_ref[k, :rows, : part.shape[1]] = part
            out_ref[k, rows : rows + 3 * extra.shape[0], :] = split_rows(extra[...]).astype(BF)


def layers_kernel(nz, zed_ref, x_ref, *outs):
    total = jnp.sum(x_ref[...].astype(F32), axis=0)
    rows = total.shape[0] // nz
    for k, out in enumerate(outs):
        want = zed_ref[0] ^ k
        value = total[:rows]
        for z in range(1, nz):
            value = jnp.where(want == z, total[z * rows : (z + 1) * rows], value)
        out[...] = value.astype(BF)


def deal_last_kernel(rows, extra, x_ref, out_ref):
    total = jnp.sum(x_ref[...].astype(F32), axis=0)
    each = rows // out_ref.shape[0]
    small = total[rows : rows + extra]
    for i in range(1, 3):
        small = small + total[rows + i * extra : rows + (i + 1) * extra]
    small = split_rows(small).astype(BF)
    for i in range(out_ref.shape[0]):
        out_ref[i] = jnp.zeros(out_ref.shape[1:], BF)
        out_ref[i, :each, :] = total[i * each : (i + 1) * each].astype(BF)
        out_ref[i, each : each + 3 * extra, :] = small


def deal_kernel(*refs):
    *parts, out_ref = refs
    at = 0
    for part in parts:
        total = jnp.sum(part[...].astype(F32), axis=0)
        rows = total.shape[0] // out_ref.shape[0]
        for i in range(out_ref.shape[0]):
            out_ref[i, at : at + rows, :] = total[i * rows : (i + 1) * rows].astype(BF)
        at += rows


def dh2_kernel(*refs):
    *parts, h_ref, cot_ref, gain_ref, dh_ref, dy_ref, gain_out = refs
    width = h_ref.shape[1]
    grad = parts[0][:, :width].astype(F32)
    for part in parts[1:]:
        grad = grad + part[:, :width].astype(F32)
    dv, gain_out[...] = norm_back(h_ref[...], gain_ref[...], grad)
    dh = cot_ref[:, :width].astype(F32) + dv
    dh_ref[...] = dh
    put(dy_ref, dh.astype(BF))


def dh1_kernel(wide, half, w_ref, dq_ref, cq_ref, h1_ref, dh2_ref, gain_ref, dh_ref, dy_ref, gain_out):
    w = w_ref[0]
    dq = jnp.concatenate([own_of(dq_ref.at[m], w, half)[:, :wide] for m in range(2)], axis=1)
    grad = dot_nt(dq, cq_ref[...])
    dv, gain_out[...] = norm_back(own_of(h1_ref, w, half), gain_ref[...], grad)
    dh = dh2_ref[...] + dv
    dh_ref[...] = dh
    put(dy_ref, dh.astype(BF))


def last_kernel(wide, half, w_ref, d_ref, weight_ref, tok_ref, dh1_ref, gain_ref, out_ref, gain_out):
    w = w_ref[0]
    d = jnp.concatenate(
        [own_of(d_ref.at[m, i], w, half)[:, :wide] for i in range(3) for m in range(2)], axis=1
    )
    grad = dot_nt(d, weight_ref[...])
    dv, gain_out[...] = norm_back(tok_ref[w].astype(F32), gain_ref[...], grad)
    out_ref[...] = dh1_ref[...] + dv


def grad_prep_kernel(nh, hs, dy_ref, w_ref, o_ref, out_ref, de_ref, dh_ref, del_ref):
    wide = nh * hs
    dy = in_blocks(dy_ref)[:, : w_ref.shape[1]]
    out_ref[...] = dy
    da = dot_nt(dy, w_ref[...]).astype(BF)
    da = jnp.concatenate([da, jnp.zeros((da.shape[0], 2 * BLK - wide), BF)], axis=1)
    terms = da.astype(F32) * o_ref[...]
    delta = [jnp.sum(head_mask(terms, h, hs), axis=1, keepdims=True) for h in range(nh)]
    dh_ref[...] = pltpu.roll(da.astype(F32), hs, 1).astype(BF)
    lane = lane_of(del_ref.shape)
    cols = jnp.zeros(del_ref.shape, F32)
    for h in range(nh):
        cols = jnp.where(lane == h, delta[h], cols)
    del_ref[...] = cols
    de = pieces_into(da.astype(F32), [-t for t in delta], wide).astype(BF)
    for i in range(de_ref.shape[0]):
        de_ref[i] = de


def grad_prep(dy, weight, o, nh, hs, copies=1, deps=()):
    rows, width = o.shape[0], weight.shape[1]
    return plain(
        functools.partial(grad_prep_kernel, nh, hs),
        [],
        [dy, weight, o],
        [
            bf_shape(rows, width),
            bf_shape(copies, rows, 2 * BLK),
            bf_shape(rows, 2 * BLK),
            f32_shape(rows, BLK),
        ],
        deps=deps,
    )


def local(
    tokens,
    encoded,
    cotangent,
    assign,
    bucket_ids,
    gain_self,
    gain_cross,
    gain_ffn,
    query_weight,
    key_weight,
    value_weight,
    out_weight,
    cross_query,
    cross_key,
    cross_value,
    cross_out,
    gate_weight,
    up_weight,
    down_weight,
    bucket_table,
):
    nctx = lax.axis_size("ctx")
    nw = lax.axis_size("wsh")
    c = lax.axis_index("ctx")
    w = lax.axis_index("wsh")
    both = ("ctx", "wsh")
    rows, width = tokens.shape
    half = rows // 2
    length = rows * nw * nctx
    buckets, heads = bucket_table.shape
    inner = query_weight.shape[1]
    hs = inner // heads
    nh = heads // nw
    wide = nh * hs
    plane = 4
    nz = nctx // plane
    spot = (c % plane) * nw + w
    zed = c // plane
    hidden = gate_weight.shape[1]
    share = hidden // (nctx * nw)
    slot = -(-share // 32) * 32

    def pair(x, axis=0, tiled=True):
        return lax.all_gather(x, "wsh", axis=axis, tiled=tiled)

    def halves(parts):
        return lax.all_to_all(parts, "wsh", 0, 0, tiled=True)

    def mate(x):
        return lax.ppermute(x, "wsh", [(i, (i + 1) % nw) for i in range(nw)])

    planes = [[z * plane + i for i in range(plane)] for z in range(nz)]
    columns = [[z * plane + i for z in range(nz)] for i in range(plane)]

    def in_plane(x):
        return lax.all_to_all(x, "ctx", 0, 0, tiled=True, axis_index_groups=planes)

    def in_column(x):
        return lax.all_to_all(x, "ctx", 0, 0, tiled=True, axis_index_groups=columns)

    padded = -(-width // BLK) * BLK

    def spread(parts, count, deps=()):
        shape = bf_shape(count, len(parts) * parts[0].shape[0], parts[0].shape[1])
        return plain(spread_kernel, [], parts, [shape], (0, 1e6, 0), deps)[0]

    def add(a, b, deps=()):
        return plain(add_kernel, [], [a, b], [bf_shape(rows, padded)] * plane, (0, 1e6, 0), deps)

    def deal(parts, count, deps=()):
        shape = bf_shape(count, sum(x.shape[1] for x in parts) // count, parts[0].shape[2])
        return plain(deal_kernel, [], parts, [shape], (0, 1e6, 0), deps)[0]

    def tree(parts):
        while len(parts) > 1:
            parts = [parts[i] + parts[i + 1] for i in range(0, len(parts), 2)]
        return parts[0]

    def near(x, k):
        return lax.ppermute(x, "ctx", [(i, i ^ k) for i in range(nctx)])

    def stacked(parts, deps=()):
        shape = bf_shape(len(parts) * parts[0].shape[0], parts[0].shape[1])
        return plain(join_kernel, [], parts, [shape], (0, 1e6, 0), deps)[0]

    cut = inner // (nctx * nw)

    def targets(count):
        index = jnp.arange(plane * nz * count * cut, dtype=jnp.int32)
        to_k, to_z = index // (nz * count * cut), index // (count * cut) % nz
        to_i, to_t = index // cut % count, index % cut
        column = ((to_z * plane + to_k) * nw + w) * cut + to_t
        which = jnp.arange(count, dtype=jnp.int32)
        return jnp.where(to_i[:, None] == which[None, :], column[:, None], -1).astype(jnp.int32)

    def owner_parts(plan, xs, ys, small=None, deps=()):
        count = sum(len(group) for group in plan)
        total = nz * count * cut
        if small is not None:
            total = -(-(total + 3 * small.shape[0]) // 16) * 16
            ys = ys + [small]
        return plain(
            functools.partial(owners_kernel, wide, plan),
            [],
            [targets(count)] + xs + ys,
            [bf_shape(plane, total, padded)],
            (3e9, 6e6, 0),
            deps,
        )[0]

    def layers(x, deps=()):
        return plain(
            functools.partial(layers_kernel, nz),
            [zed.astype(jnp.int32)[None]],
            [x],
            [bf_shape(x.shape[1] // nz, x.shape[2])] * nz,
            (0, 1e6, 0),
            deps,
        )

    def owner_sums(total, count):
        return [total[i * cut : (i + 1) * cut, :width] for i in range(count)]

    lanes = jnp.arange(nctx, dtype=jnp.int32)
    owner = jnp.sum(jnp.where(assign[None, :] == lanes[:, None], lanes[None, :], 0), axis=1)
    chip_slot = owner % plane * nz + (owner // plane ^ zed)
    near_slot = (owner ^ c) % plane * nz + owner // plane
    meta = jnp.concatenate([owner, jnp.take(assign, c)[None], chip_slot, near_slot])
    meta = meta.astype(jnp.int32)
    core = w.astype(jnp.int32)[None]
    chip = nw * rows

    gains = pair(jnp.stack([gain_self, gain_cross, gain_ffn]), axis=1).astype(F32)
    gains = [gains[i : i + 1] for i in range(3)]
    tok = pair(tokens, tiled=False)

    def head_parts(weights, deps=()):
        count = len(weights) * wide
        shape = bf_shape(nw, weights[0].shape[0], -(-count // BLK) * BLK)
        return plain(functools.partial(heads_kernel, wide), [], weights, [shape], deps=deps)[0]

    g_own = jnp.pad(cotangent, ((0, 0), (0, padded - width)))
    g_parts = [g_own] + [near(g_own, k) for k in range(1, plane)]
    all_heads = halves(
        head_parts(
            [key_weight, value_weight, cross_key, cross_value, query_weight, cross_query]
        )
    )
    n1, q, k_own, v_own, kv_own = plain(
        functools.partial(project_kernel, wide),
        [],
        [tok, all_heads, gains[0]],
        [bf_shape(chip, width)] + [bf_shape(chip, 2 * BLK)] * 3 + [bf_shape(nz, chip, 2 * wide)],
    )

    kv = in_column(kv_own).reshape(-1, 2 * wide)

    hot = (bucket_ids[None, :] == jnp.arange(buckets, dtype=jnp.int32)[:, None]).astype(BF)
    values = dot_tn(lax.dynamic_slice_in_dim(bucket_table, w * nh, nh, 1), hot)
    lines = bias_rows(values)

    enc_pair = pair(encoded)
    (ekv_own,) = plain(
        functools.partial(encode_kernel, wide),
        [],
        [enc_pair, all_heads],
        [bf_shape(enc_pair.shape[0], 4 * BLK)],
        deps=(kv, *g_parts[1:], *lines),
    )

    kv = [kv] + [near(kv, k) for k in range(1, plane)]

    ts, tt = bias_tiles(*lines, deps=(kv[0], ekv_own))

    ekv = lax.all_gather(ekv_own, "ctx", axis=0, tiled=True)
    spots = jnp.stack([(c % plane) * nw + i for i in (w, 1 - w)]).astype(jnp.int32)
    ug_own, ug_sent, wd_own, wd_sent = plain(
        functools.partial(units_kernel, nz, plane * nw, share, slot),
        [spots],
        [gate_weight, up_weight, down_weight.T],
        [bf_shape(gate_weight.shape[0], 2 * nz * slot)] * 2
        + [bf_shape(width, nz // nw * slot)] * 2,
        deps=(ts,),
    )
    g_plane = stacked(g_parts, deps=(ug_own,))
    out_mate, cross_out_mate = mate(out_weight), mate(cross_out)
    o1, a1, qe1, lse1 = self_fwd(
        meta, q, kv, ts, nh, hs, deps=(g_plane, out_mate, cross_out_mate)
    )
    a1_pair = pair(a1, tiled=False)
    h1, n2, cq = plain(
        functools.partial(middle_kernel, wide),
        [core],
        [tok, a1_pair, out_weight, out_mate, gains[1], all_heads],
        [f32_shape(chip, width), bf_shape(chip, width), bf_shape(chip, 2 * BLK)],
    )
    qg = lax.all_gather(qe1, "ctx", axis=0, tiled=True).reshape(nctx, chip, 2 * BLK)
    cq_full, ck_full, cv_full = pair(cross_query), pair(cross_key), pair(cross_value)
    qkv_full = pair(jnp.concatenate([query_weight, key_weight, value_weight], axis=1))

    o2, a2, qe2 = cross_fwd(cq, ekv, nh, hs)
    a2_pair = pair(a2, tiled=False)
    h2, n3 = plain(
        functools.partial(third_kernel, half),
        [core],
        [h1, a2_pair, cross_out, cross_out_mate, gains[2]],
        [f32_shape(rows, width), bf_shape(rows, padded)],
    )

    ug_sent, wd_sent, g_plane, _ = lax.optimization_barrier((ug_sent, wd_sent, g_plane, a2_pair))
    g_plane = g_plane, mate(g_plane)
    ug, wd = plain(
        order_kernel,
        [core],
        [ug_own, mate(ug_sent), wd_own, mate(wd_sent)],
        [bf_shape(width, 2 * nz * slot), bf_shape(width, nz * slot)],
        deps=(n3,),
    )
    (dact,) = plain(
        ffn_early_kernel, [], [*g_plane, wd], [f32_shape(nw * plane * rows, nz * slot)], deps=(n3,)
    )
    n3_plane = stacked([n3] + [near(n3, k) for k in range(1, plane)], deps=(dact,))
    n3_plane = n3_plane, mate(n3_plane)
    act, dgu, dn0, dn1 = ffn_both(n3_plane, dact, ug)
    sent = add(dn0, mate(dn1))
    got = [near(sent[k], k) for k in range(1, plane)]
    ffn, out0, out1 = ffn_late(n3_plane, g_plane, act, dgu, wd, nz, share, (sent[0], qg))
    dh2, dy2, gain3 = plain(
        dh2_kernel,
        [],
        [sent[0]] + got + [h2, g_own, gains[2]],
        [f32_shape(rows, width), bf_shape(rows, padded), f32_shape(1, width)],
        deps=(out0,),
    )

    dy2, de2, _, _ = grad_prep(pair(dy2, tiled=False), cross_out, o2, nh, hs)
    dcq, dekv = cross_bwd(qe2, de2[0], ekv, plane, nz, nh, hs)
    dekv = in_plane(dekv.reshape(plane, -1, 2 * wide))
    dcq_pair = pair(dcq, tiled=False)
    dh1, dy1, gain2 = plain(
        functools.partial(dh1_kernel, wide, half),
        [core],
        [dcq_pair, cq_full, h1, dh2, gains[1]],
        [f32_shape(rows, width), bf_shape(rows, padded), f32_shape(1, width)],
    )

    dy1, de1, dhi1, delta1 = grad_prep(pair(dy1, tiled=False), out_weight, o1, nh, hs)
    dg = [de1[0]] + [near(de1[0], plane * k) for k in range(1, nz)]
    dekv = layers(dekv, deps=(de1,))
    dg = spread(dg, plane, deps=(dekv[0], qg, ck_full, cv_full, qkv_full))
    spread_out = dg
    dekv = [dekv[0]] + [near(dekv[k], plane * k) for k in range(1, nz)]

    dq, rev = self_dq(meta, q, dhi1, lse1, delta1, kv, ts, nh, hs, deps=(dg,))
    dg = in_plane(dg).reshape(nctx, chip, 2 * BLK)
    (dekv,) = plain(output_kernel, [], dekv, [bf_shape(*dekv[0].shape)], deps=(dq,))
    dekv_pair = pair(dekv, tiled=False)
    made = owner_parts(
        (((0, 0),), ((1, 0),), ((2, 0),), ((3, 0), (3, wide))),
        [a1_pair, a2_pair, dcq_pair, dekv_pair],
        [dy1, dy2, n2, enc_pair],
        deps=(dq,),
    )
    ffn = lax.psum_scatter(
        tie(ffn, spread_out).reshape(nz, 3 * share, padded),
        "ctx",
        scatter_dimension=0,
        axis_index_groups=columns,
        tiled=True,
    )
    dqkv = self_dkv(meta, k_own, v_own, qg, dg, tt, dq, nh, hs, deps=(made,))
    made = in_plane(made)
    rev = tie(rev, dqkv)

    dqkv_pair = pair(dqkv, tiled=False).reshape(nw, 3, chip, 2 * BLK)
    dqkv = [dqkv_pair[:, i] for i in range(3)]
    tokens_grad, gain1 = plain(
        functools.partial(last_kernel, wide, half),
        [core],
        [dqkv_pair, qkv_full, tok, dh1, gains[0]],
        [f32_shape(rows, width), f32_shape(1, width)],
    )

    rev = rev.reshape(nh, 8, -1)
    by_distance = sum(rev[:, i, 1 + i : 1 + i + length] for i in range(8))
    hot_rev = (
        jnp.flip(bucket_ids)[None, :] == jnp.arange(buckets, dtype=jnp.int32)[:, None]
    ).astype(F32)
    table_own = lax.dot_general(
        hot_rev, by_distance, (((1,), (1,)), ((), ())), precision=lax.Precision.HIGHEST
    )
    table = lax.dynamic_update_slice_in_dim(
        jnp.zeros((buckets, heads), F32), table_own, w * nh, 1
    )

    small = jnp.concatenate([gain1[0], gain2[0], gain3[0], table.reshape(-1)])
    small = jnp.pad(small, (0, -small.shape[0] % padded)).reshape(-1, padded)
    extra = small.shape[0]
    second = owner_parts((((0, 0), (1, 0), (2, 0)),), dqkv, [n1], small)
    second = in_plane(tie(second, made))
    first = layers(made)
    out_sent = add(out0, mate(tie(out1, gain1)), deps=(made,))
    first = [first[0]] + [near(first[k], plane * k) for k in range(1, nz)]
    (second,) = plain(
        functools.partial(deal_last_kernel, 3 * nz * cut, extra),
        [],
        [second],
        [bf_shape(nz, -(-(3 * cut + 3 * extra) // 16) * 16, padded)],
        deps=(first[0], out_sent[0]),
    )
    dealt = second
    out_sent = [tie(m, second) for m in out_sent[1:]], out_sent[0]
    out_got = [near(m, k + 1) for k, m in enumerate(out_sent[0])]
    (output,) = plain(output_kernel, [], [h2, out_sent[1]] + out_got, [bf_shape(rows, width)])
    dekv_pair = tie(dekv_pair, second)
    second = jnp.sum(in_column(second).astype(F32), axis=0)
    small = [second[3 * cut + i * extra : 3 * cut + (i + 1) * extra] for i in range(3)]
    small = (small[0] + small[1]) + small[2]
    small = small + mate(small)
    q_t, k_t, v_t = owner_sums(second, 3)
    (first,) = plain(output_kernel, [], first, [f32_shape(5 * cut, padded)], deps=(dealt,))
    out_share, cross_out_share, cq_t, ck_t, cv_t = owner_sums(first, 5)
    ffn = ffn[0, :, :width].astype(F32).reshape(3, share, width)

    def joined(x):
        return jnp.swapaxes(x[:, :, :wide], 0, 1).reshape(-1, inner)

    def own_encoder(x):
        return lax.dynamic_slice_in_dim(x, w * encoded.shape[0], encoded.shape[0], 0)

    dek, dev = joined(dekv_pair), joined(dekv_pair[:, :, wide:])
    encoded_grad = dot_nt(own_encoder(dek), ck_full) + dot_nt(own_encoder(dev), cv_full)

    small = small.reshape(-1)
    table = small[3 * width : 3 * width + buckets * heads].reshape(buckets, heads)
    return (
        output,
        tokens_grad,
        encoded_grad,
        small[:width],
        small[width : 2 * width],
        small[2 * width : 3 * width],
        q_t.T,
        k_t.T,
        v_t.T,
        out_share,
        cq_t.T,
        ck_t.T,
        cv_t.T,
        cross_out_share,
        ffn[0].T,
        ffn[1].T,
        ffn[2],
        table,
    )


def solution(mesh):
    rows = P(("seq", "ctx", "wsh"), None)
    cols = P("seq", ("ctx", "wsh"))
    split = P("wsh", None)
    return jax.shard_map(
        local,
        mesh=mesh,
        in_specs=(rows, rows, rows, P(), P(), P("wsh"), P("wsh"), P("wsh"))
        + (split,) * 11
        + (P(),),
        out_specs=(
            rows,
            rows,
            rows,
            P("seq"),
            P("seq"),
            P("seq"),
            cols,
            cols,
            cols,
            rows,
            cols,
            cols,
            cols,
            rows,
            cols,
            cols,
            rows,
            P("seq", None),
        ),
        check_vma=False,
    )
```

```python
import functools

import jax
import jax.numpy as jnp
from jax import lax
from jax.experimental import pallas as pl
from jax.experimental.pallas import tpu as pltpu
from jax.sharding import PartitionSpec as P

EPS = 1e-06
NEG = -1e30
F32 = jnp.float32
BF = jnp.bfloat16
BLK = 128
GRP = 4
UNROLL = 3
CH = BLK * GRP
VLIM = 60 * 1024 * 1024
SLOW = 64


def dot(a, b):
    return lax.dot_general(a, b, (((1,), (0,)), ((), ())), preferred_element_type=F32)


def dot_nt(a, b):
    return lax.dot_general(a, b, (((1,), (1,)), ((), ())), preferred_element_type=F32)


def dot_tn(a, b):
    return lax.dot_general(a, b, (((0,), (0,)), ((), ())), preferred_element_type=F32)


def lane_of(shape):
    return lax.broadcasted_iota(jnp.int32, shape, 1)


def head_mask(value, head, hs):
    lane = lane_of(value.shape)
    keep = (lane >= head * hs) & (lane < (head + 1) * hs)
    return jnp.where(keep, value, jnp.zeros_like(value))


def lane_fold(value, op):
    out = value[:, :BLK]
    for i in range(1, value.shape[1] // BLK):
        out = op(out, value[:, i * BLK : (i + 1) * BLK])
    return out


def pieces_into(base, columns, first):
    lane = lane_of(base.shape)
    out = base
    for i, column in enumerate(columns):
        rest = column
        for j in range(3):
            part = rest.astype(BF).astype(F32)
            rest = rest - part
            out = jnp.where(lane == first + 3 * i + j, part, out)
    return out


def params(flops, nbytes, trans):
    return dict(
        compiler_params=pltpu.CompilerParams(vmem_limit_bytes=VLIM),
        cost_estimate=pl.CostEstimate(
            flops=int(flops) // SLOW,
            bytes_accessed=int(nbytes) // SLOW,
            transcendentals=int(trans) // SLOW,
        ),
    )


def after(value, *deps):
    return lax.optimization_barrier((value,) + deps)[0]


def f32_shape(*dims):
    return jax.ShapeDtypeStruct(dims, F32)


def bf_shape(*dims):
    return jax.ShapeDtypeStruct(dims, BF)


def plain(kernel, scalars, inputs, outputs, cost=(1e9, 4e6, 0), deps=()):
    count, late = len(scalars) + len(inputs), len(deps)

    def body(*refs):
        kernel(*refs[:count], *refs[count + late :])

    return pl.pallas_call(
        body,
        in_specs=[SM] * len(scalars) + [VM] * len(inputs) + [ANY] * late,
        out_specs=[VM] * len(outputs),
        out_shape=list(outputs),
        **params(*cost),
    )(*scalars, *inputs, *deps)


VM = pl.BlockSpec(memory_space=pltpu.VMEM)
ANY = pl.BlockSpec(memory_space=pl.ANY)
SM = pl.BlockSpec(memory_space=pltpu.SMEM)


def tie(x, *deps):
    return pl.pallas_call(
        lambda *refs: None,
        in_specs=[ANY] * (1 + len(deps)),
        out_specs=ANY,
        out_shape=jax.ShapeDtypeStruct(x.shape, x.dtype),
        input_output_aliases={0: 0},
        **params(0, 0, 0),
    )(x, *deps)


def bias_kernel(nb, nh, nat_ref, rev_ref, ts_ref, tt_ref):
    row = lax.broadcasted_iota(jnp.int32, (BLK, BLK), 0)
    col = lax.broadcasted_iota(jnp.int32, (BLK, BLK), 1)
    upper = col >= row

    def skew(line):
        eight = pltpu.roll(jnp.broadcast_to(line, (8, BLK)), 0, 1, stride=1, stride_axis=0)
        return jnp.concatenate(
            [eight] + [pltpu.roll(eight, 8 * i, 1) for i in range(1, BLK // 8)], axis=0
        )

    def step(r, carry):
        d = nb - 1 - r
        first, second = rev_ref[nb - jnp.maximum(d, 0)], rev_ref[nb - 1 - jnp.maximum(d, 0)]
        for h in range(nh):
            tile = jnp.where(upper, skew(first[h : h + 1]), skew(second[h : h + 1]))
            ts_ref[r, h] = jnp.where(d * BLK + row - col >= 0, tile, NEG).astype(BF)
        d = r - (GRP - 1)
        first, second = nat_ref[jnp.maximum(d, 0) + 1], nat_ref[jnp.maximum(d, 0)]
        for h in range(nh):
            tile = jnp.where(upper, skew(first[h : h + 1]), skew(second[h : h + 1]))
            tt_ref[r, h] = jnp.where(d * BLK + col - row >= 0, tile, NEG).astype(BF)
        return carry

    lax.fori_loop(0, nb + GRP - 1, step, 0)


def bias_rows(values):
    nh, length = values.shape
    nb = length // BLK
    zero = jnp.zeros((nh, 1), F32)
    nat = jnp.concatenate([jnp.zeros((nh, BLK), F32), values], axis=1)
    rev = jnp.concatenate([zero, jnp.flip(values, 1), jnp.zeros((nh, BLK - 1), F32)], axis=1)
    nat = jnp.transpose(nat.reshape(nh, nb + 1, BLK), (1, 0, 2))
    rev = jnp.transpose(rev.reshape(nh, nb + 1, BLK), (1, 0, 2))
    return nat, rev


def bias_tiles(nat, rev, deps=()):
    nb, nh = nat.shape[0] - 1, nat.shape[1]
    shape = bf_shape(nb + GRP - 1, nh, BLK, BLK)
    return plain(
        functools.partial(bias_kernel, nb, nh), [], [nat, rev], [shape, shape], deps=deps
    )


def gather_blocks(ref, meta_ref, nctx, first, lo, hi, base=0):
    parts = []
    for i in range(GRP):
        t = first + i
        early = t < nctx
        slot = meta_ref[base + jnp.where(early, t, 2 * nctx - 1 - t)]
        at = pl.multiple_of(jnp.where(early, 0, BLK), BLK)
        parts.append(ref[slot, pl.ds(at, BLK), lo:hi])
    return jnp.concatenate(parts, axis=0)


def fetch(parts, held_ref, sem):
    rows = parts[0].shape[0]
    copies = [
        pltpu.make_async_copy(part, held_ref.at[pl.ds(k * rows, rows)], sem.at[k])
        for k, part in enumerate(parts)
    ]
    for copy in copies:
        copy.start()
    for copy in copies:
        copy.wait()


def bias_of(ref, first):
    rows = ref.shape[1] * BLK
    return jnp.concatenate(
        [ref[first + i].reshape(rows, BLK) for i in range(GRP)], axis=1
    ).astype(F32)


def stack_heads(value, hs, nh, shift=0):
    return jnp.concatenate([head_mask(value, h + shift, hs) for h in range(nh)], axis=0)


def merge_heads(stacked, hs, nh, shift=0):
    rows = stacked.shape[0] // nh
    total = jnp.zeros((rows, stacked.shape[1]), F32)
    for h in range(nh):
        total = total + head_mask(stacked[h * rows : (h + 1) * rows], h + shift, hs)
    return total


def pick_columns(columns, nh, rows):
    out = jnp.zeros((rows, BLK), F32)
    lane = lane_of(out.shape)
    for h in range(nh):
        out = jnp.where(lane == h, columns[h * rows : (h + 1) * rows], out)
    return out


def stack_columns(ref, rows, nh):
    return jnp.concatenate([ref[rows, h : h + 1] for h in range(nh)], axis=0)


def self_fwd_kernel(count, nctx, nh, hs, meta_ref, q_ref, ts_ref, *rest):
    o_ref, a_ref, qe_ref, lse_ref, qm_ref, s_ref, acc_ref, top_ref, sum_ref, flat_ref, sem = rest[-11:]
    fetch(rest[:count], flat_ref, sem)
    kv_ref = flat_ref.reshape(nctx, 2 * BLK, flat_ref.shape[1])
    nb = 2 * nctx
    wide = nh * hs
    early = meta_ref[nctx]
    split = early // GRP + 1
    base = 2 * nctx + 1
    for half in range(2):
        qm_ref[half] = stack_heads(q_ref[half * BLK : (half + 1) * BLK, :], hs, nh)
    top_ref[...] = jnp.full(top_ref.shape, NEG, F32)
    sum_ref[...] = jnp.zeros_like(sum_ref)
    acc_ref[...] = jnp.zeros_like(acc_ref)

    def place(step):
        half = (step >= split).astype(jnp.int32)
        return half, step - half * split

    def score(step, carry):
        half, ch = place(step)
        blk = jnp.where(half == 0, early, nb - 1 - early)
        keys = gather_blocks(kv_ref, meta_ref, nctx, ch * GRP, 0, 2 * BLK, base)
        s = dot_nt(qm_ref[half], keys) + bias_of(ts_ref, nb - 1 - blk + ch * GRP)
        s_ref[step] = s
        top_ref[half] = jnp.maximum(top_ref[half], lane_fold(s, jnp.maximum))
        return carry

    steps = nb // GRP + 1
    lax.fori_loop(0, steps, score, 0, unroll=UNROLL)
    for half in range(2):
        top = jnp.max(top_ref[half], axis=1, keepdims=True)
        top_ref[half] = jnp.broadcast_to(top, top_ref.shape[1:])

    def weigh(step, carry):
        half, ch = place(step)
        vals = gather_blocks(kv_ref, meta_ref, nctx, ch * GRP, BLK, 3 * BLK, base)
        top = top_ref[half]
        p = jnp.exp(s_ref[step] - jnp.concatenate([top] * GRP, axis=1))
        acc_ref[half] += dot(p.astype(BF), vals)
        sum_ref[half] += lane_fold(p, jnp.add)
        return carry

    lax.fori_loop(0, steps, weigh, 0, unroll=UNROLL)
    for half in range(2):
        rows = slice(half * BLK, (half + 1) * BLK)
        total = jnp.sum(sum_ref[half], axis=1, keepdims=True)
        o = pltpu.roll(merge_heads(acc_ref[half] / total, hs, nh, 1), 2 * BLK - hs, 1)
        o_ref[rows, :] = o
        a_ref[rows, :] = o[:, :wide].astype(BF)
        lse = pick_columns(top_ref[half][:, :1] + jnp.log(total), nh, BLK)
        lse_ref[rows, :] = lse
        minus = [-lse[:, h : h + 1] for h in range(nh)]
        qe_ref[rows, :] = pieces_into(q_ref[rows, :].astype(F32), minus, wide).astype(BF)


def self_fwd(meta, q, kv, ts, nh, hs, deps=()):
    nctx = len(kv) * kv[0].shape[0] // (2 * BLK)
    nb = 2 * nctx
    rows = 2 * BLK
    pairs = (nb + 1) * BLK * BLK * nh
    return pl.pallas_call(
        functools.partial(self_fwd_kernel, len(kv), nctx, nh, hs),
        in_specs=[SM, VM, VM] + [ANY] * (len(kv) + len(deps)),
        out_specs=[VM] * 4,
        out_shape=[
            f32_shape(rows, rows),
            bf_shape(rows, nh * hs),
            bf_shape(rows, rows),
            f32_shape(rows, BLK),
        ],
        scratch_shapes=[
            pltpu.VMEM((2, nh * BLK, 2 * BLK), BF),
            pltpu.VMEM((nb // GRP + 1, nh * BLK, CH), F32),
            pltpu.VMEM((2, nh * BLK, 2 * BLK), F32),
            pltpu.VMEM((2, nh * BLK, BLK), F32),
            pltpu.VMEM((2, nh * BLK, BLK), F32),
            pltpu.VMEM((nb * BLK, kv[0].shape[1]), BF),
            pltpu.SemaphoreType.DMA((len(kv),)),
        ],
        **params(pairs * 2 * 512, 10e6, pairs),
    )(meta, q, ts, *kv, *deps)


def self_dq_kernel(count, nctx, nh, hs, meta_ref, q_ref, da_ref, lse_ref, del_ref, ts_ref, *rest):
    dq_ref, rev_ref, qm_ref, dm_ref, col_ref, acc_ref, flat_ref, sem = rest[-8:]
    fetch(rest[:count], flat_ref, sem)
    kv_ref = flat_ref.reshape(nctx, 2 * BLK, flat_ref.shape[1])
    nb = 2 * nctx
    early = meta_ref[nctx]
    split = early // GRP + 1
    span = CH + BLK
    rev_ref[...] = jnp.zeros_like(rev_ref)
    acc_ref[...] = jnp.zeros_like(acc_ref)
    for half in range(2):
        rows = slice(half * BLK, (half + 1) * BLK)
        qm_ref[half] = stack_heads(q_ref[rows, :], hs, nh)
        dm_ref[half] = stack_heads(da_ref[rows, :], hs, nh, 1)
        for i, ref in enumerate((lse_ref, del_ref)):
            col_ref[half, i] = jnp.broadcast_to(stack_columns(ref, rows, nh), col_ref.shape[2:])

    def step(at, carry):
        half = (at >= split).astype(jnp.int32)
        ch = at - half * split
        blk = jnp.where(half == 0, early, nb - 1 - early)
        held = gather_blocks(kv_ref, meta_ref, nctx, ch * GRP, 0, 3 * BLK, 2 * nctx + 1)
        keys, vals = held[:, : 2 * BLK], held[:, BLK:]
        off = pl.multiple_of((ch * GRP - blk + nb - 1) * BLK, BLK)
        s = dot_nt(qm_ref[half], keys) + bias_of(ts_ref, nb - 1 - blk + ch * GRP)
        p = jnp.exp(s - jnp.concatenate([col_ref[half, 0]] * GRP, axis=1))
        delta = jnp.concatenate([col_ref[half, 1]] * GRP, axis=1)
        ds = (p * (dot_nt(dm_ref[half], vals) - delta)).astype(BF)
        acc_ref[half] += dot(ds, keys)
        flat = jnp.concatenate([jnp.zeros((nh * BLK, BLK), F32), ds.astype(F32)], axis=1)
        for h in range(nh):
            line = flat[h * BLK : h * BLK + 8]
            for i in range(1, BLK // 8):
                first = h * BLK + 8 * i
                line = line + pltpu.roll(flat[first : first + 8], span - 8 * i, 1)
            rev_ref[h * 8 : (h + 1) * 8, pl.ds(off, span)] += line
        return carry

    lax.fori_loop(0, nb // GRP + 1, step, 0, unroll=UNROLL)
    for half in range(2):
        dq_ref[half * BLK : (half + 1) * BLK, :] = merge_heads(acc_ref[half], hs, nh).astype(BF)


def self_dq(meta, q, da, lse, delta, kv, ts, nh, hs, deps=()):
    nctx = len(kv) * kv[0].shape[0] // (2 * BLK)
    nb = 2 * nctx
    pairs = (nb + 1) * BLK * BLK * nh
    return pl.pallas_call(
        functools.partial(self_dq_kernel, len(kv), nctx, nh, hs),
        in_specs=[SM] + [VM] * 5 + [ANY] * (len(kv) + len(deps)),
        out_specs=[VM, VM],
        out_shape=[
            jax.ShapeDtypeStruct((2 * BLK, 2 * BLK), BF),
            jax.ShapeDtypeStruct((8 * nh, nb * BLK + CH), F32),
        ],
        scratch_shapes=[
            pltpu.VMEM((2, nh * BLK, 2 * BLK), BF),
            pltpu.VMEM((2, nh * BLK, 2 * BLK), BF),
            pltpu.VMEM((2, 2, nh * BLK, BLK), F32),
            pltpu.VMEM((2, nh * BLK, 2 * BLK), F32),
            pltpu.VMEM((nb * BLK, kv[0].shape[1]), BF),
            pltpu.SemaphoreType.DMA((len(kv),)),
        ],
        **params(pairs * 2 * 896, 10e6, pairs),
    )(meta, q, da, lse, delta, ts, *kv, *deps)


def self_dkv_kernel(
    nctx, nh, hs, meta_ref, k_ref, v_ref, qg_ref, dg_ref, tt_ref, *rest
):
    dk_ref, dv_ref, km_ref, vm_ref, ka_ref, va_ref = rest[-6:]
    nb = 2 * nctx
    wide = nh * hs
    early = meta_ref[nctx]
    late = nb - 1 - early
    split = nb // GRP - early // GRP

    def extended(value):
        lane = lane_of(value.shape)
        parts = []
        for h in range(nh):
            first = wide + 3 * h
            ones = (lane >= first) & (lane < first + 3)
            parts.append(jnp.where(ones, jnp.ones_like(value), head_mask(value, h, hs)))
        return jnp.concatenate(parts, axis=0)

    ka_ref[...] = jnp.zeros_like(ka_ref)
    va_ref[...] = jnp.zeros_like(va_ref)
    for half in range(2):
        rows = slice(half * BLK, (half + 1) * BLK)
        km_ref[half] = extended(k_ref[rows, :])
        vm_ref[half] = extended(v_ref[rows, :])

    def step(at, carry):
        half = (at >= split).astype(jnp.int32)
        blk = jnp.where(half == 0, early, late)
        ch = at - half * split + blk // GRP
        qc = gather_blocks(qg_ref, meta_ref, nctx, ch * GRP, 0, 2 * BLK)
        dc = gather_blocks(dg_ref, meta_ref, nctx, ch * GRP, 0, 2 * BLK, nctx + 1)
        p = jnp.exp(dot_nt(km_ref[half], qc) + bias_of(tt_ref, ch * GRP - blk + GRP - 1))
        ds = (p * dot_nt(vm_ref[half], dc)).astype(BF)
        ka_ref[half] += dot(ds, qc)
        va_ref[half] += dot(p.astype(BF), dc)
        return carry

    lax.fori_loop(0, nb // GRP + 1, step, 0, unroll=UNROLL)
    for half in range(2):
        rows = slice(half * BLK, (half + 1) * BLK)
        dk_ref[rows, :] = merge_heads(ka_ref[half], hs, nh).astype(BF)
        dv_ref[rows, :] = merge_heads(va_ref[half], hs, nh).astype(BF)


def self_dkv(meta, k, v, qg, dg, tt, nh, hs, deps=()):
    nctx = qg.shape[0]
    nb = 2 * nctx
    pairs = (nb + 1) * BLK * BLK * nh
    return pl.pallas_call(
        functools.partial(self_dkv_kernel, nctx, nh, hs),
        in_specs=[SM] + [VM] * 5 + [ANY] * len(deps),
        out_specs=[VM, VM],
        out_shape=[bf_shape(2 * BLK, 2 * BLK)] * 2,
        scratch_shapes=[
            pltpu.VMEM((2, nh * BLK, 2 * BLK), BF),
            pltpu.VMEM((2, nh * BLK, 2 * BLK), BF),
            pltpu.VMEM((2, nh * BLK, 2 * BLK), F32),
            pltpu.VMEM((2, nh * BLK, 2 * BLK), F32),
        ],
        **params(pairs * 2 * 1024, 10e6, pairs),
    )(meta, k, v, qg, dg, tt, *deps)


def cross_fwd_kernel(nh, hs, q_ref, e_ref, o_ref, a_ref, qe_ref, s_ref):
    wide = nh * hs
    chunks = e_ref.shape[0] // CH
    rows = q_ref.shape[0]
    q = q_ref[...]
    qm = stack_heads(q, hs, nh)
    top = jnp.full((nh * rows, BLK), NEG, F32)
    for ch in range(chunks):
        s = dot_nt(qm, e_ref[ch * CH : (ch + 1) * CH, : 2 * BLK])
        s_ref[ch] = s
        top = jnp.maximum(top, lane_fold(s, jnp.maximum))
    top = jnp.max(top, axis=1, keepdims=True)
    total = jnp.zeros((nh * rows, BLK), F32)
    acc = jnp.zeros((nh * rows, 2 * BLK), F32)
    for ch in range(chunks):
        p = jnp.exp(s_ref[ch] - top)
        total = total + lane_fold(p, jnp.add)
        acc = acc + dot(p.astype(BF), e_ref[ch * CH : (ch + 1) * CH, 2 * BLK :])
    total = jnp.sum(total, axis=1, keepdims=True)
    o = merge_heads(acc / total, hs, nh)
    o_ref[...] = o
    a_ref[...] = o[:, :wide].astype(BF)
    lse = pick_columns(top + jnp.log(total), nh, rows)
    minus = [-lse[:, h : h + 1] for h in range(nh)]
    qe_ref[...] = pieces_into(q.astype(F32), minus, wide).astype(BF)


def cross_fwd(q, e, nh, hs):
    enc = e.shape[0]
    rows = 2 * BLK
    pairs = rows * enc * nh
    return pl.pallas_call(
        functools.partial(cross_fwd_kernel, nh, hs),
        in_specs=[VM, VM],
        out_specs=[VM] * 3,
        out_shape=[f32_shape(rows, rows), bf_shape(rows, nh * hs), bf_shape(rows, rows)],
        scratch_shapes=[pltpu.VMEM((enc // CH, nh * rows, CH), F32)],
        **params(pairs * 2 * 512, 4e6, pairs),
    )(q, e)


def cross_bwd_kernel(plane, nz, nh, hs, qe_ref, de_ref, all_ref, dq_ref, dkv_ref, e_ref, acc_ref, sem):
    size = all_ref.shape[0] // (plane * nz)
    copies = []
    for k in range(plane):
        for z in range(nz):
            source = all_ref.at[pl.ds((z * plane + k) * size, size)]
            target = e_ref.at[pl.ds((k * nz + z) * size, size)]
            copies.append(pltpu.make_async_copy(source, target, sem.at[k, z]))
    for copy in copies:
        copy.start()
    for copy in copies:
        copy.wait()
    wide = nh * hs
    acc_ref[...] = jnp.zeros_like(acc_ref)

    def kept(value, h):
        lane = lane_of(value.shape)
        first = wide + 3 * h
        keep = ((lane >= h * hs) & (lane < (h + 1) * hs)) | ((lane >= first) & (lane < first + 3))
        return jnp.where(keep, value, jnp.zeros_like(value))

    qm = [kept(qe_ref[...], h) for h in range(nh)]
    dm = [kept(de_ref[...], h) for h in range(nh)]

    for ch in range(e_ref.shape[0] // CH):
        rows = slice(ch * CH, (ch + 1) * CH)
        ek = e_ref[rows, : 2 * BLK]
        ev = e_ref[rows, 2 * BLK :]
        ek_t = jnp.transpose(ek.astype(F32)).astype(BF)
        dk = jnp.zeros((CH, 2 * BLK), F32)
        dv = jnp.zeros((CH, 2 * BLK), F32)
        for h in range(nh):
            p = jnp.exp(dot_nt(ek, qm[h]))
            ds = (p * dot_nt(ev, dm[h])).astype(BF)
            dk = dk + dot(ds, qm[h])
            dv = dv + dot(p.astype(BF), dm[h])
            acc_ref[h * hs : (h + 1) * hs, :] += dot(ek_t[h * hs : (h + 1) * hs, :], ds)
        dkv_ref[rows, :] = jnp.concatenate([dk[:, :wide], dv[:, :wide]], axis=1).astype(BF)
    dq_ref[...] = jnp.transpose(acc_ref[...]).astype(BF)


def cross_bwd(qe, de, e, plane, nz, nh, hs):
    enc = e.shape[0]
    pairs = 2 * BLK * enc * nh
    return pl.pallas_call(
        functools.partial(cross_bwd_kernel, plane, nz, nh, hs),
        in_specs=[VM, VM, ANY],
        out_specs=[VM, VM],
        out_shape=[bf_shape(2 * BLK, 2 * BLK), bf_shape(enc, 2 * nh * hs)],
        scratch_shapes=[
            pltpu.VMEM((enc, 4 * BLK), BF),
            pltpu.VMEM((2 * BLK, 2 * BLK), F32),
            pltpu.SemaphoreType.DMA((plane, nz)),
        ],
        **params(pairs * 2 * 1024, 4e6, pairs),
    )(qe, de, e)


def scale_of(rows):
    return lax.rsqrt(jnp.mean(rows * rows, axis=-1, keepdims=True) + EPS)


def norm_back(rows, gain, grad):
    rr = scale_of(rows)
    scaled = gain * grad
    shared = jnp.mean(rows * scaled, axis=-1, keepdims=True)
    dv = rr * scaled - rows * (rr * rr * rr) * shared
    return dv, jnp.sum(rows * rr * grad, axis=0, keepdims=True)


def in_blocks(pair_ref):
    half = pair_ref.shape[1] // 2
    return jnp.concatenate(
        [pair_ref[m, i * half : (i + 1) * half] for i in range(2) for m in range(2)], axis=0
    )


def put(ref, value):
    cols = value.shape[1]
    ref[:, :cols] = value
    if ref.shape[1] > cols:
        ref[:, cols:] = jnp.zeros((ref.shape[0], ref.shape[1] - cols), ref.dtype)


def own_of(ref, w, half):
    return jnp.concatenate(
        [ref[pl.ds(pl.multiple_of(i * BLK + w * half, half), half), :] for i in range(2)], axis=0
    )


def project_kernel(wide, tok_ref, w_ref, gain_ref, n1_ref, q_ref, k_ref, v_ref, kv_ref):
    x = in_blocks(tok_ref).astype(F32)
    n1 = (x * scale_of(x) * gain_ref[...]).astype(BF)
    n1_ref[...] = n1
    cut = w_ref.shape[1]

    def product(first, count):
        cols = slice(first * wide, (first + count) * wide)
        return (dot(n1[:, :cut], w_ref[0, :, cols]) + dot(n1[:, cut:], w_ref[1, :, cols])).astype(BF)

    kv = product(0, 2)
    for i in range(kv_ref.shape[0]):
        kv_ref[i] = kv
    zero = jnp.zeros((x.shape[0], 2 * BLK), BF)
    for ref, value in ((k_ref, kv[:, :wide]), (v_ref, kv[:, wide:]), (q_ref, product(4, 1))):
        ref[...] = zero
        ref[:, :wide] = value


def encode_kernel(wide, enc_ref, w_ref, out_ref):
    x = enc_ref[...]
    cut = w_ref.shape[1]
    cols = slice(2 * wide, 4 * wide)
    made = dot(x[:, :cut], w_ref[0, :, cols]) + dot(x[:, cut:], w_ref[1, :, cols])
    made = made.astype(BF)
    out_ref[...] = jnp.ones(out_ref.shape, BF)
    out_ref[:, :wide] = made[:, :wide]
    out_ref[:, 2 * BLK : 2 * BLK + wide] = made[:, wide:]


def middle_kernel(
    wide, core_ref, tok_ref, a_ref, own_ref, mate_ref, gain_ref, w_ref, h_ref, n_ref, cq_ref
):
    w = core_ref[0]
    h = in_blocks(tok_ref).astype(F32)
    h = h + (dot(a_ref[w], own_ref[...]) + dot(a_ref[1 - w], mate_ref[...]))
    h_ref[...] = h
    n = (h * scale_of(h) * gain_ref[...]).astype(BF)
    n_ref[...] = n
    cut = w_ref.shape[1]
    cols = slice(5 * wide, 6 * wide)
    made = dot(n[:, :cut], w_ref[0, :, cols]) + dot(n[:, cut:], w_ref[1, :, cols])
    cq_ref[...] = jnp.zeros(cq_ref.shape, BF)
    cq_ref[:, :wide] = made.astype(BF)


def third_kernel(half, w_ref, h1_ref, a_ref, own_ref, mate_ref, gain_ref, h_ref, n_ref):
    w = w_ref[0]
    h = own_of(h1_ref, w, half)
    for m, ref in ((w, own_ref), (1 - w, mate_ref)):
        h = h + dot(own_of(a_ref.at[m], w, half), ref[...])
    h_ref[...] = h
    put(n_ref, (h * scale_of(h) * gain_ref[...]).astype(BF))


def heads_kernel(wide, *refs):
    *weights, out_ref = refs
    last = out_ref.shape[2] - len(weights) * wide
    for m in range(out_ref.shape[0] if last else 0):
        out_ref[m, :, len(weights) * wide :] = jnp.zeros((out_ref.shape[1], last), BF)
    for i, ref in enumerate(weights):
        for m in range(out_ref.shape[0]):
            out_ref[m, :, i * wide : (i + 1) * wide] = ref[:, m * wide : (m + 1) * wide]


def units_kernel(nz, step, share, slot, spot_ref, gate_ref, up_ref, down_ref, *outs):
    def move(ref, out, first, at):
        base = pl.multiple_of(jnp.minimum(first // BLK * BLK, ref.shape[1] - 2 * BLK), BLK)
        window = ref[:, pl.ds(base, 2 * BLK)].astype(F32)
        window = pltpu.roll(window, 2 * BLK - (first - base), 1)[:, :BLK]
        window = jnp.where(lane_of(window.shape) < share, window, 0.0)
        out[:, at : at + slot] = window.astype(BF)[:, :slot]

    for m in range(2):
        ug_ref, wd_ref = outs[m], outs[2 + m]
        for z in range(nz):
            first = (z * step + spot_ref[m]) * share
            move(gate_ref, ug_ref, first, z * slot)
            move(up_ref, ug_ref, first, (nz + z) * slot)
        for z in range(wd_ref.shape[1] // slot):
            move(down_ref, wd_ref, (z * step + spot_ref[m]) * share, z * slot)


def in_order(w, own_ref, mate_ref, axis):
    own, other = own_ref[...], mate_ref[...]
    return jnp.concatenate(
        [jnp.where(w == 0, own, other), jnp.where(w == 0, other, own)], axis=axis
    )


def order_kernel(core_ref, own_ref, mate_ref, down_ref, down_mate_ref, ug_ref, wd_ref):
    ug_ref[...] = in_order(core_ref[0], own_ref, mate_ref, 0)
    wd_ref[...] = in_order(core_ref[0], down_ref, down_mate_ref, 1)


def ffn_early_kernel(g0_ref, g1_ref, wd_ref, out_ref):
    width = wd_ref.shape[0]
    rows = g0_ref.shape[0]
    for i, ref in enumerate((g0_ref, g1_ref)):
        out_ref[i * rows : (i + 1) * rows, :] = dot(ref[:, :width], wd_ref[...])


def ffn_kernel(n0_ref, n1_ref, da_ref, ug_ref, act_ref, dgu_ref, d0_ref, d1_ref):
    own = pl.program_id(0) < pl.num_programs(0) // 2
    units = act_ref.shape[1]
    width = ug_ref.shape[0]
    n = jnp.where(own, n0_ref[:, :width], n1_ref[:, :width])
    gate = dot(n, ug_ref[:, :units])
    up = dot(n, ug_ref[:, units:])
    da = da_ref[...]
    scale = 0.7978845608028654
    inner = jnp.tanh(scale * (gate + 0.044715 * gate * gate * gate))
    gelu = 0.5 * gate * (1.0 + inner)
    slope = 0.5 * (1.0 + inner) + 0.5 * gate * (1.0 - inner * inner) * scale * (
        1.0 + 3.0 * 0.044715 * gate * gate
    )
    act_ref[...] = (gelu * up).astype(BF)
    dg = (da * up * slope).astype(BF)
    du = (da * gelu).astype(BF)
    dgu_ref[:, :units] = dg
    dgu_ref[:, units:] = du
    dn = (dot_nt(dg, ug_ref[:, :units]) + dot_nt(du, ug_ref[:, units:])).astype(BF)

    @pl.when(own)
    def _():
        put(d0_ref, dn)

    @pl.when(jnp.logical_not(own))
    def _():
        put(d1_ref, dn)


def half_specs(tiles, cols):
    tile = 4 * BLK
    return [
        pl.BlockSpec((tile, cols), lambda i: (jnp.minimum(i, tiles // 2 - 1), 0)),
        pl.BlockSpec((tile, cols), lambda i: (jnp.maximum(i - tiles // 2, 0), 0)),
    ]


def ffn_both(n, da, ug):
    rows, padded = 2 * n[0].shape[0], n[0].shape[1]
    width, units = ug.shape[0], ug.shape[1] // 2
    tiles = rows // (4 * BLK)

    def row(cols):
        return pl.BlockSpec((4 * BLK, cols), lambda i: (i, 0))

    halved = half_specs(tiles, padded)
    return pl.pallas_call(
        ffn_kernel,
        grid=(tiles,),
        in_specs=halved + [row(units), pl.BlockSpec(ug.shape, lambda i: (0, 0))],
        out_specs=[row(units), row(2 * units)] + halved,
        out_shape=[bf_shape(rows, units), bf_shape(rows, 2 * units)]
        + [bf_shape(rows // 2, padded)] * 2,
        **params(10 * rows * width * units, 12e6, rows * units),
    )(*n, da, ug)


def ffn_late_kernel(nz, share, late, n0_ref, n1_ref, g0_ref, g1_ref, act_ref, dgu_ref, wd_ref, *rest):
    w_ref, o0_ref, o1_ref, acc_ref = rest[late:]
    i = pl.program_id(0)
    own = i < pl.num_programs(0) // 2
    units = act_ref.shape[1]
    @pl.when(i == 0)
    def _():
        acc_ref[...] = jnp.zeros_like(acc_ref)

    n = jnp.where(own, n0_ref[...], n1_ref[...])
    g = jnp.where(own, g0_ref[...], g1_ref[...])
    acc_ref[: 2 * units, :] += dot_tn(dgu_ref[...], n)
    acc_ref[2 * units :, :] += dot_tn(act_ref[...], g)
    made = dot_nt(act_ref[...], wd_ref[...]).astype(BF)

    @pl.when(own)
    def _():
        put(o0_ref, made)

    @pl.when(jnp.logical_not(own))
    def _():
        put(o1_ref, made)

    @pl.when(i == pl.num_programs(0) - 1)
    def _():
        for z in range(nz):
            for j in range(3):
                first = j * units + z * (units // nz)
                w_ref[z, j] = acc_ref[first : first + share, :].astype(BF)


def ffn_late(n, g, act, dgu, wd, nz, share, deps):
    rows, padded = act.shape[0], n[0].shape[1]
    width, units = wd.shape
    tiles = rows // (4 * BLK)

    def row(cols):
        return pl.BlockSpec((4 * BLK, cols), lambda i: (i, 0))

    halved = half_specs(tiles, padded)
    return pl.pallas_call(
        functools.partial(ffn_late_kernel, nz, share, len(deps)),
        grid=(tiles,),
        in_specs=halved
        + halved
        + [row(units), row(2 * units), pl.BlockSpec(wd.shape, lambda i: (0, 0))]
        + [ANY] * len(deps),
        out_specs=[pl.BlockSpec((nz, 3, share, padded), lambda i: (0, 0, 0, 0))] + halved,
        out_shape=[bf_shape(nz, 3, share, padded)] + [bf_shape(rows // 2, padded)] * 2,
        scratch_shapes=[pltpu.VMEM((3 * units, padded), F32)],
        **params(8 * rows * width * units, 20e6, 0),
    )(*n, *g, act, dgu, wd, *deps)


def add_kernel(a_ref, b_ref, *outs):
    rows = outs[0].shape[0]
    for k, out in enumerate(outs):
        at = slice(k * rows, (k + 1) * rows)
        out[...] = (a_ref[at].astype(F32) + b_ref[at].astype(F32)).astype(BF)


def output_kernel(*refs):
    *parts, out_ref = refs
    width = out_ref.shape[1]
    total = parts[0][:, :width].astype(F32)
    for part in parts[1:]:
        total = total + part[:, :width].astype(F32)
    out_ref[...] = total.astype(out_ref.dtype)


def join_kernel(*refs):
    *parts, out_ref = refs
    rows = parts[0].shape[0]
    for i, part in enumerate(parts):
        out_ref[i * rows : (i + 1) * rows, :] = part[...]


def spread_kernel(*refs):
    *parts, out_ref = refs
    rows = parts[0].shape[0]
    for i in range(out_ref.shape[0]):
        for j, part in enumerate(parts):
            out_ref[i, j * rows : (j + 1) * rows, :] = part[...]


def split_rows(value):
    parts = []
    for _ in range(3):
        part = value.astype(BF).astype(F32)
        value = value - part
        parts.append(part)
    return jnp.concatenate(parts, axis=0)


def owners_kernel(wide, plan, target_ref, *refs):
    sets = 1 + max(s[0] for group in plan for s, _ in group)
    xs, ys, out_ref = refs[:sets], refs[sets : sets + len(plan)], refs[-1]
    rows = target_ref.shape[0] // out_ref.shape[0]
    extra = refs[-2] if len(refs) > sets + len(plan) + 1 else None
    count = target_ref.shape[0]
    total = jnp.zeros((count, ys[0].shape[1]), F32)
    column = 0
    for group, y in zip(plan, ys):
        picked = jnp.zeros((count, y.shape[0]), F32)
        for which, first in group:
            x = xs[which[0]]
            lane = lane_of((count, x.shape[-1]))
            inside = (lane >= first) & (lane < first + wide)
            for m in range(2):
                hit = inside & (lane - first + m * wide == target_ref[:, column : column + 1])
                picked = picked + dot_nt(hit.astype(BF), x[(m,) + which[1:]])
            column += 1
        total = total + dot(picked.astype(BF), y[...])
    for k in range(out_ref.shape[0]):
        part = total[k * rows : (k + 1) * rows].astype(BF)
        if extra is None:
            put(out_ref.at[k], part)
        else:
            out_ref[k] = jnp.zeros(out_ref.shape[1:], BF)
            out_ref[k, :rows, : part.shape[1]] = part
            out_ref[k, rows : rows + 3 * extra.shape[0], :] = split_rows(extra[...]).astype(BF)


def layers_kernel(nz, zed_ref, *refs):
    parts, outs = refs[:-nz], refs[-nz:]
    at = 0
    for part in parts:
        total = jnp.sum(part[...].astype(F32), axis=0)
        rows = total.shape[0] // nz
        for k, out in enumerate(outs):
            want = zed_ref[0] ^ k
            value = total[:rows]
            for z in range(1, nz):
                value = jnp.where(want == z, total[z * rows : (z + 1) * rows], value)
            out[at : at + rows, :] = value.astype(BF)
        at += rows


def deal_last_kernel(rows, extra, x_ref, out_ref):
    total = jnp.sum(x_ref[...].astype(F32), axis=0)
    each = rows // out_ref.shape[0]
    small = total[rows : rows + extra]
    for i in range(1, 3):
        small = small + total[rows + i * extra : rows + (i + 1) * extra]
    small = split_rows(small).astype(BF)
    for i in range(out_ref.shape[0]):
        out_ref[i] = jnp.zeros(out_ref.shape[1:], BF)
        out_ref[i, :each, :] = total[i * each : (i + 1) * each].astype(BF)
        out_ref[i, each : each + 3 * extra, :] = small


def deal_kernel(*refs):
    *parts, out_ref = refs
    at = 0
    for part in parts:
        total = jnp.sum(part[...].astype(F32), axis=0)
        rows = total.shape[0] // out_ref.shape[0]
        for i in range(out_ref.shape[0]):
            out_ref[i, at : at + rows, :] = total[i * rows : (i + 1) * rows].astype(BF)
        at += rows


def dh2_kernel(*refs):
    *parts, h_ref, cot_ref, gain_ref, dh_ref, dy_ref, gain_out = refs
    width = h_ref.shape[1]
    grad = parts[0][:, :width].astype(F32)
    for part in parts[1:]:
        grad = grad + part[:, :width].astype(F32)
    dv, gain_out[...] = norm_back(h_ref[...], gain_ref[...], grad)
    dh = cot_ref[:, :width].astype(F32) + dv
    dh_ref[...] = dh
    put(dy_ref, dh.astype(BF))


def dh1_kernel(wide, half, w_ref, dq_ref, cq_ref, h1_ref, dh2_ref, gain_ref, dh_ref, dy_ref, gain_out):
    w = w_ref[0]
    dq = jnp.concatenate([own_of(dq_ref.at[m], w, half)[:, :wide] for m in range(2)], axis=1)
    grad = dot_nt(dq, cq_ref[...])
    dv, gain_out[...] = norm_back(own_of(h1_ref, w, half), gain_ref[...], grad)
    dh = dh2_ref[...] + dv
    dh_ref[...] = dh
    put(dy_ref, dh.astype(BF))


def last_kernel(wide, half, w_ref, d_ref, weight_ref, tok_ref, dh1_ref, gain_ref, out_ref, gain_out):
    w = w_ref[0]
    d = jnp.concatenate(
        [own_of(d_ref.at[m, i], w, half)[:, :wide] for i in range(3) for m in range(2)], axis=1
    )
    grad = dot_nt(d, weight_ref[...])
    dv, gain_out[...] = norm_back(tok_ref[w].astype(F32), gain_ref[...], grad)
    out_ref[...] = dh1_ref[...] + dv


def grad_prep_kernel(nh, hs, dy_ref, w_ref, o_ref, out_ref, de_ref, dh_ref, del_ref):
    wide = nh * hs
    dy = in_blocks(dy_ref)[:, : w_ref.shape[1]]
    out_ref[...] = dy
    da = dot_nt(dy, w_ref[...]).astype(BF)
    da = jnp.concatenate([da, jnp.zeros((da.shape[0], 2 * BLK - wide), BF)], axis=1)
    terms = da.astype(F32) * o_ref[...]
    delta = [jnp.sum(head_mask(terms, h, hs), axis=1, keepdims=True) for h in range(nh)]
    dh_ref[...] = pltpu.roll(da.astype(F32), hs, 1).astype(BF)
    lane = lane_of(del_ref.shape)
    cols = jnp.zeros(del_ref.shape, F32)
    for h in range(nh):
        cols = jnp.where(lane == h, delta[h], cols)
    del_ref[...] = cols
    de = pieces_into(da.astype(F32), [-t for t in delta], wide).astype(BF)
    for i in range(de_ref.shape[0]):
        de_ref[i] = de


def grad_prep(dy, weight, o, nh, hs, copies=1, deps=()):
    rows, width = o.shape[0], weight.shape[1]
    return plain(
        functools.partial(grad_prep_kernel, nh, hs),
        [],
        [dy, weight, o],
        [
            bf_shape(rows, width),
            bf_shape(copies, rows, 2 * BLK),
            bf_shape(rows, 2 * BLK),
            f32_shape(rows, BLK),
        ],
        deps=deps,
    )


def local(
    tokens,
    encoded,
    cotangent,
    assign,
    bucket_ids,
    gain_self,
    gain_cross,
    gain_ffn,
    query_weight,
    key_weight,
    value_weight,
    out_weight,
    cross_query,
    cross_key,
    cross_value,
    cross_out,
    gate_weight,
    up_weight,
    down_weight,
    bucket_table,
):
    nctx = lax.axis_size("ctx")
    nw = lax.axis_size("wsh")
    c = lax.axis_index("ctx")
    w = lax.axis_index("wsh")
    both = ("ctx", "wsh")
    rows, width = tokens.shape
    half = rows // 2
    length = rows * nw * nctx
    buckets, heads = bucket_table.shape
    inner = query_weight.shape[1]
    hs = inner // heads
    nh = heads // nw
    wide = nh * hs
    plane = 4
    nz = nctx // plane
    spot = (c % plane) * nw + w
    zed = c // plane
    hidden = gate_weight.shape[1]
    share = hidden // (nctx * nw)
    slot = -(-share // 32) * 32

    def pair(x, axis=0, tiled=True):
        return lax.all_gather(x, "wsh", axis=axis, tiled=tiled)

    def halves(parts):
        return lax.all_to_all(parts, "wsh", 0, 0, tiled=True)

    def mate(x):
        return lax.ppermute(x, "wsh", [(i, (i + 1) % nw) for i in range(nw)])

    planes = [[z * plane + i for i in range(plane)] for z in range(nz)]
    columns = [[z * plane + i for z in range(nz)] for i in range(plane)]

    def in_plane(x):
        return lax.all_to_all(x, "ctx", 0, 0, tiled=True, axis_index_groups=planes)

    def in_column(x):
        return lax.all_to_all(x, "ctx", 0, 0, tiled=True, axis_index_groups=columns)

    padded = -(-width // BLK) * BLK

    def spread(parts, count, deps=()):
        shape = bf_shape(count, len(parts) * parts[0].shape[0], parts[0].shape[1])
        return plain(spread_kernel, [], parts, [shape], (0, 1e6, 0), deps)[0]

    def add(a, b, deps=()):
        return plain(add_kernel, [], [a, b], [bf_shape(rows, padded)] * plane, (0, 1e6, 0), deps)

    def deal(parts, count, deps=()):
        shape = bf_shape(count, sum(x.shape[1] for x in parts) // count, parts[0].shape[2])
        return plain(deal_kernel, [], parts, [shape], (0, 1e6, 0), deps)[0]

    def tree(parts):
        while len(parts) > 1:
            parts = [parts[i] + parts[i + 1] for i in range(0, len(parts), 2)]
        return parts[0]

    def near(x, k):
        return lax.ppermute(x, "ctx", [(i, i ^ k) for i in range(nctx)])

    def stacked(parts, deps=()):
        shape = bf_shape(len(parts) * parts[0].shape[0], parts[0].shape[1])
        return plain(join_kernel, [], parts, [shape], (0, 1e6, 0), deps)[0]

    cut = inner // (nctx * nw)

    def targets(count):
        index = jnp.arange(plane * nz * count * cut, dtype=jnp.int32)
        to_k, to_z = index // (nz * count * cut), index // (count * cut) % nz
        to_i, to_t = index // cut % count, index % cut
        column = ((to_z * plane + to_k) * nw + w) * cut + to_t
        which = jnp.arange(count, dtype=jnp.int32)
        return jnp.where(to_i[:, None] == which[None, :], column[:, None], -1).astype(jnp.int32)

    def owner_parts(plan, xs, ys, small=None, deps=()):
        count = sum(len(group) for group in plan)
        total = nz * count * cut
        if small is not None:
            total = -(-(total + 3 * small.shape[0]) // 16) * 16
            ys = ys + [small]
        return plain(
            functools.partial(owners_kernel, wide, plan),
            [],
            [targets(count)] + xs + ys,
            [bf_shape(plane, total, padded)],
            (3e9, 6e6, 0),
            deps,
        )[0]

    def layers(parts, deps=()):
        return plain(
            functools.partial(layers_kernel, nz),
            [zed.astype(jnp.int32)[None]],
            parts,
            [bf_shape(sum(x.shape[1] for x in parts) // nz, parts[0].shape[2])] * nz,
            (0, 1e6, 0),
            deps,
        )

    def owner_sums(total, count):
        return [total[i * cut : (i + 1) * cut, :width] for i in range(count)]

    lanes = jnp.arange(nctx, dtype=jnp.int32)
    owner = jnp.sum(jnp.where(assign[None, :] == lanes[:, None], lanes[None, :], 0), axis=1)
    chip_slot = owner % plane * nz + (owner // plane ^ zed)
    near_slot = (owner ^ c) % plane * nz + owner // plane
    meta = jnp.concatenate([owner, jnp.take(assign, c)[None], chip_slot, near_slot])
    meta = meta.astype(jnp.int32)
    core = w.astype(jnp.int32)[None]
    chip = nw * rows

    gains = pair(jnp.stack([gain_self, gain_cross, gain_ffn]), axis=1).astype(F32)
    gains = [gains[i : i + 1] for i in range(3)]
    tok = pair(tokens, tiled=False)

    def head_parts(weights, deps=()):
        count = len(weights) * wide
        shape = bf_shape(nw, weights[0].shape[0], -(-count // BLK) * BLK)
        return plain(functools.partial(heads_kernel, wide), [], weights, [shape], deps=deps)[0]

    g_own = jnp.pad(cotangent, ((0, 0), (0, padded - width)))
    g_parts = [g_own] + [near(g_own, k) for k in range(1, plane)]
    all_heads = halves(
        head_parts(
            [key_weight, value_weight, cross_key, cross_value, query_weight, cross_query]
        )
    )
    n1, q, k_own, v_own, kv_own = plain(
        functools.partial(project_kernel, wide),
        [],
        [tok, all_heads, gains[0]],
        [bf_shape(chip, width)] + [bf_shape(chip, 2 * BLK)] * 3 + [bf_shape(nz, chip, 2 * wide)],
    )

    kv = in_column(kv_own).reshape(-1, 2 * wide)

    hot = (bucket_ids[None, :] == jnp.arange(buckets, dtype=jnp.int32)[:, None]).astype(BF)
    values = dot_tn(lax.dynamic_slice_in_dim(bucket_table, w * nh, nh, 1), hot)
    lines = bias_rows(values)

    enc_pair = pair(encoded)
    (ekv_own,) = plain(
        functools.partial(encode_kernel, wide),
        [],
        [enc_pair, all_heads],
        [bf_shape(enc_pair.shape[0], 4 * BLK)],
        deps=(kv, *g_parts[1:], *lines),
    )

    kv = [kv] + [near(kv, k) for k in range(1, plane)]

    ts, tt = bias_tiles(*lines, deps=(kv[0], ekv_own))

    ekv = lax.all_gather(ekv_own, "ctx", axis=0, tiled=True)
    spots = jnp.stack([(c % plane) * nw + i for i in (w, 1 - w)]).astype(jnp.int32)
    ug_own, ug_sent, wd_own, wd_sent = plain(
        functools.partial(units_kernel, nz, plane * nw, share, slot),
        [spots],
        [gate_weight, up_weight, down_weight.T],
        [bf_shape(gate_weight.shape[0], 2 * nz * slot)] * 2
        + [bf_shape(width, nz // nw * slot)] * 2,
        deps=(ts,),
    )
    g_plane = stacked(g_parts, deps=(ug_own,))
    out_mate, cross_out_mate = mate(out_weight), mate(cross_out)
    o1, a1, qe1, lse1 = self_fwd(
        meta, q, kv, ts, nh, hs, deps=(g_plane, out_mate, cross_out_mate)
    )
    a1_pair = pair(a1, tiled=False)
    h1, n2, cq = plain(
        functools.partial(middle_kernel, wide),
        [core],
        [tok, a1_pair, out_weight, out_mate, gains[1], all_heads],
        [f32_shape(chip, width), bf_shape(chip, width), bf_shape(chip, 2 * BLK)],
    )
    qg = lax.all_gather(qe1, "ctx", axis=0, tiled=True).reshape(nctx, chip, 2 * BLK)
    cq_full, ck_full, cv_full = pair(cross_query), pair(cross_key), pair(cross_value)
    qkv_full = pair(jnp.concatenate([query_weight, key_weight, value_weight], axis=1))

    o2, a2, qe2 = cross_fwd(cq, ekv, nh, hs)
    a2_pair = pair(a2, tiled=False)
    h2, n3 = plain(
        functools.partial(third_kernel, half),
        [core],
        [h1, a2_pair, cross_out, cross_out_mate, gains[2]],
        [f32_shape(rows, width), bf_shape(rows, padded)],
    )

    ug_sent, wd_sent, g_plane, _ = lax.optimization_barrier((ug_sent, wd_sent, g_plane, a2_pair))
    g_plane = g_plane, mate(g_plane)
    ug, wd = plain(
        order_kernel,
        [core],
        [ug_own, mate(ug_sent), wd_own, mate(wd_sent)],
        [bf_shape(width, 2 * nz * slot), bf_shape(width, nz * slot)],
        deps=(n3,),
    )
    (dact,) = plain(
        ffn_early_kernel, [], [*g_plane, wd], [f32_shape(nw * plane * rows, nz * slot)], deps=(n3,)
    )
    n3_plane = stacked([n3] + [near(n3, k) for k in range(1, plane)], deps=(dact,))
    n3_plane = n3_plane, mate(n3_plane)
    act, dgu, dn0, dn1 = ffn_both(n3_plane, dact, ug)
    sent = add(dn0, mate(dn1))
    got = [near(sent[k], k) for k in range(1, plane)]
    ffn, out0, out1 = ffn_late(n3_plane, g_plane, act, dgu, wd, nz, share, (sent[0], qg))
    dh2, dy2, gain3 = plain(
        dh2_kernel,
        [],
        [sent[0]] + got + [h2, g_own, gains[2]],
        [f32_shape(rows, width), bf_shape(rows, padded), f32_shape(1, width)],
        deps=(out0,),
    )

    dy2, de2, _, _ = grad_prep(pair(dy2, tiled=False), cross_out, o2, nh, hs)
    dcq, dekv = cross_bwd(qe2, de2[0], ekv, plane, nz, nh, hs)
    dekv = in_plane(dekv.reshape(plane, -1, 2 * wide))
    dcq_pair = pair(dcq, tiled=False)
    dh1, dy1, gain2 = plain(
        functools.partial(dh1_kernel, wide, half),
        [core],
        [dcq_pair, cq_full, h1, dh2, gains[1]],
        [f32_shape(rows, width), bf_shape(rows, padded), f32_shape(1, width)],
    )

    dy1, de1, dhi1, delta1 = grad_prep(pair(dy1, tiled=False), out_weight, o1, nh, hs)
    dg = [de1[0]] + [near(de1[0], plane * k) for k in range(1, nz)]
    dekv = layers([dekv], deps=(de1,))
    dg = spread(dg, plane, deps=(dekv[0], qg, ck_full, cv_full, qkv_full))
    spread_out = dg
    dekv = [dekv[0]] + [near(dekv[k], plane * k) for k in range(1, nz)]

    dq, rev = self_dq(meta, q, dhi1, lse1, delta1, kv, ts, nh, hs, deps=(dg,))
    dg = in_plane(dg).reshape(nctx, chip, 2 * BLK)
    made = owner_parts(
        ((((0,), 0),), (((1,), 0),), (((2,), 0),)),
        [a1_pair, a2_pair, dcq_pair],
        [dy1, dy2, n2],
        deps=(dq,),
    )
    ffn = lax.psum_scatter(
        tie(ffn, spread_out).reshape(nz, 3 * share, padded),
        "ctx",
        scatter_dimension=0,
        axis_index_groups=columns,
        tiled=True,
    )
    dk, dv = self_dkv(meta, k_own, v_own, qg, dg, tt, nh, hs, deps=(made,))
    made = in_plane(made)
    rev = tie(rev, dk)
    (dekv,) = plain(output_kernel, [], dekv, [bf_shape(*dekv[0].shape)], deps=(dk,))
    dekv_pair = pair(dekv, tiled=False)
    made_too = owner_parts(((((0,), 0), ((0,), wide)),), [dekv_pair], [enc_pair])

    dqkv_pair = pair(jnp.stack([dq, dk, dv]), tiled=False).reshape(nw, 3, chip, 2 * BLK)
    made_too = tie(made_too, made)
    tokens_grad, gain1 = plain(
        functools.partial(last_kernel, wide, half),
        [core],
        [dqkv_pair, qkv_full, tok, dh1, gains[0]],
        [f32_shape(rows, width), f32_shape(1, width)],
        deps=(made_too,),
    )
    made_too = in_plane(made_too)

    rev = rev.reshape(nh, 8, -1)
    by_distance = sum(rev[:, i, 1 + i : 1 + i + length] for i in range(8))
    hot_rev = (
        jnp.flip(bucket_ids)[None, :] == jnp.arange(buckets, dtype=jnp.int32)[:, None]
    ).astype(F32)
    table_own = lax.dot_general(
        hot_rev, by_distance, (((1,), (1,)), ((), ())), precision=lax.Precision.HIGHEST
    )
    table = lax.dynamic_update_slice_in_dim(
        jnp.zeros((buckets, heads), F32), table_own, w * nh, 1
    )

    small = jnp.concatenate([gain1[0], gain2[0], gain3[0], table.reshape(-1)])
    small = jnp.pad(small, (0, -small.shape[0] % padded)).reshape(-1, padded)
    extra = small.shape[0]
    plan = ((((0, 0), 0), ((0, 1), 0), ((0, 2), 0)),)
    second = owner_parts(plan, [dqkv_pair], [n1], small)
    second = in_plane(tie(second, made_too))
    first = layers([made, made_too])
    out_sent = add(out0, mate(tie(out1, gain1)), deps=(made_too,))
    first = [first[0]] + [near(first[k], plane * k) for k in range(1, nz)]
    (second,) = plain(
        functools.partial(deal_last_kernel, 3 * nz * cut, extra),
        [],
        [second],
        [bf_shape(nz, -(-(3 * cut + 3 * extra) // 16) * 16, padded)],
        deps=(first[0], out_sent[0]),
    )
    dealt = second
    out_sent = [tie(m, second) for m in out_sent[1:]], out_sent[0]
    out_got = [near(m, k + 1) for k, m in enumerate(out_sent[0])]
    (output,) = plain(output_kernel, [], [h2, out_sent[1]] + out_got, [bf_shape(rows, width)])
    dekv_pair = tie(dekv_pair, second)
    second = jnp.sum(in_column(second).astype(F32), axis=0)
    small = [second[3 * cut + i * extra : 3 * cut + (i + 1) * extra] for i in range(3)]
    small = (small[0] + small[1]) + small[2]
    small = small + mate(small)
    q_t, k_t, v_t = owner_sums(second, 3)
    (first,) = plain(output_kernel, [], first, [f32_shape(5 * cut, padded)], deps=(dealt,))
    out_share, cross_out_share, cq_t, ck_t, cv_t = owner_sums(first, 5)
    ffn = ffn[0, :, :width].astype(F32).reshape(3, share, width)

    def joined(x):
        return jnp.swapaxes(x[:, :, :wide], 0, 1).reshape(-1, inner)

    def own_encoder(x):
        return lax.dynamic_slice_in_dim(x, w * encoded.shape[0], encoded.shape[0], 0)

    dek, dev = joined(dekv_pair), joined(dekv_pair[:, :, wide:])
    encoded_grad = dot_nt(own_encoder(dek), ck_full) + dot_nt(own_encoder(dev), cv_full)

    small = small.reshape(-1)
    table = small[3 * width : 3 * width + buckets * heads].reshape(buckets, heads)
    return (
        output,
        tokens_grad,
        encoded_grad,
        small[:width],
        small[width : 2 * width],
        small[2 * width : 3 * width],
        q_t.T,
        k_t.T,
        v_t.T,
        out_share,
        cq_t.T,
        ck_t.T,
        cv_t.T,
        cross_out_share,
        ffn[0].T,
        ffn[1].T,
        ffn[2],
        table,
    )


def solution(mesh):
    rows = P(("seq", "ctx", "wsh"), None)
    cols = P("seq", ("ctx", "wsh"))
    split = P("wsh", None)
    return jax.shard_map(
        local,
        mesh=mesh,
        in_specs=(rows, rows, rows, P(), P(), P("wsh"), P("wsh"), P("wsh"))
        + (split,) * 11
        + (P(),),
        out_specs=(
            rows,
            rows,
            rows,
            P("seq"),
            P("seq"),
            P("seq"),
            cols,
            cols,
            cols,
            rows,
            cols,
            cols,
            cols,
            rows,
            cols,
            cols,
            rows,
            P("seq", None),
        ),
        check_vma=False,
    )
```

```python
import functools

import jax
import jax.numpy as jnp
from jax import lax
from jax.experimental import pallas as pl
from jax.experimental.pallas import tpu as pltpu
from jax.sharding import PartitionSpec as P

EPS = 1e-06
NEG = -1e30
F32 = jnp.float32
BF = jnp.bfloat16
BLK = 128
GRP = 4
UNROLL = 3
CH = BLK * GRP
VLIM = 60 * 1024 * 1024
SLOW = 64


def dot(a, b):
    return lax.dot_general(a, b, (((1,), (0,)), ((), ())), preferred_element_type=F32)


def dot_nt(a, b):
    return lax.dot_general(a, b, (((1,), (1,)), ((), ())), preferred_element_type=F32)


def dot_tn(a, b):
    return lax.dot_general(a, b, (((0,), (0,)), ((), ())), preferred_element_type=F32)


def lane_of(shape):
    return lax.broadcasted_iota(jnp.int32, shape, 1)


def head_mask(value, head, hs):
    lane = lane_of(value.shape)
    keep = (lane >= head * hs) & (lane < (head + 1) * hs)
    return jnp.where(keep, value, jnp.zeros_like(value))


def lane_fold(value, op):
    out = value[:, :BLK]
    for i in range(1, value.shape[1] // BLK):
        out = op(out, value[:, i * BLK : (i + 1) * BLK])
    return out


def pieces_into(base, columns, first):
    lane = lane_of(base.shape)
    out = base
    for i, column in enumerate(columns):
        rest = column
        for j in range(3):
            part = rest.astype(BF).astype(F32)
            rest = rest - part
            out = jnp.where(lane == first + 3 * i + j, part, out)
    return out


def params(flops, nbytes, trans):
    return dict(
        compiler_params=pltpu.CompilerParams(vmem_limit_bytes=VLIM),
        cost_estimate=pl.CostEstimate(
            flops=int(flops) // SLOW,
            bytes_accessed=int(nbytes) // SLOW,
            transcendentals=int(trans) // SLOW,
        ),
    )


def after(value, *deps):
    return lax.optimization_barrier((value,) + deps)[0]


def f32_shape(*dims):
    return jax.ShapeDtypeStruct(dims, F32)


def bf_shape(*dims):
    return jax.ShapeDtypeStruct(dims, BF)


def plain(kernel, scalars, inputs, outputs, cost=(1e9, 4e6, 0), deps=()):
    count, late = len(scalars) + len(inputs), len(deps)

    def body(*refs):
        kernel(*refs[:count], *refs[count + late :])

    return pl.pallas_call(
        body,
        in_specs=[SM] * len(scalars) + [VM] * len(inputs) + [ANY] * late,
        out_specs=[VM] * len(outputs),
        out_shape=list(outputs),
        **params(*cost),
    )(*scalars, *inputs, *deps)


VM = pl.BlockSpec(memory_space=pltpu.VMEM)
ANY = pl.BlockSpec(memory_space=pl.ANY)
SM = pl.BlockSpec(memory_space=pltpu.SMEM)


def tie(x, *deps):
    return pl.pallas_call(
        lambda *refs: None,
        in_specs=[ANY] * (1 + len(deps)),
        out_specs=ANY,
        out_shape=jax.ShapeDtypeStruct(x.shape, x.dtype),
        input_output_aliases={0: 0},
        **params(0, 0, 0),
    )(x, *deps)


def bias_kernel(nb, nh, nat_ref, rev_ref, ts_ref, tt_ref):
    row = lax.broadcasted_iota(jnp.int32, (BLK, BLK), 0)
    col = lax.broadcasted_iota(jnp.int32, (BLK, BLK), 1)
    upper = col >= row

    def skew(line):
        eight = pltpu.roll(jnp.broadcast_to(line, (8, BLK)), 0, 1, stride=1, stride_axis=0)
        return jnp.concatenate(
            [eight] + [pltpu.roll(eight, 8 * i, 1) for i in range(1, BLK // 8)], axis=0
        )

    def step(r, carry):
        d = nb - 1 - r
        first, second = rev_ref[nb - jnp.maximum(d, 0)], rev_ref[nb - 1 - jnp.maximum(d, 0)]
        for h in range(nh):
            tile = jnp.where(upper, skew(first[h : h + 1]), skew(second[h : h + 1]))
            ts_ref[r, h] = jnp.where(d * BLK + row - col >= 0, tile, NEG).astype(BF)
        d = r - (GRP - 1)
        first, second = nat_ref[jnp.maximum(d, 0) + 1], nat_ref[jnp.maximum(d, 0)]
        for h in range(nh):
            tile = jnp.where(upper, skew(first[h : h + 1]), skew(second[h : h + 1]))
            tt_ref[r, h] = jnp.where(d * BLK + col - row >= 0, tile, NEG).astype(BF)
        return carry

    lax.fori_loop(0, nb + GRP - 1, step, 0)


def bias_rows(values):
    nh, length = values.shape
    nb = length // BLK
    zero = jnp.zeros((nh, 1), F32)
    nat = jnp.concatenate([jnp.zeros((nh, BLK), F32), values], axis=1)
    rev = jnp.concatenate([zero, jnp.flip(values, 1), jnp.zeros((nh, BLK - 1), F32)], axis=1)
    nat = jnp.transpose(nat.reshape(nh, nb + 1, BLK), (1, 0, 2))
    rev = jnp.transpose(rev.reshape(nh, nb + 1, BLK), (1, 0, 2))
    return nat, rev


def bias_tiles(nat, rev, deps=()):
    nb, nh = nat.shape[0] - 1, nat.shape[1]
    shape = bf_shape(nb + GRP - 1, nh, BLK, BLK)
    return plain(
        functools.partial(bias_kernel, nb, nh), [], [nat, rev], [shape, shape], deps=deps
    )


def gather_blocks(ref, meta_ref, nctx, first, lo, hi, base=0):
    parts = []
    for i in range(GRP):
        t = first + i
        early = t < nctx
        slot = meta_ref[base + jnp.where(early, t, 2 * nctx - 1 - t)]
        at = pl.multiple_of(jnp.where(early, 0, BLK), BLK)
        parts.append(ref[slot, pl.ds(at, BLK), lo:hi])
    return jnp.concatenate(parts, axis=0)


def fetch(parts, held_ref, sem):
    rows = parts[0].shape[0]
    copies = [
        pltpu.make_async_copy(part, held_ref.at[pl.ds(k * rows, rows)], sem.at[k])
        for k, part in enumerate(parts)
    ]
    for copy in copies:
        copy.start()
    for copy in copies:
        copy.wait()


def bias_of(ref, first):
    rows = ref.shape[1] * BLK
    return jnp.concatenate(
        [ref[first + i].reshape(rows, BLK) for i in range(GRP)], axis=1
    ).astype(F32)


def stack_heads(value, hs, nh, shift=0):
    return jnp.concatenate([head_mask(value, h + shift, hs) for h in range(nh)], axis=0)


def merge_heads(stacked, hs, nh, shift=0):
    rows = stacked.shape[0] // nh
    total = jnp.zeros((rows, stacked.shape[1]), F32)
    for h in range(nh):
        total = total + head_mask(stacked[h * rows : (h + 1) * rows], h + shift, hs)
    return total


def pick_columns(columns, nh, rows):
    out = jnp.zeros((rows, BLK), F32)
    lane = lane_of(out.shape)
    for h in range(nh):
        out = jnp.where(lane == h, columns[h * rows : (h + 1) * rows], out)
    return out


def stack_columns(ref, rows, nh):
    return jnp.concatenate([ref[rows, h : h + 1] for h in range(nh)], axis=0)


def self_fwd_kernel(count, nctx, nh, hs, meta_ref, q_ref, ts_ref, *rest):
    o_ref, a_ref, qe_ref, lse_ref, qm_ref, s_ref, acc_ref, top_ref, sum_ref, flat_ref, sem = rest[-11:]
    fetch(rest[:count], flat_ref, sem)
    kv_ref = flat_ref.reshape(nctx, 2 * BLK, flat_ref.shape[1])
    nb = 2 * nctx
    wide = nh * hs
    early = meta_ref[nctx]
    split = early // GRP + 1
    base = 2 * nctx + 1
    for half in range(2):
        qm_ref[half] = stack_heads(q_ref[half * BLK : (half + 1) * BLK, :], hs, nh)
    top_ref[...] = jnp.full(top_ref.shape, NEG, F32)
    sum_ref[...] = jnp.zeros_like(sum_ref)
    acc_ref[...] = jnp.zeros_like(acc_ref)

    def place(step):
        half = (step >= split).astype(jnp.int32)
        return half, step - half * split

    def score(step, carry):
        half, ch = place(step)
        blk = jnp.where(half == 0, early, nb - 1 - early)
        keys = gather_blocks(kv_ref, meta_ref, nctx, ch * GRP, 0, 2 * BLK, base)
        s = dot_nt(qm_ref[half], keys) + bias_of(ts_ref, nb - 1 - blk + ch * GRP)
        s_ref[step] = s
        top_ref[half] = jnp.maximum(top_ref[half], lane_fold(s, jnp.maximum))
        return carry

    steps = nb // GRP + 1
    lax.fori_loop(0, steps, score, 0, unroll=UNROLL)
    for half in range(2):
        top = jnp.max(top_ref[half], axis=1, keepdims=True)
        top_ref[half] = jnp.broadcast_to(top, top_ref.shape[1:])

    def weigh(step, carry):
        half, ch = place(step)
        vals = gather_blocks(kv_ref, meta_ref, nctx, ch * GRP, BLK, 3 * BLK, base)
        top = top_ref[half]
        p = jnp.exp(s_ref[step] - jnp.concatenate([top] * GRP, axis=1))
        acc_ref[half] += dot(p.astype(BF), vals)
        sum_ref[half] += lane_fold(p, jnp.add)
        return carry

    lax.fori_loop(0, steps, weigh, 0, unroll=UNROLL)
    for half in range(2):
        rows = slice(half * BLK, (half + 1) * BLK)
        total = jnp.sum(sum_ref[half], axis=1, keepdims=True)
        o = pltpu.roll(merge_heads(acc_ref[half] / total, hs, nh, 1), 2 * BLK - hs, 1)
        o_ref[rows, :] = o
        a_ref[rows, :] = o[:, :wide].astype(BF)
        lse = pick_columns(top_ref[half][:, :1] + jnp.log(total), nh, BLK)
        lse_ref[rows, :] = lse
        minus = [-lse[:, h : h + 1] for h in range(nh)]
        qe_ref[rows, :] = pieces_into(q_ref[rows, :].astype(F32), minus, wide).astype(BF)


def self_fwd(meta, q, kv, ts, nh, hs, deps=()):
    nctx = len(kv) * kv[0].shape[0] // (2 * BLK)
    nb = 2 * nctx
    rows = 2 * BLK
    pairs = (nb + 1) * BLK * BLK * nh
    return pl.pallas_call(
        functools.partial(self_fwd_kernel, len(kv), nctx, nh, hs),
        in_specs=[SM, VM, VM] + [ANY] * (len(kv) + len(deps)),
        out_specs=[VM] * 4,
        out_shape=[
            f32_shape(rows, rows),
            bf_shape(rows, nh * hs),
            bf_shape(rows, rows),
            f32_shape(rows, BLK),
        ],
        scratch_shapes=[
            pltpu.VMEM((2, nh * BLK, 2 * BLK), BF),
            pltpu.VMEM((nb // GRP + 1, nh * BLK, CH), F32),
            pltpu.VMEM((2, nh * BLK, 2 * BLK), F32),
            pltpu.VMEM((2, nh * BLK, BLK), F32),
            pltpu.VMEM((2, nh * BLK, BLK), F32),
            pltpu.VMEM((nb * BLK, kv[0].shape[1]), BF),
            pltpu.SemaphoreType.DMA((len(kv),)),
        ],
        **params(pairs * 2 * 512, 10e6, pairs),
    )(meta, q, ts, *kv, *deps)


def self_dq_kernel(count, nctx, nh, hs, meta_ref, q_ref, da_ref, lse_ref, del_ref, ts_ref, *rest):
    dq_ref, rev_ref, qm_ref, dm_ref, col_ref, acc_ref, flat_ref, sem = rest[-8:]
    fetch(rest[:count], flat_ref, sem)
    kv_ref = flat_ref.reshape(nctx, 2 * BLK, flat_ref.shape[1])
    nb = 2 * nctx
    early = meta_ref[nctx]
    split = early // GRP + 1
    span = CH + BLK
    rev_ref[...] = jnp.zeros_like(rev_ref)
    acc_ref[...] = jnp.zeros_like(acc_ref)
    for half in range(2):
        rows = slice(half * BLK, (half + 1) * BLK)
        qm_ref[half] = stack_heads(q_ref[rows, :], hs, nh)
        dm_ref[half] = stack_heads(da_ref[rows, :], hs, nh, 1)
        for i, ref in enumerate((lse_ref, del_ref)):
            col_ref[half, i] = jnp.broadcast_to(stack_columns(ref, rows, nh), col_ref.shape[2:])

    def step(at, carry):
        half = (at >= split).astype(jnp.int32)
        ch = at - half * split
        blk = jnp.where(half == 0, early, nb - 1 - early)
        held = gather_blocks(kv_ref, meta_ref, nctx, ch * GRP, 0, 3 * BLK, 2 * nctx + 1)
        keys, vals = held[:, : 2 * BLK], held[:, BLK:]
        off = pl.multiple_of((ch * GRP - blk + nb - 1) * BLK, BLK)
        s = dot_nt(qm_ref[half], keys) + bias_of(ts_ref, nb - 1 - blk + ch * GRP)
        p = jnp.exp(s - jnp.concatenate([col_ref[half, 0]] * GRP, axis=1))
        delta = jnp.concatenate([col_ref[half, 1]] * GRP, axis=1)
        ds = (p * (dot_nt(dm_ref[half], vals) - delta)).astype(BF)
        acc_ref[half] += dot(ds, keys)
        flat = jnp.concatenate([jnp.zeros((nh * BLK, BLK), F32), ds.astype(F32)], axis=1)
        for h in range(nh):
            line = flat[h * BLK : h * BLK + 8]
            for i in range(1, BLK // 8):
                first = h * BLK + 8 * i
                line = line + pltpu.roll(flat[first : first + 8], span - 8 * i, 1)
            rev_ref[h * 8 : (h + 1) * 8, pl.ds(off, span)] += line
        return carry

    lax.fori_loop(0, nb // GRP + 1, step, 0, unroll=UNROLL)
    for half in range(2):
        dq_ref[half * BLK : (half + 1) * BLK, :] = merge_heads(acc_ref[half], hs, nh).astype(BF)


def self_dq(meta, q, da, lse, delta, kv, ts, nh, hs, deps=()):
    nctx = len(kv) * kv[0].shape[0] // (2 * BLK)
    nb = 2 * nctx
    pairs = (nb + 1) * BLK * BLK * nh
    return pl.pallas_call(
        functools.partial(self_dq_kernel, len(kv), nctx, nh, hs),
        in_specs=[SM] + [VM] * 5 + [ANY] * (len(kv) + len(deps)),
        out_specs=[VM, VM],
        out_shape=[
            jax.ShapeDtypeStruct((2 * BLK, 2 * BLK), BF),
            jax.ShapeDtypeStruct((8 * nh, nb * BLK + CH), F32),
        ],
        scratch_shapes=[
            pltpu.VMEM((2, nh * BLK, 2 * BLK), BF),
            pltpu.VMEM((2, nh * BLK, 2 * BLK), BF),
            pltpu.VMEM((2, 2, nh * BLK, BLK), F32),
            pltpu.VMEM((2, nh * BLK, 2 * BLK), F32),
            pltpu.VMEM((nb * BLK, kv[0].shape[1]), BF),
            pltpu.SemaphoreType.DMA((len(kv),)),
        ],
        **params(pairs * 2 * 896, 10e6, pairs),
    )(meta, q, da, lse, delta, ts, *kv, *deps)


def self_dkv_kernel(
    nctx, nh, hs, meta_ref, k_ref, v_ref, qg_ref, dg_ref, tt_ref, *rest
):
    dk_ref, dv_ref, km_ref, vm_ref, ka_ref, va_ref = rest[-6:]
    nb = 2 * nctx
    wide = nh * hs
    early = meta_ref[nctx]
    late = nb - 1 - early
    split = nb // GRP - early // GRP

    def extended(value):
        lane = lane_of(value.shape)
        parts = []
        for h in range(nh):
            first = wide + 3 * h
            ones = (lane >= first) & (lane < first + 3)
            parts.append(jnp.where(ones, jnp.ones_like(value), head_mask(value, h, hs)))
        return jnp.concatenate(parts, axis=0)

    ka_ref[...] = jnp.zeros_like(ka_ref)
    va_ref[...] = jnp.zeros_like(va_ref)
    for half in range(2):
        rows = slice(half * BLK, (half + 1) * BLK)
        km_ref[half] = extended(k_ref[rows, :])
        vm_ref[half] = extended(v_ref[rows, :])

    def step(at, carry):
        half = (at >= split).astype(jnp.int32)
        blk = jnp.where(half == 0, early, late)
        ch = at - half * split + blk // GRP
        qc = gather_blocks(qg_ref, meta_ref, nctx, ch * GRP, 0, 2 * BLK)
        dc = gather_blocks(dg_ref, meta_ref, nctx, ch * GRP, 0, 2 * BLK, nctx + 1)
        p = jnp.exp(dot_nt(km_ref[half], qc) + bias_of(tt_ref, ch * GRP - blk + GRP - 1))
        ds = (p * dot_nt(vm_ref[half], dc)).astype(BF)
        ka_ref[half] += dot(ds, qc)
        va_ref[half] += dot(p.astype(BF), dc)
        return carry

    lax.fori_loop(0, nb // GRP + 1, step, 0, unroll=UNROLL)
    for half in range(2):
        rows = slice(half * BLK, (half + 1) * BLK)
        dk_ref[rows, :] = merge_heads(ka_ref[half], hs, nh).astype(BF)
        dv_ref[rows, :] = merge_heads(va_ref[half], hs, nh).astype(BF)


def self_dkv(meta, k, v, qg, dg, tt, nh, hs, deps=()):
    nctx = qg.shape[0]
    nb = 2 * nctx
    pairs = (nb + 1) * BLK * BLK * nh
    return pl.pallas_call(
        functools.partial(self_dkv_kernel, nctx, nh, hs),
        in_specs=[SM] + [VM] * 5 + [ANY] * len(deps),
        out_specs=[VM, VM],
        out_shape=[bf_shape(2 * BLK, 2 * BLK)] * 2,
        scratch_shapes=[
            pltpu.VMEM((2, nh * BLK, 2 * BLK), BF),
            pltpu.VMEM((2, nh * BLK, 2 * BLK), BF),
            pltpu.VMEM((2, nh * BLK, 2 * BLK), F32),
            pltpu.VMEM((2, nh * BLK, 2 * BLK), F32),
        ],
        **params(pairs * 2 * 1024, 10e6, pairs),
    )(meta, k, v, qg, dg, tt, *deps)


def cross_fwd_kernel(nh, hs, q_ref, e_ref, o_ref, a_ref, qe_ref, s_ref):
    wide = nh * hs
    chunks = e_ref.shape[0] // CH
    rows = q_ref.shape[0]
    q = q_ref[...]
    qm = stack_heads(q, hs, nh)
    top = jnp.full((nh * rows, BLK), NEG, F32)
    for ch in range(chunks):
        s = dot_nt(qm, e_ref[ch * CH : (ch + 1) * CH, : 2 * BLK])
        s_ref[ch] = s
        top = jnp.maximum(top, lane_fold(s, jnp.maximum))
    top = jnp.max(top, axis=1, keepdims=True)
    total = jnp.zeros((nh * rows, BLK), F32)
    acc = jnp.zeros((nh * rows, 2 * BLK), F32)
    for ch in range(chunks):
        p = jnp.exp(s_ref[ch] - top)
        total = total + lane_fold(p, jnp.add)
        acc = acc + dot(p.astype(BF), e_ref[ch * CH : (ch + 1) * CH, 2 * BLK :])
    total = jnp.sum(total, axis=1, keepdims=True)
    o = merge_heads(acc / total, hs, nh)
    o_ref[...] = o
    a_ref[...] = o[:, :wide].astype(BF)
    lse = pick_columns(top + jnp.log(total), nh, rows)
    minus = [-lse[:, h : h + 1] for h in range(nh)]
    qe_ref[...] = pieces_into(q.astype(F32), minus, wide).astype(BF)


def cross_fwd(q, e, nh, hs):
    enc = e.shape[0]
    rows = 2 * BLK
    pairs = rows * enc * nh
    return pl.pallas_call(
        functools.partial(cross_fwd_kernel, nh, hs),
        in_specs=[VM, VM],
        out_specs=[VM] * 3,
        out_shape=[f32_shape(rows, rows), bf_shape(rows, nh * hs), bf_shape(rows, rows)],
        scratch_shapes=[pltpu.VMEM((enc // CH, nh * rows, CH), F32)],
        **params(pairs * 2 * 512, 4e6, pairs),
    )(q, e)


def cross_bwd_kernel(plane, nz, nh, hs, qe_ref, de_ref, all_ref, dq_ref, dkv_ref, e_ref, acc_ref, sem):
    size = all_ref.shape[0] // (plane * nz)
    copies = []
    for k in range(plane):
        for z in range(nz):
            source = all_ref.at[pl.ds((z * plane + k) * size, size)]
            target = e_ref.at[pl.ds((k * nz + z) * size, size)]
            copies.append(pltpu.make_async_copy(source, target, sem.at[k, z]))
    for copy in copies:
        copy.start()
    for copy in copies:
        copy.wait()
    wide = nh * hs
    acc_ref[...] = jnp.zeros_like(acc_ref)

    def kept(value, h):
        lane = lane_of(value.shape)
        first = wide + 3 * h
        keep = ((lane >= h * hs) & (lane < (h + 1) * hs)) | ((lane >= first) & (lane < first + 3))
        return jnp.where(keep, value, jnp.zeros_like(value))

    qm = [kept(qe_ref[...], h) for h in range(nh)]
    dm = [kept(de_ref[...], h) for h in range(nh)]

    for ch in range(e_ref.shape[0] // CH):
        rows = slice(ch * CH, (ch + 1) * CH)
        ek = e_ref[rows, : 2 * BLK]
        ev = e_ref[rows, 2 * BLK :]
        ek_t = jnp.transpose(ek.astype(F32)).astype(BF)
        dk = jnp.zeros((CH, 2 * BLK), F32)
        dv = jnp.zeros((CH, 2 * BLK), F32)
        for h in range(nh):
            p = jnp.exp(dot_nt(ek, qm[h]))
            ds = (p * dot_nt(ev, dm[h])).astype(BF)
            dk = dk + dot(ds, qm[h])
            dv = dv + dot(p.astype(BF), dm[h])
            acc_ref[h * hs : (h + 1) * hs, :] += dot(ek_t[h * hs : (h + 1) * hs, :], ds)
        dkv_ref[rows, :] = jnp.concatenate([dk[:, :wide], dv[:, :wide]], axis=1).astype(BF)
    dq_ref[...] = jnp.transpose(acc_ref[...]).astype(BF)


def cross_bwd(qe, de, e, plane, nz, nh, hs):
    enc = e.shape[0]
    pairs = 2 * BLK * enc * nh
    return pl.pallas_call(
        functools.partial(cross_bwd_kernel, plane, nz, nh, hs),
        in_specs=[VM, VM, ANY],
        out_specs=[VM, VM],
        out_shape=[bf_shape(2 * BLK, 2 * BLK), bf_shape(enc, 2 * nh * hs)],
        scratch_shapes=[
            pltpu.VMEM((enc, 4 * BLK), BF),
            pltpu.VMEM((2 * BLK, 2 * BLK), F32),
            pltpu.SemaphoreType.DMA((plane, nz)),
        ],
        **params(pairs * 2 * 1024, 4e6, pairs),
    )(qe, de, e)


def scale_of(rows):
    return lax.rsqrt(jnp.mean(rows * rows, axis=-1, keepdims=True) + EPS)


def norm_back(rows, gain, grad):
    rr = scale_of(rows)
    scaled = gain * grad
    shared = jnp.mean(rows * scaled, axis=-1, keepdims=True)
    dv = rr * scaled - rows * (rr * rr * rr) * shared
    return dv, jnp.sum(rows * rr * grad, axis=0, keepdims=True)


def in_blocks(pair_ref):
    half = pair_ref.shape[1] // 2
    return jnp.concatenate(
        [pair_ref[m, i * half : (i + 1) * half] for i in range(2) for m in range(2)], axis=0
    )


def put(ref, value):
    cols = value.shape[1]
    ref[:, :cols] = value
    if ref.shape[1] > cols:
        ref[:, cols:] = jnp.zeros((ref.shape[0], ref.shape[1] - cols), ref.dtype)


def own_of(ref, w, half):
    return jnp.concatenate(
        [ref[pl.ds(pl.multiple_of(i * BLK + w * half, half), half), :] for i in range(2)], axis=0
    )


def project_kernel(wide, tok_ref, w_ref, gain_ref, n1_ref, q_ref, k_ref, v_ref, kv_ref):
    x = in_blocks(tok_ref).astype(F32)
    n1 = (x * scale_of(x) * gain_ref[...]).astype(BF)
    n1_ref[...] = n1
    cut = w_ref.shape[1]

    def product(first, count):
        cols = slice(first * wide, (first + count) * wide)
        return (dot(n1[:, :cut], w_ref[0, :, cols]) + dot(n1[:, cut:], w_ref[1, :, cols])).astype(BF)

    kv = product(0, 2)
    for i in range(kv_ref.shape[0]):
        kv_ref[i] = kv
    zero = jnp.zeros((x.shape[0], 2 * BLK), BF)
    for ref, value in ((k_ref, kv[:, :wide]), (v_ref, kv[:, wide:]), (q_ref, product(4, 1))):
        ref[...] = zero
        ref[:, :wide] = value


def encode_kernel(wide, enc_ref, w_ref, out_ref):
    x = enc_ref[...]
    cut = w_ref.shape[1]
    cols = slice(2 * wide, 4 * wide)
    made = dot(x[:, :cut], w_ref[0, :, cols]) + dot(x[:, cut:], w_ref[1, :, cols])
    made = made.astype(BF)
    out_ref[...] = jnp.ones(out_ref.shape, BF)
    out_ref[:, :wide] = made[:, :wide]
    out_ref[:, 2 * BLK : 2 * BLK + wide] = made[:, wide:]


def middle_kernel(
    wide, core_ref, tok_ref, a_ref, own_ref, mate_ref, gain_ref, w_ref, h_ref, n_ref, cq_ref
):
    w = core_ref[0]
    h = in_blocks(tok_ref).astype(F32)
    h = h + (dot(a_ref[w], own_ref[...]) + dot(a_ref[1 - w], mate_ref[...]))
    h_ref[...] = h
    n = (h * scale_of(h) * gain_ref[...]).astype(BF)
    n_ref[...] = n
    cut = w_ref.shape[1]
    cols = slice(5 * wide, 6 * wide)
    made = dot(n[:, :cut], w_ref[0, :, cols]) + dot(n[:, cut:], w_ref[1, :, cols])
    cq_ref[...] = jnp.zeros(cq_ref.shape, BF)
    cq_ref[:, :wide] = made.astype(BF)


def third_kernel(half, w_ref, h1_ref, a_ref, own_ref, mate_ref, gain_ref, h_ref, n_ref):
    w = w_ref[0]
    h = own_of(h1_ref, w, half)
    for m, ref in ((w, own_ref), (1 - w, mate_ref)):
        h = h + dot(own_of(a_ref.at[m], w, half), ref[...])
    h_ref[...] = h
    put(n_ref, (h * scale_of(h) * gain_ref[...]).astype(BF))


def heads_kernel(wide, *refs):
    *weights, out_ref = refs
    last = out_ref.shape[2] - len(weights) * wide
    for m in range(out_ref.shape[0] if last else 0):
        out_ref[m, :, len(weights) * wide :] = jnp.zeros((out_ref.shape[1], last), BF)
    for i, ref in enumerate(weights):
        for m in range(out_ref.shape[0]):
            out_ref[m, :, i * wide : (i + 1) * wide] = ref[:, m * wide : (m + 1) * wide]


def units_kernel(nz, step, share, slot, spot_ref, gate_ref, up_ref, down_ref, *outs):
    def move(ref, out, first, at):
        base = pl.multiple_of(jnp.minimum(first // BLK * BLK, ref.shape[1] - 2 * BLK), BLK)
        window = ref[:, pl.ds(base, 2 * BLK)].astype(F32)
        window = pltpu.roll(window, 2 * BLK - (first - base), 1)[:, :BLK]
        window = jnp.where(lane_of(window.shape) < share, window, 0.0)
        out[:, at : at + slot] = window.astype(BF)[:, :slot]

    for m in range(2):
        ug_ref, wd_ref = outs[m], outs[2 + m]
        for z in range(nz):
            first = (z * step + spot_ref[m]) * share
            move(gate_ref, ug_ref, first, z * slot)
            move(up_ref, ug_ref, first, (nz + z) * slot)
        for z in range(wd_ref.shape[1] // slot):
            move(down_ref, wd_ref, (z * step + spot_ref[m]) * share, z * slot)


def in_order(w, own_ref, mate_ref, axis):
    own, other = own_ref[...], mate_ref[...]
    return jnp.concatenate(
        [jnp.where(w == 0, own, other), jnp.where(w == 0, other, own)], axis=axis
    )


def order_kernel(core_ref, own_ref, mate_ref, down_ref, down_mate_ref, ug_ref, wd_ref):
    ug_ref[...] = in_order(core_ref[0], own_ref, mate_ref, 0)
    wd_ref[...] = in_order(core_ref[0], down_ref, down_mate_ref, 1)


def ffn_early_kernel(g0_ref, g1_ref, wd_ref, out_ref):
    width = wd_ref.shape[0]
    rows = g0_ref.shape[0]
    for i, ref in enumerate((g0_ref, g1_ref)):
        out_ref[i * rows : (i + 1) * rows, :] = dot(ref[:, :width], wd_ref[...])


def ffn_kernel(n0_ref, n1_ref, da_ref, ug_ref, act_ref, dgu_ref, d0_ref, d1_ref):
    own = pl.program_id(0) < pl.num_programs(0) // 2
    units = act_ref.shape[1]
    width = ug_ref.shape[0]
    n = jnp.where(own, n0_ref[:, :width], n1_ref[:, :width])
    gate = dot(n, ug_ref[:, :units])
    up = dot(n, ug_ref[:, units:])
    da = da_ref[...]
    scale = 0.7978845608028654
    inner = jnp.tanh(scale * (gate + 0.044715 * gate * gate * gate))
    gelu = 0.5 * gate * (1.0 + inner)
    slope = 0.5 * (1.0 + inner) + 0.5 * gate * (1.0 - inner * inner) * scale * (
        1.0 + 3.0 * 0.044715 * gate * gate
    )
    act_ref[...] = (gelu * up).astype(BF)
    dg = (da * up * slope).astype(BF)
    du = (da * gelu).astype(BF)
    dgu_ref[:, :units] = dg
    dgu_ref[:, units:] = du
    dn = (dot_nt(dg, ug_ref[:, :units]) + dot_nt(du, ug_ref[:, units:])).astype(BF)

    @pl.when(own)
    def _():
        put(d0_ref, dn)

    @pl.when(jnp.logical_not(own))
    def _():
        put(d1_ref, dn)


def half_specs(tiles, cols):
    tile = 4 * BLK
    return [
        pl.BlockSpec((tile, cols), lambda i: (jnp.minimum(i, tiles // 2 - 1), 0)),
        pl.BlockSpec((tile, cols), lambda i: (jnp.maximum(i - tiles // 2, 0), 0)),
    ]


def ffn_both(n, da, ug):
    rows, padded = 2 * n[0].shape[0], n[0].shape[1]
    width, units = ug.shape[0], ug.shape[1] // 2
    tiles = rows // (4 * BLK)

    def row(cols):
        return pl.BlockSpec((4 * BLK, cols), lambda i: (i, 0))

    halved = half_specs(tiles, padded)
    return pl.pallas_call(
        ffn_kernel,
        grid=(tiles,),
        in_specs=halved + [row(units), pl.BlockSpec(ug.shape, lambda i: (0, 0))],
        out_specs=[row(units), row(2 * units)] + halved,
        out_shape=[bf_shape(rows, units), bf_shape(rows, 2 * units)]
        + [bf_shape(rows // 2, padded)] * 2,
        **params(10 * rows * width * units, 12e6, rows * units),
    )(*n, da, ug)


def ffn_late_kernel(nz, share, late, n0_ref, n1_ref, g0_ref, g1_ref, act_ref, dgu_ref, wd_ref, *rest):
    w_ref, o0_ref, o1_ref, acc_ref = rest[late:]
    i = pl.program_id(0)
    own = i < pl.num_programs(0) // 2
    units = act_ref.shape[1]
    @pl.when(i == 0)
    def _():
        acc_ref[...] = jnp.zeros_like(acc_ref)

    n = jnp.where(own, n0_ref[...], n1_ref[...])
    g = jnp.where(own, g0_ref[...], g1_ref[...])
    acc_ref[: 2 * units, :] += dot_tn(dgu_ref[...], n)
    acc_ref[2 * units :, :] += dot_tn(act_ref[...], g)
    made = dot_nt(act_ref[...], wd_ref[...]).astype(BF)

    @pl.when(own)
    def _():
        put(o0_ref, made)

    @pl.when(jnp.logical_not(own))
    def _():
        put(o1_ref, made)

    @pl.when(i == pl.num_programs(0) - 1)
    def _():
        for z in range(nz):
            for j in range(3):
                first = j * units + z * (units // nz)
                w_ref[z, j] = acc_ref[first : first + share, :].astype(BF)


def ffn_late(n, g, act, dgu, wd, nz, share, deps):
    rows, padded = act.shape[0], n[0].shape[1]
    width, units = wd.shape
    tiles = rows // (4 * BLK)

    def row(cols):
        return pl.BlockSpec((4 * BLK, cols), lambda i: (i, 0))

    halved = half_specs(tiles, padded)
    return pl.pallas_call(
        functools.partial(ffn_late_kernel, nz, share, len(deps)),
        grid=(tiles,),
        in_specs=halved
        + halved
        + [row(units), row(2 * units), pl.BlockSpec(wd.shape, lambda i: (0, 0))]
        + [ANY] * len(deps),
        out_specs=[pl.BlockSpec((nz, 3, share, padded), lambda i: (0, 0, 0, 0))] + halved,
        out_shape=[bf_shape(nz, 3, share, padded)] + [bf_shape(rows // 2, padded)] * 2,
        scratch_shapes=[pltpu.VMEM((3 * units, padded), F32)],
        **params(8 * rows * width * units, 20e6, 0),
    )(*n, *g, act, dgu, wd, *deps)


def add_kernel(a_ref, b_ref, *outs):
    rows = outs[0].shape[0]
    for k, out in enumerate(outs):
        at = slice(k * rows, (k + 1) * rows)
        out[...] = (a_ref[at].astype(F32) + b_ref[at].astype(F32)).astype(BF)


def output_kernel(*refs):
    *parts, out_ref = refs
    width = out_ref.shape[1]
    total = parts[0][:, :width].astype(F32)
    for part in parts[1:]:
        total = total + part[:, :width].astype(F32)
    out_ref[...] = total.astype(out_ref.dtype)


def join_kernel(*refs):
    *parts, out_ref = refs
    rows = parts[0].shape[0]
    for i, part in enumerate(parts):
        out_ref[i * rows : (i + 1) * rows, :] = part[...]


def spread_kernel(*refs):
    *parts, out_ref = refs
    rows = parts[0].shape[0]
    for i in range(out_ref.shape[0]):
        for j, part in enumerate(parts):
            out_ref[i, j * rows : (j + 1) * rows, :] = part[...]


def split_rows(value):
    parts = []
    for _ in range(3):
        part = value.astype(BF).astype(F32)
        value = value - part
        parts.append(part)
    return jnp.concatenate(parts, axis=0)


def owners_kernel(wide, plan, target_ref, *refs):
    sets = 1 + max(s[0] for group in plan for s, _ in group)
    xs, ys, out_ref = refs[:sets], refs[sets : sets + len(plan)], refs[-1]
    rows = target_ref.shape[0] // out_ref.shape[0]
    extra = refs[-2] if len(refs) > sets + len(plan) + 1 else None
    count = target_ref.shape[0]
    total = jnp.zeros((count, ys[0].shape[1]), F32)
    column = 0
    for group, y in zip(plan, ys):
        picked = jnp.zeros((count, y.shape[0]), F32)
        for which, first in group:
            x = xs[which[0]]
            lane = lane_of((count, x.shape[-1]))
            inside = (lane >= first) & (lane < first + wide)
            for m in range(2):
                hit = inside & (lane - first + m * wide == target_ref[:, column : column + 1])
                picked = picked + dot_nt(hit.astype(BF), x[(m,) + which[1:]])
            column += 1
        total = total + dot(picked.astype(BF), y[...])
    for k in range(out_ref.shape[0]):
        part = total[k * rows : (k + 1) * rows].astype(BF)
        if extra is None:
            put(out_ref.at[k], part)
        else:
            out_ref[k] = jnp.zeros(out_ref.shape[1:], BF)
            out_ref[k, :rows, : part.shape[1]] = part
            out_ref[k, rows : rows + 3 * extra.shape[0], :] = split_rows(extra[...]).astype(BF)


def layers_kernel(nz, zed_ref, x_ref, *outs):
    total = jnp.sum(x_ref[...].astype(F32), axis=0)
    rows = total.shape[0] // nz
    for k, out in enumerate(outs):
        want = zed_ref[0] ^ k
        value = total[:rows]
        for z in range(1, nz):
            value = jnp.where(want == z, total[z * rows : (z + 1) * rows], value)
        out[...] = value.astype(BF)


def deal_last_kernel(rows, extra, x_ref, out_ref):
    total = jnp.sum(x_ref[...].astype(F32), axis=0)
    each = rows // out_ref.shape[0]
    small = total[rows : rows + extra]
    for i in range(1, 3):
        small = small + total[rows + i * extra : rows + (i + 1) * extra]
    small = split_rows(small).astype(BF)
    for i in range(out_ref.shape[0]):
        out_ref[i] = jnp.zeros(out_ref.shape[1:], BF)
        out_ref[i, :each, :] = total[i * each : (i + 1) * each].astype(BF)
        out_ref[i, each : each + 3 * extra, :] = small


def deal_kernel(*refs):
    *parts, out_ref = refs
    at = 0
    for part in parts:
        total = jnp.sum(part[...].astype(F32), axis=0)
        rows = total.shape[0] // out_ref.shape[0]
        for i in range(out_ref.shape[0]):
            out_ref[i, at : at + rows, :] = total[i * rows : (i + 1) * rows].astype(BF)
        at += rows


def dh2_kernel(*refs):
    *parts, h_ref, cot_ref, gain_ref, dh_ref, dy_ref, gain_out = refs
    width = h_ref.shape[1]
    grad = parts[0][:, :width].astype(F32)
    for part in parts[1:]:
        grad = grad + part[:, :width].astype(F32)
    dv, gain_out[...] = norm_back(h_ref[...], gain_ref[...], grad)
    dh = cot_ref[:, :width].astype(F32) + dv
    dh_ref[...] = dh
    put(dy_ref, dh.astype(BF))


def dh1_kernel(wide, half, w_ref, dq_ref, cq_ref, h1_ref, dh2_ref, gain_ref, dh_ref, dy_ref, gain_out):
    w = w_ref[0]
    dq = jnp.concatenate([own_of(dq_ref.at[m], w, half)[:, :wide] for m in range(2)], axis=1)
    grad = dot_nt(dq, cq_ref[...])
    dv, gain_out[...] = norm_back(own_of(h1_ref, w, half), gain_ref[...], grad)
    dh = dh2_ref[...] + dv
    dh_ref[...] = dh
    put(dy_ref, dh.astype(BF))


def last_kernel(wide, half, w_ref, d_ref, weight_ref, tok_ref, dh1_ref, gain_ref, out_ref, gain_out):
    w = w_ref[0]
    d = jnp.concatenate(
        [own_of(d_ref.at[m, i], w, half)[:, :wide] for i in range(3) for m in range(2)], axis=1
    )
    grad = dot_nt(d, weight_ref[...])
    dv, gain_out[...] = norm_back(tok_ref[w].astype(F32), gain_ref[...], grad)
    out_ref[...] = dh1_ref[...] + dv


def grad_prep_kernel(nh, hs, dy_ref, w_ref, o_ref, out_ref, de_ref, dh_ref, del_ref):
    wide = nh * hs
    dy = in_blocks(dy_ref)[:, : w_ref.shape[1]]
    out_ref[...] = dy
    da = dot_nt(dy, w_ref[...]).astype(BF)
    da = jnp.concatenate([da, jnp.zeros((da.shape[0], 2 * BLK - wide), BF)], axis=1)
    terms = da.astype(F32) * o_ref[...]
    delta = [jnp.sum(head_mask(terms, h, hs), axis=1, keepdims=True) for h in range(nh)]
    dh_ref[...] = pltpu.roll(da.astype(F32), hs, 1).astype(BF)
    lane = lane_of(del_ref.shape)
    cols = jnp.zeros(del_ref.shape, F32)
    for h in range(nh):
        cols = jnp.where(lane == h, delta[h], cols)
    del_ref[...] = cols
    de = pieces_into(da.astype(F32), [-t for t in delta], wide).astype(BF)
    for i in range(de_ref.shape[0]):
        de_ref[i] = de


def grad_prep(dy, weight, o, nh, hs, copies=1, deps=()):
    rows, width = o.shape[0], weight.shape[1]
    return plain(
        functools.partial(grad_prep_kernel, nh, hs),
        [],
        [dy, weight, o],
        [
            bf_shape(rows, width),
            bf_shape(copies, rows, 2 * BLK),
            bf_shape(rows, 2 * BLK),
            f32_shape(rows, BLK),
        ],
        deps=deps,
    )


def local(
    tokens,
    encoded,
    cotangent,
    assign,
    bucket_ids,
    gain_self,
    gain_cross,
    gain_ffn,
    query_weight,
    key_weight,
    value_weight,
    out_weight,
    cross_query,
    cross_key,
    cross_value,
    cross_out,
    gate_weight,
    up_weight,
    down_weight,
    bucket_table,
):
    nctx = lax.axis_size("ctx")
    nw = lax.axis_size("wsh")
    c = lax.axis_index("ctx")
    w = lax.axis_index("wsh")
    both = ("ctx", "wsh")
    rows, width = tokens.shape
    half = rows // 2
    length = rows * nw * nctx
    buckets, heads = bucket_table.shape
    inner = query_weight.shape[1]
    hs = inner // heads
    nh = heads // nw
    wide = nh * hs
    plane = 4
    nz = nctx // plane
    spot = (c % plane) * nw + w
    zed = c // plane
    hidden = gate_weight.shape[1]
    share = hidden // (nctx * nw)
    slot = -(-share // 32) * 32

    def pair(x, axis=0, tiled=True):
        return lax.all_gather(x, "wsh", axis=axis, tiled=tiled)

    def halves(parts):
        return lax.all_to_all(parts, "wsh", 0, 0, tiled=True)

    def mate(x):
        return lax.ppermute(x, "wsh", [(i, (i + 1) % nw) for i in range(nw)])

    planes = [[z * plane + i for i in range(plane)] for z in range(nz)]
    columns = [[z * plane + i for z in range(nz)] for i in range(plane)]

    def in_plane(x):
        return lax.all_to_all(x, "ctx", 0, 0, tiled=True, axis_index_groups=planes)

    def in_column(x):
        return lax.all_to_all(x, "ctx", 0, 0, tiled=True, axis_index_groups=columns)

    padded = -(-width // BLK) * BLK

    def spread(parts, count, deps=()):
        shape = bf_shape(count, len(parts) * parts[0].shape[0], parts[0].shape[1])
        return plain(spread_kernel, [], parts, [shape], (0, 1e6, 0), deps)[0]

    def add(a, b, deps=()):
        return plain(add_kernel, [], [a, b], [bf_shape(rows, padded)] * plane, (0, 1e6, 0), deps)

    def deal(parts, count, deps=()):
        shape = bf_shape(count, sum(x.shape[1] for x in parts) // count, parts[0].shape[2])
        return plain(deal_kernel, [], parts, [shape], (0, 1e6, 0), deps)[0]

    def tree(parts):
        while len(parts) > 1:
            parts = [parts[i] + parts[i + 1] for i in range(0, len(parts), 2)]
        return parts[0]

    def near(x, k):
        return lax.ppermute(x, "ctx", [(i, i ^ k) for i in range(nctx)])

    def stacked(parts, deps=()):
        shape = bf_shape(len(parts) * parts[0].shape[0], parts[0].shape[1])
        return plain(join_kernel, [], parts, [shape], (0, 1e6, 0), deps)[0]

    cut = inner // (nctx * nw)

    def targets(count):
        index = jnp.arange(plane * nz * count * cut, dtype=jnp.int32)
        to_k, to_z = index // (nz * count * cut), index // (count * cut) % nz
        to_i, to_t = index // cut % count, index % cut
        column = ((to_z * plane + to_k) * nw + w) * cut + to_t
        which = jnp.arange(count, dtype=jnp.int32)
        return jnp.where(to_i[:, None] == which[None, :], column[:, None], -1).astype(jnp.int32)

    def owner_parts(plan, xs, ys, small=None, deps=()):
        count = sum(len(group) for group in plan)
        total = nz * count * cut
        if small is not None:
            total = -(-(total + 3 * small.shape[0]) // 16) * 16
            ys = ys + [small]
        return plain(
            functools.partial(owners_kernel, wide, plan),
            [],
            [targets(count)] + xs + ys,
            [bf_shape(plane, total, padded)],
            (3e9, 6e6, 0),
            deps,
        )[0]

    def layers(x, deps=()):
        return plain(
            functools.partial(layers_kernel, nz),
            [zed.astype(jnp.int32)[None]],
            [x],
            [bf_shape(x.shape[1] // nz, x.shape[2])] * nz,
            (0, 1e6, 0),
            deps,
        )

    def owner_sums(total, count):
        return [total[i * cut : (i + 1) * cut, :width] for i in range(count)]

    lanes = jnp.arange(nctx, dtype=jnp.int32)
    owner = jnp.sum(jnp.where(assign[None, :] == lanes[:, None], lanes[None, :], 0), axis=1)
    chip_slot = owner % plane * nz + (owner // plane ^ zed)
    near_slot = (owner ^ c) % plane * nz + owner // plane
    meta = jnp.concatenate([owner, jnp.take(assign, c)[None], chip_slot, near_slot])
    meta = meta.astype(jnp.int32)
    core = w.astype(jnp.int32)[None]
    chip = nw * rows

    gains = pair(jnp.stack([gain_self, gain_cross, gain_ffn]), axis=1).astype(F32)
    gains = [gains[i : i + 1] for i in range(3)]
    tok = pair(tokens, tiled=False)

    def head_parts(weights, deps=()):
        count = len(weights) * wide
        shape = bf_shape(nw, weights[0].shape[0], -(-count // BLK) * BLK)
        return plain(functools.partial(heads_kernel, wide), [], weights, [shape], deps=deps)[0]

    g_own = jnp.pad(cotangent, ((0, 0), (0, padded - width)))
    g_parts = [g_own] + [near(g_own, k) for k in range(1, plane)]
    all_heads = halves(
        head_parts(
            [key_weight, value_weight, cross_key, cross_value, query_weight, cross_query]
        )
    )
    n1, q, k_own, v_own, kv_own = plain(
        functools.partial(project_kernel, wide),
        [],
        [tok, all_heads, gains[0]],
        [bf_shape(chip, width)] + [bf_shape(chip, 2 * BLK)] * 3 + [bf_shape(nz, chip, 2 * wide)],
    )

    kv = in_column(kv_own).reshape(-1, 2 * wide)

    hot = (bucket_ids[None, :] == jnp.arange(buckets, dtype=jnp.int32)[:, None]).astype(BF)
    values = dot_tn(lax.dynamic_slice_in_dim(bucket_table, w * nh, nh, 1), hot)
    lines = bias_rows(values)

    enc_pair = pair(encoded)
    (ekv_own,) = plain(
        functools.partial(encode_kernel, wide),
        [],
        [enc_pair, all_heads],
        [bf_shape(enc_pair.shape[0], 4 * BLK)],
        deps=(kv, *g_parts[1:], *lines),
    )

    kv = [kv] + [near(kv, k) for k in range(1, plane)]

    ts, tt = bias_tiles(*lines, deps=(kv[0], ekv_own))

    ekv = lax.all_gather(ekv_own, "ctx", axis=0, tiled=True)
    spots = jnp.stack([(c % plane) * nw + i for i in (w, 1 - w)]).astype(jnp.int32)
    ug_own, ug_sent, wd_own, wd_sent = plain(
        functools.partial(units_kernel, nz, plane * nw, share, slot),
        [spots],
        [gate_weight, up_weight, down_weight.T],
        [bf_shape(gate_weight.shape[0], 2 * nz * slot)] * 2
        + [bf_shape(width, nz // nw * slot)] * 2,
        deps=(ts,),
    )
    g_plane = stacked(g_parts, deps=(ug_own,))
    out_mate, cross_out_mate = mate(out_weight), mate(cross_out)
    o1, a1, qe1, lse1 = self_fwd(
        meta, q, kv, ts, nh, hs, deps=(g_plane, out_mate, cross_out_mate)
    )
    a1_pair = pair(a1, tiled=False)
    h1, n2, cq = plain(
        functools.partial(middle_kernel, wide),
        [core],
        [tok, a1_pair, out_weight, out_mate, gains[1], all_heads],
        [f32_shape(chip, width), bf_shape(chip, width), bf_shape(chip, 2 * BLK)],
    )
    qg = lax.all_gather(qe1, "ctx", axis=0, tiled=True).reshape(nctx, chip, 2 * BLK)
    cq_full, ck_full, cv_full = pair(cross_query), pair(cross_key), pair(cross_value)
    qkv_full = pair(jnp.concatenate([query_weight, key_weight, value_weight], axis=1))

    o2, a2, qe2 = cross_fwd(cq, ekv, nh, hs)
    a2_pair = pair(a2, tiled=False)
    h2, n3 = plain(
        functools.partial(third_kernel, half),
        [core],
        [h1, a2_pair, cross_out, cross_out_mate, gains[2]],
        [f32_shape(rows, width), bf_shape(rows, padded)],
    )

    ug_sent, wd_sent, g_plane, _ = lax.optimization_barrier((ug_sent, wd_sent, g_plane, a2_pair))
    g_plane = g_plane, mate(g_plane)
    ug, wd = plain(
        order_kernel,
        [core],
        [ug_own, mate(ug_sent), wd_own, mate(wd_sent)],
        [bf_shape(width, 2 * nz * slot), bf_shape(width, nz * slot)],
        deps=(n3,),
    )
    (dact,) = plain(
        ffn_early_kernel, [], [*g_plane, wd], [f32_shape(nw * plane * rows, nz * slot)], deps=(n3,)
    )
    n3_plane = stacked([n3] + [near(n3, k) for k in range(1, plane)], deps=(dact,))
    n3_plane = n3_plane, mate(n3_plane)
    act, dgu, dn0, dn1 = ffn_both(n3_plane, dact, ug)
    sent = add(dn0, mate(dn1))
    got = [near(sent[k], k) for k in range(1, plane)]
    ffn, out0, out1 = ffn_late(n3_plane, g_plane, act, dgu, wd, nz, share, (sent[0], qg))
    dh2, dy2, gain3 = plain(
        dh2_kernel,
        [],
        [sent[0]] + got + [h2, g_own, gains[2]],
        [f32_shape(rows, width), bf_shape(rows, padded), f32_shape(1, width)],
        deps=(out0,),
    )

    dy2, de2, _, _ = grad_prep(pair(dy2, tiled=False), cross_out, o2, nh, hs)
    dcq, dekv = cross_bwd(qe2, de2[0], ekv, plane, nz, nh, hs)
    dekv = in_plane(dekv.reshape(plane, -1, 2 * wide))
    dcq_pair = pair(dcq, tiled=False)
    dh1, dy1, gain2 = plain(
        functools.partial(dh1_kernel, wide, half),
        [core],
        [dcq_pair, cq_full, h1, dh2, gains[1]],
        [f32_shape(rows, width), bf_shape(rows, padded), f32_shape(1, width)],
    )

    dy1, de1, dhi1, delta1 = grad_prep(pair(dy1, tiled=False), out_weight, o1, nh, hs)
    dg = [de1[0]] + [near(de1[0], plane * k) for k in range(1, nz)]
    dekv = layers(dekv, deps=(de1,))
    dg = spread(dg, plane, deps=(dekv[0], qg, ck_full, cv_full, qkv_full))
    spread_out = dg
    dekv = [dekv[0]] + [near(dekv[k], plane * k) for k in range(1, nz)]

    dq, rev = self_dq(meta, q, dhi1, lse1, delta1, kv, ts, nh, hs, deps=(dg,))
    dg = in_plane(dg).reshape(nctx, chip, 2 * BLK)
    (dekv,) = plain(output_kernel, [], dekv, [bf_shape(*dekv[0].shape)], deps=(dq,))
    dekv_pair = pair(dekv, tiled=False)
    made = owner_parts(
        ((((0,), 0),), (((1,), 0),), (((2,), 0),), (((3,), 0), ((3,), wide))),
        [a1_pair, a2_pair, dcq_pair, dekv_pair],
        [dy1, dy2, n2, enc_pair],
        deps=(dq,),
    )
    ffn = lax.psum_scatter(
        tie(ffn, spread_out).reshape(nz, 3 * share, padded),
        "ctx",
        scatter_dimension=0,
        axis_index_groups=columns,
        tiled=True,
    )
    dk, dv = self_dkv(meta, k_own, v_own, qg, dg, tt, nh, hs, deps=(made, dq))
    made = in_plane(made)
    rev = tie(rev, dk)

    dqkv_pair = pair(jnp.stack([dq, dk, dv]), tiled=False).reshape(nw, 3, chip, 2 * BLK)
    tokens_grad, gain1 = plain(
        functools.partial(last_kernel, wide, half),
        [core],
        [dqkv_pair, qkv_full, tok, dh1, gains[0]],
        [f32_shape(rows, width), f32_shape(1, width)],
    )

    rev = rev.reshape(nh, 8, -1)
    by_distance = sum(rev[:, i, 1 + i : 1 + i + length] for i in range(8))
    hot_rev = (
        jnp.flip(bucket_ids)[None, :] == jnp.arange(buckets, dtype=jnp.int32)[:, None]
    ).astype(F32)
    table_own = lax.dot_general(
        hot_rev, by_distance, (((1,), (1,)), ((), ())), precision=lax.Precision.HIGHEST
    )
    table = lax.dynamic_update_slice_in_dim(
        jnp.zeros((buckets, heads), F32), table_own, w * nh, 1
    )

    small = jnp.concatenate([gain1[0], gain2[0], gain3[0], table.reshape(-1)])
    small = jnp.pad(small, (0, -small.shape[0] % padded)).reshape(-1, padded)
    extra = small.shape[0]
    plan = ((((0, 0), 0), ((0, 1), 0), ((0, 2), 0)),)
    second = owner_parts(plan, [dqkv_pair], [n1], small)
    second = in_plane(tie(second, made))
    first = layers(made)
    out_sent = add(out0, mate(tie(out1, gain1)), deps=(made,))
    first = [first[0]] + [near(first[k], plane * k) for k in range(1, nz)]
    (second,) = plain(
        functools.partial(deal_last_kernel, 3 * nz * cut, extra),
        [],
        [second],
        [bf_shape(nz, -(-(3 * cut + 3 * extra) // 16) * 16, padded)],
        deps=(first[0], out_sent[0]),
    )
    dealt = second
    out_sent = [tie(m, second) for m in out_sent[1:]], out_sent[0]
    out_got = [near(m, k + 1) for k, m in enumerate(out_sent[0])]
    dekv_pair = tie(dekv_pair, second)
    second = jnp.sum(in_column(second).astype(F32), axis=0)
    small = [second[3 * cut + i * extra : 3 * cut + (i + 1) * extra] for i in range(3)]
    small = (small[0] + small[1]) + small[2]
    small = small + mate(small)
    q_t, k_t, v_t = owner_sums(second, 3)
    (first,) = plain(output_kernel, [], first, [f32_shape(5 * cut, padded)], deps=(dealt,))
    out_share, cross_out_share, cq_t, ck_t, cv_t = owner_sums(first, 5)
    ffn = ffn[0, :, :width].astype(F32).reshape(3, share, width)

    def joined(x):
        return jnp.swapaxes(x[:, :, :wide], 0, 1).reshape(-1, inner)

    def own_encoder(x):
        return lax.dynamic_slice_in_dim(x, w * encoded.shape[0], encoded.shape[0], 0)

    dek, dev = joined(dekv_pair), joined(dekv_pair[:, :, wide:])
    encoded_grad = dot_nt(own_encoder(dek), ck_full) + dot_nt(own_encoder(dev), cv_full)
    (output,) = plain(
        output_kernel,
        [],
        [h2, out_sent[1]] + out_got,
        [bf_shape(rows, width)],
        deps=(second, ffn, encoded_grad),
    )

    small = small.reshape(-1)
    table = small[3 * width : 3 * width + buckets * heads].reshape(buckets, heads)
    return (
        output,
        tokens_grad,
        encoded_grad,
        small[:width],
        small[width : 2 * width],
        small[2 * width : 3 * width],
        q_t.T,
        k_t.T,
        v_t.T,
        out_share,
        cq_t.T,
        ck_t.T,
        cv_t.T,
        cross_out_share,
        ffn[0].T,
        ffn[1].T,
        ffn[2],
        table,
    )


def solution(mesh):
    rows = P(("seq", "ctx", "wsh"), None)
    cols = P("seq", ("ctx", "wsh"))
    split = P("wsh", None)
    return jax.shard_map(
        local,
        mesh=mesh,
        in_specs=(rows, rows, rows, P(), P(), P("wsh"), P("wsh"), P("wsh"))
        + (split,) * 11
        + (P(),),
        out_specs=(
            rows,
            rows,
            rows,
            P("seq"),
            P("seq"),
            P("seq"),
            cols,
            cols,
            cols,
            rows,
            cols,
            cols,
            cols,
            rows,
            cols,
            cols,
            rows,
            P("seq", None),
        ),
        check_vma=False,
    )
```

```python
import functools

import jax
import jax.numpy as jnp
from jax import lax
from jax.experimental import pallas as pl
from jax.experimental.pallas import tpu as pltpu
from jax.sharding import PartitionSpec as P

EPS = 1e-06
NEG = -1e30
F32 = jnp.float32
BF = jnp.bfloat16
BLK = 128
GRP = 4
UNROLL = 3
CH = BLK * GRP
VLIM = 60 * 1024 * 1024
SLOW = 64


def unrolled(steps):
    return steps if steps <= 3 * UNROLL else UNROLL


def dot(a, b):
    return lax.dot_general(a, b, (((1,), (0,)), ((), ())), preferred_element_type=F32)


def dot_nt(a, b):
    return lax.dot_general(a, b, (((1,), (1,)), ((), ())), preferred_element_type=F32)


def dot_tn(a, b):
    return lax.dot_general(a, b, (((0,), (0,)), ((), ())), preferred_element_type=F32)


def lane_of(shape):
    return lax.broadcasted_iota(jnp.int32, shape, 1)


def head_mask(value, head, hs):
    lane = lane_of(value.shape)
    keep = (lane >= head * hs) & (lane < (head + 1) * hs)
    return jnp.where(keep, value, jnp.zeros_like(value))


def lane_fold(value, op):
    out = value[:, :BLK]
    for i in range(1, value.shape[1] // BLK):
        out = op(out, value[:, i * BLK : (i + 1) * BLK])
    return out


def pieces_into(base, columns, first):
    lane = lane_of(base.shape)
    out = base
    for i, column in enumerate(columns):
        rest = column
        for j in range(3):
            part = rest.astype(BF).astype(F32)
            rest = rest - part
            out = jnp.where(lane == first + 3 * i + j, part, out)
    return out


def params(flops, nbytes, trans):
    return dict(
        compiler_params=pltpu.CompilerParams(vmem_limit_bytes=VLIM),
        cost_estimate=pl.CostEstimate(
            flops=int(flops) // SLOW,
            bytes_accessed=int(nbytes) // SLOW,
            transcendentals=int(trans) // SLOW,
        ),
    )


def after(value, *deps):
    return lax.optimization_barrier((value,) + deps)[0]


def f32_shape(*dims):
    return jax.ShapeDtypeStruct(dims, F32)


def bf_shape(*dims):
    return jax.ShapeDtypeStruct(dims, BF)


def plain(kernel, scalars, inputs, outputs, cost=(1e9, 4e6, 0), deps=()):
    count, late = len(scalars) + len(inputs), len(deps)

    def body(*refs):
        kernel(*refs[:count], *refs[count + late :])

    return pl.pallas_call(
        body,
        in_specs=[SM] * len(scalars) + [VM] * len(inputs) + [ANY] * late,
        out_specs=[VM] * len(outputs),
        out_shape=list(outputs),
        **params(*cost),
    )(*scalars, *inputs, *deps)


VM = pl.BlockSpec(memory_space=pltpu.VMEM)
ANY = pl.BlockSpec(memory_space=pl.ANY)
SM = pl.BlockSpec(memory_space=pltpu.SMEM)


def tie(x, *deps):
    return pl.pallas_call(
        lambda *refs: None,
        in_specs=[ANY] * (1 + len(deps)),
        out_specs=ANY,
        out_shape=jax.ShapeDtypeStruct(x.shape, x.dtype),
        input_output_aliases={0: 0},
        **params(0, 0, 0),
    )(x, *deps)


def bias_kernel(nb, nh, nat_ref, rev_ref, ts_ref, tt_ref):
    row = lax.broadcasted_iota(jnp.int32, (BLK, BLK), 0)
    col = lax.broadcasted_iota(jnp.int32, (BLK, BLK), 1)
    upper = col >= row

    def skew(line):
        eight = pltpu.roll(jnp.broadcast_to(line, (8, BLK)), 0, 1, stride=1, stride_axis=0)
        return jnp.concatenate(
            [eight] + [pltpu.roll(eight, 8 * i, 1) for i in range(1, BLK // 8)], axis=0
        )

    def step(r, carry):
        d = nb - 1 - r
        first, second = rev_ref[nb - jnp.maximum(d, 0)], rev_ref[nb - 1 - jnp.maximum(d, 0)]
        for h in range(nh):
            tile = jnp.where(upper, skew(first[h : h + 1]), skew(second[h : h + 1]))
            ts_ref[r, h] = jnp.where(d * BLK + row - col >= 0, tile, NEG).astype(BF)
        d = r - (GRP - 1)
        first, second = nat_ref[jnp.maximum(d, 0) + 1], nat_ref[jnp.maximum(d, 0)]
        for h in range(nh):
            tile = jnp.where(upper, skew(first[h : h + 1]), skew(second[h : h + 1]))
            tt_ref[r, h] = jnp.where(d * BLK + col - row >= 0, tile, NEG).astype(BF)
        return carry

    lax.fori_loop(0, nb + GRP - 1, step, 0)


def bias_rows(values):
    nh, length = values.shape
    nb = length // BLK
    zero = jnp.zeros((nh, 1), F32)
    nat = jnp.concatenate([jnp.zeros((nh, BLK), F32), values], axis=1)
    rev = jnp.concatenate([zero, jnp.flip(values, 1), jnp.zeros((nh, BLK - 1), F32)], axis=1)
    nat = jnp.transpose(nat.reshape(nh, nb + 1, BLK), (1, 0, 2))
    rev = jnp.transpose(rev.reshape(nh, nb + 1, BLK), (1, 0, 2))
    return nat, rev


def bias_tiles(nat, rev, deps=()):
    nb, nh = nat.shape[0] - 1, nat.shape[1]
    shape = bf_shape(nb + GRP - 1, nh, BLK, BLK)
    return plain(
        functools.partial(bias_kernel, nb, nh), [], [nat, rev], [shape, shape], deps=deps
    )


def gather_blocks(ref, meta_ref, nctx, first, lo, hi, base=0):
    parts = []
    for i in range(GRP):
        t = first + i
        early = t < nctx
        slot = meta_ref[base + jnp.where(early, t, 2 * nctx - 1 - t)]
        at = pl.multiple_of(jnp.where(early, 0, BLK), BLK)
        parts.append(ref[slot, pl.ds(at, BLK), lo:hi])
    return jnp.concatenate(parts, axis=0)


def fetch(parts, held_ref, sem):
    rows = parts[0].shape[0]
    copies = [
        pltpu.make_async_copy(part, held_ref.at[pl.ds(k * rows, rows)], sem.at[k])
        for k, part in enumerate(parts)
    ]
    for copy in copies:
        copy.start()
    for copy in copies:
        copy.wait()


def bias_of(ref, first):
    rows = ref.shape[1] * BLK
    return jnp.concatenate(
        [ref[first + i].reshape(rows, BLK) for i in range(GRP)], axis=1
    ).astype(F32)


def stack_heads(value, hs, nh, shift=0):
    return jnp.concatenate([head_mask(value, h + shift, hs) for h in range(nh)], axis=0)


def merge_heads(stacked, hs, nh, shift=0):
    rows = stacked.shape[0] // nh
    total = jnp.zeros((rows, stacked.shape[1]), F32)
    for h in range(nh):
        total = total + head_mask(stacked[h * rows : (h + 1) * rows], h + shift, hs)
    return total


def pick_columns(columns, nh, rows):
    out = jnp.zeros((rows, BLK), F32)
    lane = lane_of(out.shape)
    for h in range(nh):
        out = jnp.where(lane == h, columns[h * rows : (h + 1) * rows], out)
    return out


def stack_columns(ref, rows, nh):
    return jnp.concatenate([ref[rows, h : h + 1] for h in range(nh)], axis=0)


def self_fwd_kernel(count, nctx, nh, hs, meta_ref, q_ref, ts_ref, *rest):
    o_ref, a_ref, qe_ref, lse_ref, qm_ref, s_ref, acc_ref, top_ref, sum_ref, flat_ref, sem = rest[-11:]
    fetch(rest[:count], flat_ref, sem)
    kv_ref = flat_ref.reshape(nctx, 2 * BLK, flat_ref.shape[1])
    nb = 2 * nctx
    wide = nh * hs
    early = meta_ref[nctx]
    split = early // GRP + 1
    base = 2 * nctx + 1
    for half in range(2):
        qm_ref[half] = stack_heads(q_ref[half * BLK : (half + 1) * BLK, :], hs, nh)
    top_ref[...] = jnp.full(top_ref.shape, NEG, F32)
    sum_ref[...] = jnp.zeros_like(sum_ref)
    acc_ref[...] = jnp.zeros_like(acc_ref)

    def place(step):
        half = (step >= split).astype(jnp.int32)
        return half, step - half * split

    def score(step, carry):
        half, ch = place(step)
        blk = jnp.where(half == 0, early, nb - 1 - early)
        keys = gather_blocks(kv_ref, meta_ref, nctx, ch * GRP, 0, 2 * BLK, base)
        s = dot_nt(qm_ref[half], keys) + bias_of(ts_ref, nb - 1 - blk + ch * GRP)
        s_ref[step] = s
        top_ref[half] = jnp.maximum(top_ref[half], lane_fold(s, jnp.maximum))
        return carry

    steps = nb // GRP + 1
    lax.fori_loop(0, steps, score, 0, unroll=unrolled(nb // GRP + 1))
    for half in range(2):
        top = jnp.max(top_ref[half], axis=1, keepdims=True)
        top_ref[half] = jnp.broadcast_to(top, top_ref.shape[1:])

    def weigh(step, carry):
        half, ch = place(step)
        vals = gather_blocks(kv_ref, meta_ref, nctx, ch * GRP, BLK, 3 * BLK, base)
        top = top_ref[half]
        p = jnp.exp(s_ref[step] - jnp.concatenate([top] * GRP, axis=1))
        acc_ref[half] += dot(p.astype(BF), vals)
        sum_ref[half] += lane_fold(p, jnp.add)
        return carry

    lax.fori_loop(0, steps, weigh, 0, unroll=unrolled(nb // GRP + 1))
    for half in range(2):
        rows = slice(half * BLK, (half + 1) * BLK)
        total = jnp.sum(sum_ref[half], axis=1, keepdims=True)
        o = pltpu.roll(merge_heads(acc_ref[half] / total, hs, nh, 1), 2 * BLK - hs, 1)
        o_ref[rows, :] = o
        a_ref[rows, :] = o[:, :wide].astype(BF)
        lse = pick_columns(top_ref[half][:, :1] + jnp.log(total), nh, BLK)
        lse_ref[rows, :] = lse
        minus = [-lse[:, h : h + 1] for h in range(nh)]
        qe_ref[rows, :] = pieces_into(q_ref[rows, :].astype(F32), minus, wide).astype(BF)


def self_fwd(meta, q, kv, ts, nh, hs, deps=()):
    nctx = len(kv) * kv[0].shape[0] // (2 * BLK)
    nb = 2 * nctx
    rows = 2 * BLK
    pairs = (nb + 1) * BLK * BLK * nh
    return pl.pallas_call(
        functools.partial(self_fwd_kernel, len(kv), nctx, nh, hs),
        in_specs=[SM, VM, VM] + [ANY] * (len(kv) + len(deps)),
        out_specs=[VM] * 4,
        out_shape=[
            f32_shape(rows, rows),
            bf_shape(rows, nh * hs),
            bf_shape(rows, rows),
            f32_shape(rows, BLK),
        ],
        scratch_shapes=[
            pltpu.VMEM((2, nh * BLK, 2 * BLK), BF),
            pltpu.VMEM((nb // GRP + 1, nh * BLK, CH), F32),
            pltpu.VMEM((2, nh * BLK, 2 * BLK), F32),
            pltpu.VMEM((2, nh * BLK, BLK), F32),
            pltpu.VMEM((2, nh * BLK, BLK), F32),
            pltpu.VMEM((nb * BLK, kv[0].shape[1]), BF),
            pltpu.SemaphoreType.DMA((len(kv),)),
        ],
        **params(pairs * 2 * 512, 10e6, pairs),
    )(meta, q, ts, *kv, *deps)


def self_dq_kernel(count, nctx, nh, hs, meta_ref, q_ref, da_ref, lse_ref, del_ref, ts_ref, *rest):
    dq_ref, rev_ref, qm_ref, dm_ref, col_ref, acc_ref, flat_ref, sem = rest[-8:]
    fetch(rest[:count], flat_ref, sem)
    kv_ref = flat_ref.reshape(nctx, 2 * BLK, flat_ref.shape[1])
    nb = 2 * nctx
    early = meta_ref[nctx]
    split = early // GRP + 1
    span = CH + BLK
    rev_ref[...] = jnp.zeros_like(rev_ref)
    acc_ref[...] = jnp.zeros_like(acc_ref)
    for half in range(2):
        rows = slice(half * BLK, (half + 1) * BLK)
        qm_ref[half] = stack_heads(q_ref[rows, :], hs, nh)
        dm_ref[half] = stack_heads(da_ref[rows, :], hs, nh, 1)
        for i, ref in enumerate((lse_ref, del_ref)):
            col_ref[half, i] = jnp.broadcast_to(stack_columns(ref, rows, nh), col_ref.shape[2:])

    def step(at, carry):
        half = (at >= split).astype(jnp.int32)
        ch = at - half * split
        blk = jnp.where(half == 0, early, nb - 1 - early)
        held = gather_blocks(kv_ref, meta_ref, nctx, ch * GRP, 0, 3 * BLK, 2 * nctx + 1)
        keys, vals = held[:, : 2 * BLK], held[:, BLK:]
        off = pl.multiple_of((ch * GRP - blk + nb - 1) * BLK, BLK)
        s = dot_nt(qm_ref[half], keys) + bias_of(ts_ref, nb - 1 - blk + ch * GRP)
        p = jnp.exp(s - jnp.concatenate([col_ref[half, 0]] * GRP, axis=1))
        delta = jnp.concatenate([col_ref[half, 1]] * GRP, axis=1)
        ds = (p * (dot_nt(dm_ref[half], vals) - delta)).astype(BF)
        acc_ref[half] += dot(ds, keys)
        flat = jnp.concatenate([jnp.zeros((nh * BLK, BLK), F32), ds.astype(F32)], axis=1)
        for h in range(nh):
            line = flat[h * BLK : h * BLK + 8]
            for i in range(1, BLK // 8):
                first = h * BLK + 8 * i
                line = line + pltpu.roll(flat[first : first + 8], span - 8 * i, 1)
            rev_ref[h * 8 : (h + 1) * 8, pl.ds(off, span)] += line
        return carry

    lax.fori_loop(0, nb // GRP + 1, step, 0, unroll=unrolled(nb // GRP + 1))
    for half in range(2):
        dq_ref[half * BLK : (half + 1) * BLK, :] = merge_heads(acc_ref[half], hs, nh).astype(BF)


def self_dq(meta, q, da, lse, delta, kv, ts, nh, hs, deps=()):
    nctx = len(kv) * kv[0].shape[0] // (2 * BLK)
    nb = 2 * nctx
    pairs = (nb + 1) * BLK * BLK * nh
    return pl.pallas_call(
        functools.partial(self_dq_kernel, len(kv), nctx, nh, hs),
        in_specs=[SM] + [VM] * 5 + [ANY] * (len(kv) + len(deps)),
        out_specs=[VM, VM],
        out_shape=[
            jax.ShapeDtypeStruct((2 * BLK, 2 * BLK), BF),
            jax.ShapeDtypeStruct((8 * nh, nb * BLK + CH), F32),
        ],
        scratch_shapes=[
            pltpu.VMEM((2, nh * BLK, 2 * BLK), BF),
            pltpu.VMEM((2, nh * BLK, 2 * BLK), BF),
            pltpu.VMEM((2, 2, nh * BLK, BLK), F32),
            pltpu.VMEM((2, nh * BLK, 2 * BLK), F32),
            pltpu.VMEM((nb * BLK, kv[0].shape[1]), BF),
            pltpu.SemaphoreType.DMA((len(kv),)),
        ],
        **params(pairs * 2 * 896, 10e6, pairs),
    )(meta, q, da, lse, delta, ts, *kv, *deps)


def self_dkv_kernel(
    nctx, nh, hs, meta_ref, k_ref, v_ref, qg_ref, dg_ref, tt_ref, *rest
):
    dk_ref, dv_ref, km_ref, vm_ref, ka_ref, va_ref = rest[-6:]
    nb = 2 * nctx
    wide = nh * hs
    early = meta_ref[nctx]
    late = nb - 1 - early
    split = nb // GRP - early // GRP

    def extended(value):
        lane = lane_of(value.shape)
        parts = []
        for h in range(nh):
            first = wide + 3 * h
            ones = (lane >= first) & (lane < first + 3)
            parts.append(jnp.where(ones, jnp.ones_like(value), head_mask(value, h, hs)))
        return jnp.concatenate(parts, axis=0)

    ka_ref[...] = jnp.zeros_like(ka_ref)
    va_ref[...] = jnp.zeros_like(va_ref)
    for half in range(2):
        rows = slice(half * BLK, (half + 1) * BLK)
        km_ref[half] = extended(k_ref[rows, :])
        vm_ref[half] = extended(v_ref[rows, :])

    def step(at, carry):
        half = (at >= split).astype(jnp.int32)
        blk = jnp.where(half == 0, early, late)
        ch = at - half * split + blk // GRP
        qc = gather_blocks(qg_ref, meta_ref, nctx, ch * GRP, 0, 2 * BLK)
        dc = gather_blocks(dg_ref, meta_ref, nctx, ch * GRP, 0, 2 * BLK, nctx + 1)
        p = jnp.exp(dot_nt(km_ref[half], qc) + bias_of(tt_ref, ch * GRP - blk + GRP - 1))
        ds = (p * dot_nt(vm_ref[half], dc)).astype(BF)
        ka_ref[half] += dot(ds, qc)
        va_ref[half] += dot(p.astype(BF), dc)
        return carry

    lax.fori_loop(0, nb // GRP + 1, step, 0, unroll=unrolled(nb // GRP + 1))
    for half in range(2):
        rows = slice(half * BLK, (half + 1) * BLK)
        dk_ref[rows, :] = merge_heads(ka_ref[half], hs, nh).astype(BF)
        dv_ref[rows, :] = merge_heads(va_ref[half], hs, nh).astype(BF)


def self_dkv(meta, k, v, qg, dg, tt, nh, hs, deps=()):
    nctx = qg.shape[0]
    nb = 2 * nctx
    pairs = (nb + 1) * BLK * BLK * nh
    return pl.pallas_call(
        functools.partial(self_dkv_kernel, nctx, nh, hs),
        in_specs=[SM] + [VM] * 5 + [ANY] * len(deps),
        out_specs=[VM, VM],
        out_shape=[bf_shape(2 * BLK, 2 * BLK)] * 2,
        scratch_shapes=[
            pltpu.VMEM((2, nh * BLK, 2 * BLK), BF),
            pltpu.VMEM((2, nh * BLK, 2 * BLK), BF),
            pltpu.VMEM((2, nh * BLK, 2 * BLK), F32),
            pltpu.VMEM((2, nh * BLK, 2 * BLK), F32),
        ],
        **params(pairs * 2 * 1024, 10e6, pairs),
    )(meta, k, v, qg, dg, tt, *deps)


def cross_fwd_kernel(nh, hs, q_ref, e_ref, o_ref, a_ref, qe_ref, s_ref):
    wide = nh * hs
    chunks = e_ref.shape[0] // CH
    rows = q_ref.shape[0]
    q = q_ref[...]
    qm = stack_heads(q, hs, nh)
    top = jnp.full((nh * rows, BLK), NEG, F32)
    for ch in range(chunks):
        s = dot_nt(qm, e_ref[ch * CH : (ch + 1) * CH, : 2 * BLK])
        s_ref[ch] = s
        top = jnp.maximum(top, lane_fold(s, jnp.maximum))
    top = jnp.max(top, axis=1, keepdims=True)
    total = jnp.zeros((nh * rows, BLK), F32)
    acc = jnp.zeros((nh * rows, 2 * BLK), F32)
    for ch in range(chunks):
        p = jnp.exp(s_ref[ch] - top)
        total = total + lane_fold(p, jnp.add)
        acc = acc + dot(p.astype(BF), e_ref[ch * CH : (ch + 1) * CH, 2 * BLK :])
    total = jnp.sum(total, axis=1, keepdims=True)
    o = merge_heads(acc / total, hs, nh)
    o_ref[...] = o
    a_ref[...] = o[:, :wide].astype(BF)
    lse = pick_columns(top + jnp.log(total), nh, rows)
    minus = [-lse[:, h : h + 1] for h in range(nh)]
    qe_ref[...] = pieces_into(q.astype(F32), minus, wide).astype(BF)


def cross_fwd(q, e, nh, hs):
    enc = e.shape[0]
    rows = 2 * BLK
    pairs = rows * enc * nh
    return pl.pallas_call(
        functools.partial(cross_fwd_kernel, nh, hs),
        in_specs=[VM, VM],
        out_specs=[VM] * 3,
        out_shape=[f32_shape(rows, rows), bf_shape(rows, nh * hs), bf_shape(rows, rows)],
        scratch_shapes=[pltpu.VMEM((enc // CH, nh * rows, CH), F32)],
        **params(pairs * 2 * 512, 4e6, pairs),
    )(q, e)


def cross_bwd_kernel(plane, nz, nh, hs, qe_ref, de_ref, all_ref, dq_ref, dkv_ref, e_ref, acc_ref, sem):
    size = all_ref.shape[0] // (plane * nz)
    copies = []
    for k in range(plane):
        for z in range(nz):
            source = all_ref.at[pl.ds((z * plane + k) * size, size)]
            target = e_ref.at[pl.ds((k * nz + z) * size, size)]
            copies.append(pltpu.make_async_copy(source, target, sem.at[k, z]))
    for copy in copies:
        copy.start()
    for copy in copies:
        copy.wait()
    wide = nh * hs
    acc_ref[...] = jnp.zeros_like(acc_ref)

    def kept(value, h):
        lane = lane_of(value.shape)
        first = wide + 3 * h
        keep = ((lane >= h * hs) & (lane < (h + 1) * hs)) | ((lane >= first) & (lane < first + 3))
        return jnp.where(keep, value, jnp.zeros_like(value))

    qm = [kept(qe_ref[...], h) for h in range(nh)]
    dm = [kept(de_ref[...], h) for h in range(nh)]

    for ch in range(e_ref.shape[0] // CH):
        rows = slice(ch * CH, (ch + 1) * CH)
        ek = e_ref[rows, : 2 * BLK]
        ev = e_ref[rows, 2 * BLK :]
        ek_t = jnp.transpose(ek.astype(F32)).astype(BF)
        dk = jnp.zeros((CH, 2 * BLK), F32)
        dv = jnp.zeros((CH, 2 * BLK), F32)
        for h in range(nh):
            p = jnp.exp(dot_nt(ek, qm[h]))
            ds = (p * dot_nt(ev, dm[h])).astype(BF)
            dk = dk + dot(ds, qm[h])
            dv = dv + dot(p.astype(BF), dm[h])
            acc_ref[h * hs : (h + 1) * hs, :] += dot(ek_t[h * hs : (h + 1) * hs, :], ds)
        dkv_ref[rows, :] = jnp.concatenate([dk[:, :wide], dv[:, :wide]], axis=1).astype(BF)
    dq_ref[...] = jnp.transpose(acc_ref[...]).astype(BF)


def cross_bwd(qe, de, e, plane, nz, nh, hs):
    enc = e.shape[0]
    pairs = 2 * BLK * enc * nh
    return pl.pallas_call(
        functools.partial(cross_bwd_kernel, plane, nz, nh, hs),
        in_specs=[VM, VM, ANY],
        out_specs=[VM, VM],
        out_shape=[bf_shape(2 * BLK, 2 * BLK), bf_shape(enc, 2 * nh * hs)],
        scratch_shapes=[
            pltpu.VMEM((enc, 4 * BLK), BF),
            pltpu.VMEM((2 * BLK, 2 * BLK), F32),
            pltpu.SemaphoreType.DMA((plane, nz)),
        ],
        **params(pairs * 2 * 1024, 4e6, pairs),
    )(qe, de, e)


def scale_of(rows):
    return lax.rsqrt(jnp.mean(rows * rows, axis=-1, keepdims=True) + EPS)


def norm_back(rows, gain, grad):
    rr = scale_of(rows)
    scaled = gain * grad
    shared = jnp.mean(rows * scaled, axis=-1, keepdims=True)
    dv = rr * scaled - rows * (rr * rr * rr) * shared
    return dv, jnp.sum(rows * rr * grad, axis=0, keepdims=True)


def in_blocks(pair_ref):
    half = pair_ref.shape[1] // 2
    return jnp.concatenate(
        [pair_ref[m, i * half : (i + 1) * half] for i in range(2) for m in range(2)], axis=0
    )


def put(ref, value):
    cols = value.shape[1]
    ref[:, :cols] = value
    if ref.shape[1] > cols:
        ref[:, cols:] = jnp.zeros((ref.shape[0], ref.shape[1] - cols), ref.dtype)


def own_of(ref, w, half):
    return jnp.concatenate(
        [ref[pl.ds(pl.multiple_of(i * BLK + w * half, half), half), :] for i in range(2)], axis=0
    )


def project_kernel(wide, tok_ref, w_ref, gain_ref, n1_ref, q_ref, k_ref, v_ref, kv_ref):
    x = in_blocks(tok_ref).astype(F32)
    n1 = (x * scale_of(x) * gain_ref[...]).astype(BF)
    n1_ref[...] = n1
    cut = w_ref.shape[1]

    def product(first, count):
        cols = slice(first * wide, (first + count) * wide)
        return (dot(n1[:, :cut], w_ref[0, :, cols]) + dot(n1[:, cut:], w_ref[1, :, cols])).astype(BF)

    kv = product(0, 2)
    for i in range(kv_ref.shape[0]):
        kv_ref[i] = kv
    zero = jnp.zeros((x.shape[0], 2 * BLK), BF)
    for ref, value in ((k_ref, kv[:, :wide]), (v_ref, kv[:, wide:]), (q_ref, product(4, 1))):
        ref[...] = zero
        ref[:, :wide] = value


def encode_kernel(wide, enc_ref, w_ref, out_ref):
    x = enc_ref[...]
    cut = w_ref.shape[1]
    cols = slice(2 * wide, 4 * wide)
    made = dot(x[:, :cut], w_ref[0, :, cols]) + dot(x[:, cut:], w_ref[1, :, cols])
    made = made.astype(BF)
    out_ref[...] = jnp.ones(out_ref.shape, BF)
    out_ref[:, :wide] = made[:, :wide]
    out_ref[:, 2 * BLK : 2 * BLK + wide] = made[:, wide:]


def middle_kernel(
    wide, core_ref, tok_ref, a_ref, own_ref, mate_ref, gain_ref, w_ref, h_ref, n_ref, cq_ref
):
    w = core_ref[0]
    h = in_blocks(tok_ref).astype(F32)
    h = h + (dot(a_ref[w], own_ref[...]) + dot(a_ref[1 - w], mate_ref[...]))
    h_ref[...] = h
    n = (h * scale_of(h) * gain_ref[...]).astype(BF)
    n_ref[...] = n
    cut = w_ref.shape[1]
    cols = slice(5 * wide, 6 * wide)
    made = dot(n[:, :cut], w_ref[0, :, cols]) + dot(n[:, cut:], w_ref[1, :, cols])
    cq_ref[...] = jnp.zeros(cq_ref.shape, BF)
    cq_ref[:, :wide] = made.astype(BF)


def third_kernel(half, w_ref, h1_ref, a_ref, own_ref, mate_ref, gain_ref, h_ref, n_ref):
    w = w_ref[0]
    h = own_of(h1_ref, w, half)
    for m, ref in ((w, own_ref), (1 - w, mate_ref)):
        h = h + dot(own_of(a_ref.at[m], w, half), ref[...])
    h_ref[...] = h
    put(n_ref, (h * scale_of(h) * gain_ref[...]).astype(BF))


def heads_kernel(wide, *refs):
    *weights, out_ref = refs
    last = out_ref.shape[2] - len(weights) * wide
    for m in range(out_ref.shape[0] if last else 0):
        out_ref[m, :, len(weights) * wide :] = jnp.zeros((out_ref.shape[1], last), BF)
    for i, ref in enumerate(weights):
        for m in range(out_ref.shape[0]):
            out_ref[m, :, i * wide : (i + 1) * wide] = ref[:, m * wide : (m + 1) * wide]


def units_kernel(nz, step, share, slot, spot_ref, gate_ref, up_ref, down_ref, *outs):
    def move(ref, out, first, at):
        base = pl.multiple_of(jnp.minimum(first // BLK * BLK, ref.shape[1] - 2 * BLK), BLK)
        window = ref[:, pl.ds(base, 2 * BLK)].astype(F32)
        window = pltpu.roll(window, 2 * BLK - (first - base), 1)[:, :BLK]
        window = jnp.where(lane_of(window.shape) < share, window, 0.0)
        out[:, at : at + slot] = window.astype(BF)[:, :slot]

    for m in range(2):
        ug_ref, wd_ref = outs[m], outs[2 + m]
        for z in range(nz):
            first = (z * step + spot_ref[m]) * share
            move(gate_ref, ug_ref, first, z * slot)
            move(up_ref, ug_ref, first, (nz + z) * slot)
        for z in range(wd_ref.shape[1] // slot):
            move(down_ref, wd_ref, (z * step + spot_ref[m]) * share, z * slot)


def in_order(w, own_ref, mate_ref, axis):
    own, other = own_ref[...], mate_ref[...]
    return jnp.concatenate(
        [jnp.where(w == 0, own, other), jnp.where(w == 0, other, own)], axis=axis
    )


def order_kernel(core_ref, own_ref, mate_ref, down_ref, down_mate_ref, ug_ref, wd_ref):
    ug_ref[...] = in_order(core_ref[0], own_ref, mate_ref, 0)
    wd_ref[...] = in_order(core_ref[0], down_ref, down_mate_ref, 1)


def ffn_early_kernel(g0_ref, g1_ref, wd_ref, out_ref):
    width = wd_ref.shape[0]
    rows = g0_ref.shape[0]
    for i, ref in enumerate((g0_ref, g1_ref)):
        out_ref[i * rows : (i + 1) * rows, :] = dot(ref[:, :width], wd_ref[...])


def ffn_kernel(n0_ref, n1_ref, da_ref, ug_ref, act_ref, dgu_ref, d0_ref, d1_ref):
    own = pl.program_id(0) < pl.num_programs(0) // 2
    units = act_ref.shape[1]
    width = ug_ref.shape[0]
    n = jnp.where(own, n0_ref[:, :width], n1_ref[:, :width])
    gate = dot(n, ug_ref[:, :units])
    up = dot(n, ug_ref[:, units:])
    da = da_ref[...]
    scale = 0.7978845608028654
    inner = jnp.tanh(scale * (gate + 0.044715 * gate * gate * gate))
    gelu = 0.5 * gate * (1.0 + inner)
    slope = 0.5 * (1.0 + inner) + 0.5 * gate * (1.0 - inner * inner) * scale * (
        1.0 + 3.0 * 0.044715 * gate * gate
    )
    act_ref[...] = (gelu * up).astype(BF)
    dg = (da * up * slope).astype(BF)
    du = (da * gelu).astype(BF)
    dgu_ref[:, :units] = dg
    dgu_ref[:, units:] = du
    dn = (dot_nt(dg, ug_ref[:, :units]) + dot_nt(du, ug_ref[:, units:])).astype(BF)

    @pl.when(own)
    def _():
        put(d0_ref, dn)

    @pl.when(jnp.logical_not(own))
    def _():
        put(d1_ref, dn)


def half_specs(tiles, cols):
    tile = 4 * BLK
    return [
        pl.BlockSpec((tile, cols), lambda i: (jnp.minimum(i, tiles // 2 - 1), 0)),
        pl.BlockSpec((tile, cols), lambda i: (jnp.maximum(i - tiles // 2, 0), 0)),
    ]


def ffn_both(n, da, ug):
    rows, padded = 2 * n[0].shape[0], n[0].shape[1]
    width, units = ug.shape[0], ug.shape[1] // 2
    tiles = rows // (4 * BLK)

    def row(cols):
        return pl.BlockSpec((4 * BLK, cols), lambda i: (i, 0))

    halved = half_specs(tiles, padded)
    return pl.pallas_call(
        ffn_kernel,
        grid=(tiles,),
        in_specs=halved + [row(units), pl.BlockSpec(ug.shape, lambda i: (0, 0))],
        out_specs=[row(units), row(2 * units)] + halved,
        out_shape=[bf_shape(rows, units), bf_shape(rows, 2 * units)]
        + [bf_shape(rows // 2, padded)] * 2,
        **params(10 * rows * width * units, 12e6, rows * units),
    )(*n, da, ug)


def ffn_late_kernel(nz, share, late, n0_ref, n1_ref, g0_ref, g1_ref, act_ref, dgu_ref, wd_ref, *rest):
    w_ref, o0_ref, o1_ref, acc_ref = rest[late:]
    i = pl.program_id(0)
    own = i < pl.num_programs(0) // 2
    units = act_ref.shape[1]
    @pl.when(i == 0)
    def _():
        acc_ref[...] = jnp.zeros_like(acc_ref)

    n = jnp.where(own, n0_ref[...], n1_ref[...])
    g = jnp.where(own, g0_ref[...], g1_ref[...])
    acc_ref[: 2 * units, :] += dot_tn(dgu_ref[...], n)
    acc_ref[2 * units :, :] += dot_tn(act_ref[...], g)
    made = dot_nt(act_ref[...], wd_ref[...]).astype(BF)

    @pl.when(own)
    def _():
        put(o0_ref, made)

    @pl.when(jnp.logical_not(own))
    def _():
        put(o1_ref, made)

    @pl.when(i == pl.num_programs(0) - 1)
    def _():
        for z in range(nz):
            for j in range(3):
                first = j * units + z * (units // nz)
                w_ref[z, j] = acc_ref[first : first + share, :].astype(BF)


def ffn_late(n, g, act, dgu, wd, nz, share, deps):
    rows, padded = act.shape[0], n[0].shape[1]
    width, units = wd.shape
    tiles = rows // (4 * BLK)

    def row(cols):
        return pl.BlockSpec((4 * BLK, cols), lambda i: (i, 0))

    halved = half_specs(tiles, padded)
    return pl.pallas_call(
        functools.partial(ffn_late_kernel, nz, share, len(deps)),
        grid=(tiles,),
        in_specs=halved
        + halved
        + [row(units), row(2 * units), pl.BlockSpec(wd.shape, lambda i: (0, 0))]
        + [ANY] * len(deps),
        out_specs=[pl.BlockSpec((nz, 3, share, padded), lambda i: (0, 0, 0, 0))] + halved,
        out_shape=[bf_shape(nz, 3, share, padded)] + [bf_shape(rows // 2, padded)] * 2,
        scratch_shapes=[pltpu.VMEM((3 * units, padded), F32)],
        **params(8 * rows * width * units, 20e6, 0),
    )(*n, *g, act, dgu, wd, *deps)


def add_kernel(a_ref, b_ref, *outs):
    rows = outs[0].shape[0]
    for k, out in enumerate(outs):
        at = slice(k * rows, (k + 1) * rows)
        out[...] = (a_ref[at].astype(F32) + b_ref[at].astype(F32)).astype(BF)


def output_kernel(*refs):
    *parts, out_ref = refs
    width = out_ref.shape[1]
    total = parts[0][:, :width].astype(F32)
    for part in parts[1:]:
        total = total + part[:, :width].astype(F32)
    out_ref[...] = total.astype(out_ref.dtype)


def join_kernel(*refs):
    *parts, out_ref = refs
    rows = parts[0].shape[0]
    for i, part in enumerate(parts):
        out_ref[i * rows : (i + 1) * rows, :] = part[...]


def spread_kernel(*refs):
    *parts, out_ref = refs
    rows = parts[0].shape[0]
    for i in range(out_ref.shape[0]):
        for j, part in enumerate(parts):
            out_ref[i, j * rows : (j + 1) * rows, :] = part[...]


def split_rows(value):
    parts = []
    for _ in range(3):
        part = value.astype(BF).astype(F32)
        value = value - part
        parts.append(part)
    return jnp.concatenate(parts, axis=0)


def owners_kernel(wide, plan, target_ref, *refs):
    sets = 1 + max(s[0] for group in plan for s, _ in group)
    xs, ys, out_ref = refs[:sets], refs[sets : sets + len(plan)], refs[-1]
    rows = target_ref.shape[0] // out_ref.shape[0]
    extra = refs[-2] if len(refs) > sets + len(plan) + 1 else None
    count = target_ref.shape[0]
    total = jnp.zeros((count, ys[0].shape[1]), F32)
    column = 0
    for group, y in zip(plan, ys):
        picked = jnp.zeros((count, y.shape[0]), F32)
        for which, first in group:
            x = xs[which[0]]
            lane = lane_of((count, x.shape[-1]))
            inside = (lane >= first) & (lane < first + wide)
            for m in range(2):
                hit = inside & (lane - first + m * wide == target_ref[:, column : column + 1])
                picked = picked + dot_nt(hit.astype(BF), x[(m,) + which[1:]])
            column += 1
        total = total + dot(picked.astype(BF), y[...])
    for k in range(out_ref.shape[0]):
        part = total[k * rows : (k + 1) * rows].astype(BF)
        if extra is None:
            put(out_ref.at[k], part)
        else:
            out_ref[k] = jnp.zeros(out_ref.shape[1:], BF)
            out_ref[k, :rows, : part.shape[1]] = part
            out_ref[k, rows : rows + 3 * extra.shape[0], :] = split_rows(extra[...]).astype(BF)


def layers_kernel(nz, zed_ref, x_ref, *outs):
    total = jnp.sum(x_ref[...].astype(F32), axis=0)
    rows = total.shape[0] // nz
    for k, out in enumerate(outs):
        want = zed_ref[0] ^ k
        value = total[:rows]
        for z in range(1, nz):
            value = jnp.where(want == z, total[z * rows : (z + 1) * rows], value)
        out[...] = value.astype(BF)


def deal_last_kernel(rows, extra, x_ref, out_ref):
    total = jnp.sum(x_ref[...].astype(F32), axis=0)
    each = rows // out_ref.shape[0]
    small = total[rows : rows + extra]
    for i in range(1, 3):
        small = small + total[rows + i * extra : rows + (i + 1) * extra]
    small = split_rows(small).astype(BF)
    for i in range(out_ref.shape[0]):
        out_ref[i] = jnp.zeros(out_ref.shape[1:], BF)
        out_ref[i, :each, :] = total[i * each : (i + 1) * each].astype(BF)
        out_ref[i, each : each + 3 * extra, :] = small


def deal_kernel(*refs):
    *parts, out_ref = refs
    at = 0
    for part in parts:
        total = jnp.sum(part[...].astype(F32), axis=0)
        rows = total.shape[0] // out_ref.shape[0]
        for i in range(out_ref.shape[0]):
            out_ref[i, at : at + rows, :] = total[i * rows : (i + 1) * rows].astype(BF)
        at += rows


def dh2_kernel(*refs):
    *parts, h_ref, cot_ref, gain_ref, dh_ref, dy_ref, gain_out = refs
    width = h_ref.shape[1]
    grad = parts[0][:, :width].astype(F32)
    for part in parts[1:]:
        grad = grad + part[:, :width].astype(F32)
    dv, gain_out[...] = norm_back(h_ref[...], gain_ref[...], grad)
    dh = cot_ref[:, :width].astype(F32) + dv
    dh_ref[...] = dh
    put(dy_ref, dh.astype(BF))


def dh1_kernel(wide, half, w_ref, dq_ref, cq_ref, h1_ref, dh2_ref, gain_ref, dh_ref, dy_ref, gain_out):
    w = w_ref[0]
    dq = jnp.concatenate([own_of(dq_ref.at[m], w, half)[:, :wide] for m in range(2)], axis=1)
    grad = dot_nt(dq, cq_ref[...])
    dv, gain_out[...] = norm_back(own_of(h1_ref, w, half), gain_ref[...], grad)
    dh = dh2_ref[...] + dv
    dh_ref[...] = dh
    put(dy_ref, dh.astype(BF))


def last_kernel(wide, half, w_ref, d_ref, weight_ref, tok_ref, dh1_ref, gain_ref, out_ref, gain_out):
    w = w_ref[0]
    d = jnp.concatenate(
        [own_of(d_ref.at[m, i], w, half)[:, :wide] for i in range(3) for m in range(2)], axis=1
    )
    grad = dot_nt(d, weight_ref[...])
    dv, gain_out[...] = norm_back(tok_ref[w].astype(F32), gain_ref[...], grad)
    out_ref[...] = dh1_ref[...] + dv


def grad_prep_kernel(nh, hs, dy_ref, w_ref, o_ref, out_ref, de_ref, dh_ref, del_ref):
    wide = nh * hs
    dy = in_blocks(dy_ref)[:, : w_ref.shape[1]]
    out_ref[...] = dy
    da = dot_nt(dy, w_ref[...]).astype(BF)
    da = jnp.concatenate([da, jnp.zeros((da.shape[0], 2 * BLK - wide), BF)], axis=1)
    terms = da.astype(F32) * o_ref[...]
    delta = [jnp.sum(head_mask(terms, h, hs), axis=1, keepdims=True) for h in range(nh)]
    dh_ref[...] = pltpu.roll(da.astype(F32), hs, 1).astype(BF)
    lane = lane_of(del_ref.shape)
    cols = jnp.zeros(del_ref.shape, F32)
    for h in range(nh):
        cols = jnp.where(lane == h, delta[h], cols)
    del_ref[...] = cols
    de = pieces_into(da.astype(F32), [-t for t in delta], wide).astype(BF)
    for i in range(de_ref.shape[0]):
        de_ref[i] = de


def grad_prep(dy, weight, o, nh, hs, copies=1, deps=()):
    rows, width = o.shape[0], weight.shape[1]
    return plain(
        functools.partial(grad_prep_kernel, nh, hs),
        [],
        [dy, weight, o],
        [
            bf_shape(rows, width),
            bf_shape(copies, rows, 2 * BLK),
            bf_shape(rows, 2 * BLK),
            f32_shape(rows, BLK),
        ],
        deps=deps,
    )


def local(
    tokens,
    encoded,
    cotangent,
    assign,
    bucket_ids,
    gain_self,
    gain_cross,
    gain_ffn,
    query_weight,
    key_weight,
    value_weight,
    out_weight,
    cross_query,
    cross_key,
    cross_value,
    cross_out,
    gate_weight,
    up_weight,
    down_weight,
    bucket_table,
):
    nctx = lax.axis_size("ctx")
    nw = lax.axis_size("wsh")
    c = lax.axis_index("ctx")
    w = lax.axis_index("wsh")
    both = ("ctx", "wsh")
    rows, width = tokens.shape
    half = rows // 2
    length = rows * nw * nctx
    buckets, heads = bucket_table.shape
    inner = query_weight.shape[1]
    hs = inner // heads
    nh = heads // nw
    wide = nh * hs
    plane = 4
    nz = nctx // plane
    spot = (c % plane) * nw + w
    zed = c // plane
    hidden = gate_weight.shape[1]
    share = hidden // (nctx * nw)
    slot = -(-share // 32) * 32

    def pair(x, axis=0, tiled=True):
        return lax.all_gather(x, "wsh", axis=axis, tiled=tiled)

    def halves(parts):
        return lax.all_to_all(parts, "wsh", 0, 0, tiled=True)

    def mate(x):
        return lax.ppermute(x, "wsh", [(i, (i + 1) % nw) for i in range(nw)])

    planes = [[z * plane + i for i in range(plane)] for z in range(nz)]
    columns = [[z * plane + i for z in range(nz)] for i in range(plane)]

    def in_plane(x):
        return lax.all_to_all(x, "ctx", 0, 0, tiled=True, axis_index_groups=planes)

    def in_column(x):
        return lax.all_to_all(x, "ctx", 0, 0, tiled=True, axis_index_groups=columns)

    padded = -(-width // BLK) * BLK

    def spread(parts, count, deps=()):
        shape = bf_shape(count, len(parts) * parts[0].shape[0], parts[0].shape[1])
        return plain(spread_kernel, [], parts, [shape], (0, 1e6, 0), deps)[0]

    def add(a, b, deps=()):
        return plain(add_kernel, [], [a, b], [bf_shape(rows, padded)] * plane, (0, 1e6, 0), deps)

    def deal(parts, count, deps=()):
        shape = bf_shape(count, sum(x.shape[1] for x in parts) // count, parts[0].shape[2])
        return plain(deal_kernel, [], parts, [shape], (0, 1e6, 0), deps)[0]

    def tree(parts):
        while len(parts) > 1:
            parts = [parts[i] + parts[i + 1] for i in range(0, len(parts), 2)]
        return parts[0]

    def near(x, k):
        return lax.ppermute(x, "ctx", [(i, i ^ k) for i in range(nctx)])

    def stacked(parts, deps=()):
        shape = bf_shape(len(parts) * parts[0].shape[0], parts[0].shape[1])
        return plain(join_kernel, [], parts, [shape], (0, 1e6, 0), deps)[0]

    cut = inner // (nctx * nw)

    def targets(count):
        index = jnp.arange(plane * nz * count * cut, dtype=jnp.int32)
        to_k, to_z = index // (nz * count * cut), index // (count * cut) % nz
        to_i, to_t = index // cut % count, index % cut
        column = ((to_z * plane + to_k) * nw + w) * cut + to_t
        which = jnp.arange(count, dtype=jnp.int32)
        return jnp.where(to_i[:, None] == which[None, :], column[:, None], -1).astype(jnp.int32)

    def owner_parts(plan, xs, ys, small=None, deps=()):
        count = sum(len(group) for group in plan)
        total = nz * count * cut
        if small is not None:
            total = -(-(total + 3 * small.shape[0]) // 16) * 16
            ys = ys + [small]
        return plain(
            functools.partial(owners_kernel, wide, plan),
            [],
            [targets(count)] + xs + ys,
            [bf_shape(plane, total, padded)],
            (3e9, 6e6, 0),
            deps,
        )[0]

    def layers(x, deps=()):
        return plain(
            functools.partial(layers_kernel, nz),
            [zed.astype(jnp.int32)[None]],
            [x],
            [bf_shape(x.shape[1] // nz, x.shape[2])] * nz,
            (0, 1e6, 0),
            deps,
        )

    def owner_sums(total, count):
        return [total[i * cut : (i + 1) * cut, :width] for i in range(count)]

    lanes = jnp.arange(nctx, dtype=jnp.int32)
    owner = jnp.sum(jnp.where(assign[None, :] == lanes[:, None], lanes[None, :], 0), axis=1)
    chip_slot = owner % plane * nz + (owner // plane ^ zed)
    near_slot = (owner ^ c) % plane * nz + owner // plane
    meta = jnp.concatenate([owner, jnp.take(assign, c)[None], chip_slot, near_slot])
    meta = meta.astype(jnp.int32)
    core = w.astype(jnp.int32)[None]
    chip = nw * rows

    gains = pair(jnp.stack([gain_self, gain_cross, gain_ffn]), axis=1).astype(F32)
    gains = [gains[i : i + 1] for i in range(3)]
    tok = pair(tokens, tiled=False)

    def head_parts(weights, deps=()):
        count = len(weights) * wide
        shape = bf_shape(nw, weights[0].shape[0], -(-count // BLK) * BLK)
        return plain(functools.partial(heads_kernel, wide), [], weights, [shape], deps=deps)[0]

    g_own = jnp.pad(cotangent, ((0, 0), (0, padded - width)))
    g_parts = [g_own] + [near(g_own, k) for k in range(1, plane)]
    all_heads = halves(
        head_parts(
            [key_weight, value_weight, cross_key, cross_value, query_weight, cross_query]
        )
    )
    n1, q, k_own, v_own, kv_own = plain(
        functools.partial(project_kernel, wide),
        [],
        [tok, all_heads, gains[0]],
        [bf_shape(chip, width)] + [bf_shape(chip, 2 * BLK)] * 3 + [bf_shape(nz, chip, 2 * wide)],
    )

    kv = in_column(kv_own).reshape(-1, 2 * wide)

    hot = (bucket_ids[None, :] == jnp.arange(buckets, dtype=jnp.int32)[:, None]).astype(BF)
    values = dot_tn(lax.dynamic_slice_in_dim(bucket_table, w * nh, nh, 1), hot)
    lines = bias_rows(values)

    enc_pair = pair(encoded)
    (ekv_own,) = plain(
        functools.partial(encode_kernel, wide),
        [],
        [enc_pair, all_heads],
        [bf_shape(enc_pair.shape[0], 4 * BLK)],
        deps=(kv, *g_parts[1:], *lines),
    )

    kv = [kv] + [near(kv, k) for k in range(1, plane)]

    ts, tt = bias_tiles(*lines, deps=(kv[0], ekv_own))

    ekv = lax.all_gather(ekv_own, "ctx", axis=0, tiled=True)
    spots = jnp.stack([(c % plane) * nw + i for i in (w, 1 - w)]).astype(jnp.int32)
    ug_own, ug_sent, wd_own, wd_sent = plain(
        functools.partial(units_kernel, nz, plane * nw, share, slot),
        [spots],
        [gate_weight, up_weight, down_weight.T],
        [bf_shape(gate_weight.shape[0], 2 * nz * slot)] * 2
        + [bf_shape(width, nz // nw * slot)] * 2,
        deps=(ts,),
    )
    g_plane = stacked(g_parts, deps=(ug_own,))
    out_mate, cross_out_mate = mate(out_weight), mate(cross_out)
    o1, a1, qe1, lse1 = self_fwd(
        meta, q, kv, ts, nh, hs, deps=(g_plane, out_mate, cross_out_mate)
    )
    a1_pair = pair(a1, tiled=False)
    h1, n2, cq = plain(
        functools.partial(middle_kernel, wide),
        [core],
        [tok, a1_pair, out_weight, out_mate, gains[1], all_heads],
        [f32_shape(chip, width), bf_shape(chip, width), bf_shape(chip, 2 * BLK)],
    )
    qg = lax.all_gather(qe1, "ctx", axis=0, tiled=True).reshape(nctx, chip, 2 * BLK)
    cq_full, ck_full, cv_full = pair(cross_query), pair(cross_key), pair(cross_value)
    qkv_full = pair(jnp.concatenate([query_weight, key_weight, value_weight], axis=1))

    o2, a2, qe2 = cross_fwd(cq, ekv, nh, hs)
    a2_pair = pair(a2, tiled=False)
    h2, n3 = plain(
        functools.partial(third_kernel, half),
        [core],
        [h1, a2_pair, cross_out, cross_out_mate, gains[2]],
        [f32_shape(rows, width), bf_shape(rows, padded)],
    )

    ug_sent, wd_sent, g_plane, _ = lax.optimization_barrier((ug_sent, wd_sent, g_plane, a2_pair))
    g_plane = g_plane, mate(g_plane)
    ug, wd = plain(
        order_kernel,
        [core],
        [ug_own, mate(ug_sent), wd_own, mate(wd_sent)],
        [bf_shape(width, 2 * nz * slot), bf_shape(width, nz * slot)],
        deps=(n3,),
    )
    (dact,) = plain(
        ffn_early_kernel, [], [*g_plane, wd], [f32_shape(nw * plane * rows, nz * slot)], deps=(n3,)
    )
    n3_plane = stacked([n3] + [near(n3, k) for k in range(1, plane)], deps=(dact,))
    n3_plane = n3_plane, mate(n3_plane)
    act, dgu, dn0, dn1 = ffn_both(n3_plane, dact, ug)
    sent = add(dn0, mate(dn1))
    got = [near(sent[k], k) for k in range(1, plane)]
    ffn, out0, out1 = ffn_late(n3_plane, g_plane, act, dgu, wd, nz, share, (sent[0], qg))
    dh2, dy2, gain3 = plain(
        dh2_kernel,
        [],
        [sent[0]] + got + [h2, g_own, gains[2]],
        [f32_shape(rows, width), bf_shape(rows, padded), f32_shape(1, width)],
        deps=(out0,),
    )

    dy2, de2, _, _ = grad_prep(pair(dy2, tiled=False), cross_out, o2, nh, hs)
    dcq, dekv = cross_bwd(qe2, de2[0], ekv, plane, nz, nh, hs)
    dekv = in_plane(dekv.reshape(plane, -1, 2 * wide))
    dcq_pair = pair(dcq, tiled=False)
    dh1, dy1, gain2 = plain(
        functools.partial(dh1_kernel, wide, half),
        [core],
        [dcq_pair, cq_full, h1, dh2, gains[1]],
        [f32_shape(rows, width), bf_shape(rows, padded), f32_shape(1, width)],
    )

    dy1, de1, dhi1, delta1 = grad_prep(pair(dy1, tiled=False), out_weight, o1, nh, hs)
    dg = [de1[0]] + [near(de1[0], plane * k) for k in range(1, nz)]
    dekv = layers(dekv, deps=(de1,))
    dg = spread(dg, plane, deps=(dekv[0], qg, ck_full, cv_full, qkv_full))
    spread_out = dg
    dekv = [dekv[0]] + [near(dekv[k], plane * k) for k in range(1, nz)]

    dq, rev = self_dq(meta, q, dhi1, lse1, delta1, kv, ts, nh, hs, deps=(dg,))
    dg = in_plane(dg).reshape(nctx, chip, 2 * BLK)
    (dekv,) = plain(output_kernel, [], dekv, [bf_shape(*dekv[0].shape)], deps=(dq,))
    dekv_pair = pair(dekv, tiled=False)
    made = owner_parts(
        ((((0,), 0),), (((1,), 0),), (((2,), 0),), (((3,), 0), ((3,), wide))),
        [a1_pair, a2_pair, dcq_pair, dekv_pair],
        [dy1, dy2, n2, enc_pair],
        deps=(dq,),
    )
    ffn = lax.psum_scatter(
        tie(ffn, spread_out).reshape(nz, 3 * share, padded),
        "ctx",
        scatter_dimension=0,
        axis_index_groups=columns,
        tiled=True,
    )
    dk, dv = self_dkv(meta, k_own, v_own, qg, dg, tt, nh, hs, deps=(made, dq))
    made = in_plane(made)
    rev = tie(rev, dk)

    dqkv_pair = pair(jnp.stack([dq, dk, dv]), tiled=False).reshape(nw, 3, chip, 2 * BLK)
    tokens_grad, gain1 = plain(
        functools.partial(last_kernel, wide, half),
        [core],
        [dqkv_pair, qkv_full, tok, dh1, gains[0]],
        [f32_shape(rows, width), f32_shape(1, width)],
    )

    rev = rev.reshape(nh, 8, -1)
    by_distance = sum(rev[:, i, 1 + i : 1 + i + length] for i in range(8))
    hot_rev = (
        jnp.flip(bucket_ids)[None, :] == jnp.arange(buckets, dtype=jnp.int32)[:, None]
    ).astype(F32)
    table_own = lax.dot_general(
        hot_rev, by_distance, (((1,), (1,)), ((), ())), precision=lax.Precision.HIGHEST
    )
    table = lax.dynamic_update_slice_in_dim(
        jnp.zeros((buckets, heads), F32), table_own, w * nh, 1
    )

    small = jnp.concatenate([gain1[0], gain2[0], gain3[0], table.reshape(-1)])
    small = jnp.pad(small, (0, -small.shape[0] % padded)).reshape(-1, padded)
    extra = small.shape[0]
    plan = ((((0, 0), 0), ((0, 1), 0), ((0, 2), 0)),)
    second = owner_parts(plan, [dqkv_pair], [n1], small)
    second = in_plane(tie(second, made))
    first = layers(made)
    out_sent = add(out0, mate(tie(out1, gain1)), deps=(made,))
    first = [first[0]] + [near(first[k], plane * k) for k in range(1, nz)]
    (second,) = plain(
        functools.partial(deal_last_kernel, 3 * nz * cut, extra),
        [],
        [second],
        [bf_shape(nz, -(-(3 * cut + 3 * extra) // 16) * 16, padded)],
        deps=(first[0], out_sent[0]),
    )
    dealt = second
    out_sent = [tie(m, second) for m in out_sent[1:]], out_sent[0]
    out_got = [near(m, k + 1) for k, m in enumerate(out_sent[0])]
    dekv_pair = tie(dekv_pair, second)
    second = jnp.sum(in_column(second).astype(F32), axis=0)
    small = [second[3 * cut + i * extra : 3 * cut + (i + 1) * extra] for i in range(3)]
    small = (small[0] + small[1]) + small[2]
    small = small + mate(small)
    q_t, k_t, v_t = owner_sums(second, 3)
    (first,) = plain(output_kernel, [], first, [f32_shape(5 * cut, padded)], deps=(dealt,))
    out_share, cross_out_share, cq_t, ck_t, cv_t = owner_sums(first, 5)
    ffn = ffn[0, :, :width].astype(F32).reshape(3, share, width)

    def joined(x):
        return jnp.swapaxes(x[:, :, :wide], 0, 1).reshape(-1, inner)

    def own_encoder(x):
        return lax.dynamic_slice_in_dim(x, w * encoded.shape[0], encoded.shape[0], 0)

    dek, dev = joined(dekv_pair), joined(dekv_pair[:, :, wide:])
    encoded_grad = dot_nt(own_encoder(dek), ck_full) + dot_nt(own_encoder(dev), cv_full)
    (output,) = plain(
        output_kernel,
        [],
        [h2, out_sent[1]] + out_got,
        [bf_shape(rows, width)],
        deps=(second, ffn, encoded_grad),
    )

    small = small.reshape(-1)
    table = small[3 * width : 3 * width + buckets * heads].reshape(buckets, heads)
    return (
        output,
        tokens_grad,
        encoded_grad,
        small[:width],
        small[width : 2 * width],
        small[2 * width : 3 * width],
        q_t.T,
        k_t.T,
        v_t.T,
        out_share,
        cq_t.T,
        ck_t.T,
        cv_t.T,
        cross_out_share,
        ffn[0].T,
        ffn[1].T,
        ffn[2],
        table,
    )


def solution(mesh):
    rows = P(("seq", "ctx", "wsh"), None)
    cols = P("seq", ("ctx", "wsh"))
    split = P("wsh", None)
    return jax.shard_map(
        local,
        mesh=mesh,
        in_specs=(rows, rows, rows, P(), P(), P("wsh"), P("wsh"), P("wsh"))
        + (split,) * 11
        + (P(),),
        out_specs=(
            rows,
            rows,
            rows,
            P("seq"),
            P("seq"),
            P("seq"),
            cols,
            cols,
            cols,
            rows,
            cols,
            cols,
            cols,
            rows,
            cols,
            cols,
            rows,
            P("seq", None),
        ),
        check_vma=False,
    )
```
